32 devices in a mesh: group: 4 (over y, core), dp: 4 (over z), tensor: 2 (over x).
Axes of the slice: x: 2, y: 2, z: 4, core: 2. Of those that a mesh axis runs over, the one named last changes fastest.
Arguments:
- patches: bfloat16 [2, 4, 4, 1568, 1536], P(None, 'group', 'dp'), may hold values from -6 to 6
- visible: int32 [2, 4, 4, 160], P(None, 'group', 'dp'), may hold values from 0 to 1567, as said below
- frames_valid: int32 [2, 4, 4], P(None, 'group', 'dp'), may hold values from 1 to 8, as said below
- clip_valid: int32 [2, 4, 4], P(None, 'group', 'dp'), may hold values from 0 to 1, as said below
- rep_weights: float32 [2076672], P('dp'), may hold values from -6 to 6
- ten_weights: float32 [2, 4423680], P('tensor', 'dp'), may hold values from -6 to 6
- rep_m: float32 [4, 2076672], P('group', 'dp'), may hold values from -1 to 1
- rep_v: float32 [4, 2076672], P('group', 'dp'), may hold values from 0 to 1
- ten_m: float32 [4, 2, 4423680], P('group', 'tensor', 'dp'), may hold values from -1 to 1
- ten_v: float32 [4, 2, 4423680], P('group', 'tensor', 'dp'), may hold values from 0 to 1
- rep_outer: float32 [2076672], P('dp'), may hold values from -1 to 1
- ten_outer: float32 [2, 4423680], P('tensor', 'dp'), may hold values from -1 to 1
Outputs:
- loss_sum: float32 [2, 4], P(None, 'group')
- loss_count: float32 [2, 4], P(None, 'group')
- clip_norm: float32 [2, 4], P(None, 'group')
- rep_first: float32 [4, 2076672], P('group', 'dp')
- rep_second: float32 [4, 2076672], P('group', 'dp')
- ten_first: float32 [4, 2, 4423680], P('group', 'tensor', 'dp')
- ten_second: float32 [4, 2, 4423680], P('group', 'tensor', 'dp')
- rep_diff: float32 [2076672], P('dp')
- ten_diff: float32 [2, 4423680], P('tensor', 'dp')
- rep_momentum: float32 [2076672], P('dp')
- ten_momentum: float32 [2, 4423680], P('tensor', 'dp')
- rep_master: float32 [2076672], P('dp')
- ten_master: float32 [2, 4423680], P('tensor', 'dp')
The draws below stay inside these ranges and needn't reach their ends.
Inputs may be any that keep to these rules, and one draw needn't show every extreme that they name: `visible`: each clip's indices are distinct and ascending. `frames_valid`: the last clip slot of every inner step and group holds all 8 time positions. `clip_valid`: clip slot 0 of every inner step and group is real.
All inputs are finite; a program needn't handle non-finite values.
Results may differ from the reference program's by a relative error of at most 0.0033.
The reference program's roundings to bfloat16 on the way count: a program that leaves them out, or rounds other values in their place, can miss the bound.
Values may be sent and summed in bfloat16 or wider, within the bound.
A program may use at most 384 MiB of HBM per device.

```python
import math
import jax
import jax.numpy as jnp
from jax import lax

D = 768
HDIM = 64
FF = 3072
DD = 384
DFF = 1536
PATCH = 1536
TUBES = 1568
FRAMES = 8
VIS = 160
STEPS = 2
STEP_BEFORE = 6
CLIPS = 4
GROUPS = 4
TSPLIT = 2
PR = 2076672
PT = 4423680


CLIP = 0.001


def grad_entry():
    return CLIP / math.sqrt(PR + TSPLIT * PT)


def fill_flat(key, layout):
    pieces = []
    for number, (length, draw_kind, spread) in enumerate(layout):
        sub_key = jax.random.fold_in(key, number)
        if draw_kind == 'gain':
            pieces.append(0.6 + 0.8 * jax.random.uniform(sub_key, (length,), jnp.float32))
        else:
            pieces.append(spread * jnp.clip(jax.random.normal(sub_key, (length,), jnp.float32), -5.0, 5.0))
    return jnp.concatenate(pieces)


def rep_layout():
    layout = [(PATCH * D, 'normal', PATCH ** (-0.5)), (D * DD, 'normal', D ** (-0.5)), (DD * PATCH, 'normal', DD ** (-0.5))]
    enc_rows = ['bias', 'gain', 'bias', 'bias', 'gain', 'bias', 'bias', 'gain', 'bias']
    dec_rows = ['bias', 'token', 'gain', 'bias', 'bias', 'gain', 'bias', 'bias', 'gain', 'bias']
    layout += [(D, draw_kind, 0.2) for draw_kind in enc_rows]
    layout += [(DD, draw_kind, 1.0 if draw_kind == 'token' else 0.2) for draw_kind in dec_rows]
    layout += [(PATCH, 'bias', 0.2)]
    return layout


def ten_layout():
    enc_cols = D // TSPLIT
    dec_cols = DD // TSPLIT
    return [(D * 3 * enc_cols, 'normal', D ** (-0.5)), (enc_cols * D, 'normal', VIS ** 0.5 / (2.0 * D ** 0.5)), (D * (FF // TSPLIT), 'normal', D ** (-0.5)), (FF // TSPLIT * D, 'normal', FF ** (-0.5)), (DD * 3 * dec_cols, 'normal', DD ** (-0.5)), (dec_cols * DD, 'normal', TUBES ** 0.5 / (2.0 * DD ** 0.5)), (DD * (DFF // TSPLIT), 'normal', DD ** (-0.5)), (DFF // TSPLIT * DD, 'normal', DFF ** (-0.5))]


def first_moment(key, dims):
    return 0.111 * grad_entry() * jnp.clip(jax.random.normal(key, dims, jnp.float32), -5.0, 5.0)


def second_moment(key, dims):
    factor = jnp.exp(jax.random.uniform(key, dims, jnp.float32, math.log(0.5), math.log(8.0)))
    return 0.0526 * grad_entry() ** 2 * factor


def draw_visible(key, part):
    key = jax.random.fold_in(key, 11)
    keys_all = jax.random.split(key, STEPS * GROUPS * CLIPS)
    chosen = jax.vmap(lambda sub_key: jnp.sort(jax.random.permutation(sub_key, TUBES)[:VIS]))(keys_all)
    return chosen.reshape(STEPS, GROUPS, CLIPS, VIS).astype(jnp.int32)


def draw_frames_valid(key, part):
    key = jax.random.fold_in(key, 12)
    clip_ids = jnp.arange(CLIPS)
    lowest = max(FRAMES // 3, 1)
    base_frames = lowest + (FRAMES - lowest) * clip_ids // max(CLIPS - 1, 1)
    jitter = jax.random.randint(key, (STEPS, GROUPS, CLIPS), 0, 2)
    frames = jnp.clip(base_frames[None, None, :] - jitter, 1, FRAMES)
    frames = jnp.where(clip_ids[None, None, :] == CLIPS - 1, FRAMES, frames)
    return frames.astype(jnp.int32)


def draw_clip_valid(key, part):
    key = jax.random.fold_in(key, 13)
    keep = (jax.random.randint(key, (STEPS, GROUPS, CLIPS), 0, 3) > 0).astype(jnp.int32)
    return keep.at[:, :, 0].set(1)


def draw_rep_weights(key, part):
    key = jax.random.fold_in(key, 21)
    return fill_flat(key, rep_layout())


def draw_ten_weights(key, part):
    key = jax.random.fold_in(key, 22)
    return jnp.stack([fill_flat(jax.random.fold_in(key, rank), ten_layout()) for rank in range(TSPLIT)])


def draw_rep_m(key, part):
    key = jax.random.fold_in(key, 31)
    return first_moment(key, (GROUPS, PR))


def draw_rep_v(key, part):
    key = jax.random.fold_in(key, 32)
    return second_moment(key, (GROUPS, PR))


def draw_ten_m(key, part):
    key = jax.random.fold_in(key, 33)
    return first_moment(key, (GROUPS, TSPLIT, PT))


def draw_ten_v(key, part):
    key = jax.random.fold_in(key, 34)
    return second_moment(key, (GROUPS, TSPLIT, PT))


def draw_rep_outer(key, part):
    key = jax.random.fold_in(key, 41)
    return 0.01 * jnp.clip(jax.random.normal(key, (PR,), jnp.float32), -5.0, 5.0)


def draw_ten_outer(key, part):
    key = jax.random.fold_in(key, 42)
    return 0.01 * jnp.clip(jax.random.normal(key, (TSPLIT, PT), jnp.float32), -5.0, 5.0)


def levels(rng, shape, cuts, low, largest):
    def one(position, blocks):
        heights = jax.random.uniform(jax.random.fold_in(jax.random.fold_in(rng, 6), position), (blocks,), jnp.float32, low / len(cuts), largest / len(cuts))
        return jnp.repeat(jnp.exp(heights), shape[position] // blocks).reshape((-1,) + (1,) * (len(shape) - position - 1))

    loudness = one(*cuts[0])
    for cut in cuts[1:]:
        loudness = loudness * one(*cut)
    return loudness


def centred(own_key, extent, scale, bound, cuts=(), dtype=jnp.bfloat16):
    array = scale * jax.random.normal(own_key, extent, jnp.float32)
    if cuts:
        array = array * levels(own_key, extent, cuts, -0.22, 0.18)
    return jnp.clip(array, -bound, bound).astype(dtype)


def setup_inputs(seed: int = 0) -> dict:
    keys = jax.random.split(jax.random.key(seed), 13)
    patches = centred(keys[0], (STEPS, GROUPS, CLIPS, TUBES, PATCH), 1.0, 6.0, ((1, 4), (2, 4)))
    visible = draw_visible(jax.random.fold_in(keys[12], 71), 0)
    frames_valid = draw_frames_valid(jax.random.fold_in(keys[12], 71), 0)
    clip_valid = draw_clip_valid(jax.random.fold_in(keys[12], 71), 0)
    rep_weights = draw_rep_weights(jax.random.fold_in(keys[12], 71), 0)
    ten_weights = draw_ten_weights(jax.random.fold_in(keys[12], 71), 0)
    rep_m = draw_rep_m(jax.random.fold_in(keys[12], 71), 0)
    rep_v = draw_rep_v(jax.random.fold_in(keys[12], 71), 0)
    ten_m = draw_ten_m(jax.random.fold_in(keys[12], 71), 0)
    ten_v = draw_ten_v(jax.random.fold_in(keys[12], 71), 0)
    rep_outer = draw_rep_outer(jax.random.fold_in(keys[12], 71), 0)
    ten_outer = draw_ten_outer(jax.random.fold_in(keys[12], 71), 0)
    return {"patches": patches, "visible": visible, "frames_valid": frames_valid, "clip_valid": clip_valid, "rep_weights": rep_weights, "ten_weights": ten_weights, "rep_m": rep_m, "rep_v": rep_v, "ten_m": ten_m, "ten_v": ten_v, "rep_outer": rep_outer, "ten_outer": ten_outer}


CLIP = 0.001
LR_IN = 0.01
BETA1 = 0.9
BETA2 = 0.95
EPS = 1e-08
DECAY = 0.05
LR_OUT = 0.7
MOMENTUM = 0.9
HIGH = lax.Precision.HIGHEST

@jax.custom_vjp
def low(v):
    return lax.optimization_barrier(v.astype(jnp.bfloat16)).astype(jnp.float32)

@jax.custom_vjp
def low_back(v):
    return v

def low_keep(v):
    return (low(v), None)

def low_pass(kept, grad):
    return (grad,)

def back_keep(v):
    return (v, None)

def back_low(kept, grad):
    return (low(grad),)
low.defvjp(low_keep, low_pass)
low_back.defvjp(back_keep, back_low)

def matmul(left, right):
    return jnp.dot(left, right, precision=HIGH)

def sinus(count, width):
    places = jnp.arange(count).astype(jnp.float32)[:, None]
    column = jnp.arange(width)
    decays = jnp.power(10000.0, -2.0 * (column // 2).astype(jnp.float32) / width)
    angles = places * decays[None, :]
    return jnp.where(column % 2 == 0, jnp.sin(angles), jnp.cos(angles)).astype(jnp.float32)

def layer_norm(stream, gain, bias):
    center = lax.optimization_barrier(jnp.mean(stream, -1, keepdims=True))
    spread = lax.optimization_barrier(jnp.mean((stream - center) ** 2, -1, keepdims=True))
    return (stream - center) * lax.rsqrt(spread + 1e-06) * gain + bias

def split_flat(flat, shapes):
    pieces = []
    offset = 0
    for shapes_one in shapes:
        length = math.prod(shapes_one)
        pieces.append(flat[offset:offset + length].reshape(shapes_one))
        offset += length
    return pieces

def rep_shapes():
    return [(PATCH, D), (D, DD), (DD, PATCH), (9, D), (10, DD), (PATCH,)]

def ten_shapes(splits):
    enc_cols = D // splits
    dec_cols = DD // splits
    return [(D, 3 * enc_cols), (enc_cols, D), (D, FF // splits), (FF // splits, D), (DD, 3 * dec_cols), (dec_cols, DD), (DD, DFF // splits), (DFF // splits, DD)]

def join_mats(rank_pieces, first):
    qkv_parts = [pieces[first] for pieces in rank_pieces]
    column_count = qkv_parts[0].shape[1] // 3
    full_qkv = jnp.concatenate([jnp.concatenate([piece_qkv[:, third_id * column_count:(third_id + 1) * column_count] for piece_qkv in qkv_parts], 1) for third_id in range(3)], 1)
    w_out = jnp.concatenate([pieces[first + 1] for pieces in rank_pieces], 0)
    w_up = jnp.concatenate([pieces[first + 2] for pieces in rank_pieces], 1)
    w_down = jnp.concatenate([pieces[first + 3] for pieces in rank_pieces], 0)
    return (full_qkv, w_out, w_up, w_down)

def block(stream, mats, vecs):
    w_qkv, w_out, w_up, w_down = mats
    gain_one, bias_one, out_bias, gain_two, bias_two, down_bias = vecs
    head_cols = w_out.shape[0]
    nheads = head_cols // HDIM
    length = stream.shape[0]
    normed = low(layer_norm(stream, gain_one, bias_one))
    joined = low(low_back(matmul(normed, w_qkv)))
    queries, key_rows, values = [joined[:, third_id * head_cols:(third_id + 1) * head_cols].reshape(length, nheads, HDIM) for third_id in range(3)]
    scores = low_back(jnp.einsum('qhd,khd->hqk', queries, key_rows, precision=HIGH) * HDIM ** (-0.5))
    probs = low(jax.nn.softmax(scores, axis=-1))
    blended = low(low_back(jnp.einsum('hqk,khd->qhd', probs, values, precision=HIGH))).reshape(length, head_cols)
    attended = stream + low_back(matmul(blended, w_out)) + out_bias
    second = low(layer_norm(attended, gain_two, bias_two))
    upward = low_back(matmul(second, w_up))
    activated = low(jax.nn.gelu(upward, approximate=False))
    return attended + low_back(matmul(activated, w_down)) + down_bias

def clip_loss(rep, ten, patch, visible_ids, weight_row):
    patch_w, e2d_w, head_w, enc_vec, dec_vec, head_b = split_flat(low(rep), rep_shapes())
    ten_low = low(ten)
    rank_pieces = [split_flat(ten_low[rank], ten_shapes(TSPLIT)) for rank in range(TSPLIT)]
    enc_mats = join_mats(rank_pieces, 0)
    dec_mats = join_mats(rank_pieces, 4)
    pixels = patch.astype(jnp.float32)
    shown_rows = pixels[visible_ids]
    embedded = low_back(matmul(shown_rows, patch_w)) + enc_vec[0] + sinus(TUBES, D)[visible_ids]
    encoded = block(embedded, enc_mats, [enc_vec[i] for i in range(1, 7)])
    final_enc = low(layer_norm(encoded, enc_vec[7], enc_vec[8]))
    reduced = low_back(matmul(final_enc, e2d_w)) + dec_vec[0]
    tokens_in = jnp.broadcast_to(dec_vec[1], (TUBES, DD)).at[visible_ids].set(reduced) + sinus(TUBES, DD)
    decoded = block(tokens_in, dec_mats, [dec_vec[i] for i in range(2, 8)])
    final_dec = low(layer_norm(decoded, dec_vec[8], dec_vec[9]))
    predicted = low_back(matmul(final_dec, head_w)) + head_b
    center = lax.optimization_barrier(jnp.mean(pixels, -1, keepdims=True))
    spread = lax.optimization_barrier(jnp.mean((pixels - center) ** 2, -1, keepdims=True))
    target = (pixels - center) * lax.rsqrt(spread + 1e-06)
    errors = lax.optimization_barrier(jnp.mean((predicted - target) ** 2, -1))
    return jnp.sum(errors * weight_row)

def adamw(master, first, second, clipped, number):
    first = BETA1 * first + (1 - BETA1) * clipped
    second = BETA2 * second + (1 - BETA2) * clipped * clipped
    first_hat = first / (1 - BETA1 ** number)
    second_hat = second / (1 - BETA2 ** number)
    master = master - LR_IN * (first_hat / (jnp.sqrt(second_hat) + EPS) + DECAY * master)
    return (master, first, second)

def reference(patches, visible, frames_valid, clip_valid, rep_weights, ten_weights, rep_m, rep_v, ten_m, ten_v, rep_outer, ten_outer):
    tube_ids = jnp.arange(TUBES)
    losses, counts, norms = ([], [], [])
    rep_firsts, rep_seconds, ten_firsts, ten_seconds, rep_changes, ten_changes = ([], [], [], [], [], [])
    for group_id in range(GROUPS):
        rep, ten = (rep_weights, ten_weights)
        rep_first, rep_second = (rep_m[group_id], rep_v[group_id])
        ten_first, ten_second = (ten_m[group_id], ten_v[group_id])
        step_losses, step_counts, step_norms = ([], [], [])
        for inner_step in range(STEPS):
            visible_ids = visible[inner_step, group_id]
            shown = jnp.any(visible_ids[:, :, None] == tube_ids[None, None, :], axis=1)
            weight_rows = (jnp.where(shown, 0.0, 1.0) * (tube_ids[None, :] // (TUBES // FRAMES) < frames_valid[inner_step, group_id][:, None]) * (clip_valid[inner_step, group_id][:, None] == 1)).astype(jnp.float32)

            def one_clip(carry, item):
                patch, clip_ids, weight_row = item
                value, pull = jax.vjp(lambda rep_in, ten_in: clip_loss(rep_in, ten_in, patch, clip_ids, weight_row), rep, ten)
                rep_grad, ten_grad = pull(jnp.ones((), jnp.float32))
                return ((carry[0] + value, carry[1] + rep_grad, carry[2] + ten_grad), None)
            start_carry = (jnp.zeros((), jnp.float32), jnp.zeros_like(rep), jnp.zeros_like(ten))
            (loss_total, rep_grad, ten_grad), _ = lax.scan(one_clip, start_carry, (patches[inner_step, group_id], visible_ids, weight_rows))
            count_total = jnp.sum(weight_rows)
            norm_value = jnp.sqrt(jnp.sum(rep_grad * rep_grad) + jnp.sum(ten_grad * ten_grad) + 1e-30) / count_total
            factor = jnp.minimum(1.0, CLIP / norm_value) / count_total
            number = STEP_BEFORE + inner_step + 1
            rep, rep_first, rep_second = adamw(rep, rep_first, rep_second, rep_grad * factor, number)
            ten, ten_first, ten_second = adamw(ten, ten_first, ten_second, ten_grad * factor, number)
            step_losses.append(loss_total)
            step_counts.append(count_total)
            step_norms.append(norm_value)
        losses.append(jnp.stack(step_losses))
        counts.append(jnp.stack(step_counts))
        norms.append(jnp.stack(step_norms))
        rep_firsts.append(rep_first)
        rep_seconds.append(rep_second)
        ten_firsts.append(ten_first)
        ten_seconds.append(ten_second)
        rep_changes.append(rep_weights - rep)
        ten_changes.append(ten_weights - ten)
    rep_diff = lax.optimization_barrier(jnp.mean(jnp.stack(rep_changes), 0))
    ten_diff = lax.optimization_barrier(jnp.mean(jnp.stack(ten_changes), 0))
    rep_momentum = MOMENTUM * rep_outer + rep_diff
    ten_momentum = MOMENTUM * ten_outer + ten_diff
    rep_master = rep_weights - LR_OUT * (rep_diff + MOMENTUM * rep_momentum)
    ten_master = ten_weights - LR_OUT * (ten_diff + MOMENTUM * ten_momentum)
    return (jnp.stack(losses, 1), jnp.stack(counts, 1), jnp.stack(norms, 1), jnp.stack(rep_firsts), jnp.stack(rep_seconds), jnp.stack(ten_firsts), jnp.stack(ten_seconds), rep_diff, ten_diff, rep_momentum, ten_momentum, rep_master, ten_master)
```

```python
import functools
import math

import jax
import jax.numpy as jnp
from jax import lax
from jax.experimental import pallas as pl
from jax.experimental.pallas import tpu as pltpu
from jax.sharding import PartitionSpec as P

D = 768
HDIM = 64
FF = 3072
DD = 384
DFF = 1536
PATCH = 1536
TUBES = 1568
FRAMES = 8
STEPS = 2
STEP_BEFORE = 6


CLIP = 0.001
LR_IN = 0.01
BETA1 = 0.9
BETA2 = 0.95
EPS = 1e-08
DECAY = 0.05
LR_OUT = 0.7
MOMENTUM = 0.9
FLOAT = jnp.float32
HALF = jnp.bfloat16


def sinus(count, width):
    places = jnp.arange(count).astype(jnp.float32)[:, None]
    column = jnp.arange(width)
    decays = jnp.power(10000.0, -2.0 * (column // 2).astype(jnp.float32) / width)
    angles = places * decays[None, :]
    return jnp.where(column % 2 == 0, jnp.sin(angles), jnp.cos(angles))


def layer_norm(stream, gain, bias):
    center = jnp.mean(stream, -1, keepdims=True)
    spread = jnp.mean((stream - center) ** 2, -1, keepdims=True)
    return (stream - center) * lax.rsqrt(spread + 1e-06) * gain + bias


def norm_back(stream, gain, bias, cotangent):
    _, pull = jax.vjp(layer_norm, stream, gain, bias)
    return pull(cotangent)


def gelu_exact(values):
    return jax.nn.gelu(values, approximate=False)


def split_flat(flat, shapes):
    pieces = []
    offset = 0
    for shapes_one in shapes:
        length = math.prod(shapes_one)
        pieces.append(flat[offset : offset + length].reshape(shapes_one))
        offset += length
    return pieces


def own_rows(stream, axis_dim):
    count = stream.shape[axis_dim] // lax.axis_size("tensor")
    return lax.dynamic_slice_in_dim(stream, lax.axis_index("tensor") * count, count, axis_dim)


def rows_sum(partial_rows):
    return lax.psum_scatter(partial_rows, "tensor", scatter_dimension=1, tiled=True)


def rows_full(own_part):
    return lax.all_gather(own_part, "tensor", axis=1, tiled=True)


def block_forward(stream, mats, vecs):
    w_qkv, w_out, w_up, w_down = mats
    gain_one, bias_one, out_bias, gain_two, bias_two, down_bias = vecs
    nclips, length, _ = stream.shape
    head_cols = w_out.shape[0]
    nheads = head_cols // HDIM
    normed = layer_norm(stream, gain_one, bias_one).astype(HALF)
    joined = jnp.dot(normed, w_qkv, preferred_element_type=FLOAT).astype(HALF)
    queries, key_rows, values = [
        joined[:, :, third_id * head_cols : (third_id + 1) * head_cols].reshape(
            nclips, length, nheads, HDIM
        )
        for third_id in range(3)
    ]
    scores = jnp.einsum(
        "cqhd,ckhd->chqk", queries, key_rows, preferred_element_type=FLOAT
    ) * HDIM ** (-0.5)
    highest = jnp.max(scores, -1, keepdims=True)
    totals = jnp.log(jnp.sum(jnp.exp(scores - highest), -1, keepdims=True)) + highest
    probs_low = jnp.exp(scores - totals).astype(HALF)
    blended = (
        jnp.einsum("chqk,ckhd->cqhd", probs_low, values, preferred_element_type=FLOAT)
        .astype(HALF)
        .reshape(nclips, length, head_cols)
    )
    attended = (
        rows_sum(jnp.dot(blended, w_out, preferred_element_type=FLOAT))
        + own_rows(stream, 1)
        + out_bias
    )
    second = layer_norm(attended, gain_two, bias_two).astype(HALF)
    second_all = lax.all_gather(second, "tensor", axis=1, tiled=True)
    upward = jnp.dot(second_all, w_up, preferred_element_type=FLOAT)
    activated = gelu_exact(upward).astype(HALF)
    result = (
        rows_sum(jnp.dot(activated, w_down, preferred_element_type=FLOAT)) + attended + down_bias
    )
    stored = (
        stream,
        normed,
        queries,
        key_rows,
        values,
        totals,
        blended,
        attended,
        second_all,
        upward,
        activated,
    )
    return (rows_full(result), stored)


def block_backward(grad_out, mats, vecs, stored):
    w_qkv, w_out, w_up, w_down = mats
    gain_one, bias_one, out_bias, gain_two, bias_two, down_bias = vecs
    (
        stream,
        normed,
        queries,
        key_rows,
        values,
        totals,
        blended,
        attended,
        second_all,
        upward,
        activated,
    ) = stored
    nclips, length, _ = stream.shape
    head_cols = w_out.shape[0]
    grad_low = grad_out.astype(HALF)
    grad_down = jnp.einsum("ctf,ctd->fd", activated, grad_low, preferred_element_type=FLOAT)
    down_bias_grad = jnp.sum(own_rows(grad_out, 1), (0, 1))
    grad_act = jnp.dot(grad_low, w_down.T, preferred_element_type=FLOAT)
    _, gelu_pull = jax.vjp(gelu_exact, upward)
    grad_up_in = gelu_pull(grad_act)[0].astype(HALF)
    grad_up = jnp.einsum("ctd,ctf->df", second_all, grad_up_in, preferred_element_type=FLOAT)
    grad_second = rows_sum(jnp.dot(grad_up_in, w_up.T, preferred_element_type=FLOAT))
    grad_att, gain_two_grad, bias_two_grad = norm_back(attended, gain_two, bias_two, grad_second)
    grad_att = grad_att + own_rows(grad_out, 1)
    out_bias_grad = jnp.sum(grad_att, (0, 1))
    grad_mid = rows_full(grad_att)
    mid_low = grad_mid.astype(HALF)
    grad_wout = jnp.einsum("cth,ctd->hd", blended, mid_low, preferred_element_type=FLOAT)
    nheads = head_cols // HDIM
    grad_blend = (
        jnp.dot(mid_low, w_out.T, preferred_element_type=FLOAT)
        .astype(HALF)
        .reshape(nclips, length, nheads, HDIM)
    )
    scores = jnp.einsum(
        "cqhd,ckhd->chqk", queries, key_rows, preferred_element_type=FLOAT
    ) * HDIM ** (-0.5)
    probs_full = jnp.exp(scores - totals)
    probs_low = probs_full.astype(HALF)
    grad_values = jnp.einsum("chqk,cqhd->ckhd", probs_low, grad_blend, preferred_element_type=FLOAT)
    grad_probs = jnp.einsum("cqhd,ckhd->chqk", grad_blend, values, preferred_element_type=FLOAT)
    grad_scores = (
        probs_full * (grad_probs - jnp.sum(probs_full * grad_probs, -1, keepdims=True))
    ).astype(HALF)
    grad_queries = jnp.einsum(
        "chqk,ckhd->cqhd", grad_scores, key_rows, preferred_element_type=FLOAT
    ) * HDIM ** (-0.5)
    grad_keys = jnp.einsum(
        "chqk,cqhd->ckhd", grad_scores, queries, preferred_element_type=FLOAT
    ) * HDIM ** (-0.5)
    grad_joined = jnp.concatenate(
        [
            part_grad.reshape(nclips, length, head_cols)
            for part_grad in (grad_queries, grad_keys, grad_values)
        ],
        -1,
    ).astype(HALF)
    grad_qkv = jnp.einsum("ctd,cte->de", normed, grad_joined, preferred_element_type=FLOAT)
    grad_norm_in = rows_sum(jnp.dot(grad_joined, w_qkv.T, preferred_element_type=FLOAT))
    grad_in, gain_one_grad, bias_one_grad = norm_back(
        own_rows(stream, 1), gain_one, bias_one, grad_norm_in
    )
    grad_in = grad_in + grad_att
    vec_grads = jnp.stack(
        [gain_one_grad, bias_one_grad, out_bias_grad, gain_two_grad, bias_two_grad, down_bias_grad]
    )
    return (rows_full(grad_in), (grad_qkv, grad_wout, grad_up, grad_down), vec_grads)


def group_step(patch_rows, visible_ids, shown, weight_rows, rep_full, ten_full):
    splits = lax.axis_size("tensor")
    patch_w, e2d_w, head_w, enc_vec, dec_vec, head_b = split_flat(
        rep_full, [(PATCH, D), (D, DD), (DD, PATCH), (9, D), (10, DD), (PATCH,)]
    )
    enc_vec = enc_vec.astype(FLOAT)
    dec_vec = dec_vec.astype(FLOAT)
    head_b = head_b.astype(FLOAT)
    enc_cols = D // splits
    dec_cols = DD // splits
    ten_pieces = split_flat(
        ten_full,
        [
            (D, 3 * enc_cols),
            (enc_cols, D),
            (D, FF // splits),
            (FF // splits, D),
            (DD, 3 * dec_cols),
            (dec_cols, DD),
            (DD, DFF // splits),
            (DFF // splits, DD),
        ],
    )
    enc_mats = ten_pieces[0:4]
    dec_mats = ten_pieces[4:8]
    enc_vecs = [enc_vec[i] for i in range(1, 7)]
    dec_vecs = [dec_vec[i] for i in range(2, 8)]
    shown_rows = jnp.take_along_axis(patch_rows, visible_ids[:, :, None], 1)
    embedded = (
        jnp.dot(shown_rows, patch_w, preferred_element_type=FLOAT)
        + enc_vec[0]
        + sinus(TUBES, D)[visible_ids]
    )
    encoded, enc_stored = block_forward(embedded, enc_mats, enc_vecs)
    final_enc = layer_norm(encoded, enc_vec[7], enc_vec[8]).astype(HALF)
    reduced = jnp.dot(final_enc, e2d_w, preferred_element_type=FLOAT) + dec_vec[0]
    blank = jnp.broadcast_to(dec_vec[1], (TUBES, DD))
    tokens_in = jax.vmap(lambda clip_ids, clip_rows: blank.at[clip_ids].set(clip_rows))(
        visible_ids, reduced
    ) + sinus(TUBES, DD)
    decoded, dec_stored = block_forward(tokens_in, dec_mats, dec_vecs)
    own_dec = own_rows(decoded, 1)
    final_low = layer_norm(own_dec, dec_vec[8], dec_vec[9]).astype(HALF)
    predicted = jnp.dot(final_low, head_w, preferred_element_type=FLOAT) + head_b
    pixels = own_rows(patch_rows, 1).astype(FLOAT)
    center = jnp.mean(pixels, -1, keepdims=True)
    spread = jnp.mean((pixels - center) ** 2, -1, keepdims=True)
    target = (pixels - center) * lax.rsqrt(spread + 1e-06)
    differ = predicted - target
    counted = own_rows(weight_rows, 1)
    loss_part = jnp.sum(jnp.mean(differ**2, -1) * counted)
    grad_pred = 2.0 / PATCH * differ * counted[:, :, None]
    pred_low = grad_pred.astype(HALF)
    head_w_grad = jnp.einsum("ctd,ctp->dp", final_low, pred_low, preferred_element_type=FLOAT)
    head_b_grad = jnp.sum(grad_pred, (0, 1))
    grad_final = jnp.dot(pred_low, head_w.T, preferred_element_type=FLOAT)
    grad_dec_own, dec_gain_grad, dec_bias_grad = norm_back(
        own_dec, dec_vec[8], dec_vec[9], grad_final
    )
    grad_tokens, dec_mat_grads, dec_vec_grads = block_backward(
        rows_full(grad_dec_own), dec_mats, dec_vecs, dec_stored
    )
    masked_own = own_rows(1.0 - shown.astype(FLOAT), 1)
    mask_grad = jnp.sum(own_rows(grad_tokens, 1) * masked_own[:, :, None], (0, 1))
    grad_reduced = own_rows(jnp.take_along_axis(grad_tokens, visible_ids[:, :, None], 1), 1)
    reduced_low = grad_reduced.astype(HALF)
    e2d_grad = jnp.einsum(
        "ctd,cte->de", own_rows(final_enc, 1), reduced_low, preferred_element_type=FLOAT
    )
    e2d_b_grad = jnp.sum(grad_reduced, (0, 1))
    grad_enc_final = jnp.dot(reduced_low, e2d_w.T, preferred_element_type=FLOAT)
    grad_enc_own, enc_gain_grad, enc_bias_grad = norm_back(
        own_rows(encoded, 1), enc_vec[7], enc_vec[8], grad_enc_final
    )
    grad_embedded, enc_mat_grads, enc_vec_grads = block_backward(
        rows_full(grad_enc_own), enc_mats, enc_vecs, enc_stored
    )
    own_embedded = own_rows(grad_embedded, 1)
    patch_grad = jnp.einsum(
        "ctp,ctd->pd",
        own_rows(shown_rows, 1),
        own_embedded.astype(HALF),
        preferred_element_type=FLOAT,
    )
    patch_b_grad = jnp.sum(own_embedded, (0, 1))
    enc_vec_grad = jnp.concatenate(
        [patch_b_grad[None], enc_vec_grads, enc_gain_grad[None], enc_bias_grad[None]], 0
    )
    dec_vec_grad = jnp.concatenate(
        [
            e2d_b_grad[None],
            mask_grad[None],
            dec_vec_grads,
            dec_gain_grad[None],
            dec_bias_grad[None],
        ],
        0,
    )
    rep_grad = jnp.concatenate(
        [
            patch_grad.reshape(-1),
            e2d_grad.reshape(-1),
            head_w_grad.reshape(-1),
            enc_vec_grad.reshape(-1),
            dec_vec_grad.reshape(-1),
            head_b_grad,
        ]
    )
    ten_grad = jnp.concatenate(
        [mat_grad.reshape(-1) for mat_grad in list(enc_mat_grads) + list(dec_mat_grads)]
    )
    return (loss_part, rep_grad, ten_grad)


def adamw(master, first, second, clipped, number):
    first = BETA1 * first + (1 - BETA1) * clipped
    second = BETA2 * second + (1 - BETA2) * clipped * clipped
    first_hat = first / (1 - BETA1**number)
    second_hat = second / (1 - BETA2**number)
    master = master - LR_IN * (first_hat / (jnp.sqrt(second_hat) + EPS) + DECAY * master)
    return (master, first, second)


def on_device(
    patches,
    visible,
    frames_valid,
    clip_valid,
    rep_weights,
    ten_weights,
    rep_m,
    rep_v,
    ten_m,
    ten_v,
    rep_outer,
    ten_outer,
):
    splits = lax.axis_size("tensor")
    owners = lax.axis_size("dp")
    tube_ids = jnp.arange(TUBES)
    rep_master, ten_master = (rep_weights, ten_weights[0])
    rep_first, rep_second = (rep_m[0], rep_v[0])
    ten_first, ten_second = (ten_m[0, 0], ten_v[0, 0])
    loss_list, count_list, norm_list = ([], [], [])
    for inner_step in range(STEPS):
        rep_full, ten_full = (
            lax.all_gather(rep_master.astype(HALF), "dp", axis=0, tiled=True),
            lax.all_gather(ten_master.astype(HALF), "dp", axis=0, tiled=True),
        )
        visible_ids = visible[inner_step, 0]
        shown = jnp.any(visible_ids[:, :, None] == tube_ids[None, None, :], axis=1)
        weight_rows = (
            jnp.where(shown, 0.0, 1.0)
            * (tube_ids[None, :] // (TUBES // FRAMES) < frames_valid[inner_step, 0][:, None])
            * (clip_valid[inner_step, 0][:, None] == 1)
        ).astype(FLOAT)
        count_part = jnp.sum(own_rows(weight_rows, 1))
        loss_part, rep_grad, ten_grad = group_step(
            patches[inner_step, 0], visible_ids, shown, weight_rows, rep_full, ten_full
        )
        rep_recv, ten_recv = (
            lax.all_to_all(
                rep_grad.reshape(owners, -1), "dp", split_axis=0, concat_axis=0, tiled=True
            ),
            lax.all_to_all(
                ten_grad.reshape(owners, -1), "dp", split_axis=0, concat_axis=0, tiled=True
            ),
        )
        rep_part = lax.psum(jnp.sum(rep_recv, 0), "tensor")
        ten_part = jnp.sum(ten_recv, 0)
        squares = jnp.sum(ten_part * ten_part) + jnp.sum(rep_part * rep_part) / splits
        square_all, loss_all, count_all = lax.psum(
            (squares, loss_part, count_part), ("dp", "tensor")
        )
        norm_value = jnp.sqrt(square_all + 1e-30) / count_all
        factor = jnp.minimum(1.0, CLIP / norm_value) / count_all
        number = STEP_BEFORE + inner_step + 1
        rep_master, rep_first, rep_second = adamw(
            rep_master, rep_first, rep_second, rep_part * factor, number
        )
        ten_master, ten_first, ten_second = adamw(
            ten_master, ten_first, ten_second, ten_part * factor, number
        )
        loss_list.append(loss_all)
        count_list.append(count_all)
        norm_list.append(norm_value)
    rep_sum, ten_sum = lax.psum((rep_weights - rep_master, ten_weights[0] - ten_master), "group")
    groups_count = lax.axis_size("group")
    rep_diff = rep_sum / groups_count
    ten_diff = ten_sum / groups_count
    rep_momentum = MOMENTUM * rep_outer + rep_diff
    ten_momentum = MOMENTUM * ten_outer[0] + ten_diff
    rep_new = rep_weights - LR_OUT * (rep_diff + MOMENTUM * rep_momentum)
    ten_new = ten_weights[0] - LR_OUT * (ten_diff + MOMENTUM * ten_momentum)
    return (
        jnp.stack(loss_list)[:, None],
        jnp.stack(count_list)[:, None],
        jnp.stack(norm_list)[:, None],
        rep_first[None],
        rep_second[None],
        ten_first[None, None],
        ten_second[None, None],
        rep_diff,
        ten_diff[None],
        rep_momentum,
        ten_momentum[None],
        rep_new,
        ten_new[None],
    )


NT=(((1,),(1,)),((),()))
NN=(((1,),(0,)),((),()))
TILE=224
def dot(a,b,dims): return lax.dot_general(a,b,dims,preferred_element_type=FLOAT)

def attn_forward_kernel(q_ref,k_ref,v_ref,out_ref,lse_ref):
    heads=q_ref.shape[1]//HDIM; tiles=q_ref.shape[0]//TILE
    for h in range(heads):
        cols=slice(h*HDIM,(h+1)*HDIM)
        keys=k_ref[:,cols]*HALF(HDIM**-0.5)
        vt=v_ref[:,cols].T
        def step(t,_):
            rows=pl.ds(pl.multiple_of(t*TILE,TILE),TILE)
            s=dot(keys,q_ref[rows,cols],NT)
            m=jnp.max(s,0,keepdims=True)
            e=jnp.exp(s-m)
            total=jnp.sum(e,0,keepdims=True)
            p=(e*(1.0/total)).astype(HALF)
            bt=dot(vt,p,NN)
            out_ref[rows,cols]=bt.T.astype(HALF)
            lse_ref[h,pl.ds(t,1),:]=m+jnp.log(total)
            return 0
        lax.fori_loop(0,tiles,step,0)

def attn_forward(q,k,v):
    rows,width=q.shape
    vm=pl.BlockSpec(memory_space=pltpu.VMEM)
    return pl.pallas_call(attn_forward_kernel,name="attn_forward",
      out_shape=(jax.ShapeDtypeStruct((rows,width),HALF),jax.ShapeDtypeStruct((width//HDIM,rows//TILE,TILE),FLOAT)),
      in_specs=[vm]*3,out_specs=(vm,vm),
      compiler_params=pltpu.CompilerParams(vmem_limit_bytes=48<<20),
      cost_estimate=pl.CostEstimate(flops=4*rows*rows*width,bytes_accessed=rows*width*8,transcendentals=rows*rows*width//HDIM))(q,k,v)

def attn_backward_kernel(q_ref,k_ref,v_ref,g_ref,lse_ref,out_ref,dk_ref,dv_ref):
    width=q_ref.shape[1]
    heads=width//HDIM; tiles=q_ref.shape[0]//TILE
    for h in range(heads):
        cols=slice(h*HDIM,(h+1)*HDIM)
        keys=k_ref[:,cols]*HALF(HDIM**-0.5)
        values=v_ref[:,cols]
        kt=keys.T
        dk_ref[...]=jnp.zeros_like(dk_ref); dv_ref[...]=jnp.zeros_like(dv_ref)
        def step(t,_):
            rows=pl.ds(pl.multiple_of(t*TILE,TILE),TILE)
            q=q_ref[rows,cols]; g=g_ref[rows,cols]
            p=jnp.exp(dot(keys,q,NT)-lse_ref[h,pl.ds(t,1),:])
            dv_ref[...]+=dot(p.astype(HALF),g,NN)
            dp=dot(values,g,NT)
            ds=(p*(dp-jnp.sum(p*dp,0,keepdims=True))).astype(HALF)
            dk_ref[...]+=dot(ds,q,NN)
            out_ref[rows,cols]=dot(kt,ds,NN).T.astype(HALF)
            return 0
        lax.fori_loop(0,tiles,step,0)
        out_ref[:,width+h*HDIM:width+(h+1)*HDIM]=(dk_ref[...]*HDIM**-0.5).astype(HALF)
        out_ref[:,2*width+h*HDIM:2*width+(h+1)*HDIM]=dv_ref[...].astype(HALF)

def attn_backward(q,k,v,g,lse):
    rows,width=q.shape
    vm=pl.BlockSpec(memory_space=pltpu.VMEM)
    return pl.pallas_call(attn_backward_kernel,name="attn_backward",
      out_shape=jax.ShapeDtypeStruct((rows,3*width),HALF),
      in_specs=[vm]*5,out_specs=vm,
      scratch_shapes=[pltpu.VMEM((rows,HDIM),FLOAT),pltpu.VMEM((rows,HDIM),FLOAT)],
      compiler_params=pltpu.CompilerParams(vmem_limit_bytes=48<<20),
      cost_estimate=pl.CostEstimate(flops=10*rows*rows*width,bytes_accessed=rows*width*14,transcendentals=rows*rows*width//HDIM))(q,k,v,g,lse)


HOST = 1
LAST = 3
SWAP = [(0, 1), (1, 0)]
ENC_SHAPES = [(D, 3 * D // 2), (D // 2, D), (D, FF // 2), (FF // 2, D)]
DEC_SHAPES = [(DD, 3 * DD // 2), (DD // 2, DD), (DD, DFF // 2), (DFF // 2, DD)]
ENC_SIZE = sum(math.prod(one) for one in ENC_SHAPES)
DEC_SIZE = sum(math.prod(one) for one in DEC_SHAPES)
PATCH_SIZE = PATCH * D
E2D_SIZE = D * DD
HEAD_SIZE = DD * PATCH
ENC_VECS = 9 * D
DEC_VECS = 10 * DD


def hop(value, *moves):
    pairs = [(2 * a + b, 2 * c + d) for (a, b), (c, d) in moves]
    return lax.ppermute(value, ("dp", "tensor"), pairs)


def hop_both(value, *moves):
    return hop(value, *[((a, side), (b, side)) for a, b in moves for side in range(2)])


def swap(value, *where):
    if where:
        return hop(value, *[((z, side), (z, 1 - side)) for z in where for side in range(2)])
    return lax.ppermute(value, "tensor", SWAP)


def partner(value):
    count = lax.axis_size("group")
    return lax.ppermute(value, "group", [(g, g ^ 1) for g in range(count)])


def mm(left, right):
    return jnp.dot(left, right, preferred_element_type=FLOAT)


def mm_nt(left, right):
    return lax.dot_general(left, right, (((1,), (1,)), ((), ())), preferred_element_type=FLOAT)


def mm_tn(left, right):
    return lax.dot_general(left, right, (((0,), (0,)), ((), ())), preferred_element_type=FLOAT)


def sinus_at(ids, width):
    column = jnp.arange(width)
    decays = jnp.power(10000.0, -2.0 * (column // 2).astype(FLOAT) / width)
    angles = ids.astype(FLOAT)[:, None] * decays[None, :]
    return jnp.where(column % 2 == 0, jnp.sin(angles), jnp.cos(angles))


(
    QKV,
    SQUARE,
    UP,
    PATCH_ROWS,
    E2D,
    HEAD,
    HEAD_LATE,
    VECS,
    DEC_QKV,
    DEC_OUT,
    DEC_UP,
    DEC_DOWN,
    HEAD_HALF,
    PATCH_LOW,
    PATCH_HIGH,
    W_QKV,
    W_OUT,
    W_UP,
    W_DOWN,
    E2D_W,
    HEAD_UP,
    SEND_ENC,
    SEND_MATE,
    CHAIN,
    CROSS,
    MATE_OWN,
    MATE_OTHER,
) = range(27)
TEN_ROWS = [
    [(QKV, 768), (SQUARE, 288)],
    [(SQUARE, 96), (UP, 672)],
    [(UP, 96), (SQUARE, 1248)],
    [(SQUARE, 288), (DEC_QKV, 384), (DEC_OUT, 192), (DEC_UP, 384), (DEC_DOWN, 768)],
]
REP_ROWS = [
    [(PATCH_ROWS, 676)],
    [(PATCH_ROWS, 676)],
    [(PATCH_ROWS, 184), (E2D, 768), (HEAD, 54)],
    [(HEAD_LATE, 330), (VECS, 16)],
]
PIECES = {
    QKV: (768, 1152),
    SQUARE: (1248, 768),
    UP: (672, 1536),
    PATCH_ROWS: (704, 768),
    E2D: (768, 384),
    HEAD: (64, 1536),
    HEAD_LATE: (384, 1536),
    VECS: (16, 768),
    DEC_QKV: (384, 576),
    DEC_OUT: (192, 384),
    DEC_UP: (384, 768),
    DEC_DOWN: (768, 384),
}


def owned_pieces(rep_master, ten_master):
    def branch(ten_rows, rep_rows):
        def fill(ten, rep):
            out = {}
            for flat, rows in ((ten, ten_rows), (rep, rep_rows)):
                offset = 0
                for name, count in rows:
                    width = PIECES[name][1]
                    piece = flat[offset : offset + count * width].astype(HALF).reshape(count, width)
                    offset += count * width
                    top = PIECES[name][0] - count if name == HEAD_LATE else 0
                    out[name] = jnp.pad(piece, ((top, PIECES[name][0] - count - top), (0, 0)))
            return [out.get(name, jnp.zeros(PIECES[name], HALF)) for name in PIECES]

        return fill

    branches = [branch(ten_rows, rep_rows) for ten_rows, rep_rows in zip(TEN_ROWS, REP_ROWS)]
    return dict(zip(PIECES, lax.switch(lax.axis_index("dp"), branches, ten_master, rep_master)))


DEC_PARTS = [DEC_QKV, DEC_OUT, DEC_UP, DEC_DOWN, HEAD_HALF]
SENT = [QKV, SQUARE, UP, PATCH_ROWS, E2D, HEAD, VECS] + DEC_PARTS
ENC_PARTS = [
    (PATCH_LOW, 704, 0, PATCH_ROWS, 0),
    (W_QKV, 768, 0, QKV, 0),
    (W_OUT, 288, 0, SQUARE, 0),
    (W_OUT, 96, 1, SQUARE, 288),
    (PATCH_HIGH, 192, 2, PATCH_ROWS, 0),
    (W_UP, 672, 1, UP, 0),
    (W_UP, 96, 2, UP, 672),
    (W_DOWN, 1248, 2, SQUARE, 0),
    (W_DOWN, 288, 3, SQUARE, 1248),
    (E2D_W, 768, 2, E2D, 0),
]
GOT = {
    PATCH_LOW: (704, 768),
    PATCH_HIGH: (192, 768),
    W_QKV: (768, 1152),
    W_OUT: (384, 768),
    W_UP: (768, 1536),
    W_DOWN: (1536, 768),
    E2D_W: (768, 384),
    HEAD: (64, 1536),
    VECS: (16, 768),
}
MESH_ID = pl.DeviceIdType.MESH


def weights_kernel(shared, *refs):
    sent = dict(zip(SENT, refs[: len(SENT)]))
    refs = refs[len(SENT) :]
    got = dict(zip(GOT, refs[: len(GOT)]))
    refs = refs[len(GOT) :]
    own = dict(zip(DEC_PARTS, refs[: len(DEC_PARTS)]))
    other = dict(zip(DEC_PARTS, refs[len(DEC_PARTS) : 2 * len(DEC_PARTS)]))
    send_sem, recv_sem, local_sem = refs[2 * len(DEC_PARTS) :]
    g, z, x = lax.axis_index("group"), lax.axis_index("dp"), lax.axis_index("tensor")
    odd = lax.rem(g, 2)
    mate = (g + 1 - 2 * odd, z, x)
    across = (g, z, 1 - x)

    def at(row):
        return (g, row, x)

    def greet(peer):
        pl.semaphore_signal(barrier, inc=1, device_id=peer, device_id_type=MESH_ID)

    barrier = pltpu.get_barrier_semaphore()
    greet(across)
    near = {0: [1], 1: [0, 2, 3], 2: [1, 3], 3: [2, 1]}
    if shared:
        greet(mate)
    for row, peers in near.items():

        @pl.when(z == row)
        def _():
            for peer in peers:
                greet(at(peer))
            pl.semaphore_wait(barrier, len(peers) + (2 if shared else 1))

    def part(ref, start, count, half):
        if not half:
            return ref.at[pl.ds(start, count)]
        return ref.at[pl.ds(pl.multiple_of(start + odd * (count // 2), 16), count // 2)]

    numbers = {}

    def copy(key, source, target, peer):
        index = numbers.setdefault(key, len(numbers))
        return pltpu.make_async_remote_copy(
            src_ref=source,
            dst_ref=target,
            send_sem=send_sem.at[index],
            recv_sem=recv_sem.at[index],
            device_id=peer,
            device_id_type=MESH_ID,
        )

    def enc_copy(item):
        name, count, owner, piece, first = item
        return copy(
            (SEND_ENC, name, first),
            part(sent[piece], 0, count, shared),
            part(got[name], first, count, shared),
            at(HOST),
        )

    def enc_mate(item):
        name, count, owner, piece, first = item
        half = part(got[name], first, count, True)
        return copy((SEND_MATE, name, first), half, half, mate)

    def local(index, source, target):
        return pltpu.make_async_copy(source, target, local_sem.at[index])

    def chain(name, source, peer):
        target = got[name] if name in got else own[name]
        rows = source.shape[0]
        half = shared and name in own
        return copy((CHAIN, name), part(source, 0, rows, half), part(target, 0, rows, half), at(peer))

    def cross(name, source):
        rows = source.shape[0]
        return copy(
            (CROSS, name), part(source, 0, rows, shared), part(other[name], 0, rows, shared), across
        )

    def mates(name, ref, label):
        half = part(ref, 0, ref.shape[0], True)
        return copy((label, name), half, half, mate)

    def owned(row):
        return [item for item in ENC_PARTS if item[2] == row and row != HOST]

    for item in ENC_PARTS:
        numbers[(SEND_ENC, item[0], item[4])] = len(numbers)
        numbers[(SEND_MATE, item[0], item[4])] = len(numbers)
    for name in DEC_PARTS + [VECS, HEAD, HEAD_UP]:
        for label in (CHAIN, CROSS, MATE_OWN, MATE_OTHER):
            numbers[(label, name)] = len(numbers)

    def head_up():
        return copy((CHAIN, HEAD_UP), sent[HEAD], got[HEAD], at(LAST))

    def finish_dec(name, source, here):
        cross(name, source).start()
        if shared and not here:
            mates(name, own[name], MATE_OWN).start()

    def end_dec(name, source, here):
        cross(name, source).wait()
        if shared:
            mates(name, other[name], MATE_OTHER).start()

    def end_mates(name, here):
        if shared:
            if not here:
                mates(name, own[name], MATE_OWN).wait()
            mates(name, other[name], MATE_OTHER).wait()

    @pl.when(z == LAST)
    def _():
        for item in owned(LAST):
            enc_copy(item).start()
        chain(VECS, sent[VECS], 2).start()
        for name in DEC_PARTS:
            chain(name, sent[name], 2).start()
            finish_dec(name, sent[name], True)
        locals_ = [local(i, sent[name], own[name]) for i, name in enumerate(DEC_PARTS)]
        locals_.append(local(len(DEC_PARTS), sent[VECS], got[VECS]))
        for one in locals_:
            one.start()
        for name in DEC_PARTS:
            end_dec(name, sent[name], True)
        for item in owned(LAST):
            enc_copy(item).wait_send()
        chain(VECS, sent[VECS], 2).wait_send()
        for name in DEC_PARTS:
            chain(name, sent[name], 2).wait_send()
            end_mates(name, True)
        for one in locals_:
            one.wait()
        head_up().wait_recv()

    @pl.when(z == 2)
    def _():
        head_up().start()
        chain(HEAD, sent[HEAD], HOST).start()
        first = local(0, sent[HEAD], got[HEAD])
        first.start()
        for item in owned(2):
            enc_copy(item).start()
        chain(VECS, sent[VECS], 2).wait_recv()
        chain(VECS, got[VECS], HOST).start()
        waited = False
        for name in DEC_PARTS:
            chain(name, sent[name], 2).wait_recv()
            finish_dec(name, own[name], False)
            if not waited:
                for item in owned(2):
                    enc_copy(item).wait_send()
                waited = True
            chain(name, own[name], HOST).start()
        for name in DEC_PARTS:
            end_dec(name, own[name], False)
        for name in DEC_PARTS:
            chain(name, own[name], HOST).wait_send()
            end_mates(name, False)
        chain(VECS, got[VECS], HOST).wait_send()
        chain(HEAD, sent[HEAD], HOST).wait_send()
        head_up().wait_send()
        first.wait()

    @pl.when(z == HOST)
    def _():
        mine = [
            local(i, sent[piece].at[pl.ds(0, count)], got[name].at[pl.ds(first, count)])
            for i, (name, count, owner, piece, first) in enumerate(ENC_PARTS)
            if owner == HOST
        ]
        for one in mine:
            one.start()
        chain(HEAD, sent[HEAD], HOST).wait_recv()
        chain(HEAD, got[HEAD], 0).start()
        chain(VECS, sent[VECS], HOST).wait_recv()
        chain(VECS, got[VECS], 0).start()
        away = [item for item in ENC_PARTS if item[2] != HOST]
        if shared:
            for item in away:
                enc_copy(item).wait_recv()
                enc_mate(item).start()
        for name in DEC_PARTS:
            chain(name, sent[name], HOST).wait_recv()
            chain(name, own[name], 0).start()
            finish_dec(name, own[name], False)
        for name in DEC_PARTS:
            end_dec(name, own[name], False)
        for item in away:
            if shared:
                enc_mate(item).wait()
            else:
                enc_copy(item).wait_recv()
        for name in DEC_PARTS:
            chain(name, own[name], 0).wait_send()
            end_mates(name, False)
        chain(VECS, got[VECS], 0).wait_send()
        chain(HEAD, got[HEAD], 0).wait_send()
        for one in mine:
            one.wait()

    @pl.when(z == 0)
    def _():
        for item in owned(0):
            enc_copy(item).start()
        for name in DEC_PARTS:
            chain(name, sent[name], 0).wait_recv()
            finish_dec(name, own[name], False)
        for name in DEC_PARTS:
            end_dec(name, own[name], False)
        for name in DEC_PARTS:
            end_mates(name, False)
        chain(VECS, sent[VECS], 0).wait_recv()
        chain(HEAD, sent[HEAD], 0).wait_recv()
        for item in owned(0):
            enc_copy(item).wait_send()


def hosted_weights(rep_master, ten_master, shared):
    side = lax.axis_index("tensor")
    pieces = owned_pieces(rep_master, ten_master)
    columns = PATCH // 2
    pieces[HEAD_HALF] = lax.dynamic_slice_in_dim(pieces[HEAD_LATE], side * columns, columns, 1)
    anywhere = pl.BlockSpec(memory_space=pl.ANY)
    shapes = list(GOT.values()) + 2 * [pieces[name].shape for name in DEC_PARTS]
    count = 2 * len(ENC_PARTS) + 4 * (len(DEC_PARTS) + 3)
    out = pl.pallas_call(
        functools.partial(weights_kernel, shared),
        name="weights",
        out_shape=[jax.ShapeDtypeStruct(shape, HALF) for shape in shapes],
        in_specs=[anywhere] * len(SENT),
        out_specs=[anywhere] * len(shapes),
        scratch_shapes=[
            pltpu.SemaphoreType.DMA((count,)),
            pltpu.SemaphoreType.DMA((count,)),
            pltpu.SemaphoreType.DMA((len(ENC_PARTS),)),
        ],
        compiler_params=pltpu.CompilerParams(collective_id=1 if shared else 2, has_side_effects=True),
    )(*[pieces[name] for name in SENT])
    got = dict(zip(GOT, out))
    own = out[len(GOT) : len(GOT) + len(DEC_PARTS)]
    other = out[len(GOT) + len(DEC_PARTS) :]
    low, high = jnp.where(side == 0, own[4], other[4]), jnp.where(side == 0, other[4], own[4])
    head_w = jnp.concatenate([low, high], 1)
    top = got[HEAD].shape[0]
    head_w = jnp.concatenate([head_w[:top] + got[HEAD], head_w[top:]], 0)
    vecs = got[VECS].reshape(-1)
    enc_vec, dec_vec, head_b = split_flat(vecs, [(9, D), (10, DD), (PATCH,)])
    return (
        (
            (got[PATCH_LOW], pieces[PATCH_ROWS], got[PATCH_HIGH]),
            tuple(got[name] for name in (W_QKV, W_OUT, W_UP, W_DOWN)),
            got[E2D_W],
            jnp.pad(enc_vec.astype(FLOAT), ((0, 7), (0, 0))),
        ),
        (own[:4], other[:4], head_w, dec_vec.astype(FLOAT), head_b.astype(FLOAT)),
    )


VISIBLE = 160
OWN = 2 * VISIBLE
ALL = 4 * VISIBLE
SPAN = (0, 768, 1536)
DEPTH = (704, 704, 192)
WIDE = 1792
SQRT_HALF = 0.5**0.5


def norm_parts(x):
    center = jnp.mean(x, -1, keepdims=True)
    moved = x - center
    scale = lax.rsqrt(jnp.mean(moved * moved, -1, keepdims=True) + 1e-06)
    return moved * scale, scale


def norm_to(x, gain, bias):
    return norm_parts(x)[0] * gain + bias


def norm_from(x, gain, cotangent):
    hat, scale = norm_parts(x)
    inner = cotangent * gain
    grad = scale * (
        inner - jnp.mean(inner, -1, keepdims=True) - hat * jnp.mean(inner * hat, -1, keepdims=True)
    )
    return grad, jnp.sum(cotangent * hat, 0, keepdims=True), jnp.sum(cotangent, 0, keepdims=True)


def gelu_to(x):
    return 0.5 * x * (1.0 + lax.erf(x * SQRT_HALF))


def gelu_slope(x):
    return 0.5 * (1.0 + lax.erf(x * SQRT_HALF)) + x * jnp.exp(-0.5 * x * x) * (2.0 * math.pi) ** -0.5


def rows_at(index, count=VISIBLE):
    return pl.ds(index * count, count)


class Links:
    def __init__(self, send_sem, recv_sem):
        self.send_sem, self.recv_sem, self.keys = send_sem, recv_sem, {}

    def copy(self, key, source, target, peer):
        index = self.keys.setdefault(key, len(self.keys))
        return pltpu.make_async_remote_copy(
            src_ref=source,
            dst_ref=target,
            send_sem=self.send_sem.at[index],
            recv_sem=self.recv_sem.at[index],
            device_id=peer,
            device_id_type=MESH_ID,
        )


def encoder_forward_kernel(
    shown, places, patch_low, patch_mid, patch_high, w_qkv, w_out, w_up, w_down, e2d_w, vec,
    reduced, stream, normed, joined, blended, attended, second, upward, activated, encoded, final_enc,
    part_sent, part_got, reduced_own, send_sem, recv_sem, local_sem,
):
    g, z, x = lax.axis_index("group"), lax.axis_index("dp"), lax.axis_index("tensor")
    barrier = pltpu.get_barrier_semaphore()
    links = Links(send_sem, recv_sem)

    def at(row, column):
        return (g, row, column)

    def greet(peer):
        pl.semaphore_signal(barrier, inc=1, device_id=peer, device_id_type=MESH_ID)

    for row in range(4):

        @pl.when((z == row) & ((row != HOST) | (x == 1)))
        def _():
            greet(at(HOST, row // 2))

    @pl.when((z == HOST) & (x == 0))
    def _():
        greet(at(HOST, 1))
        pl.semaphore_wait(barrier, 3)

    @pl.when((z == HOST) & (x == 1))
    def _():
        pl.semaphore_wait(barrier, 5)

    def give(column, clip):
        row = 2 * column + clip
        out = []
        for side in range(2):
            if (row, side) != (HOST, column):
                out.append(links.copy(8 + 2 * clip + side, reduced_own.at[clip], reduced, at(row, side)))
        return out

    @pl.when(z == HOST)
    def _():
        across = at(HOST, 1 - x)

        def normed_copy(i):
            return links.copy(i, normed.at[rows_at(i)], normed.at[rows_at(2 + i)], across)

        def out_copy(i):
            return links.copy(2 + i, part_sent.at[rows_at(i)], part_got.at[rows_at(i)], across)

        def second_copy(i):
            return links.copy(4 + i, second.at[rows_at(i)], second.at[rows_at(2 + i)], across)

        def down_copy(i):
            return links.copy(6 + i, part_sent.at[rows_at(2 + i)], part_got.at[rows_at(2 + i)], across)

        for i in range(2):
            rows = rows_at(i)
            emb = places[rows] + vec[0:1]
            for start, depth, weight in zip(SPAN, DEPTH, (patch_low, patch_mid, patch_high)):
                emb = emb + mm(shown[rows, start : start + depth], weight[...])
            stream[rows] = emb
            normed[rows] = norm_to(emb, vec[1:2], vec[2:3]).astype(HALF)
            normed_copy(i).start()

        def attend(c):
            rows = rows_at(c)
            joined[rows] = mm(normed[rows], w_qkv[...]).astype(HALF)
            width = D // 2
            for h in range(width // HDIM):
                column = h * HDIM
                queries = joined[rows, column : column + HDIM]
                keys = joined[rows, width + column : width + column + HDIM]
                values = joined[rows, 2 * width + column : 2 * width + column + HDIM]
                scores = mm_nt(queries, keys) * HDIM**-0.5
                weights = jnp.exp(scores - jnp.max(scores, -1, keepdims=True))
                probs = weights * (1.0 / jnp.sum(weights, -1, keepdims=True))
                blended[rows, column : column + HDIM] = mm(probs.astype(HALF), values).astype(HALF)
            return mm(blended[rows], w_out[...])

        for i in range(2):
            attended[rows_at(i)] = attend(i) + stream[rows_at(i)] + vec[3:4]
            normed_copy(i).wait_recv()
            part_sent[rows_at(i)] = attend(2 + i).astype(HALF)
            out_copy(i).start()

        def feed(c):
            rows = rows_at(c)
            up = mm(second[rows], w_up[...])
            upward[rows] = up
            activated[rows] = gelu_to(up).astype(HALF)
            return mm(activated[rows], w_down[...])

        for i in range(2):
            rows = rows_at(i)
            out_copy(i).wait_recv()
            after = attended[rows] + part_got[rows].astype(FLOAT)
            attended[rows] = after
            second[rows] = norm_to(after, vec[4:5], vec[5:6]).astype(HALF)
            second_copy(i).start()
        for i in range(2):
            rows = rows_at(i)
            encoded[rows] = feed(i) + attended[rows] + vec[6:7]
            second_copy(i).wait_recv()
            part_sent[rows_at(2 + i)] = feed(2 + i).astype(HALF)
            down_copy(i).start()
        for i in range(2):
            rows = rows_at(i)
            down_copy(i).wait_recv()
            after = encoded[rows] + part_got[rows_at(2 + i)].astype(FLOAT)
            encoded[rows] = after
            low = norm_to(after, vec[7:8], vec[8:9]).astype(HALF)
            final_enc[rows] = low
            reduced_own[i] = mm(low, e2d_w[...])
            for column in range(2):

                @pl.when(x == column)
                def _():
                    for one in give(column, i):
                        one.start()

        for i in range(2):
            normed_copy(i).wait_send()
            out_copy(i).wait_send()
            second_copy(i).wait_send()
            down_copy(i).wait_send()
        for column in range(2):

            @pl.when(x == column)
            def _():
                for i in range(2):
                    for one in give(column, i):
                        one.wait_send()

    @pl.when((z == HOST) & (x == 0))
    def _():
        mine = pltpu.make_async_copy(reduced_own.at[1], reduced, local_sem)
        mine.start()
        mine.wait()

    for row in range(4):
        for side in range(2):
            if (row, side) != (HOST, 0):

                @pl.when((z == row) & (x == side))
                def _():
                    key = 8 + 2 * (row % 2) + side
                    links.copy(key, reduced_own.at[row % 2], reduced, at(HOST, row // 2)).wait_recv()


def encoder_forward(number, shown_own, places, weights):
    patch_pieces, mats, e2d_w, vec = weights
    vmem = pl.BlockSpec(memory_space=pltpu.VMEM)
    stored = [
        ((OWN, D), FLOAT),
        ((ALL, D), HALF),
        ((ALL, 3 * D // 2), HALF),
        ((ALL, D // 2), HALF),
        ((OWN, D), FLOAT),
        ((ALL, D), HALF),
        ((ALL, FF // 2), FLOAT),
        ((ALL, FF // 2), HALF),
        ((OWN, D), FLOAT),
        ((OWN, D), HALF),
    ]
    shapes = [((VISIBLE, DD), FLOAT)] + stored
    out = pl.pallas_call(
        encoder_forward_kernel,
        name="encoder_forward",
        out_shape=[jax.ShapeDtypeStruct(*one) for one in shapes],
        in_specs=[vmem] * 11,
        out_specs=[vmem] * len(shapes),
        scratch_shapes=[
            pltpu.VMEM((ALL, D), HALF),
            pltpu.VMEM((ALL, D), HALF),
            pltpu.VMEM((2, VISIBLE, DD), FLOAT),
            pltpu.SemaphoreType.DMA((12,)),
            pltpu.SemaphoreType.DMA((12,)),
            pltpu.SemaphoreType.DMA,
        ],
        compiler_params=pltpu.CompilerParams(
            collective_id=number, has_side_effects=True, vmem_limit_bytes=56 << 20
        ),
    )(shown_own, places, *patch_pieces, *mats, e2d_w, vec)
    return out[0], out[1:]


def encoder_backward_kernel(
    picked, shown, w_qkv, w_out, w_up, w_down, e2d_w, vec,
    stream, normed, joined, blended, attended, second, upward, activated, encoded, final_enc,
    qkv_out, square_out, up_out, patch_out, e2d_out, vec_out,
    picks_got, low, grad_up_in, mid, grad_blend, grad_joined, part_sent, part_got, own_rows_grad, own_part,
    emb_low, emb_got, down_grad, up_grad, out_grad, qkv_grad, patch_low, patch_mid, patch_high, e2d_part, e2d_got, e2d_grad,
    vec_part, vec_got, send_sem, recv_sem, local_sem,
):
    g, z, x = lax.axis_index("group"), lax.axis_index("dp"), lax.axis_index("tensor")
    barrier = pltpu.get_barrier_semaphore()
    links = Links(send_sem, recv_sem)

    def at(row, column):
        return (g, row, column)

    def greet(peer):
        pl.semaphore_signal(barrier, inc=1, device_id=peer, device_id_type=MESH_ID)

    @pl.when(z != HOST)
    def _():
        greet(at(HOST, x))
        pl.semaphore_wait(barrier, 1)

    for column in range(2):

        @pl.when((z == HOST) & (x == column))
        def _():
            greet(at(HOST, 1 - column))
            for row in (2 * column, 2 * column + 1):
                if row != HOST:
                    for side in range(2):
                        greet(at(row, side))
            pl.semaphore_wait(barrier, 4)

    def pick_copy(row, side):
        return links.copy((row % 2) * 2 + side, picked, picks_got.at[row % 2, side], at(HOST, row // 2))

    for row in range(4):
        for side in range(2):
            if (row, side) != (HOST, 0):

                @pl.when((z == row) & (x == side))
                def _():
                    pick_copy(row, side).start()

    numbers = iter(range(4, 64))
    low_number = [next(numbers), next(numbers)]
    second_number = [next(numbers), next(numbers)]
    mid_number = [next(numbers), next(numbers)]
    normed_number = [next(numbers), next(numbers)]
    emb_number = [next(numbers), next(numbers)]
    e2d_number, vec_number = next(numbers), next(numbers)

    def row_copies(numbers_two, ref):
        return [
            links.copy(numbers_two[i], ref.at[rows_at(i)], ref.at[rows_at(2 + i)], at(HOST, 1 - x)) for i in range(2)
        ]

    def part_copies(numbers_two, first):
        return [
            links.copy(
                numbers_two[i], part_sent.at[rows_at(first + i)], part_got.at[rows_at(first + i)], at(HOST, 1 - x)
            )
            for i in range(2)
        ]

    out_rows, up_rows, down_rows = 288, 672, 1248
    down_far = links.copy(next(numbers), down_grad.at[pl.ds(down_rows, 288)], square_out.at[pl.ds(0, 288)], at(LAST, x))
    down_near = links.copy(next(numbers), down_grad.at[pl.ds(0, down_rows)], square_out, at(2, x))
    up_near = links.copy(next(numbers), up_grad.at[pl.ds(up_rows, 96)], up_out.at[pl.ds(0, 96)], at(2, x))
    out_near = links.copy(
        next(numbers), out_grad.at[pl.ds(0, out_rows)], square_out.at[pl.ds(0, out_rows)], at(0, x)
    )
    qkv_near = links.copy(next(numbers), qkv_grad, qkv_out, at(0, x))
    patch_one = links.copy(next(numbers), patch_low, patch_out, at(0, x))
    patch_two = links.copy(next(numbers), patch_high, patch_out.at[pl.ds(0, 192)], at(2, x))
    e2d_near = links.copy(next(numbers), e2d_grad, e2d_out, at(2, x))
    vec_far = links.copy(next(numbers), vec_part, vec_out, at(LAST, x))

    def tall_product(left, right, target, step):
        def body(t, carry):
            columns = pl.ds(pl.multiple_of(t * step, step), step)
            target[columns] = mm_tn(left[:, columns], right[...]).astype(HALF)
            return carry

        lax.fori_loop(0, target.shape[0] // step, body, 0)

    @pl.when(z == HOST)
    def _():
        low_sent, mid_sent = row_copies(low_number, low), row_copies(mid_number, mid)
        second_sent, normed_sent = part_copies(second_number, 0), part_copies(normed_number, 2)
        emb_sent = [
            links.copy(
                emb_number[i],
                emb_low.at[1 - x, rows_at(i)],
                emb_got.at[rows_at(i)],
                at(HOST, 1 - x),
            )
            for i in range(2)
        ]
        e2d_sent = links.copy(e2d_number, e2d_part.at[1 - x], e2d_got, at(HOST, 1 - x))
        vec_sent = links.copy(vec_number, vec_part, vec_got, at(HOST, 1 - x))

        vec_part[...] = jnp.zeros_like(vec_part)

        def count(row, value):
            vec_part[row : row + 1] += value

        @pl.when(x == 0)
        def _():
            mine = pltpu.make_async_copy(picked, picks_got.at[1, 0], local_sem.at[0])
            mine.start()
            mine.wait()

        for clip in range(2):
            for side in range(2):
                waiting = links.copy(clip * 2 + side, picked, picks_got.at[clip, side], at(HOST, 0))
                if clip == HOST % 2 and side == 0:

                    @pl.when(x == 1)
                    def _():
                        waiting.wait_recv()

                else:
                    waiting.wait_recv()
        reduced_low = []
        for i in range(2):
            rows = rows_at(i)
            one = picks_got[i, 0] + picks_got[i, 1]
            reduced_low.append(one)
            grad, gain, bias = norm_from(encoded[rows], vec[7:8], mm_nt(one, e2d_w[...]))
            count(7, gain)
            count(8, bias)
            count(6, jnp.sum(grad, 0, keepdims=True))
            own_rows_grad[rows] = grad
            low[rows] = grad.astype(HALF)
            low_sent[i].start()
        whole_low = jnp.concatenate(reduced_low, 0)
        product = mm_tn(final_enc[...], whole_low).astype(HALF)
        e2d_part[0] = product[: D // 2]
        e2d_part[1] = product[D // 2 :]
        e2d_sent.start()

        def feed_back(c):
            rows = rows_at(c)
            grad_up_in[rows] = (mm_nt(low[rows], w_down[...]) * gelu_slope(upward[rows])).astype(HALF)
            return mm_nt(grad_up_in[rows], w_up[...])

        for i in range(2):
            own_part[rows_at(i)] = feed_back(i)
            low_sent[i].wait_recv()
            part_sent[rows_at(i)] = feed_back(2 + i).astype(HALF)
            second_sent[i].start()
        tall_product(activated, low, down_grad, 256)
        down_far.start()
        down_near.start()
        for i in range(2):
            rows = rows_at(i)
            second_sent[i].wait_recv()
            total = own_part[rows] + part_got[rows].astype(FLOAT)
            grad, gain, bias = norm_from(attended[rows], vec[4:5], total)
            count(4, gain)
            count(5, bias)
            grad = grad + own_rows_grad[rows]
            count(3, jnp.sum(grad, 0, keepdims=True))
            own_rows_grad[rows] = grad
            mid[rows] = grad.astype(HALF)
            mid_sent[i].start()
        e2d_sent.wait()
        e2d_grad[...] = (e2d_part[x].astype(FLOAT) + e2d_got[...].astype(FLOAT)).astype(HALF)
        e2d_near.start()

        def attend_back(c):
            rows = rows_at(c)
            width = D // 2
            grad_blend[...] = mm_nt(mid[rows], w_out[...]).astype(HALF)
            for h in range(width // HDIM):
                column = h * HDIM
                queries = joined[rows, column : column + HDIM]
                keys = joined[rows, width + column : width + column + HDIM]
                values = joined[rows, 2 * width + column : 2 * width + column + HDIM]
                grads = grad_blend[:, column : column + HDIM]
                scores = mm_nt(queries, keys) * HDIM**-0.5
                weights = jnp.exp(scores - jnp.max(scores, -1, keepdims=True))
                probs = weights * (1.0 / jnp.sum(weights, -1, keepdims=True))
                grad_values = mm_tn(probs.astype(HALF), grads)
                grad_probs = mm_nt(grads, values)
                grad_scores = (
                    probs * (grad_probs - jnp.sum(probs * grad_probs, -1, keepdims=True))
                ).astype(HALF)
                for third, value in enumerate(
                    (mm(grad_scores, keys) * HDIM**-0.5, mm_tn(grad_scores, queries) * HDIM**-0.5, grad_values)
                ):
                    start = third * width + column
                    grad_joined[rows, start : start + HDIM] = value.astype(HALF)
            return mm_nt(grad_joined[rows], w_qkv[...])

        for i in range(2):
            own_part[rows_at(i)] = attend_back(i)
            mid_sent[i].wait_recv()
            part_sent[rows_at(2 + i)] = attend_back(2 + i).astype(HALF)
            normed_sent[i].start()
        tall_product(second, grad_up_in, up_grad, 256)
        up_near.start()
        tall_product(blended, mid, out_grad, 128)
        out_near.start()
        for i in range(2):
            rows = rows_at(i)
            normed_sent[i].wait_recv()
            total = own_part[rows] + part_got[rows_at(2 + i)].astype(FLOAT)
            grad, gain, bias = norm_from(stream[rows], vec[1:2], total)
            count(1, gain)
            count(2, bias)
            grad = grad + own_rows_grad[rows]
            count(0, jnp.sum(grad, 0, keepdims=True))
            grad_low = grad.astype(HALF)
            emb_low[0, rows] = grad_low[:, : D // 2]
            emb_low[1, rows] = grad_low[:, D // 2 :]
            emb_sent[i].start()
        vec_sent.start()
        tall_product(normed, grad_joined, qkv_grad, 256)
        qkv_near.start()
        for one in emb_sent:
            one.wait()
        columns = jnp.concatenate([emb_low[x], emb_got[...]], 0)
        for start, depth, target in zip(SPAN, DEPTH, (patch_low, patch_mid, patch_high)):
            target[...] = mm_tn(shown[:, start : start + depth], columns).astype(HALF)
        patch_one.start()
        patch_two.start()
        vec_sent.wait()
        vec_part[...] += vec_got[...]
        vec_far.start()
        mine = [
            pltpu.make_async_copy(out_grad.at[pl.ds(out_rows, 96)], square_out.at[pl.ds(0, 96)], local_sem.at[1]),
            pltpu.make_async_copy(up_grad.at[pl.ds(0, up_rows)], up_out, local_sem.at[2]),
            pltpu.make_async_copy(patch_mid, patch_out, local_sem.at[3]),
        ]
        for one in mine:
            one.start()
        for one in low_sent + mid_sent + second_sent + normed_sent:
            one.wait_send()
        for one in (down_far, down_near, up_near, out_near, qkv_near, patch_one, patch_two, e2d_near, vec_far):
            one.wait_send()
        for one in mine:
            one.wait()

    for row in range(4):
        for side in range(2):
            if (row, side) != (HOST, 0):

                @pl.when((z == row) & (x == side))
                def _():
                    pick_copy(row, side).wait_send()

    for row, ones in ((0, (out_near, qkv_near, patch_one)), (2, (down_near, up_near, patch_two, e2d_near)), (LAST, (down_far, vec_far))):

        @pl.when(z == row)
        def _():
            for one in ones:
                one.wait_recv()


def encoder_backward(number, picked, shown, weights, stored):
    _, mats, e2d_w, vec = weights
    vmem = pl.BlockSpec(memory_space=pltpu.VMEM)
    anywhere = pl.BlockSpec(memory_space=pl.ANY)
    shapes = [
        ((D, 3 * D // 2), HALF),
        ((1248, D), HALF),
        ((672, FF // 2), HALF),
        ((704, D // 2), HALF),
        ((D // 2, DD), HALF),
        ((16, D), FLOAT),
    ]
    scratch = [
        ((2, 2, VISIBLE, DD), HALF),
        ((ALL, D), HALF),
        ((ALL, FF // 2), HALF),
        ((ALL, D), HALF),
        ((VISIBLE, D // 2), HALF),
        ((ALL, 3 * D // 2), HALF),
        ((ALL, D), HALF),
        ((ALL, D), HALF),
        ((OWN, D), FLOAT),
        ((OWN, D), FLOAT),
        ((2, OWN, D // 2), HALF),
        ((OWN, D // 2), HALF),
        ((FF // 2, D), HALF),
        ((D, FF // 2), HALF),
        ((D // 2, D), HALF),
        ((D, 3 * D // 2), HALF),
        ((704, D // 2), HALF),
        ((704, D // 2), HALF),
        ((192, D // 2), HALF),
        ((2, D // 2, DD), HALF),
        ((D // 2, DD), HALF),
        ((D // 2, DD), HALF),
        ((16, D), FLOAT),
        ((16, D), FLOAT),
    ]
    return pl.pallas_call(
        encoder_backward_kernel,
        name="encoder_backward",
        out_shape=[jax.ShapeDtypeStruct(*one) for one in shapes],
        in_specs=[vmem] * 18,
        out_specs=[anywhere] * len(shapes),
        scratch_shapes=[pltpu.VMEM(*one) for one in scratch]
        + [pltpu.SemaphoreType.DMA((28,)), pltpu.SemaphoreType.DMA((28,)), pltpu.SemaphoreType.DMA((4,))],
        compiler_params=pltpu.CompilerParams(
            collective_id=number, has_side_effects=True, vmem_limit_bytes=60 << 20
        ),
    )(picked, shown, *mats, e2d_w, vec, *stored)


def decoder_round(tokens, pixels_low, counted, weights):
    own, other, head_w, vec, head_b = weights
    count = pixels_low.shape[0]
    width = DD // 2
    normed = layer_norm(tokens, vec[2], vec[3]).astype(HALF)
    joined = mm(normed, own[0]).astype(HALF)
    queries, keys, values = [joined[:, i * width : (i + 1) * width] for i in range(3)]
    blended, totals = attn_forward(queries, keys, values)
    blend_own = blended[:count]
    blend_other = swap(blended[count:])
    stream = tokens[:count]
    attended = mm(blend_own, own[1]) + mm(blend_other, other[1]) + stream + vec[4]
    second = layer_norm(attended, vec[5], vec[6]).astype(HALF)
    w_up = jnp.concatenate([own[2], other[2]], 1)
    w_down = jnp.concatenate([own[3], other[3]], 0)
    upward = mm(second, w_up)
    activated = gelu_exact(upward).astype(HALF)
    decoded = mm(activated, w_down) + attended + vec[7]
    final_low = layer_norm(decoded, vec[8], vec[9]).astype(HALF)
    predicted = mm(final_low, head_w) + head_b
    pixels = pixels_low.astype(FLOAT)
    center = jnp.mean(pixels, -1, keepdims=True)
    spread = jnp.mean((pixels - center) ** 2, -1, keepdims=True)
    differ = predicted - (pixels - center) * lax.rsqrt(spread + 1e-06)
    loss = jnp.sum(jnp.mean(differ**2, -1) * counted)
    grad_pred = 2.0 / PATCH * differ * counted[:, None]
    pred_low = grad_pred.astype(HALF)
    head_grad = mm_tn(final_low, pred_low)
    head_b_grad = jnp.sum(grad_pred, 0)
    grad_out, gain_end, bias_end = norm_back(decoded, vec[8], vec[9], mm_nt(pred_low, head_w))
    grad_low = grad_out.astype(HALF)
    down_grad = mm_tn(activated, grad_low)
    down_bias = jnp.sum(grad_out, 0)
    _, gelu_pull = jax.vjp(gelu_exact, upward)
    grad_up_in = gelu_pull(mm_nt(grad_low, w_down))[0].astype(HALF)
    up_grad = mm_tn(second, grad_up_in)
    grad_att, gain_two, bias_two = norm_back(attended, vec[5], vec[6], mm_nt(grad_up_in, w_up))
    grad_att = grad_att + grad_out
    out_bias = jnp.sum(grad_att, 0)
    mid = grad_att.astype(HALF)
    grad_other = swap(mm_nt(mid, other[1]).astype(HALF))
    grad_blend = jnp.concatenate([mm_nt(mid, own[1]).astype(HALF), grad_other], 0)
    out_own, out_other = mm_tn(blend_own, mid), mm_tn(blend_other, mid)
    side = lax.axis_index("tensor")
    head_cols = PATCH // 2
    wide_other = jnp.concatenate(
        [
            up_grad[:, DFF // 2 :].astype(HALF),
            lax.dynamic_slice_in_dim(head_grad, (1 - side) * head_cols, head_cols, 1).astype(HALF),
        ],
        1,
    )
    tall_other = jnp.concatenate([down_grad[DFF // 2 :], out_other], 0).astype(HALF)
    wide = jnp.concatenate(
        [up_grad[:, : DFF // 2], lax.dynamic_slice_in_dim(head_grad, side * head_cols, head_cols, 1)], 1
    ) + swap(wide_other)
    tall = jnp.concatenate([down_grad[: DFF // 2], out_own], 0) + swap(tall_other)
    grad_joined = attn_backward(queries, keys, values, grad_blend, totals)
    joined_other = swap(grad_joined[count:])
    qkv_grad = mm_tn(normed, grad_joined)
    grad_normed = mm_nt(grad_joined[:count], own[0]) + mm_nt(joined_other, other[0])
    grad_in, gain_one, bias_one = norm_back(stream, vec[2], vec[3], grad_normed)
    grad_in = grad_in + grad_att
    vec_rows = [gain_one, bias_one, out_bias, gain_two, bias_two, down_bias, gain_end, bias_end]
    return loss, grad_in, (wide, tall, qkv_grad), vec_rows, head_b_grad


def tree_sum(part):
    z = lax.axis_index("dp")
    low = part.astype(HALF)
    part = part + hop_both(low, (0, 1), (2, 3)).astype(FLOAT)
    return part + hop_both(part.astype(HALF), (1, 3)).astype(FLOAT)


def hosted_round(
    patches,
    visible,
    frames_valid,
    clip_valid,
    rep_weights,
    ten_weights,
    rep_m,
    rep_v,
    ten_m,
    ten_v,
    rep_outer,
    ten_outer,
):
    side = lax.axis_index("tensor")
    z = lax.axis_index("dp")
    half_rows = TUBES // 2
    tube_ids = (jnp.arange(TUBES) + side * half_rows) % TUBES
    ids_one = hop(visible[:, 0, 0], ((0, 0), (HOST, 0)), ((2, 1), (HOST, 1)))
    ids_two = hop(visible[:, 0, 0], ((3, 1), (HOST, 1)))
    ids_two = jnp.where(side == 0, visible[:, 0, 0], ids_two)
    dec_places = sinus_at(tube_ids, DD)
    rep_master, ten_master = rep_weights, ten_weights[0]
    rep_first, rep_second = rep_m[0], rep_v[0]
    ten_first, ten_second = ten_m[0, 0], ten_v[0, 0]
    quarter = ten_master.shape[0]
    rep_quarter = rep_master.shape[0]
    rest = ENC_SIZE - 3 * quarter
    shown_steps = []
    for s in range(STEPS):
        picks = (visible[s, 0, 0][:, None] == jnp.arange(TUBES)[None, :]).astype(HALF)
        rows = mm(picks, patches[s, 0, 0]).astype(HALF)
        cuts = (0, rep_quarter // D, 2 * (rep_quarter // D), PATCH)
        rows = jnp.concatenate(
            [
                jnp.pad(rows[:, cuts[i] : cuts[i + 1]], ((0, 0), (0, room - cuts[i + 1] + cuts[i])))
                for i, room in enumerate((768, 768, 256))
            ],
            1,
        )
        one = hop(rows, ((0, 0), (HOST, 0)), ((2, 1), (HOST, 1)))
        two = hop(rows, ((3, 1), (HOST, 1)))
        own = jnp.concatenate([one, jnp.where(side == 0, rows, two)], 0)
        shown_steps.append(jnp.concatenate([own, swap(own, HOST)], 0))
    loss_list, count_list, norm_list = [], [], []
    for s in range(STEPS):
        enc_weights, dec_weights = hosted_weights(rep_master, ten_master, s == 0)
        ids = visible[s, 0, 0]
        picks = tube_ids[:, None] == ids[None, :]
        shown_here = jnp.any(picks, 1)
        counted = (
            jnp.where(shown_here, 0.0, 1.0)
            * (tube_ids // (TUBES // FRAMES) < frames_valid[s, 0, 0])
            * (clip_valid[s, 0, 0] == 1)
        ).astype(FLOAT)[:half_rows]
        shown = shown_steps[s]
        vis = ids.shape[0]
        ids_own = jnp.concatenate([ids_one[s], ids_two[s]])
        reduced_clip, enc_stored = encoder_forward(3 + s, shown[: 2 * vis], sinus_at(ids_own, D), enc_weights)
        dec_vec = dec_weights[3]
        placed = jnp.dot(
            picks.astype(FLOAT), reduced_clip + dec_vec[0], precision=lax.Precision.HIGHEST
        )
        tokens = jnp.where(shown_here[:, None], placed, dec_vec[1]) + dec_places
        pixels_low = lax.dynamic_slice_in_dim(patches[s, 0, 0], side * half_rows, half_rows, 0)
        loss, grad_tokens, (wide, tall, qkv_grad), vec_rows, head_b_grad = decoder_round(
            tokens, pixels_low, counted, dec_weights
        )
        shown_own = shown_here[:half_rows, None]
        e2d_b_grad = jnp.sum(jnp.where(shown_own, grad_tokens, 0.0), 0)
        mask_grad = jnp.sum(jnp.where(shown_own, 0.0, grad_tokens), 0)
        picked = mm_tn(picks[:half_rows].astype(HALF), grad_tokens.astype(HALF)).astype(HALF)
        small = jnp.concatenate(
            [jnp.stack([e2d_b_grad, mask_grad] + vec_rows).reshape(-1), head_b_grad]
        )
        small = small + swap(small)
        small = small + hop_both(small, (0, 1), (2, 3))
        small = small + hop_both(small, (1, 3))
        wide, tall, qkv_sum = tree_sum(wide), tree_sum(tall), tree_sum(qkv_grad)
        qkv_got, square_got, up_got, patch_got, e2d_got, vec_got = encoder_backward(
            5 + s, picked, shown, enc_weights, enc_stored
        )
        head_rows = (3 * rep_quarter - PATCH_SIZE - E2D_SIZE) // PATCH
        head_cols = PATCH // 2
        head_low = wide[:, DFF // 2 :].astype(HALF)
        head_three = hop_both(head_low[:head_rows], (LAST, 2))
        head_low = jnp.where(
            z == LAST, head_low, jnp.concatenate([head_three, jnp.zeros((DD - head_rows, head_cols), HALF)], 0)
        )
        head_other = swap(head_low, 2, LAST)
        head_sum = jnp.concatenate(
            [jnp.where(side == 0, head_low, head_other), jnp.where(side == 0, head_other, head_low)], 1
        )
        patch_cut = rep_quarter // D
        patch_tail = PATCH - 2 * patch_cut
        narrow = jnp.concatenate(
            [patch_got[:192], jnp.where(z == 2, jnp.pad(e2d_got, ((0, 128), (0, 0))), patch_got[192:])], 0
        )
        narrow_other = swap(narrow, 0, 1, 2)
        narrow_low = jnp.where(side == 0, narrow, narrow_other)
        narrow_high = jnp.where(side == 0, narrow_other, narrow)
        flats = lambda *parts: jnp.concatenate([one.astype(FLOAT).reshape(-1) for one in parts])

        def patch_rows(count):
            return jnp.concatenate([narrow_low[:count], narrow_high[:count]], 1)

        def first_owner():
            return flats(qkv_got, square_got[:288]), flats(patch_rows(patch_cut))

        def second_owner():
            return flats(square_got[:96], up_got), flats(patch_rows(patch_cut))

        def third_owner():
            return flats(up_got[:96], square_got), flats(
                patch_rows(patch_tail),
                narrow_low[192 : 192 + D // 2],
                narrow_high[192 : 192 + D // 2],
                head_sum[:head_rows],
            )

        def last_owner():
            return flats(
                square_got[:288], qkv_sum, tall[DFF // 2 :], wide[:, : DFF // 2], tall[: DFF // 2]
            ), flats(head_sum[head_rows:], vec_got[:9], small)

        ten_part, rep_part = lax.switch(z, [first_owner, second_owner, third_owner, last_owner])
        squares = jnp.sum(ten_part * ten_part) + jnp.sum(rep_part * rep_part) / 2
        square_all, loss_all, count_all = lax.psum((squares, loss, jnp.sum(counted)), ("dp", "tensor"))
        norm_value = jnp.sqrt(square_all + 1e-30) / count_all
        factor = jnp.minimum(1.0, CLIP / norm_value) / count_all
        number = STEP_BEFORE + s + 1
        rep_master, rep_first, rep_second = adamw(rep_master, rep_first, rep_second, rep_part * factor, number)
        ten_master, ten_first, ten_second = adamw(ten_master, ten_first, ten_second, ten_part * factor, number)
        loss_list.append(loss_all)
        count_list.append(count_all)
        norm_list.append(norm_value)
    groups_count = lax.axis_size("group")
    rep_diff, ten_diff = group_mean(rep_weights - rep_master), group_mean(ten_weights[0] - ten_master)
    rep_momentum = MOMENTUM * rep_outer + rep_diff
    ten_momentum = MOMENTUM * ten_outer[0] + ten_diff
    rep_new = rep_weights - LR_OUT * (rep_diff + MOMENTUM * rep_momentum)
    ten_new = ten_weights[0] - LR_OUT * (ten_diff + MOMENTUM * ten_momentum)
    return (
        jnp.stack(loss_list)[:, None],
        jnp.stack(count_list)[:, None],
        jnp.stack(norm_list)[:, None],
        rep_first[None],
        rep_second[None],
        ten_first[None, None],
        ten_second[None, None],
        rep_diff,
        ten_diff[None],
        rep_momentum,
        ten_momentum[None],
        rep_new,
        ten_new[None],
    )


def group_mean(diff):
    if lax.axis_size("group") != 4:
        return lax.psum(diff, "group") / lax.axis_size("group")
    odd = lax.axis_index("group") % 2 == 1
    half = diff.shape[0] // 2
    low, high = diff[:half], diff[half:]
    part = jnp.where(odd, high, low) + partner(jnp.where(odd, low, high))
    part_low = part.astype(HALF)
    far = lax.ppermute(part_low, "group", [(g, g ^ 2) for g in range(4)])
    total = (part_low.astype(FLOAT) + far.astype(FLOAT)) * 0.25
    other = partner(total)
    return jnp.concatenate([jnp.where(odd, other, total), jnp.where(odd, total, other)])


def solution(mesh):
    placed = (
        P(None, "group", "dp", None, None),
        P(None, "group", "dp", None),
        P(None, "group", "dp"),
        P(None, "group", "dp"),
        P("dp"),
        P("tensor", "dp"),
        P("group", "dp"),
        P("group", "dp"),
        P("group", "tensor", "dp"),
        P("group", "tensor", "dp"),
        P("dp"),
        P("tensor", "dp"),
    )
    return jax.shard_map(
        hosted_round if mesh.shape["dp"] == 4 and mesh.shape["tensor"] == 2 and mesh.shape["group"] % 2 == 0 else on_device,
        mesh=mesh,
        in_specs=placed,
        out_specs=(
            P(None, "group"),
            P(None, "group"),
            P(None, "group"),
            P("group", "dp"),
            P("group", "dp"),
            P("group", "tensor", "dp"),
            P("group", "tensor", "dp"),
            P("dp"),
            P("tensor", "dp"),
            P("dp"),
            P("tensor", "dp"),
            P("dp"),
            P("tensor", "dp"),
        ),
        check_vma=False,
    )
```

```python
import functools
import math

import jax
import jax.numpy as jnp
from jax import lax
from jax.experimental import pallas as pl
from jax.experimental.pallas import tpu as pltpu
from jax.sharding import PartitionSpec as P

D = 768
HDIM = 64
FF = 3072
DD = 384
DFF = 1536
PATCH = 1536
TUBES = 1568
FRAMES = 8
STEPS = 2
STEP_BEFORE = 6


CLIP = 0.001
LR_IN = 0.01
BETA1 = 0.9
BETA2 = 0.95
EPS = 1e-08
DECAY = 0.05
LR_OUT = 0.7
MOMENTUM = 0.9
FLOAT = jnp.float32
HALF = jnp.bfloat16


def sinus(count, width):
    places = jnp.arange(count).astype(jnp.float32)[:, None]
    column = jnp.arange(width)
    decays = jnp.power(10000.0, -2.0 * (column // 2).astype(jnp.float32) / width)
    angles = places * decays[None, :]
    return jnp.where(column % 2 == 0, jnp.sin(angles), jnp.cos(angles))


def layer_norm(stream, gain, bias):
    center = jnp.mean(stream, -1, keepdims=True)
    spread = jnp.mean((stream - center) ** 2, -1, keepdims=True)
    return (stream - center) * lax.rsqrt(spread + 1e-06) * gain + bias


def norm_back(stream, gain, bias, cotangent):
    _, pull = jax.vjp(layer_norm, stream, gain, bias)
    return pull(cotangent)


def gelu_exact(values):
    return jax.nn.gelu(values, approximate=False)


def split_flat(flat, shapes):
    pieces = []
    offset = 0
    for shapes_one in shapes:
        length = math.prod(shapes_one)
        pieces.append(flat[offset : offset + length].reshape(shapes_one))
        offset += length
    return pieces


def own_rows(stream, axis_dim):
    count = stream.shape[axis_dim] // lax.axis_size("tensor")
    return lax.dynamic_slice_in_dim(stream, lax.axis_index("tensor") * count, count, axis_dim)


def rows_sum(partial_rows):
    return lax.psum_scatter(partial_rows, "tensor", scatter_dimension=1, tiled=True)


def rows_full(own_part):
    return lax.all_gather(own_part, "tensor", axis=1, tiled=True)


def block_forward(stream, mats, vecs):
    w_qkv, w_out, w_up, w_down = mats
    gain_one, bias_one, out_bias, gain_two, bias_two, down_bias = vecs
    nclips, length, _ = stream.shape
    head_cols = w_out.shape[0]
    nheads = head_cols // HDIM
    normed = layer_norm(stream, gain_one, bias_one).astype(HALF)
    joined = jnp.dot(normed, w_qkv, preferred_element_type=FLOAT).astype(HALF)
    queries, key_rows, values = [
        joined[:, :, third_id * head_cols : (third_id + 1) * head_cols].reshape(
            nclips, length, nheads, HDIM
        )
        for third_id in range(3)
    ]
    scores = jnp.einsum(
        "cqhd,ckhd->chqk", queries, key_rows, preferred_element_type=FLOAT
    ) * HDIM ** (-0.5)
    highest = jnp.max(scores, -1, keepdims=True)
    totals = jnp.log(jnp.sum(jnp.exp(scores - highest), -1, keepdims=True)) + highest
    probs_low = jnp.exp(scores - totals).astype(HALF)
    blended = (
        jnp.einsum("chqk,ckhd->cqhd", probs_low, values, preferred_element_type=FLOAT)
        .astype(HALF)
        .reshape(nclips, length, head_cols)
    )
    attended = (
        rows_sum(jnp.dot(blended, w_out, preferred_element_type=FLOAT))
        + own_rows(stream, 1)
        + out_bias
    )
    second = layer_norm(attended, gain_two, bias_two).astype(HALF)
    second_all = lax.all_gather(second, "tensor", axis=1, tiled=True)
    upward = jnp.dot(second_all, w_up, preferred_element_type=FLOAT)
    activated = gelu_exact(upward).astype(HALF)
    result = (
        rows_sum(jnp.dot(activated, w_down, preferred_element_type=FLOAT)) + attended + down_bias
    )
    stored = (
        stream,
        normed,
        queries,
        key_rows,
        values,
        totals,
        blended,
        attended,
        second_all,
        upward,
        activated,
    )
    return (rows_full(result), stored)


def block_backward(grad_out, mats, vecs, stored):
    w_qkv, w_out, w_up, w_down = mats
    gain_one, bias_one, out_bias, gain_two, bias_two, down_bias = vecs
    (
        stream,
        normed,
        queries,
        key_rows,
        values,
        totals,
        blended,
        attended,
        second_all,
        upward,
        activated,
    ) = stored
    nclips, length, _ = stream.shape
    head_cols = w_out.shape[0]
    grad_low = grad_out.astype(HALF)
    grad_down = jnp.einsum("ctf,ctd->fd", activated, grad_low, preferred_element_type=FLOAT)
    down_bias_grad = jnp.sum(own_rows(grad_out, 1), (0, 1))
    grad_act = jnp.dot(grad_low, w_down.T, preferred_element_type=FLOAT)
    _, gelu_pull = jax.vjp(gelu_exact, upward)
    grad_up_in = gelu_pull(grad_act)[0].astype(HALF)
    grad_up = jnp.einsum("ctd,ctf->df", second_all, grad_up_in, preferred_element_type=FLOAT)
    grad_second = rows_sum(jnp.dot(grad_up_in, w_up.T, preferred_element_type=FLOAT))
    grad_att, gain_two_grad, bias_two_grad = norm_back(attended, gain_two, bias_two, grad_second)
    grad_att = grad_att + own_rows(grad_out, 1)
    out_bias_grad = jnp.sum(grad_att, (0, 1))
    grad_mid = rows_full(grad_att)
    mid_low = grad_mid.astype(HALF)
    grad_wout = jnp.einsum("cth,ctd->hd", blended, mid_low, preferred_element_type=FLOAT)
    nheads = head_cols // HDIM
    grad_blend = (
        jnp.dot(mid_low, w_out.T, preferred_element_type=FLOAT)
        .astype(HALF)
        .reshape(nclips, length, nheads, HDIM)
    )
    scores = jnp.einsum(
        "cqhd,ckhd->chqk", queries, key_rows, preferred_element_type=FLOAT
    ) * HDIM ** (-0.5)
    probs_full = jnp.exp(scores - totals)
    probs_low = probs_full.astype(HALF)
    grad_values = jnp.einsum("chqk,cqhd->ckhd", probs_low, grad_blend, preferred_element_type=FLOAT)
    grad_probs = jnp.einsum("cqhd,ckhd->chqk", grad_blend, values, preferred_element_type=FLOAT)
    grad_scores = (
        probs_full * (grad_probs - jnp.sum(probs_full * grad_probs, -1, keepdims=True))
    ).astype(HALF)
    grad_queries = jnp.einsum(
        "chqk,ckhd->cqhd", grad_scores, key_rows, preferred_element_type=FLOAT
    ) * HDIM ** (-0.5)
    grad_keys = jnp.einsum(
        "chqk,cqhd->ckhd", grad_scores, queries, preferred_element_type=FLOAT
    ) * HDIM ** (-0.5)
    grad_joined = jnp.concatenate(
        [
            part_grad.reshape(nclips, length, head_cols)
            for part_grad in (grad_queries, grad_keys, grad_values)
        ],
        -1,
    ).astype(HALF)
    grad_qkv = jnp.einsum("ctd,cte->de", normed, grad_joined, preferred_element_type=FLOAT)
    grad_norm_in = rows_sum(jnp.dot(grad_joined, w_qkv.T, preferred_element_type=FLOAT))
    grad_in, gain_one_grad, bias_one_grad = norm_back(
        own_rows(stream, 1), gain_one, bias_one, grad_norm_in
    )
    grad_in = grad_in + grad_att
    vec_grads = jnp.stack(
        [gain_one_grad, bias_one_grad, out_bias_grad, gain_two_grad, bias_two_grad, down_bias_grad]
    )
    return (rows_full(grad_in), (grad_qkv, grad_wout, grad_up, grad_down), vec_grads)


def group_step(patch_rows, visible_ids, shown, weight_rows, rep_full, ten_full):
    splits = lax.axis_size("tensor")
    patch_w, e2d_w, head_w, enc_vec, dec_vec, head_b = split_flat(
        rep_full, [(PATCH, D), (D, DD), (DD, PATCH), (9, D), (10, DD), (PATCH,)]
    )
    enc_vec = enc_vec.astype(FLOAT)
    dec_vec = dec_vec.astype(FLOAT)
    head_b = head_b.astype(FLOAT)
    enc_cols = D // splits
    dec_cols = DD // splits
    ten_pieces = split_flat(
        ten_full,
        [
            (D, 3 * enc_cols),
            (enc_cols, D),
            (D, FF // splits),
            (FF // splits, D),
            (DD, 3 * dec_cols),
            (dec_cols, DD),
            (DD, DFF // splits),
            (DFF // splits, DD),
        ],
    )
    enc_mats = ten_pieces[0:4]
    dec_mats = ten_pieces[4:8]
    enc_vecs = [enc_vec[i] for i in range(1, 7)]
    dec_vecs = [dec_vec[i] for i in range(2, 8)]
    shown_rows = jnp.take_along_axis(patch_rows, visible_ids[:, :, None], 1)
    embedded = (
        jnp.dot(shown_rows, patch_w, preferred_element_type=FLOAT)
        + enc_vec[0]
        + sinus(TUBES, D)[visible_ids]
    )
    encoded, enc_stored = block_forward(embedded, enc_mats, enc_vecs)
    final_enc = layer_norm(encoded, enc_vec[7], enc_vec[8]).astype(HALF)
    reduced = jnp.dot(final_enc, e2d_w, preferred_element_type=FLOAT) + dec_vec[0]
    blank = jnp.broadcast_to(dec_vec[1], (TUBES, DD))
    tokens_in = jax.vmap(lambda clip_ids, clip_rows: blank.at[clip_ids].set(clip_rows))(
        visible_ids, reduced
    ) + sinus(TUBES, DD)
    decoded, dec_stored = block_forward(tokens_in, dec_mats, dec_vecs)
    own_dec = own_rows(decoded, 1)
    final_low = layer_norm(own_dec, dec_vec[8], dec_vec[9]).astype(HALF)
    predicted = jnp.dot(final_low, head_w, preferred_element_type=FLOAT) + head_b
    pixels = own_rows(patch_rows, 1).astype(FLOAT)
    center = jnp.mean(pixels, -1, keepdims=True)
    spread = jnp.mean((pixels - center) ** 2, -1, keepdims=True)
    target = (pixels - center) * lax.rsqrt(spread + 1e-06)
    differ = predicted - target
    counted = own_rows(weight_rows, 1)
    loss_part = jnp.sum(jnp.mean(differ**2, -1) * counted)
    grad_pred = 2.0 / PATCH * differ * counted[:, :, None]
    pred_low = grad_pred.astype(HALF)
    head_w_grad = jnp.einsum("ctd,ctp->dp", final_low, pred_low, preferred_element_type=FLOAT)
    head_b_grad = jnp.sum(grad_pred, (0, 1))
    grad_final = jnp.dot(pred_low, head_w.T, preferred_element_type=FLOAT)
    grad_dec_own, dec_gain_grad, dec_bias_grad = norm_back(
        own_dec, dec_vec[8], dec_vec[9], grad_final
    )
    grad_tokens, dec_mat_grads, dec_vec_grads = block_backward(
        rows_full(grad_dec_own), dec_mats, dec_vecs, dec_stored
    )
    masked_own = own_rows(1.0 - shown.astype(FLOAT), 1)
    mask_grad = jnp.sum(own_rows(grad_tokens, 1) * masked_own[:, :, None], (0, 1))
    grad_reduced = own_rows(jnp.take_along_axis(grad_tokens, visible_ids[:, :, None], 1), 1)
    reduced_low = grad_reduced.astype(HALF)
    e2d_grad = jnp.einsum(
        "ctd,cte->de", own_rows(final_enc, 1), reduced_low, preferred_element_type=FLOAT
    )
    e2d_b_grad = jnp.sum(grad_reduced, (0, 1))
    grad_enc_final = jnp.dot(reduced_low, e2d_w.T, preferred_element_type=FLOAT)
    grad_enc_own, enc_gain_grad, enc_bias_grad = norm_back(
        own_rows(encoded, 1), enc_vec[7], enc_vec[8], grad_enc_final
    )
    grad_embedded, enc_mat_grads, enc_vec_grads = block_backward(
        rows_full(grad_enc_own), enc_mats, enc_vecs, enc_stored
    )
    own_embedded = own_rows(grad_embedded, 1)
    patch_grad = jnp.einsum(
        "ctp,ctd->pd",
        own_rows(shown_rows, 1),
        own_embedded.astype(HALF),
        preferred_element_type=FLOAT,
    )
    patch_b_grad = jnp.sum(own_embedded, (0, 1))
    enc_vec_grad = jnp.concatenate(
        [patch_b_grad[None], enc_vec_grads, enc_gain_grad[None], enc_bias_grad[None]], 0
    )
    dec_vec_grad = jnp.concatenate(
        [
            e2d_b_grad[None],
            mask_grad[None],
            dec_vec_grads,
            dec_gain_grad[None],
            dec_bias_grad[None],
        ],
        0,
    )
    rep_grad = jnp.concatenate(
        [
            patch_grad.reshape(-1),
            e2d_grad.reshape(-1),
            head_w_grad.reshape(-1),
            enc_vec_grad.reshape(-1),
            dec_vec_grad.reshape(-1),
            head_b_grad,
        ]
    )
    ten_grad = jnp.concatenate(
        [mat_grad.reshape(-1) for mat_grad in list(enc_mat_grads) + list(dec_mat_grads)]
    )
    return (loss_part, rep_grad, ten_grad)


def adamw(master, first, second, clipped, number):
    first = BETA1 * first + (1 - BETA1) * clipped
    second = BETA2 * second + (1 - BETA2) * clipped * clipped
    first_hat = first / (1 - BETA1**number)
    second_hat = second / (1 - BETA2**number)
    master = master - LR_IN * (first_hat / (jnp.sqrt(second_hat) + EPS) + DECAY * master)
    return (master, first, second)


def on_device(
    patches,
    visible,
    frames_valid,
    clip_valid,
    rep_weights,
    ten_weights,
    rep_m,
    rep_v,
    ten_m,
    ten_v,
    rep_outer,
    ten_outer,
):
    splits = lax.axis_size("tensor")
    owners = lax.axis_size("dp")
    tube_ids = jnp.arange(TUBES)
    rep_master, ten_master = (rep_weights, ten_weights[0])
    rep_first, rep_second = (rep_m[0], rep_v[0])
    ten_first, ten_second = (ten_m[0, 0], ten_v[0, 0])
    loss_list, count_list, norm_list = ([], [], [])
    for inner_step in range(STEPS):
        rep_full, ten_full = (
            lax.all_gather(rep_master.astype(HALF), "dp", axis=0, tiled=True),
            lax.all_gather(ten_master.astype(HALF), "dp", axis=0, tiled=True),
        )
        visible_ids = visible[inner_step, 0]
        shown = jnp.any(visible_ids[:, :, None] == tube_ids[None, None, :], axis=1)
        weight_rows = (
            jnp.where(shown, 0.0, 1.0)
            * (tube_ids[None, :] // (TUBES // FRAMES) < frames_valid[inner_step, 0][:, None])
            * (clip_valid[inner_step, 0][:, None] == 1)
        ).astype(FLOAT)
        count_part = jnp.sum(own_rows(weight_rows, 1))
        loss_part, rep_grad, ten_grad = group_step(
            patches[inner_step, 0], visible_ids, shown, weight_rows, rep_full, ten_full
        )
        rep_recv, ten_recv = (
            lax.all_to_all(
                rep_grad.reshape(owners, -1), "dp", split_axis=0, concat_axis=0, tiled=True
            ),
            lax.all_to_all(
                ten_grad.reshape(owners, -1), "dp", split_axis=0, concat_axis=0, tiled=True
            ),
        )
        rep_part = lax.psum(jnp.sum(rep_recv, 0), "tensor")
        ten_part = jnp.sum(ten_recv, 0)
        squares = jnp.sum(ten_part * ten_part) + jnp.sum(rep_part * rep_part) / splits
        square_all, loss_all, count_all = lax.psum(
            (squares, loss_part, count_part), ("dp", "tensor")
        )
        norm_value = jnp.sqrt(square_all + 1e-30) / count_all
        factor = jnp.minimum(1.0, CLIP / norm_value) / count_all
        number = STEP_BEFORE + inner_step + 1
        rep_master, rep_first, rep_second = adamw(
            rep_master, rep_first, rep_second, rep_part * factor, number
        )
        ten_master, ten_first, ten_second = adamw(
            ten_master, ten_first, ten_second, ten_part * factor, number
        )
        loss_list.append(loss_all)
        count_list.append(count_all)
        norm_list.append(norm_value)
    rep_sum, ten_sum = lax.psum((rep_weights - rep_master, ten_weights[0] - ten_master), "group")
    groups_count = lax.axis_size("group")
    rep_diff = rep_sum / groups_count
    ten_diff = ten_sum / groups_count
    rep_momentum = MOMENTUM * rep_outer + rep_diff
    ten_momentum = MOMENTUM * ten_outer[0] + ten_diff
    rep_new = rep_weights - LR_OUT * (rep_diff + MOMENTUM * rep_momentum)
    ten_new = ten_weights[0] - LR_OUT * (ten_diff + MOMENTUM * ten_momentum)
    return (
        jnp.stack(loss_list)[:, None],
        jnp.stack(count_list)[:, None],
        jnp.stack(norm_list)[:, None],
        rep_first[None],
        rep_second[None],
        ten_first[None, None],
        ten_second[None, None],
        rep_diff,
        ten_diff[None],
        rep_momentum,
        ten_momentum[None],
        rep_new,
        ten_new[None],
    )


NT=(((1,),(1,)),((),()))
NN=(((1,),(0,)),((),()))
TILE=224
def dot(a,b,dims): return lax.dot_general(a,b,dims,preferred_element_type=FLOAT)

def attn_forward_kernel(q_ref,k_ref,v_ref,out_ref,lse_ref):
    heads=q_ref.shape[1]//HDIM; tiles=q_ref.shape[0]//TILE
    for h in range(heads):
        cols=slice(h*HDIM,(h+1)*HDIM)
        keys=k_ref[:,cols]*HALF(HDIM**-0.5)
        vt=v_ref[:,cols].T
        def step(t,_):
            rows=pl.ds(pl.multiple_of(t*TILE,TILE),TILE)
            s=dot(keys,q_ref[rows,cols],NT)
            m=jnp.max(s,0,keepdims=True)
            e=jnp.exp(s-m)
            total=jnp.sum(e,0,keepdims=True)
            p=(e*(1.0/total)).astype(HALF)
            bt=dot(vt,p,NN)
            out_ref[rows,cols]=bt.T.astype(HALF)
            lse_ref[h,pl.ds(t,1),:]=m+jnp.log(total)
            return 0
        lax.fori_loop(0,tiles,step,0)

def attn_forward(q,k,v):
    rows,width=q.shape
    vm=pl.BlockSpec(memory_space=pltpu.VMEM)
    return pl.pallas_call(attn_forward_kernel,name="attn_forward",
      out_shape=(jax.ShapeDtypeStruct((rows,width),HALF),jax.ShapeDtypeStruct((width//HDIM,rows//TILE,TILE),FLOAT)),
      in_specs=[vm]*3,out_specs=(vm,vm),
      compiler_params=pltpu.CompilerParams(vmem_limit_bytes=48<<20),
      cost_estimate=pl.CostEstimate(flops=4*rows*rows*width,bytes_accessed=rows*width*8,transcendentals=rows*rows*width//HDIM))(q,k,v)

def attn_backward_kernel(q_ref,k_ref,v_ref,g_ref,lse_ref,out_ref,dk_ref,dv_ref):
    width=q_ref.shape[1]
    heads=width//HDIM; tiles=q_ref.shape[0]//TILE
    for h in range(heads):
        cols=slice(h*HDIM,(h+1)*HDIM)
        keys=k_ref[:,cols]*HALF(HDIM**-0.5)
        values=v_ref[:,cols]
        kt=keys.T
        dk_ref[...]=jnp.zeros_like(dk_ref); dv_ref[...]=jnp.zeros_like(dv_ref)
        def step(t,_):
            rows=pl.ds(pl.multiple_of(t*TILE,TILE),TILE)
            q=q_ref[rows,cols]; g=g_ref[rows,cols]
            p=jnp.exp(dot(keys,q,NT)-lse_ref[h,pl.ds(t,1),:])
            dv_ref[...]+=dot(p.astype(HALF),g,NN)
            dp=dot(values,g,NT)
            ds=(p*(dp-jnp.sum(p*dp,0,keepdims=True))).astype(HALF)
            dk_ref[...]+=dot(ds,q,NN)
            out_ref[rows,cols]=dot(kt,ds,NN).T.astype(HALF)
            return 0
        lax.fori_loop(0,tiles,step,0)
        out_ref[:,width+h*HDIM:width+(h+1)*HDIM]=(dk_ref[...]*HDIM**-0.5).astype(HALF)
        out_ref[:,2*width+h*HDIM:2*width+(h+1)*HDIM]=dv_ref[...].astype(HALF)

def attn_backward(q,k,v,g,lse):
    rows,width=q.shape
    vm=pl.BlockSpec(memory_space=pltpu.VMEM)
    return pl.pallas_call(attn_backward_kernel,name="attn_backward",
      out_shape=jax.ShapeDtypeStruct((rows,3*width),HALF),
      in_specs=[vm]*5,out_specs=vm,
      scratch_shapes=[pltpu.VMEM((rows,HDIM),FLOAT),pltpu.VMEM((rows,HDIM),FLOAT)],
      compiler_params=pltpu.CompilerParams(vmem_limit_bytes=48<<20),
      cost_estimate=pl.CostEstimate(flops=10*rows*rows*width,bytes_accessed=rows*width*14,transcendentals=rows*rows*width//HDIM))(q,k,v,g,lse)


HOST = 1
LAST = 3
SWAP = [(0, 1), (1, 0)]
ENC_SHAPES = [(D, 3 * D // 2), (D // 2, D), (D, FF // 2), (FF // 2, D)]
DEC_SHAPES = [(DD, 3 * DD // 2), (DD // 2, DD), (DD, DFF // 2), (DFF // 2, DD)]
ENC_SIZE = sum(math.prod(one) for one in ENC_SHAPES)
DEC_SIZE = sum(math.prod(one) for one in DEC_SHAPES)
PATCH_SIZE = PATCH * D
E2D_SIZE = D * DD
HEAD_SIZE = DD * PATCH
ENC_VECS = 9 * D
DEC_VECS = 10 * DD


def hop(value, *moves):
    pairs = [(2 * a + b, 2 * c + d) for (a, b), (c, d) in moves]
    return lax.ppermute(value, ("dp", "tensor"), pairs)


def hop_both(value, *moves):
    return hop(value, *[((a, side), (b, side)) for a, b in moves for side in range(2)])


def swap(value, *where):
    if where:
        return hop(value, *[((z, side), (z, 1 - side)) for z in where for side in range(2)])
    return lax.ppermute(value, "tensor", SWAP)


def partner(value):
    count = lax.axis_size("group")
    return lax.ppermute(value, "group", [(g, g ^ 1) for g in range(count)])


def mm(left, right):
    return jnp.dot(left, right, preferred_element_type=FLOAT)


def mm_nt(left, right):
    return lax.dot_general(left, right, (((1,), (1,)), ((), ())), preferred_element_type=FLOAT)


def mm_tn(left, right):
    return lax.dot_general(left, right, (((0,), (0,)), ((), ())), preferred_element_type=FLOAT)


def sinus_at(ids, width):
    column = jnp.arange(width)
    decays = jnp.power(10000.0, -2.0 * (column // 2).astype(FLOAT) / width)
    angles = ids.astype(FLOAT)[:, None] * decays[None, :]
    return jnp.where(column % 2 == 0, jnp.sin(angles), jnp.cos(angles))


(
    QKV,
    SQUARE,
    UP,
    PATCH_ROWS,
    E2D,
    HEAD,
    VECS,
    DEC_QKV,
    DEC_OUT,
    DEC_UP,
    DEC_DOWN,
    HEAD_HALF,
    PATCH_LOW,
    PATCH_HIGH,
    W_QKV,
    W_OUT,
    W_UP,
    W_DOWN,
    E2D_W,
    HEAD_UP,
    SEND_ENC,
    SEND_MATE,
    CHAIN,
    CROSS,
    MATE_OWN,
    MATE_OTHER,
) = range(26)
PIECES = {
    QKV: (768, 1152),
    SQUARE: (1248, 768),
    UP: (672, 1536),
    PATCH_ROWS: (704, 768),
    E2D: (768, 384),
    HEAD: (64, 1536),
    VECS: (16, 768),
    DEC_QKV: (384, 576),
    DEC_OUT: (192, 384),
    DEC_UP: (384, 768),
    DEC_DOWN: (768, 384),
}


DEC_PARTS = [DEC_QKV, DEC_OUT, DEC_UP, DEC_DOWN, HEAD_HALF]
SENT = [QKV, SQUARE, UP, PATCH_ROWS, E2D, HEAD, VECS] + DEC_PARTS
ENC_PARTS = [
    (PATCH_LOW, 704, 0, PATCH_ROWS, 0),
    (W_QKV, 768, 0, QKV, 0),
    (W_OUT, 288, 0, SQUARE, 0),
    (W_OUT, 96, 1, SQUARE, 288),
    (PATCH_HIGH, 192, 2, PATCH_ROWS, 0),
    (W_UP, 672, 1, UP, 0),
    (W_UP, 96, 2, UP, 672),
    (W_DOWN, 1248, 2, SQUARE, 0),
    (W_DOWN, 288, 3, SQUARE, 1248),
    (E2D_W, 768, 2, E2D, 0),
]
GOT = {
    PATCH_LOW: (704, 768),
    PATCH_HIGH: (192, 768),
    W_QKV: (768, 1152),
    W_OUT: (384, 768),
    W_UP: (768, 1536),
    W_DOWN: (1536, 768),
    E2D_W: (768, 384),
    HEAD: (64, 1536),
    VECS: (16, 768),
}
MESH_ID = pl.DeviceIdType.MESH


def weights_kernel(shared, *refs):
    sent = dict(zip(SENT, refs[: len(SENT)]))
    refs = refs[len(SENT) :]
    got = dict(zip(GOT, refs[: len(GOT)]))
    refs = refs[len(GOT) :]
    own = dict(zip(DEC_PARTS, refs[: len(DEC_PARTS)]))
    other = dict(zip(DEC_PARTS, refs[len(DEC_PARTS) : 2 * len(DEC_PARTS)]))
    send_sem, recv_sem, local_sem = refs[2 * len(DEC_PARTS) :]
    g, z, x = lax.axis_index("group"), lax.axis_index("dp"), lax.axis_index("tensor")
    odd = lax.rem(g, 2)
    mate = (g + 1 - 2 * odd, z, x)
    across = (g, z, 1 - x)

    def at(row):
        return (g, row, x)

    def greet(peer):
        pl.semaphore_signal(barrier, inc=1, device_id=peer, device_id_type=MESH_ID)

    barrier = pltpu.get_barrier_semaphore()
    greet(across)
    near = {0: [1], 1: [0, 2, 3], 2: [1, 3], 3: [2, 1]}
    if shared:
        greet(mate)
    for row, peers in near.items():

        @pl.when(z == row)
        def _():
            for peer in peers:
                greet(at(peer))
            pl.semaphore_wait(barrier, len(peers) + (2 if shared else 1))

    def part(ref, start, count, half):
        if not half:
            return ref.at[pl.ds(start, count)]
        return ref.at[pl.ds(pl.multiple_of(start + odd * (count // 2), 16), count // 2)]

    numbers = {}

    def copy(key, source, target, peer):
        index = numbers.setdefault(key, len(numbers))
        return pltpu.make_async_remote_copy(
            src_ref=source,
            dst_ref=target,
            send_sem=send_sem.at[index],
            recv_sem=recv_sem.at[index],
            device_id=peer,
            device_id_type=MESH_ID,
        )

    def enc_copy(item):
        name, count, owner, piece, first = item
        return copy(
            (SEND_ENC, name, first),
            part(sent[piece], 0, count, shared),
            part(got[name], first, count, shared),
            at(HOST),
        )

    def enc_mate(item):
        name, count, owner, piece, first = item
        half = part(got[name], first, count, True)
        return copy((SEND_MATE, name, first), half, half, mate)

    def local(index, source, target):
        return pltpu.make_async_copy(source, target, local_sem.at[index])

    def chain(name, source, peer):
        target = got[name] if name in got else own[name]
        rows = source.shape[0]
        half = shared and name in own
        return copy((CHAIN, name), part(source, 0, rows, half), part(target, 0, rows, half), at(peer))

    def cross(name, source):
        rows = source.shape[0]
        return copy(
            (CROSS, name), part(source, 0, rows, shared), part(other[name], 0, rows, shared), across
        )

    def mates(name, ref, label):
        half = part(ref, 0, ref.shape[0], True)
        return copy((label, name), half, half, mate)

    def owned(row):
        return [item for item in ENC_PARTS if item[2] == row and row != HOST]

    for item in ENC_PARTS:
        numbers[(SEND_ENC, item[0], item[4])] = len(numbers)
        numbers[(SEND_MATE, item[0], item[4])] = len(numbers)
    for name in DEC_PARTS + [VECS, HEAD, HEAD_UP]:
        for label in (CHAIN, CROSS, MATE_OWN, MATE_OTHER):
            numbers[(label, name)] = len(numbers)

    def head_up():
        return copy((CHAIN, HEAD_UP), sent[HEAD], got[HEAD], at(LAST))

    def finish_dec(name, source, here):
        cross(name, source).start()
        if shared and not here:
            mates(name, own[name], MATE_OWN).start()

    def end_dec(name, source, here):
        cross(name, source).wait()
        if shared:
            mates(name, other[name], MATE_OTHER).start()

    def end_mates(name, here):
        if shared:
            if not here:
                mates(name, own[name], MATE_OWN).wait()
            mates(name, other[name], MATE_OTHER).wait()

    @pl.when(z == LAST)
    def _():
        for item in owned(LAST):
            enc_copy(item).start()
        chain(VECS, sent[VECS], 2).start()
        for name in DEC_PARTS:
            chain(name, sent[name], 2).start()
            finish_dec(name, sent[name], True)
        locals_ = [local(i, sent[name], own[name]) for i, name in enumerate(DEC_PARTS)]
        locals_.append(local(len(DEC_PARTS), sent[VECS], got[VECS]))
        for one in locals_:
            one.start()
        for name in DEC_PARTS:
            end_dec(name, sent[name], True)
        for item in owned(LAST):
            enc_copy(item).wait_send()
        chain(VECS, sent[VECS], 2).wait_send()
        for name in DEC_PARTS:
            chain(name, sent[name], 2).wait_send()
            end_mates(name, True)
        for one in locals_:
            one.wait()
        head_up().wait_recv()

    @pl.when(z == 2)
    def _():
        head_up().start()
        chain(HEAD, sent[HEAD], HOST).start()
        first = local(0, sent[HEAD], got[HEAD])
        first.start()
        for item in owned(2):
            enc_copy(item).start()
        chain(VECS, sent[VECS], 2).wait_recv()
        chain(VECS, got[VECS], HOST).start()
        waited = False
        for name in DEC_PARTS:
            chain(name, sent[name], 2).wait_recv()
            finish_dec(name, own[name], False)
            if not waited:
                for item in owned(2):
                    enc_copy(item).wait_send()
                waited = True
            chain(name, own[name], HOST).start()
        for name in DEC_PARTS:
            end_dec(name, own[name], False)
        for name in DEC_PARTS:
            chain(name, own[name], HOST).wait_send()
            end_mates(name, False)
        chain(VECS, got[VECS], HOST).wait_send()
        chain(HEAD, sent[HEAD], HOST).wait_send()
        head_up().wait_send()
        first.wait()

    @pl.when(z == HOST)
    def _():
        mine = [
            local(i, sent[piece].at[pl.ds(0, count)], got[name].at[pl.ds(first, count)])
            for i, (name, count, owner, piece, first) in enumerate(ENC_PARTS)
            if owner == HOST
        ]
        for one in mine:
            one.start()
        chain(HEAD, sent[HEAD], HOST).wait_recv()
        chain(HEAD, got[HEAD], 0).start()
        chain(VECS, sent[VECS], HOST).wait_recv()
        chain(VECS, got[VECS], 0).start()
        away = [item for item in ENC_PARTS if item[2] != HOST]
        if shared:
            for item in away:
                enc_copy(item).wait_recv()
                enc_mate(item).start()
        for name in DEC_PARTS:
            chain(name, sent[name], HOST).wait_recv()
            chain(name, own[name], 0).start()
            finish_dec(name, own[name], False)
        for name in DEC_PARTS:
            end_dec(name, own[name], False)
        for item in away:
            if shared:
                enc_mate(item).wait()
            else:
                enc_copy(item).wait_recv()
        for name in DEC_PARTS:
            chain(name, own[name], 0).wait_send()
            end_mates(name, False)
        chain(VECS, got[VECS], 0).wait_send()
        chain(HEAD, got[HEAD], 0).wait_send()
        for one in mine:
            one.wait()

    @pl.when(z == 0)
    def _():
        for item in owned(0):
            enc_copy(item).start()
        for name in DEC_PARTS:
            chain(name, sent[name], 0).wait_recv()
            finish_dec(name, own[name], False)
        for name in DEC_PARTS:
            end_dec(name, own[name], False)
        for name in DEC_PARTS:
            end_mates(name, False)
        chain(VECS, sent[VECS], 0).wait_recv()
        chain(HEAD, sent[HEAD], 0).wait_recv()
        for item in owned(0):
            enc_copy(item).wait_send()


def hosted_weights(pieces, shared):
    side = lax.axis_index("tensor")
    anywhere = pl.BlockSpec(memory_space=pl.ANY)
    shapes = list(GOT.values()) + 2 * [pieces[name].shape for name in DEC_PARTS]
    count = 2 * len(ENC_PARTS) + 4 * (len(DEC_PARTS) + 3)
    out = pl.pallas_call(
        functools.partial(weights_kernel, shared),
        name="weights",
        out_shape=[jax.ShapeDtypeStruct(shape, HALF) for shape in shapes],
        in_specs=[anywhere] * len(SENT),
        out_specs=[anywhere] * len(shapes),
        scratch_shapes=[
            pltpu.SemaphoreType.DMA((count,)),
            pltpu.SemaphoreType.DMA((count,)),
            pltpu.SemaphoreType.DMA((len(ENC_PARTS),)),
        ],
        compiler_params=pltpu.CompilerParams(collective_id=1 if shared else 2, has_side_effects=True),
    )(*[pieces[name] for name in SENT])
    got = dict(zip(GOT, out))
    own = out[len(GOT) : len(GOT) + len(DEC_PARTS)]
    other = out[len(GOT) + len(DEC_PARTS) :]
    low, high = jnp.where(side == 0, own[4], other[4]), jnp.where(side == 0, other[4], own[4])
    head_w = jnp.concatenate([low, high], 1)
    top = got[HEAD].shape[0]
    head_w = jnp.concatenate([head_w[:top] + got[HEAD], head_w[top:]], 0)
    vecs = got[VECS].reshape(-1)
    enc_vec, dec_vec, head_b = split_flat(vecs, [(9, D), (10, DD), (PATCH,)])
    return (
        (
            (got[PATCH_LOW], pieces[PATCH_ROWS], got[PATCH_HIGH]),
            tuple(got[name] for name in (W_QKV, W_OUT, W_UP, W_DOWN)),
            got[E2D_W],
            jnp.pad(enc_vec.astype(FLOAT), ((0, 7), (0, 0))),
        ),
        (own[:4], other[:4], head_w, dec_vec.astype(FLOAT), head_b.astype(FLOAT)),
    )


VISIBLE = 160
OWN = 2 * VISIBLE
ALL = 4 * VISIBLE
SPAN = (0, 768, 1536)
DEPTH = (704, 704, 192)
WIDE = 1792
SQRT_HALF = 0.5**0.5


def norm_parts(x):
    center = jnp.mean(x, -1, keepdims=True)
    moved = x - center
    scale = lax.rsqrt(jnp.mean(moved * moved, -1, keepdims=True) + 1e-06)
    return moved * scale, scale


def norm_to(x, gain, bias):
    return norm_parts(x)[0] * gain + bias


def norm_from(x, gain, cotangent):
    hat, scale = norm_parts(x)
    inner = cotangent * gain
    grad = scale * (
        inner - jnp.mean(inner, -1, keepdims=True) - hat * jnp.mean(inner * hat, -1, keepdims=True)
    )
    return grad, jnp.sum(cotangent * hat, 0, keepdims=True), jnp.sum(cotangent, 0, keepdims=True)


def gelu_to(x):
    return 0.5 * x * (1.0 + lax.erf(x * SQRT_HALF))


def gelu_slope(x):
    return 0.5 * (1.0 + lax.erf(x * SQRT_HALF)) + x * jnp.exp(-0.5 * x * x) * (2.0 * math.pi) ** -0.5


def rows_at(index, count=VISIBLE):
    return pl.ds(index * count, count)


class Links:
    def __init__(self, send_sem, recv_sem):
        self.send_sem, self.recv_sem, self.keys = send_sem, recv_sem, {}

    def copy(self, key, source, target, peer):
        index = self.keys.setdefault(key, len(self.keys))
        return pltpu.make_async_remote_copy(
            src_ref=source,
            dst_ref=target,
            send_sem=self.send_sem.at[index],
            recv_sem=self.recv_sem.at[index],
            device_id=peer,
            device_id_type=MESH_ID,
        )


def encoder_forward_kernel(
    shown, places, patch_low, patch_mid, patch_high, w_qkv, w_out, w_up, w_down, e2d_w, vec,
    reduced, stream, normed, joined, blended, attended, second, upward, activated, encoded, final_enc,
    part_sent, part_got, reduced_own, send_sem, recv_sem, local_sem,
):
    g, z, x = lax.axis_index("group"), lax.axis_index("dp"), lax.axis_index("tensor")
    barrier = pltpu.get_barrier_semaphore()
    links = Links(send_sem, recv_sem)

    def at(row, column):
        return (g, row, column)

    def greet(peer):
        pl.semaphore_signal(barrier, inc=1, device_id=peer, device_id_type=MESH_ID)

    for row in range(4):

        @pl.when((z == row) & ((row != HOST) | (x == 1)))
        def _():
            greet(at(HOST, row // 2))

    @pl.when((z == HOST) & (x == 0))
    def _():
        greet(at(HOST, 1))
        pl.semaphore_wait(barrier, 3)

    @pl.when((z == HOST) & (x == 1))
    def _():
        pl.semaphore_wait(barrier, 5)

    def give(column, clip):
        row = 2 * column + clip
        out = []
        for side in range(2):
            if (row, side) != (HOST, column):
                out.append(links.copy(8 + 2 * clip + side, reduced_own.at[clip], reduced, at(row, side)))
        return out

    @pl.when(z == HOST)
    def _():
        across = at(HOST, 1 - x)

        def normed_copy(i):
            return links.copy(i, normed.at[rows_at(i)], normed.at[rows_at(2 + i)], across)

        def out_copy(i):
            return links.copy(2 + i, part_sent.at[rows_at(i)], part_got.at[rows_at(i)], across)

        def second_copy(i):
            return links.copy(4 + i, second.at[rows_at(i)], second.at[rows_at(2 + i)], across)

        def down_copy(i):
            return links.copy(6 + i, part_sent.at[rows_at(2 + i)], part_got.at[rows_at(2 + i)], across)

        for i in range(2):
            rows = rows_at(i)
            emb = places[rows] + vec[0:1]
            for start, depth, weight in zip(SPAN, DEPTH, (patch_low, patch_mid, patch_high)):
                emb = emb + mm(shown[rows, start : start + depth], weight[...])
            stream[rows] = emb
            normed[rows] = norm_to(emb, vec[1:2], vec[2:3]).astype(HALF)
            normed_copy(i).start()

        def attend(c):
            rows = rows_at(c)
            joined[rows] = mm(normed[rows], w_qkv[...]).astype(HALF)
            width = D // 2
            for h in range(width // HDIM):
                column = h * HDIM
                queries = joined[rows, column : column + HDIM]
                keys = joined[rows, width + column : width + column + HDIM]
                values = joined[rows, 2 * width + column : 2 * width + column + HDIM]
                scores = mm_nt(queries, keys) * HDIM**-0.5
                weights = jnp.exp(scores - jnp.max(scores, -1, keepdims=True))
                probs = weights * (1.0 / jnp.sum(weights, -1, keepdims=True))
                blended[rows, column : column + HDIM] = mm(probs.astype(HALF), values).astype(HALF)
            return mm(blended[rows], w_out[...])

        for i in range(2):
            attended[rows_at(i)] = attend(i) + stream[rows_at(i)] + vec[3:4]
            normed_copy(i).wait_recv()
            part_sent[rows_at(i)] = attend(2 + i).astype(HALF)
            out_copy(i).start()

        def feed(c):
            rows = rows_at(c)
            up = mm(second[rows], w_up[...])
            upward[rows] = up
            activated[rows] = gelu_to(up).astype(HALF)
            return mm(activated[rows], w_down[...])

        for i in range(2):
            rows = rows_at(i)
            out_copy(i).wait_recv()
            after = attended[rows] + part_got[rows].astype(FLOAT)
            attended[rows] = after
            second[rows] = norm_to(after, vec[4:5], vec[5:6]).astype(HALF)
            second_copy(i).start()
        for i in range(2):
            rows = rows_at(i)
            encoded[rows] = feed(i) + attended[rows] + vec[6:7]
            second_copy(i).wait_recv()
            part_sent[rows_at(2 + i)] = feed(2 + i).astype(HALF)
            down_copy(i).start()
        for i in range(2):
            rows = rows_at(i)
            down_copy(i).wait_recv()
            after = encoded[rows] + part_got[rows_at(2 + i)].astype(FLOAT)
            encoded[rows] = after
            low = norm_to(after, vec[7:8], vec[8:9]).astype(HALF)
            final_enc[rows] = low
            reduced_own[i] = mm(low, e2d_w[...])
            for column in range(2):

                @pl.when(x == column)
                def _():
                    for one in give(column, i):
                        one.start()

        for i in range(2):
            normed_copy(i).wait_send()
            out_copy(i).wait_send()
            second_copy(i).wait_send()
            down_copy(i).wait_send()
        for column in range(2):

            @pl.when(x == column)
            def _():
                for i in range(2):
                    for one in give(column, i):
                        one.wait_send()

    @pl.when((z == HOST) & (x == 0))
    def _():
        mine = pltpu.make_async_copy(reduced_own.at[1], reduced, local_sem)
        mine.start()
        mine.wait()

    for row in range(4):
        for side in range(2):
            if (row, side) != (HOST, 0):

                @pl.when((z == row) & (x == side))
                def _():
                    key = 8 + 2 * (row % 2) + side
                    links.copy(key, reduced_own.at[row % 2], reduced, at(HOST, row // 2)).wait_recv()


def encoder_forward(number, shown_own, places, weights):
    patch_pieces, mats, e2d_w, vec = weights
    vmem = pl.BlockSpec(memory_space=pltpu.VMEM)
    stored = [
        ((OWN, D), FLOAT),
        ((ALL, D), HALF),
        ((ALL, 3 * D // 2), HALF),
        ((ALL, D // 2), HALF),
        ((OWN, D), FLOAT),
        ((ALL, D), HALF),
        ((ALL, FF // 2), FLOAT),
        ((ALL, FF // 2), HALF),
        ((OWN, D), FLOAT),
        ((OWN, D), HALF),
    ]
    shapes = [((VISIBLE, DD), FLOAT)] + stored
    out = pl.pallas_call(
        encoder_forward_kernel,
        name="encoder_forward",
        out_shape=[jax.ShapeDtypeStruct(*one) for one in shapes],
        in_specs=[vmem] * 11,
        out_specs=[vmem] * len(shapes),
        scratch_shapes=[
            pltpu.VMEM((ALL, D), HALF),
            pltpu.VMEM((ALL, D), HALF),
            pltpu.VMEM((2, VISIBLE, DD), FLOAT),
            pltpu.SemaphoreType.DMA((12,)),
            pltpu.SemaphoreType.DMA((12,)),
            pltpu.SemaphoreType.DMA,
        ],
        compiler_params=pltpu.CompilerParams(
            collective_id=number, has_side_effects=True, vmem_limit_bytes=56 << 20
        ),
    )(shown_own, places, *patch_pieces, *mats, e2d_w, vec)
    return out[0], out[1:]


def encoder_backward_kernel(
    picked, shown, w_qkv, w_out, w_up, w_down, e2d_w, vec,
    stream, normed, joined, blended, attended, second, upward, activated, encoded, final_enc,
    wide, tall, dec_qkv, small,
    qkv_out, square_out, up_out, patch_out, e2d_out, vec_out,
    one_wide, one_tall, one_qkv, one_small, two_wide, two_tall, two_qkv, two_small,
    wide_sent, tall_sent, dec_qkv_sent, small_sent, wide_got, tall_got, dec_qkv_got, small_got,
    picks_got, low, grad_up_in, mid, grad_blend, grad_joined, part_sent, part_got, own_rows_grad, own_part,
    emb_low, emb_got, down_grad, up_grad, out_grad, qkv_grad, patch_low, patch_mid, patch_high, e2d_part, e2d_got, e2d_grad,
    vec_part, vec_got, send_sem, recv_sem, local_sem,
):
    g, z, x = lax.axis_index("group"), lax.axis_index("dp"), lax.axis_index("tensor")
    barrier = pltpu.get_barrier_semaphore()
    links = Links(send_sem, recv_sem)

    def at(row, column):
        return (g, row, column)

    def greet(peer):
        pl.semaphore_signal(barrier, inc=1, device_id=peer, device_id_type=MESH_ID)

    @pl.when(z != HOST)
    def _():
        greet(at(HOST, x))

    @pl.when(z == LAST)
    def _():
        greet(at(2, x))

    @pl.when((z == HOST) & (x == 0))
    def _():
        for peer in ((0, 0), (0, 1), (HOST, 1)):
            greet(at(*peer))

    @pl.when((z == HOST) & (x == 1))
    def _():
        for peer in ((2, 0), (2, 1), (3, 0), (3, 1), (0, 1), (HOST, 0)):
            greet(at(*peer))

    @pl.when(z == HOST)
    def _():
        pl.semaphore_wait(barrier, 4)

    @pl.when((z == 2) | ((z == 0) & (x == 1)))
    def _():
        pl.semaphore_wait(barrier, 2)

    @pl.when((z == LAST) | ((z == 0) & (x == 0)))
    def _():
        pl.semaphore_wait(barrier, 1)

    def pick_copy(row, side):
        return links.copy((row % 2) * 2 + side, picked, picks_got.at[row % 2, side], at(HOST, row // 2))

    for row in range(4):
        for side in range(2):
            if (row, side) != (HOST, 0):

                @pl.when((z == row) & (x == side))
                def _():
                    pick_copy(row, side).start()

    numbers = iter(range(4, 64))
    low_number = [next(numbers), next(numbers)]
    second_number = [next(numbers), next(numbers)]
    mid_number = [next(numbers), next(numbers)]
    normed_number = [next(numbers), next(numbers)]
    emb_number = [next(numbers), next(numbers)]
    e2d_number, vec_number = next(numbers), next(numbers)

    def row_copies(numbers_two, ref):
        return [
            links.copy(numbers_two[i], ref.at[rows_at(i)], ref.at[rows_at(2 + i)], at(HOST, 1 - x)) for i in range(2)
        ]

    def part_copies(numbers_two, first):
        return [
            links.copy(
                numbers_two[i], part_sent.at[rows_at(first + i)], part_got.at[rows_at(first + i)], at(HOST, 1 - x)
            )
            for i in range(2)
        ]

    out_rows, up_rows, down_rows = 288, 672, 1248
    down_far = links.copy(next(numbers), down_grad.at[pl.ds(down_rows, 288)], square_out.at[pl.ds(0, 288)], at(LAST, x))
    down_near = links.copy(next(numbers), down_grad.at[pl.ds(0, down_rows)], square_out, at(2, x))
    up_near = links.copy(next(numbers), up_grad.at[pl.ds(up_rows, 96)], up_out.at[pl.ds(0, 96)], at(2, x))
    out_near = links.copy(
        next(numbers), out_grad.at[pl.ds(0, out_rows)], square_out.at[pl.ds(0, out_rows)], at(0, x)
    )
    qkv_near = links.copy(next(numbers), qkv_grad, qkv_out, at(0, x))
    patch_one = links.copy(next(numbers), patch_low, patch_out, at(0, x))
    patch_two = links.copy(next(numbers), patch_high, patch_out.at[pl.ds(0, 192)], at(2, x))
    e2d_near = links.copy(next(numbers), e2d_grad, e2d_out, at(2, x))
    vec_far = links.copy(next(numbers), vec_part, vec_out, at(LAST, x))

    own_dec = (wide, tall, dec_qkv, small)
    sent_dec = (wide_sent, tall_sent, dec_qkv_sent, small_sent)
    got_dec = (wide_got, tall_got, dec_qkv_got, small_got)
    one_dec = (one_wide, one_tall, one_qkv, one_small)
    two_dec = (two_wide, two_tall, two_qkv, two_small)
    next_row = jnp.minimum(z + 1, LAST)
    tree_one = [links.copy(next(numbers), sent_dec[i], got_dec[i], at(next_row, x)) for i in range(4)]
    tree_two = [links.copy(next(numbers), sent_dec[i], two_dec[i], at(LAST, x)) for i in range(4)]

    @pl.when((z == 0) | (z == 2))
    def _():
        for i in (3, 0, 1, 2):
            sent_dec[i][...] = own_dec[i][...].astype(sent_dec[i].dtype)
            tree_one[i].start()

    def pass_on():
        for i in (3, 0, 1, 2):
            tree_one[i].wait_recv()
            sent_dec[i][...] = (own_dec[i][...] + got_dec[i][...].astype(FLOAT)).astype(sent_dec[i].dtype)
            tree_two[i].start()

    def tall_product(left, right, target, step):
        def body(t, carry):
            columns = pl.ds(pl.multiple_of(t * step, step), step)
            target[columns] = mm_tn(left[:, columns], right[...]).astype(HALF)
            return carry

        lax.fori_loop(0, target.shape[0] // step, body, 0)

    @pl.when(z == HOST)
    def _():
        low_sent, mid_sent = row_copies(low_number, low), row_copies(mid_number, mid)
        second_sent, normed_sent = part_copies(second_number, 0), part_copies(normed_number, 2)
        emb_sent = [
            links.copy(
                emb_number[i],
                emb_low.at[1 - x, rows_at(i)],
                emb_got.at[rows_at(i)],
                at(HOST, 1 - x),
            )
            for i in range(2)
        ]
        e2d_sent = links.copy(e2d_number, e2d_part.at[1 - x], e2d_got, at(HOST, 1 - x))
        vec_sent = links.copy(vec_number, vec_part, vec_got, at(HOST, 1 - x))

        vec_part[...] = jnp.zeros_like(vec_part)

        def count(row, value):
            vec_part[row : row + 1] += value

        @pl.when(x == 0)
        def _():
            mine = pltpu.make_async_copy(picked, picks_got.at[1, 0], local_sem.at[0])
            mine.start()
            mine.wait()

        for clip in range(2):
            for side in range(2):
                waiting = links.copy(clip * 2 + side, picked, picks_got.at[clip, side], at(HOST, 0))
                if clip == HOST % 2 and side == 0:

                    @pl.when(x == 1)
                    def _():
                        waiting.wait_recv()

                else:
                    waiting.wait_recv()
        reduced_low = []
        for i in range(2):
            rows = rows_at(i)
            one = picks_got[i, 0] + picks_got[i, 1]
            reduced_low.append(one)
            grad, gain, bias = norm_from(encoded[rows], vec[7:8], mm_nt(one, e2d_w[...]))
            count(7, gain)
            count(8, bias)
            count(6, jnp.sum(grad, 0, keepdims=True))
            own_rows_grad[rows] = grad
            low[rows] = grad.astype(HALF)
            low_sent[i].start()
        whole_low = jnp.concatenate(reduced_low, 0)
        product = mm_tn(final_enc[...], whole_low).astype(HALF)
        e2d_part[0] = product[: D // 2]
        e2d_part[1] = product[D // 2 :]
        e2d_sent.start()

        def feed_back(c):
            rows = rows_at(c)
            grad_up_in[rows] = (mm_nt(low[rows], w_down[...]) * gelu_slope(upward[rows])).astype(HALF)
            return mm_nt(grad_up_in[rows], w_up[...])

        for i in range(2):
            own_part[rows_at(i)] = feed_back(i)
            low_sent[i].wait_recv()
            part_sent[rows_at(i)] = feed_back(2 + i).astype(HALF)
            second_sent[i].start()
        tall_product(activated, low, down_grad, 256)
        down_far.start()
        down_near.start()
        for i in range(2):
            rows = rows_at(i)
            second_sent[i].wait_recv()
            total = own_part[rows] + part_got[rows].astype(FLOAT)
            grad, gain, bias = norm_from(attended[rows], vec[4:5], total)
            count(4, gain)
            count(5, bias)
            grad = grad + own_rows_grad[rows]
            count(3, jnp.sum(grad, 0, keepdims=True))
            own_rows_grad[rows] = grad
            mid[rows] = grad.astype(HALF)
            mid_sent[i].start()
        e2d_sent.wait()
        e2d_grad[...] = (e2d_part[x].astype(FLOAT) + e2d_got[...].astype(FLOAT)).astype(HALF)
        e2d_near.start()

        def attend_back(c):
            rows = rows_at(c)
            width = D // 2
            grad_blend[...] = mm_nt(mid[rows], w_out[...]).astype(HALF)
            for h in range(width // HDIM):
                column = h * HDIM
                queries = joined[rows, column : column + HDIM]
                keys = joined[rows, width + column : width + column + HDIM]
                values = joined[rows, 2 * width + column : 2 * width + column + HDIM]
                grads = grad_blend[:, column : column + HDIM]
                scores = mm_nt(queries, keys) * HDIM**-0.5
                weights = jnp.exp(scores - jnp.max(scores, -1, keepdims=True))
                probs = weights * (1.0 / jnp.sum(weights, -1, keepdims=True))
                grad_values = mm_tn(probs.astype(HALF), grads)
                grad_probs = mm_nt(grads, values)
                grad_scores = (
                    probs * (grad_probs - jnp.sum(probs * grad_probs, -1, keepdims=True))
                ).astype(HALF)
                for third, value in enumerate(
                    (mm(grad_scores, keys) * HDIM**-0.5, mm_tn(grad_scores, queries) * HDIM**-0.5, grad_values)
                ):
                    start = third * width + column
                    grad_joined[rows, start : start + HDIM] = value.astype(HALF)
            return mm_nt(grad_joined[rows], w_qkv[...])

        for i in range(2):
            own_part[rows_at(i)] = attend_back(i)
            mid_sent[i].wait_recv()
            part_sent[rows_at(2 + i)] = attend_back(2 + i).astype(HALF)
            normed_sent[i].start()
            if i == 0:
                pass_on()
        tall_product(second, grad_up_in, up_grad, 256)
        up_near.start()
        tall_product(blended, mid, out_grad, 128)
        out_near.start()
        for i in range(2):
            rows = rows_at(i)
            normed_sent[i].wait_recv()
            total = own_part[rows] + part_got[rows_at(2 + i)].astype(FLOAT)
            grad, gain, bias = norm_from(stream[rows], vec[1:2], total)
            count(1, gain)
            count(2, bias)
            grad = grad + own_rows_grad[rows]
            count(0, jnp.sum(grad, 0, keepdims=True))
            grad_low = grad.astype(HALF)
            emb_low[0, rows] = grad_low[:, : D // 2]
            emb_low[1, rows] = grad_low[:, D // 2 :]
            emb_sent[i].start()
        vec_sent.start()
        tall_product(normed, grad_joined, qkv_grad, 256)
        qkv_near.start()
        for one in emb_sent:
            one.wait()
        columns = jnp.concatenate([emb_low[x], emb_got[...]], 0)
        for start, depth, target in zip(SPAN, DEPTH, (patch_low, patch_mid, patch_high)):
            target[...] = mm_tn(shown[:, start : start + depth], columns).astype(HALF)
        patch_one.start()
        patch_two.start()
        vec_sent.wait()
        vec_part[...] += vec_got[...]
        vec_far.start()
        mine = [
            pltpu.make_async_copy(out_grad.at[pl.ds(out_rows, 96)], square_out.at[pl.ds(0, 96)], local_sem.at[1]),
            pltpu.make_async_copy(up_grad.at[pl.ds(0, up_rows)], up_out, local_sem.at[2]),
            pltpu.make_async_copy(patch_mid, patch_out, local_sem.at[3]),
        ]
        for one in mine:
            one.start()
        for one in low_sent + mid_sent + second_sent + normed_sent:
            one.wait_send()
        for one in (down_far, down_near, up_near, out_near, qkv_near, patch_one, patch_two, e2d_near, vec_far):
            one.wait_send()
        for one in tree_two:
            one.wait_send()
        for one in mine:
            one.wait()

    for row in range(4):
        for side in range(2):
            if (row, side) != (HOST, 0):

                @pl.when((z == row) & (x == side))
                def _():
                    pick_copy(row, side).wait_send()

    for row, ones in ((0, (out_near, qkv_near, patch_one)), (2, (down_near, up_near, patch_two, e2d_near)), (LAST, (down_far, vec_far))):

        @pl.when(z == row)
        def _():
            for one in ones:
                one.wait_recv()

    @pl.when((z == 0) | (z == 2))
    def _():
        for one in tree_one:
            one.wait_send()

    @pl.when(z == LAST)
    def _():
        kept = []
        for i in range(4):
            tree_one[i].wait_recv()
            kept.append(pltpu.make_async_copy(got_dec[i], one_dec[i], local_sem.at[i]))
            kept[i].start()
        for i in range(4):
            tree_two[i].wait_recv()
            kept[i].wait()


def encoder_backward(number, picked, shown, weights, stored, dec_grads):
    _, mats, e2d_w, vec = weights
    vmem = pl.BlockSpec(memory_space=pltpu.VMEM)
    anywhere = pl.BlockSpec(memory_space=pl.ANY)
    shapes = [
        ((D, 3 * D // 2), HALF),
        ((1248, D), HALF),
        ((672, FF // 2), HALF),
        ((704, D // 2), HALF),
        ((D // 2, DD), HALF),
        ((16, D), FLOAT),
    ]
    tree = [(one.shape, HALF) for one in dec_grads[:3]] + [(dec_grads[3].shape, FLOAT)]
    shapes = shapes + 2 * tree
    scratch = 2 * tree + [
        ((2, 2, VISIBLE, DD), HALF),
        ((ALL, D), HALF),
        ((ALL, FF // 2), HALF),
        ((ALL, D), HALF),
        ((VISIBLE, D // 2), HALF),
        ((ALL, 3 * D // 2), HALF),
        ((ALL, D), HALF),
        ((ALL, D), HALF),
        ((OWN, D), FLOAT),
        ((OWN, D), FLOAT),
        ((2, OWN, D // 2), HALF),
        ((OWN, D // 2), HALF),
        ((FF // 2, D), HALF),
        ((D, FF // 2), HALF),
        ((D // 2, D), HALF),
        ((D, 3 * D // 2), HALF),
        ((704, D // 2), HALF),
        ((704, D // 2), HALF),
        ((192, D // 2), HALF),
        ((2, D // 2, DD), HALF),
        ((D // 2, DD), HALF),
        ((D // 2, DD), HALF),
        ((16, D), FLOAT),
        ((16, D), FLOAT),
    ]
    return pl.pallas_call(
        encoder_backward_kernel,
        name="encoder_backward",
        out_shape=[jax.ShapeDtypeStruct(*one) for one in shapes],
        in_specs=[vmem] * 22,
        out_specs=[anywhere] * len(shapes),
        scratch_shapes=[pltpu.VMEM(*one) for one in scratch]
        + [pltpu.SemaphoreType.DMA((36,)), pltpu.SemaphoreType.DMA((36,)), pltpu.SemaphoreType.DMA((4,))],
        compiler_params=pltpu.CompilerParams(
            collective_id=number, has_side_effects=True, vmem_limit_bytes=60 << 20
        ),
    )(picked, shown, *mats, e2d_w, vec, *stored, *dec_grads)


LANES = 128
STEP_ROWS = 96
TEN_LANES = 8640
REP_LANES = 4056
LAID = [QKV, SQUARE, UP, PATCH_ROWS, E2D, HEAD, VECS, DEC_QKV, DEC_OUT, DEC_UP, DEC_DOWN, HEAD_HALF]
LAID_SHAPES = {**PIECES, HEAD_HALF: (384, 768)}
TEN_PLACES = [
    [(QKV, 768, 0), (SQUARE, 288, 6912)],
    [(SQUARE, 96, 0), (UP, 672, 576)],
    [(UP, 96, 0), (SQUARE, 1248, 1152)],
    [(SQUARE, 288, 0), (DEC_OUT, 192, 3456), (DEC_UP, 384, 4032), (DEC_DOWN, 768, 6336)],
]
DEC_QKV_PLACE = 1728
PATCH_COUNTS = (676, 676, 184)
E2D_PLACE = 1104
HEAD_PLACE = 3408
HEAD_TOP = 54
VEC_PLACE = 3960


def spread_rows(flat, place, blocks, count, read):
    def put(first, value):
        rows = value.shape[0]
        for j in range(blocks):
            flat[pl.ds(place + first * blocks + j, rows, stride=blocks), :] = value[:, j * LANES : (j + 1) * LANES]

    def body(t, carry):
        put(t * STEP_ROWS, read(pl.multiple_of(t * STEP_ROWS, 16), STEP_ROWS))
        return carry

    whole = count // STEP_ROWS
    if whole:
        lax.fori_loop(0, whole, body, 0)
    rest = count - whole * STEP_ROWS
    if rest:
        put(whole * STEP_ROWS, read(whole * STEP_ROWS, -(-rest // 16) * 16)[:rest])


def gather_rows(piece, flat, place, blocks, count):
    def put(first, rows, padded):
        for j in range(blocks):
            value = flat[pl.ds(place + first * blocks + j, rows, stride=blocks), :]
            if padded > rows:
                value = jnp.concatenate([value, jnp.zeros((padded - rows, LANES), FLOAT)], 0)
            piece[pl.ds(first, padded), j * LANES : (j + 1) * LANES] = value.astype(HALF)

    def body(t, carry):
        put(pl.multiple_of(t * STEP_ROWS, 16), STEP_ROWS, STEP_ROWS)
        return carry

    whole = count // STEP_ROWS
    if whole:
        lax.fori_loop(0, whole, body, 0)
    rest = count - whole * STEP_ROWS
    if rest:
        put(whole * STEP_ROWS, rest, -(-rest // 16) * 16)


def lay_out(z, x, ten, rep, pieces, wide_rows):
    for row in range(4):

        @pl.when(z == row)
        def _():
            for name, count, place in TEN_PLACES[row]:
                gather_rows(pieces[name], ten, place, PIECES[name][1] // LANES, count)
            if row < LAST:
                gather_rows(pieces[PATCH_ROWS], rep, 0, D // LANES, PATCH_COUNTS[row])
            if row < 2:
                pieces[PATCH_ROWS][pl.ds(688, 16)] = jnp.zeros((16, D), HALF)
            if row == 2:
                gather_rows(pieces[E2D], rep, E2D_PLACE, DD // LANES, D)
                gather_rows(pieces[HEAD], rep, HEAD_PLACE, PATCH // LANES, HEAD_TOP)
            if row == LAST:
                gather_rows(pieces[VECS], rep, VEC_PLACE, D // LANES, 16)
                for j in range(4):
                    wide_rows[j, pl.ds(0, 192, stride=2), :] = ten[pl.ds(DEC_QKV_PLACE + j, 192, stride=9), :]
                middle = ten[pl.ds(DEC_QKV_PLACE + 4, 192, stride=9), :]
                late = [middle[:, 64:]] + [ten[pl.ds(DEC_QKV_PLACE + 5 + j, 192, stride=9), :] for j in range(4)]
                late = jnp.concatenate(late + [jnp.zeros((192, 64), FLOAT)], 1)
                wide_rows[4, pl.ds(0, 192, stride=2), :] = middle
                for j in range(5):
                    columns = slice(j * LANES, (j + 1) * LANES)
                    wide_rows[j, pl.ds(1, 192, stride=2), :] = late[:, columns]
                for j in range(4):
                    columns = slice(j * LANES, (j + 1) * LANES)
                    pieces[DEC_QKV][:, columns] = wide_rows[j].astype(HALF)
                pieces[DEC_QKV][:, 512:576] = wide_rows[4][:, :64].astype(HALF)
                half = pieces[HEAD_HALF]
                blocks, offset = PATCH // LANES, x * 6
                half[pl.ds(0, 48)] = jnp.zeros((48, D), HALF)
                for j in range(6):
                    columns = slice(j * LANES, (j + 1) * LANES)
                    value = rep[pl.ds(offset + j, 42, stride=blocks), :]
                    half[pl.ds(48, 48), columns] = jnp.concatenate(
                        [jnp.zeros((6, LANES), FLOAT), value], 0
                    ).astype(HALF)
                    for t in range(1, 4):
                        value = rep[pl.ds((96 * t - HEAD_TOP) * blocks + offset + j, 96, stride=blocks), :]
                        half[pl.ds(96 * t, 96), columns] = value.astype(HALF)


def lay_out_kernel(ten, rep, *refs):
    pieces = dict(zip(LAID, refs))
    lay_out(lax.axis_index("dp"), lax.axis_index("tensor"), ten, rep, pieces, refs[len(LAID)])


def first_pieces(ten, rep):
    vmem = pl.BlockSpec(memory_space=pltpu.VMEM)
    out = pl.pallas_call(
        lay_out_kernel,
        name="lay_out",
        out_shape=[jax.ShapeDtypeStruct(LAID_SHAPES[name], HALF) for name in LAID],
        in_specs=[vmem] * 2,
        out_specs=[vmem] * len(LAID),
        scratch_shapes=[pltpu.VMEM((5, 384, LANES), FLOAT)],
        compiler_params=pltpu.CompilerParams(vmem_limit_bytes=48 << 20),
    )(ten, rep)
    return dict(zip(LAID, out))


def update_kernel(
    number, last,
    stats, qkv, square, up, patch, e2d, vec, wide, tall, dec_qkv, small,
    one_wide, one_tall, one_qkv, one_small, two_wide, two_tall, two_qkv, two_small,
    *refs,
):
    masters, refs = refs[:6], refs[6:]
    stats_out, outs, refs = refs[0], refs[1:7], refs[7:]
    pieces = {}
    if not last:
        pieces, refs = dict(zip(LAID, refs)), refs[len(LAID) :]
    held, refs = refs[:6], refs[6:]
    grad_ten, grad_rep, wide_rows, patch_other, e2d_other, head_own, head_other, slots, send_sem, recv_sem, local_sem = refs
    g, z, x = lax.axis_index("group"), lax.axis_index("dp"), lax.axis_index("tensor")
    me = 2 * z + x
    links = Links(send_sem, recv_sem)
    barrier = pltpu.get_barrier_semaphore()
    loads = [pltpu.make_async_copy(masters[i], held[i], local_sem.at[i]) for i in range(6)]
    for one in loads:
        one.start()

    def peer(shift):
        other = lax.rem(me + shift, 8)
        return (g, other // 2, lax.rem(other, 2))

    for shift in range(1, 8):
        pl.semaphore_signal(barrier, inc=1, device_id=peer(shift), device_id_type=MESH_ID)
    pl.semaphore_wait(barrier, 7)

    across = (g, z, 1 - x)
    patch_swap = links.copy(0, patch, patch_other, across)
    e2d_swap = links.copy(1, e2d, e2d_other, across)
    head_swap = links.copy(2, head_own, head_other, across)
    top_own = links.copy(3, head_own.at[pl.ds(0, 64)], head_own.at[pl.ds(0, 64)], (g, 2, x))
    top_other = links.copy(4, head_other.at[pl.ds(0, 64)], head_other.at[pl.ds(0, 64)], (g, 2, x))

    def plain(ref):
        return lambda first, rows: ref[pl.ds(first, rows)].astype(FLOAT)

    def joined(own, other):
        def read(first, rows):
            one, two = own[pl.ds(first, rows)].astype(FLOAT), other[pl.ds(first, rows)].astype(FLOAT)
            return jnp.concatenate([jnp.where(x == 0, one, two), jnp.where(x == 0, two, one)], 1)

        return read

    def total(own, one, two, top, columns):
        def read(first, rows):
            at = pl.ds(top + first, rows)
            return own[at, columns] + one[at, columns].astype(FLOAT) + two[at, columns].astype(FLOAT)

        return read

    @pl.when(z < LAST)
    def _():
        patch_swap.start()

    @pl.when(z == 2)
    def _():
        e2d_swap.start()

    fc = DFF // 2

    @pl.when(z == LAST)
    def _():
        head_own[...] = total(wide, one_wide, two_wide, 0, slice(fc, 2 * fc))(0, DD).astype(HALF)
        head_swap.start()
        top_own.start()
        whole = slice(0, DD)
        spread_rows(grad_ten, 0, 6, 288, plain(square))
        spread_rows(grad_ten, 3456, 3, 192, total(tall, one_tall, two_tall, fc, whole))
        spread_rows(grad_ten, 4032, 6, 384, total(wide, one_wide, two_wide, 0, slice(0, fc)))
        spread_rows(grad_ten, 6336, 3, 768, total(tall, one_tall, two_tall, 0, whole))
        for j in range(4):
            columns = slice(j * LANES, (j + 1) * LANES)
            wide_rows[j] = total(dec_qkv, one_qkv, two_qkv, 0, columns)(0, DD)
        tail = total(dec_qkv, one_qkv, two_qkv, 0, slice(512, 576))(0, DD)
        wide_rows[4] = jnp.concatenate([tail, jnp.zeros((DD, 64), FLOAT)], 1)
        for j in range(4):
            grad_ten[pl.ds(DEC_QKV_PLACE + j, 192, stride=9), :] = wide_rows[j, pl.ds(0, 192, stride=2), :]
        late = jnp.concatenate([wide_rows[j, pl.ds(1, 192, stride=2), :] for j in range(5)], 1)
        early = wide_rows[4, pl.ds(0, 192, stride=2), :]
        grad_ten[pl.ds(DEC_QKV_PLACE + 4, 192, stride=9), :] = jnp.concatenate([early[:, :64], late[:, :64]], 1)
        for j in range(4):
            start = 64 + j * LANES
            grad_ten[pl.ds(DEC_QKV_PLACE + 5 + j, 192, stride=9), :] = late[:, start : start + LANES]
        for j in range(6):
            columns = slice(j * LANES, (j + 1) * LANES)
            grad_rep[pl.ds(VEC_PLACE + j, 9, stride=6), :] = vec[0:9, columns]
        grad_rep[pl.ds(VEC_PLACE + 54, 42), :] = small[0:42] + one_small[0:42] + two_small[0:42]
        head_swap.wait_recv()
        top_other.start()
        read = joined(head_own, head_other)

        def put(first, value):
            rows = value.shape[0]
            for j in range(12):
                grad_rep[pl.ds(first * 12 + j, rows, stride=12), :] = value[:, j * LANES : (j + 1) * LANES]

        put(0, read(48, 48)[6:])
        for t in range(1, 4):
            put(96 * t - HEAD_TOP, read(96 * t, 96))

    for row in range(3):

        @pl.when(z == row)
        def _():
            refs_of = {QKV: qkv, SQUARE: square, UP: up}
            for name, count, place in TEN_PLACES[row]:
                spread_rows(grad_ten, place, PIECES[name][1] // LANES, count, plain(refs_of[name]))
            patch_swap.wait_recv()
            spread_rows(grad_rep, 0, 6, PATCH_COUNTS[row], joined(patch, patch_other))
            if row == 2:
                e2d_swap.wait_recv()
                for half in range(2):

                    def read(first, rows):
                        one, two = e2d[pl.ds(first, rows)].astype(FLOAT), e2d_other[pl.ds(first, rows)].astype(FLOAT)
                        return jnp.where(x == half, one, two)

                    spread_rows(grad_rep, E2D_PLACE + half * 1152, 3, 384, read)
                top_own.wait_recv()
                top_other.wait_recv()
                spread_rows(grad_rep, HEAD_PLACE, 12, HEAD_TOP, joined(head_own, head_other))

    def square_sum(flat, step):
        def body(t, carry):
            value = flat[pl.ds(pl.multiple_of(t * step, 8), step), :]
            return carry + jnp.sum((value * value).reshape(step // 8, 8, LANES), 0)

        return jnp.sum(lax.fori_loop(0, flat.shape[0] // step, body, jnp.zeros((8, LANES), FLOAT)))

    squares = square_sum(grad_ten, 360) + square_sum(grad_rep, 312) * 0.5
    line = lax.broadcasted_iota(jnp.int32, (8, LANES), 0)
    slots[me] = jnp.where(line == 0, squares, stats[...])
    shares = [links.copy(4 + shift, slots.at[me], slots.at[me], peer(shift)) for shift in range(1, 8)]
    for one in shares:
        one.start()
    for one in shares:
        one.wait()
    whole = slots[0]
    for i in range(1, 8):
        whole = whole + slots[i]
    square_all, loss_all, count_all = whole[0:1], whole[1:2], whole[2:3]
    norm = jnp.sqrt(square_all + 1e-30) / count_all
    factor = jnp.minimum(1.0, CLIP / norm) / count_all
    stats_out[...] = jnp.where(line == 0, norm, whole)
    for one in loads:
        one.wait()

    def adam(master, first, second, grad, step):
        def body(t, carry):
            at = pl.ds(pl.multiple_of(t * step, 8), step)
            new = adamw(master[at, :], first[at, :], second[at, :], grad[at, :] * factor, number)
            master[at, :], first[at, :], second[at, :] = new
            return carry

        lax.fori_loop(0, master.shape[0] // step, body, 0)

    stores = [pltpu.make_async_copy(held[i], outs[i], local_sem.at[i]) for i in range(6)]
    adam(*held[:3], grad_ten, 72)
    for one in stores[:3]:
        one.start()
    adam(*held[3:], grad_rep, 104)
    for one in stores[3:]:
        one.start()
    if not last:
        lay_out(z, x, held[0], held[3], pieces, wide_rows)

    @pl.when(z < LAST)
    def _():
        patch_swap.wait_send()

    @pl.when(z == 2)
    def _():
        e2d_swap.wait_send()

    @pl.when(z == LAST)
    def _():
        head_swap.wait_send()
        top_own.wait_send()
        top_other.wait_send()

    for one in stores:
        one.wait()


def update(identity, number, last, stats, gradients, states):
    vmem = pl.BlockSpec(memory_space=pltpu.VMEM)
    anywhere = pl.BlockSpec(memory_space=pl.ANY)
    laid = [] if last else LAID
    flat = [(TEN_LANES, LANES)] * 3 + [(REP_LANES, LANES)] * 3
    scratch = [(one, FLOAT) for one in flat + [(TEN_LANES, LANES), (REP_LANES, LANES), (5, 384, LANES)]] + [
        ((704, D // 2), HALF),
        ((D // 2, DD), HALF),
        ((DD, PATCH // 2), HALF),
        ((DD, PATCH // 2), HALF),
        ((8, 8, LANES), FLOAT),
    ]
    out = pl.pallas_call(
        functools.partial(update_kernel, number, last),
        name="update",
        out_shape=[jax.ShapeDtypeStruct((8, LANES), FLOAT)]
        + [jax.ShapeDtypeStruct(one, FLOAT) for one in flat]
        + [jax.ShapeDtypeStruct(LAID_SHAPES[name], HALF) for name in laid],
        in_specs=[vmem] * (1 + len(gradients)) + [anywhere] * 6,
        out_specs=[vmem] + [anywhere] * 6 + [vmem] * len(laid),
        scratch_shapes=[pltpu.VMEM(*one) for one in scratch]
        + [pltpu.SemaphoreType.DMA((12,)), pltpu.SemaphoreType.DMA((12,)), pltpu.SemaphoreType.DMA((6,))],
        compiler_params=pltpu.CompilerParams(
            collective_id=identity, has_side_effects=True, vmem_limit_bytes=61 << 20
        ),
    )(stats, *gradients, *states)
    return out[0], out[1:7], dict(zip(laid, out[7:]))


def decoder_round(tokens, pixels_low, counted, weights):
    own, other, head_w, vec, head_b = weights
    count = pixels_low.shape[0]
    width = DD // 2
    normed = layer_norm(tokens, vec[2], vec[3]).astype(HALF)
    joined = mm(normed, own[0]).astype(HALF)
    queries, keys, values = [joined[:, i * width : (i + 1) * width] for i in range(3)]
    blended, totals = attn_forward(queries, keys, values)
    blend_own = blended[:count]
    blend_other = swap(blended[count:])
    stream = tokens[:count]
    attended = mm(blend_own, own[1]) + mm(blend_other, other[1]) + stream + vec[4]
    second = layer_norm(attended, vec[5], vec[6]).astype(HALF)
    w_up = jnp.concatenate([own[2], other[2]], 1)
    w_down = jnp.concatenate([own[3], other[3]], 0)
    upward = mm(second, w_up)
    activated = gelu_exact(upward).astype(HALF)
    decoded = mm(activated, w_down) + attended + vec[7]
    final_low = layer_norm(decoded, vec[8], vec[9]).astype(HALF)
    predicted = mm(final_low, head_w) + head_b
    pixels = pixels_low.astype(FLOAT)
    center = jnp.mean(pixels, -1, keepdims=True)
    spread = jnp.mean((pixels - center) ** 2, -1, keepdims=True)
    differ = predicted - (pixels - center) * lax.rsqrt(spread + 1e-06)
    loss = jnp.sum(jnp.mean(differ**2, -1) * counted)
    grad_pred = 2.0 / PATCH * differ * counted[:, None]
    pred_low = grad_pred.astype(HALF)
    head_grad = mm_tn(final_low, pred_low)
    head_b_grad = jnp.sum(grad_pred, 0)
    grad_out, gain_end, bias_end = norm_back(decoded, vec[8], vec[9], mm_nt(pred_low, head_w))
    grad_low = grad_out.astype(HALF)
    down_grad = mm_tn(activated, grad_low)
    down_bias = jnp.sum(grad_out, 0)
    _, gelu_pull = jax.vjp(gelu_exact, upward)
    grad_up_in = gelu_pull(mm_nt(grad_low, w_down))[0].astype(HALF)
    up_grad = mm_tn(second, grad_up_in)
    grad_att, gain_two, bias_two = norm_back(attended, vec[5], vec[6], mm_nt(grad_up_in, w_up))
    grad_att = grad_att + grad_out
    out_bias = jnp.sum(grad_att, 0)
    mid = grad_att.astype(HALF)
    grad_other = swap(mm_nt(mid, other[1]).astype(HALF))
    grad_blend = jnp.concatenate([mm_nt(mid, own[1]).astype(HALF), grad_other], 0)
    out_own, out_other = mm_tn(blend_own, mid), mm_tn(blend_other, mid)
    side = lax.axis_index("tensor")
    head_cols = PATCH // 2
    wide_other = jnp.concatenate(
        [
            up_grad[:, DFF // 2 :].astype(HALF),
            lax.dynamic_slice_in_dim(head_grad, (1 - side) * head_cols, head_cols, 1).astype(HALF),
        ],
        1,
    )
    tall_other = jnp.concatenate([down_grad[DFF // 2 :], out_other], 0).astype(HALF)
    wide = jnp.concatenate(
        [up_grad[:, : DFF // 2], lax.dynamic_slice_in_dim(head_grad, side * head_cols, head_cols, 1)], 1
    ) + swap(wide_other)
    tall = jnp.concatenate([down_grad[: DFF // 2], out_own], 0) + swap(tall_other)
    grad_joined = attn_backward(queries, keys, values, grad_blend, totals)
    joined_other = swap(grad_joined[count:])
    qkv_grad = mm_tn(normed, grad_joined)
    grad_normed = mm_nt(grad_joined[:count], own[0]) + mm_nt(joined_other, other[0])
    grad_in, gain_one, bias_one = norm_back(stream, vec[2], vec[3], grad_normed)
    grad_in = grad_in + grad_att
    vec_rows = [gain_one, bias_one, out_bias, gain_two, bias_two, down_bias, gain_end, bias_end]
    return loss, grad_in, (wide, tall, qkv_grad), vec_rows, head_b_grad


def hosted_round(
    patches,
    visible,
    frames_valid,
    clip_valid,
    rep_weights,
    ten_weights,
    rep_m,
    rep_v,
    ten_m,
    ten_v,
    rep_outer,
    ten_outer,
):
    side = lax.axis_index("tensor")
    z = lax.axis_index("dp")
    half_rows = TUBES // 2
    tube_ids = (jnp.arange(TUBES) + side * half_rows) % TUBES
    ids_one = hop(visible[:, 0, 0], ((0, 0), (HOST, 0)), ((2, 1), (HOST, 1)))
    ids_two = hop(visible[:, 0, 0], ((3, 1), (HOST, 1)))
    ids_two = jnp.where(side == 0, visible[:, 0, 0], ids_two)
    dec_places = sinus_at(tube_ids, DD)
    states = [one.reshape(TEN_LANES, LANES) for one in (ten_weights, ten_m, ten_v)]
    states = states + [one.reshape(REP_LANES, LANES) for one in (rep_weights, rep_m, rep_v)]
    starts = states[0], states[3]
    pieces = first_pieces(*starts)
    rep_quarter = rep_weights.shape[0]
    shown_steps = []
    for s in range(STEPS):
        picks = (visible[s, 0, 0][:, None] == jnp.arange(TUBES)[None, :]).astype(HALF)
        rows = mm(picks, patches[s, 0, 0]).astype(HALF)
        cuts = (0, rep_quarter // D, 2 * (rep_quarter // D), PATCH)
        rows = jnp.concatenate(
            [
                jnp.pad(rows[:, cuts[i] : cuts[i + 1]], ((0, 0), (0, room - cuts[i + 1] + cuts[i])))
                for i, room in enumerate((768, 768, 256))
            ],
            1,
        )
        one = hop(rows, ((0, 0), (HOST, 0)), ((2, 1), (HOST, 1)))
        two = hop(rows, ((3, 1), (HOST, 1)))
        own = jnp.concatenate([one, jnp.where(side == 0, rows, two)], 0)
        shown_steps.append(jnp.concatenate([own, swap(own, HOST)], 0))
    loss_list, count_list, norm_list = [], [], []
    for s in range(STEPS):
        enc_weights, dec_weights = hosted_weights(pieces, s == 0)
        ids = visible[s, 0, 0]
        picks = tube_ids[:, None] == ids[None, :]
        shown_here = jnp.any(picks, 1)
        counted = (
            jnp.where(shown_here, 0.0, 1.0)
            * (tube_ids // (TUBES // FRAMES) < frames_valid[s, 0, 0])
            * (clip_valid[s, 0, 0] == 1)
        ).astype(FLOAT)[:half_rows]
        shown = shown_steps[s]
        vis = ids.shape[0]
        ids_own = jnp.concatenate([ids_one[s], ids_two[s]])
        reduced_clip, enc_stored = encoder_forward(3 + s, shown[: 2 * vis], sinus_at(ids_own, D), enc_weights)
        dec_vec = dec_weights[3]
        placed = jnp.dot(
            picks.astype(FLOAT), reduced_clip + dec_vec[0], precision=lax.Precision.HIGHEST
        )
        tokens = jnp.where(shown_here[:, None], placed, dec_vec[1]) + dec_places
        pixels_low = lax.dynamic_slice_in_dim(patches[s, 0, 0], side * half_rows, half_rows, 0)
        loss, grad_tokens, (wide, tall, qkv_grad), vec_rows, head_b_grad = decoder_round(
            tokens, pixels_low, counted, dec_weights
        )
        shown_own = shown_here[:half_rows, None]
        e2d_b_grad = jnp.sum(jnp.where(shown_own, grad_tokens, 0.0), 0)
        mask_grad = jnp.sum(jnp.where(shown_own, 0.0, grad_tokens), 0)
        picked = mm_tn(picks[:half_rows].astype(HALF), grad_tokens.astype(HALF)).astype(HALF)
        small = jnp.concatenate(
            [jnp.stack([e2d_b_grad, mask_grad] + vec_rows).reshape(-1), head_b_grad]
        )
        small = small + swap(small)
        small = jnp.pad(small.reshape(-1, LANES), ((0, 6), (0, 0)))
        back = encoder_backward(5 + s, picked, shown, enc_weights, enc_stored, (wide, tall, qkv_grad, small))
        line = jnp.arange(8)[:, None]
        stats = jnp.where(line == 1, loss, jnp.where(line == 2, jnp.sum(counted), 0.0))
        stats = jnp.broadcast_to(stats, (8, LANES))
        stats, states, pieces = update(
            7 + s, STEP_BEFORE + s + 1, s == STEPS - 1, stats, (*back[:6], wide, tall, qkv_grad, small, *back[6:]), states
        )
        norm_list.append(stats[0, 0])
        loss_list.append(stats[1, 0])
        count_list.append(stats[2, 0])
    ten_first, ten_second, rep_first, rep_second = [one.reshape(-1) for one in (*states[1:3], *states[4:])]
    ten_diff, rep_diff = [group_mean(starts[i] - states[3 * i]).reshape(-1) for i in range(2)]
    rep_momentum = MOMENTUM * rep_outer + rep_diff
    ten_momentum = MOMENTUM * ten_outer[0] + ten_diff
    rep_new = rep_weights - LR_OUT * (rep_diff + MOMENTUM * rep_momentum)
    ten_new = ten_weights[0] - LR_OUT * (ten_diff + MOMENTUM * ten_momentum)
    return (
        jnp.stack(loss_list)[:, None],
        jnp.stack(count_list)[:, None],
        jnp.stack(norm_list)[:, None],
        rep_first[None],
        rep_second[None],
        ten_first[None, None],
        ten_second[None, None],
        rep_diff,
        ten_diff[None],
        rep_momentum,
        ten_momentum[None],
        rep_new,
        ten_new[None],
    )


def group_mean(diff):
    if lax.axis_size("group") != 4:
        return lax.psum(diff, "group") / lax.axis_size("group")
    odd = lax.axis_index("group") % 2 == 1
    half = diff.shape[0] // 2
    low, high = diff[:half], diff[half:]
    part = jnp.where(odd, high, low) + partner(jnp.where(odd, low, high))
    part_low = part.astype(HALF)
    far = lax.ppermute(part_low, "group", [(g, g ^ 2) for g in range(4)])
    total = (part_low.astype(FLOAT) + far.astype(FLOAT)) * 0.25
    other = partner(total)
    return jnp.concatenate([jnp.where(odd, other, total), jnp.where(odd, total, other)])


def solution(mesh):
    placed = (
        P(None, "group", "dp", None, None),
        P(None, "group", "dp", None),
        P(None, "group", "dp"),
        P(None, "group", "dp"),
        P("dp"),
        P("tensor", "dp"),
        P("group", "dp"),
        P("group", "dp"),
        P("group", "tensor", "dp"),
        P("group", "tensor", "dp"),
        P("dp"),
        P("tensor", "dp"),
    )
    return jax.shard_map(
        hosted_round if mesh.shape["dp"] == 4 and mesh.shape["tensor"] == 2 and mesh.shape["group"] % 2 == 0 else on_device,
        mesh=mesh,
        in_specs=placed,
        out_specs=(
            P(None, "group"),
            P(None, "group"),
            P(None, "group"),
            P("group", "dp"),
            P("group", "dp"),
            P("group", "tensor", "dp"),
            P("group", "tensor", "dp"),
            P("dp"),
            P("tensor", "dp"),
            P("dp"),
            P("tensor", "dp"),
            P("dp"),
            P("tensor", "dp"),
        ),
        check_vma=False,
    )
```

```python
import functools
import math

import jax
import jax.numpy as jnp
from jax import lax
from jax.experimental import pallas as pl
from jax.experimental.pallas import tpu as pltpu
from jax.sharding import PartitionSpec as P

D = 768
HDIM = 64
FF = 3072
DD = 384
DFF = 1536
PATCH = 1536
TUBES = 1568
FRAMES = 8
STEPS = 2
STEP_BEFORE = 6


CLIP = 0.001
LR_IN = 0.01
BETA1 = 0.9
BETA2 = 0.95
EPS = 1e-08
DECAY = 0.05
LR_OUT = 0.7
MOMENTUM = 0.9
FLOAT = jnp.float32
HALF = jnp.bfloat16


def sinus(count, width):
    places = jnp.arange(count).astype(jnp.float32)[:, None]
    column = jnp.arange(width)
    decays = jnp.power(10000.0, -2.0 * (column // 2).astype(jnp.float32) / width)
    angles = places * decays[None, :]
    return jnp.where(column % 2 == 0, jnp.sin(angles), jnp.cos(angles))


def layer_norm(stream, gain, bias):
    center = jnp.mean(stream, -1, keepdims=True)
    spread = jnp.mean((stream - center) ** 2, -1, keepdims=True)
    return (stream - center) * lax.rsqrt(spread + 1e-06) * gain + bias


def norm_back(stream, gain, bias, cotangent):
    _, pull = jax.vjp(layer_norm, stream, gain, bias)
    return pull(cotangent)


def gelu_exact(values):
    return jax.nn.gelu(values, approximate=False)


def split_flat(flat, shapes):
    pieces = []
    offset = 0
    for shapes_one in shapes:
        length = math.prod(shapes_one)
        pieces.append(flat[offset : offset + length].reshape(shapes_one))
        offset += length
    return pieces


def own_rows(stream, axis_dim):
    count = stream.shape[axis_dim] // lax.axis_size("tensor")
    return lax.dynamic_slice_in_dim(stream, lax.axis_index("tensor") * count, count, axis_dim)


def rows_sum(partial_rows):
    return lax.psum_scatter(partial_rows, "tensor", scatter_dimension=1, tiled=True)


def rows_full(own_part):
    return lax.all_gather(own_part, "tensor", axis=1, tiled=True)


def block_forward(stream, mats, vecs):
    w_qkv, w_out, w_up, w_down = mats
    gain_one, bias_one, out_bias, gain_two, bias_two, down_bias = vecs
    nclips, length, _ = stream.shape
    head_cols = w_out.shape[0]
    nheads = head_cols // HDIM
    normed = layer_norm(stream, gain_one, bias_one).astype(HALF)
    joined = jnp.dot(normed, w_qkv, preferred_element_type=FLOAT).astype(HALF)
    queries, key_rows, values = [
        joined[:, :, third_id * head_cols : (third_id + 1) * head_cols].reshape(
            nclips, length, nheads, HDIM
        )
        for third_id in range(3)
    ]
    scores = jnp.einsum(
        "cqhd,ckhd->chqk", queries, key_rows, preferred_element_type=FLOAT
    ) * HDIM ** (-0.5)
    highest = jnp.max(scores, -1, keepdims=True)
    totals = jnp.log(jnp.sum(jnp.exp(scores - highest), -1, keepdims=True)) + highest
    probs_low = jnp.exp(scores - totals).astype(HALF)
    blended = (
        jnp.einsum("chqk,ckhd->cqhd", probs_low, values, preferred_element_type=FLOAT)
        .astype(HALF)
        .reshape(nclips, length, head_cols)
    )
    attended = (
        rows_sum(jnp.dot(blended, w_out, preferred_element_type=FLOAT))
        + own_rows(stream, 1)
        + out_bias
    )
    second = layer_norm(attended, gain_two, bias_two).astype(HALF)
    second_all = lax.all_gather(second, "tensor", axis=1, tiled=True)
    upward = jnp.dot(second_all, w_up, preferred_element_type=FLOAT)
    activated = gelu_exact(upward).astype(HALF)
    result = (
        rows_sum(jnp.dot(activated, w_down, preferred_element_type=FLOAT)) + attended + down_bias
    )
    stored = (
        stream,
        normed,
        queries,
        key_rows,
        values,
        totals,
        blended,
        attended,
        second_all,
        upward,
        activated,
    )
    return (rows_full(result), stored)


def block_backward(grad_out, mats, vecs, stored):
    w_qkv, w_out, w_up, w_down = mats
    gain_one, bias_one, out_bias, gain_two, bias_two, down_bias = vecs
    (
        stream,
        normed,
        queries,
        key_rows,
        values,
        totals,
        blended,
        attended,
        second_all,
        upward,
        activated,
    ) = stored
    nclips, length, _ = stream.shape
    head_cols = w_out.shape[0]
    grad_low = grad_out.astype(HALF)
    grad_down = jnp.einsum("ctf,ctd->fd", activated, grad_low, preferred_element_type=FLOAT)
    down_bias_grad = jnp.sum(own_rows(grad_out, 1), (0, 1))
    grad_act = jnp.dot(grad_low, w_down.T, preferred_element_type=FLOAT)
    _, gelu_pull = jax.vjp(gelu_exact, upward)
    grad_up_in = gelu_pull(grad_act)[0].astype(HALF)
    grad_up = jnp.einsum("ctd,ctf->df", second_all, grad_up_in, preferred_element_type=FLOAT)
    grad_second = rows_sum(jnp.dot(grad_up_in, w_up.T, preferred_element_type=FLOAT))
    grad_att, gain_two_grad, bias_two_grad = norm_back(attended, gain_two, bias_two, grad_second)
    grad_att = grad_att + own_rows(grad_out, 1)
    out_bias_grad = jnp.sum(grad_att, (0, 1))
    grad_mid = rows_full(grad_att)
    mid_low = grad_mid.astype(HALF)
    grad_wout = jnp.einsum("cth,ctd->hd", blended, mid_low, preferred_element_type=FLOAT)
    nheads = head_cols // HDIM
    grad_blend = (
        jnp.dot(mid_low, w_out.T, preferred_element_type=FLOAT)
        .astype(HALF)
        .reshape(nclips, length, nheads, HDIM)
    )
    scores = jnp.einsum(
        "cqhd,ckhd->chqk", queries, key_rows, preferred_element_type=FLOAT
    ) * HDIM ** (-0.5)
    probs_full = jnp.exp(scores - totals)
    probs_low = probs_full.astype(HALF)
    grad_values = jnp.einsum("chqk,cqhd->ckhd", probs_low, grad_blend, preferred_element_type=FLOAT)
    grad_probs = jnp.einsum("cqhd,ckhd->chqk", grad_blend, values, preferred_element_type=FLOAT)
    grad_scores = (
        probs_full * (grad_probs - jnp.sum(probs_full * grad_probs, -1, keepdims=True))
    ).astype(HALF)
    grad_queries = jnp.einsum(
        "chqk,ckhd->cqhd", grad_scores, key_rows, preferred_element_type=FLOAT
    ) * HDIM ** (-0.5)
    grad_keys = jnp.einsum(
        "chqk,cqhd->ckhd", grad_scores, queries, preferred_element_type=FLOAT
    ) * HDIM ** (-0.5)
    grad_joined = jnp.concatenate(
        [
            part_grad.reshape(nclips, length, head_cols)
            for part_grad in (grad_queries, grad_keys, grad_values)
        ],
        -1,
    ).astype(HALF)
    grad_qkv = jnp.einsum("ctd,cte->de", normed, grad_joined, preferred_element_type=FLOAT)
    grad_norm_in = rows_sum(jnp.dot(grad_joined, w_qkv.T, preferred_element_type=FLOAT))
    grad_in, gain_one_grad, bias_one_grad = norm_back(
        own_rows(stream, 1), gain_one, bias_one, grad_norm_in
    )
    grad_in = grad_in + grad_att
    vec_grads = jnp.stack(
        [gain_one_grad, bias_one_grad, out_bias_grad, gain_two_grad, bias_two_grad, down_bias_grad]
    )
    return (rows_full(grad_in), (grad_qkv, grad_wout, grad_up, grad_down), vec_grads)


def group_step(patch_rows, visible_ids, shown, weight_rows, rep_full, ten_full):
    splits = lax.axis_size("tensor")
    patch_w, e2d_w, head_w, enc_vec, dec_vec, head_b = split_flat(
        rep_full, [(PATCH, D), (D, DD), (DD, PATCH), (9, D), (10, DD), (PATCH,)]
    )
    enc_vec = enc_vec.astype(FLOAT)
    dec_vec = dec_vec.astype(FLOAT)
    head_b = head_b.astype(FLOAT)
    enc_cols = D // splits
    dec_cols = DD // splits
    ten_pieces = split_flat(
        ten_full,
        [
            (D, 3 * enc_cols),
            (enc_cols, D),
            (D, FF // splits),
            (FF // splits, D),
            (DD, 3 * dec_cols),
            (dec_cols, DD),
            (DD, DFF // splits),
            (DFF // splits, DD),
        ],
    )
    enc_mats = ten_pieces[0:4]
    dec_mats = ten_pieces[4:8]
    enc_vecs = [enc_vec[i] for i in range(1, 7)]
    dec_vecs = [dec_vec[i] for i in range(2, 8)]
    shown_rows = jnp.take_along_axis(patch_rows, visible_ids[:, :, None], 1)
    embedded = (
        jnp.dot(shown_rows, patch_w, preferred_element_type=FLOAT)
        + enc_vec[0]
        + sinus(TUBES, D)[visible_ids]
    )
    encoded, enc_stored = block_forward(embedded, enc_mats, enc_vecs)
    final_enc = layer_norm(encoded, enc_vec[7], enc_vec[8]).astype(HALF)
    reduced = jnp.dot(final_enc, e2d_w, preferred_element_type=FLOAT) + dec_vec[0]
    blank = jnp.broadcast_to(dec_vec[1], (TUBES, DD))
    tokens_in = jax.vmap(lambda clip_ids, clip_rows: blank.at[clip_ids].set(clip_rows))(
        visible_ids, reduced
    ) + sinus(TUBES, DD)
    decoded, dec_stored = block_forward(tokens_in, dec_mats, dec_vecs)
    own_dec = own_rows(decoded, 1)
    final_low = layer_norm(own_dec, dec_vec[8], dec_vec[9]).astype(HALF)
    predicted = jnp.dot(final_low, head_w, preferred_element_type=FLOAT) + head_b
    pixels = own_rows(patch_rows, 1).astype(FLOAT)
    center = jnp.mean(pixels, -1, keepdims=True)
    spread = jnp.mean((pixels - center) ** 2, -1, keepdims=True)
    target = (pixels - center) * lax.rsqrt(spread + 1e-06)
    differ = predicted - target
    counted = own_rows(weight_rows, 1)
    loss_part = jnp.sum(jnp.mean(differ**2, -1) * counted)
    grad_pred = 2.0 / PATCH * differ * counted[:, :, None]
    pred_low = grad_pred.astype(HALF)
    head_w_grad = jnp.einsum("ctd,ctp->dp", final_low, pred_low, preferred_element_type=FLOAT)
    head_b_grad = jnp.sum(grad_pred, (0, 1))
    grad_final = jnp.dot(pred_low, head_w.T, preferred_element_type=FLOAT)
    grad_dec_own, dec_gain_grad, dec_bias_grad = norm_back(
        own_dec, dec_vec[8], dec_vec[9], grad_final
    )
    grad_tokens, dec_mat_grads, dec_vec_grads = block_backward(
        rows_full(grad_dec_own), dec_mats, dec_vecs, dec_stored
    )
    masked_own = own_rows(1.0 - shown.astype(FLOAT), 1)
    mask_grad = jnp.sum(own_rows(grad_tokens, 1) * masked_own[:, :, None], (0, 1))
    grad_reduced = own_rows(jnp.take_along_axis(grad_tokens, visible_ids[:, :, None], 1), 1)
    reduced_low = grad_reduced.astype(HALF)
    e2d_grad = jnp.einsum(
        "ctd,cte->de", own_rows(final_enc, 1), reduced_low, preferred_element_type=FLOAT
    )
    e2d_b_grad = jnp.sum(grad_reduced, (0, 1))
    grad_enc_final = jnp.dot(reduced_low, e2d_w.T, preferred_element_type=FLOAT)
    grad_enc_own, enc_gain_grad, enc_bias_grad = norm_back(
        own_rows(encoded, 1), enc_vec[7], enc_vec[8], grad_enc_final
    )
    grad_embedded, enc_mat_grads, enc_vec_grads = block_backward(
        rows_full(grad_enc_own), enc_mats, enc_vecs, enc_stored
    )
    own_embedded = own_rows(grad_embedded, 1)
    patch_grad = jnp.einsum(
        "ctp,ctd->pd",
        own_rows(shown_rows, 1),
        own_embedded.astype(HALF),
        preferred_element_type=FLOAT,
    )
    patch_b_grad = jnp.sum(own_embedded, (0, 1))
    enc_vec_grad = jnp.concatenate(
        [patch_b_grad[None], enc_vec_grads, enc_gain_grad[None], enc_bias_grad[None]], 0
    )
    dec_vec_grad = jnp.concatenate(
        [
            e2d_b_grad[None],
            mask_grad[None],
            dec_vec_grads,
            dec_gain_grad[None],
            dec_bias_grad[None],
        ],
        0,
    )
    rep_grad = jnp.concatenate(
        [
            patch_grad.reshape(-1),
            e2d_grad.reshape(-1),
            head_w_grad.reshape(-1),
            enc_vec_grad.reshape(-1),
            dec_vec_grad.reshape(-1),
            head_b_grad,
        ]
    )
    ten_grad = jnp.concatenate(
        [mat_grad.reshape(-1) for mat_grad in list(enc_mat_grads) + list(dec_mat_grads)]
    )
    return (loss_part, rep_grad, ten_grad)


def adamw(master, first, second, clipped, number):
    first = BETA1 * first + (1 - BETA1) * clipped
    second = BETA2 * second + (1 - BETA2) * clipped * clipped
    first_hat = first / (1 - BETA1**number)
    second_hat = second / (1 - BETA2**number)
    master = master - LR_IN * (first_hat / (jnp.sqrt(second_hat) + EPS) + DECAY * master)
    return (master, first, second)


def on_device(
    patches,
    visible,
    frames_valid,
    clip_valid,
    rep_weights,
    ten_weights,
    rep_m,
    rep_v,
    ten_m,
    ten_v,
    rep_outer,
    ten_outer,
):
    splits = lax.axis_size("tensor")
    owners = lax.axis_size("dp")
    tube_ids = jnp.arange(TUBES)
    rep_master, ten_master = (rep_weights, ten_weights[0])
    rep_first, rep_second = (rep_m[0], rep_v[0])
    ten_first, ten_second = (ten_m[0, 0], ten_v[0, 0])
    loss_list, count_list, norm_list = ([], [], [])
    for inner_step in range(STEPS):
        rep_full, ten_full = (
            lax.all_gather(rep_master.astype(HALF), "dp", axis=0, tiled=True),
            lax.all_gather(ten_master.astype(HALF), "dp", axis=0, tiled=True),
        )
        visible_ids = visible[inner_step, 0]
        shown = jnp.any(visible_ids[:, :, None] == tube_ids[None, None, :], axis=1)
        weight_rows = (
            jnp.where(shown, 0.0, 1.0)
            * (tube_ids[None, :] // (TUBES // FRAMES) < frames_valid[inner_step, 0][:, None])
            * (clip_valid[inner_step, 0][:, None] == 1)
        ).astype(FLOAT)
        count_part = jnp.sum(own_rows(weight_rows, 1))
        loss_part, rep_grad, ten_grad = group_step(
            patches[inner_step, 0], visible_ids, shown, weight_rows, rep_full, ten_full
        )
        rep_recv, ten_recv = (
            lax.all_to_all(
                rep_grad.reshape(owners, -1), "dp", split_axis=0, concat_axis=0, tiled=True
            ),
            lax.all_to_all(
                ten_grad.reshape(owners, -1), "dp", split_axis=0, concat_axis=0, tiled=True
            ),
        )
        rep_part = lax.psum(jnp.sum(rep_recv, 0), "tensor")
        ten_part = jnp.sum(ten_recv, 0)
        squares = jnp.sum(ten_part * ten_part) + jnp.sum(rep_part * rep_part) / splits
        square_all, loss_all, count_all = lax.psum(
            (squares, loss_part, count_part), ("dp", "tensor")
        )
        norm_value = jnp.sqrt(square_all + 1e-30) / count_all
        factor = jnp.minimum(1.0, CLIP / norm_value) / count_all
        number = STEP_BEFORE + inner_step + 1
        rep_master, rep_first, rep_second = adamw(
            rep_master, rep_first, rep_second, rep_part * factor, number
        )
        ten_master, ten_first, ten_second = adamw(
            ten_master, ten_first, ten_second, ten_part * factor, number
        )
        loss_list.append(loss_all)
        count_list.append(count_all)
        norm_list.append(norm_value)
    rep_sum, ten_sum = lax.psum((rep_weights - rep_master, ten_weights[0] - ten_master), "group")
    groups_count = lax.axis_size("group")
    rep_diff = rep_sum / groups_count
    ten_diff = ten_sum / groups_count
    rep_momentum = MOMENTUM * rep_outer + rep_diff
    ten_momentum = MOMENTUM * ten_outer[0] + ten_diff
    rep_new = rep_weights - LR_OUT * (rep_diff + MOMENTUM * rep_momentum)
    ten_new = ten_weights[0] - LR_OUT * (ten_diff + MOMENTUM * ten_momentum)
    return (
        jnp.stack(loss_list)[:, None],
        jnp.stack(count_list)[:, None],
        jnp.stack(norm_list)[:, None],
        rep_first[None],
        rep_second[None],
        ten_first[None, None],
        ten_second[None, None],
        rep_diff,
        ten_diff[None],
        rep_momentum,
        ten_momentum[None],
        rep_new,
        ten_new[None],
    )


NT=(((1,),(1,)),((),()))
NN=(((1,),(0,)),((),()))
TILE=224
def dot(a,b,dims): return lax.dot_general(a,b,dims,preferred_element_type=FLOAT)

def attn_forward_kernel(q_ref,k_ref,v_ref,out_ref,lse_ref):
    heads=q_ref.shape[1]//HDIM; tiles=q_ref.shape[0]//TILE
    for h in range(heads):
        cols=slice(h*HDIM,(h+1)*HDIM)
        keys=k_ref[:,cols]*HALF(HDIM**-0.5)
        vt=v_ref[:,cols].T
        def step(t,_):
            rows=pl.ds(pl.multiple_of(t*TILE,TILE),TILE)
            s=dot(keys,q_ref[rows,cols],NT)
            m=jnp.max(s,0,keepdims=True)
            e=jnp.exp(s-m)
            total=jnp.sum(e,0,keepdims=True)
            p=(e*(1.0/total)).astype(HALF)
            bt=dot(vt,p,NN)
            out_ref[rows,cols]=bt.T.astype(HALF)
            lse_ref[h,pl.ds(t,1),:]=m+jnp.log(total)
            return 0
        lax.fori_loop(0,tiles,step,0)

def attn_forward(q,k,v):
    rows,width=q.shape
    vm=pl.BlockSpec(memory_space=pltpu.VMEM)
    return pl.pallas_call(attn_forward_kernel,name="attn_forward",
      out_shape=(jax.ShapeDtypeStruct((rows,width),HALF),jax.ShapeDtypeStruct((width//HDIM,rows//TILE,TILE),FLOAT)),
      in_specs=[vm]*3,out_specs=(vm,vm),
      compiler_params=pltpu.CompilerParams(vmem_limit_bytes=48<<20),
      cost_estimate=pl.CostEstimate(flops=4*rows*rows*width,bytes_accessed=rows*width*8,transcendentals=rows*rows*width//HDIM))(q,k,v)

def attn_backward_kernel(q_ref,k_ref,v_ref,g_ref,lse_ref,out_ref,dk_ref,dv_ref):
    width=q_ref.shape[1]
    heads=width//HDIM; tiles=q_ref.shape[0]//TILE
    for h in range(heads):
        cols=slice(h*HDIM,(h+1)*HDIM)
        keys=k_ref[:,cols]*HALF(HDIM**-0.5)
        values=v_ref[:,cols]
        kt=keys.T
        dk_ref[...]=jnp.zeros_like(dk_ref); dv_ref[...]=jnp.zeros_like(dv_ref)
        def step(t,_):
            rows=pl.ds(pl.multiple_of(t*TILE,TILE),TILE)
            q=q_ref[rows,cols]; g=g_ref[rows,cols]
            p=jnp.exp(dot(keys,q,NT)-lse_ref[h,pl.ds(t,1),:])
            dv_ref[...]+=dot(p.astype(HALF),g,NN)
            dp=dot(values,g,NT)
            ds=(p*(dp-jnp.sum(p*dp,0,keepdims=True))).astype(HALF)
            dk_ref[...]+=dot(ds,q,NN)
            out_ref[rows,cols]=dot(kt,ds,NN).T.astype(HALF)
            return 0
        lax.fori_loop(0,tiles,step,0)
        out_ref[:,width+h*HDIM:width+(h+1)*HDIM]=(dk_ref[...]*HDIM**-0.5).astype(HALF)
        out_ref[:,2*width+h*HDIM:2*width+(h+1)*HDIM]=dv_ref[...].astype(HALF)

def attn_backward(q,k,v,g,lse):
    rows,width=q.shape
    vm=pl.BlockSpec(memory_space=pltpu.VMEM)
    return pl.pallas_call(attn_backward_kernel,name="attn_backward",
      out_shape=jax.ShapeDtypeStruct((rows,3*width),HALF),
      in_specs=[vm]*5,out_specs=vm,
      scratch_shapes=[pltpu.VMEM((rows,HDIM),FLOAT),pltpu.VMEM((rows,HDIM),FLOAT)],
      compiler_params=pltpu.CompilerParams(vmem_limit_bytes=48<<20),
      cost_estimate=pl.CostEstimate(flops=10*rows*rows*width,bytes_accessed=rows*width*14,transcendentals=rows*rows*width//HDIM))(q,k,v,g,lse)


HOST = 1
LAST = 3
SWAP = [(0, 1), (1, 0)]
ENC_SHAPES = [(D, 3 * D // 2), (D // 2, D), (D, FF // 2), (FF // 2, D)]
DEC_SHAPES = [(DD, 3 * DD // 2), (DD // 2, DD), (DD, DFF // 2), (DFF // 2, DD)]
ENC_SIZE = sum(math.prod(one) for one in ENC_SHAPES)
DEC_SIZE = sum(math.prod(one) for one in DEC_SHAPES)
PATCH_SIZE = PATCH * D
E2D_SIZE = D * DD
HEAD_SIZE = DD * PATCH
ENC_VECS = 9 * D
DEC_VECS = 10 * DD


def hop(value, *moves):
    pairs = [(2 * a + b, 2 * c + d) for (a, b), (c, d) in moves]
    return lax.ppermute(value, ("dp", "tensor"), pairs)


def hop_both(value, *moves):
    return hop(value, *[((a, side), (b, side)) for a, b in moves for side in range(2)])


def swap(value, *where):
    if where:
        return hop(value, *[((z, side), (z, 1 - side)) for z in where for side in range(2)])
    return lax.ppermute(value, "tensor", SWAP)


def partner(value):
    count = lax.axis_size("group")
    return lax.ppermute(value, "group", [(g, g ^ 1) for g in range(count)])


def mm(left, right):
    return jnp.dot(left, right, preferred_element_type=FLOAT)


def mm_nt(left, right):
    return lax.dot_general(left, right, (((1,), (1,)), ((), ())), preferred_element_type=FLOAT)


def mm_tn(left, right):
    return lax.dot_general(left, right, (((0,), (0,)), ((), ())), preferred_element_type=FLOAT)


def sinus_parts(width):
    column = jnp.arange(width)
    decays = jnp.power(10000.0, -2.0 * (column // 2).astype(FLOAT) / width)
    far = (32 * jnp.arange(-(-TUBES // 32))).astype(FLOAT)[:, None] * decays
    near = jnp.arange(32).astype(FLOAT)[:, None] * decays
    even = column % 2 == 0
    near_one = jnp.where(even, jnp.cos(near), -jnp.sin(near))
    near_two = jnp.where(even, jnp.sin(near), jnp.cos(near))
    return jnp.concatenate([jnp.sin(far), jnp.cos(far)], 1), jnp.concatenate([near_one, near_two], 1)


def sinus_all(width):
    far, near = sinus_parts(width)
    table = far[:, None, :width] * near[None, :, :width] + far[:, None, width:] * near[None, :, width:]
    return table.reshape(-1, width)[:TUBES]


def thirds_of(rows):
    thirds = []
    for _ in range(3):
        thirds.append(lax.optimization_barrier(rows.astype(HALF)))
        rows = rows - thirds[-1].astype(FLOAT)
    return thirds


(
    QKV,
    SQUARE,
    UP,
    PATCH_ROWS,
    E2D,
    HEAD,
    VECS,
    DEC_QKV,
    DEC_OUT,
    DEC_UP,
    DEC_DOWN,
    HEAD_HALF,
    PATCH_LOW,
    PATCH_HIGH,
    W_QKV,
    W_OUT,
    W_UP,
    W_DOWN,
    E2D_W,
    HEAD_UP,
    SEND_ENC,
    SEND_MATE,
    CHAIN,
    CROSS,
    MATE_OWN,
    MATE_OTHER,
) = range(26)
PIECES = {
    QKV: (768, 1152),
    SQUARE: (1248, 768),
    UP: (672, 1536),
    PATCH_ROWS: (704, 768),
    E2D: (768, 384),
    HEAD: (64, 1536),
    VECS: (16, 768),
    DEC_QKV: (384, 576),
    DEC_OUT: (192, 384),
    DEC_UP: (384, 768),
    DEC_DOWN: (768, 384),
}


DEC_PARTS = [DEC_QKV, DEC_OUT, DEC_UP, DEC_DOWN, HEAD_HALF]
SENT = [QKV, SQUARE, UP, PATCH_ROWS, E2D, HEAD, VECS] + DEC_PARTS
ENC_PARTS = [
    (PATCH_LOW, 704, 0, PATCH_ROWS, 0),
    (W_QKV, 768, 0, QKV, 0),
    (W_OUT, 288, 0, SQUARE, 0),
    (W_OUT, 96, 1, SQUARE, 288),
    (PATCH_HIGH, 192, 2, PATCH_ROWS, 0),
    (W_UP, 672, 1, UP, 0),
    (W_UP, 96, 2, UP, 672),
    (W_DOWN, 1248, 2, SQUARE, 0),
    (W_DOWN, 288, 3, SQUARE, 1248),
    (E2D_W, 768, 2, E2D, 0),
]
MESH_ID = pl.DeviceIdType.MESH


VISIBLE = 160
OWN = 2 * VISIBLE
ALL = 4 * VISIBLE
SPAN = (0, 768, 1536)
DEPTH = (704, 704, 192)
WIDE = 1792
SQRT_HALF = 0.5**0.5


def norm_parts(x):
    center = jnp.mean(x, -1, keepdims=True)
    moved = x - center
    scale = lax.rsqrt(jnp.mean(moved * moved, -1, keepdims=True) + 1e-06)
    return moved * scale, scale


def norm_to(x, gain, bias):
    return norm_parts(x)[0] * gain + bias


def norm_from(x, gain, cotangent):
    hat, scale = norm_parts(x)
    inner = cotangent * gain
    grad = scale * (
        inner - jnp.mean(inner, -1, keepdims=True) - hat * jnp.mean(inner * hat, -1, keepdims=True)
    )
    return grad, jnp.sum(cotangent * hat, 0, keepdims=True), jnp.sum(cotangent, 0, keepdims=True)


def gelu_to(x):
    return 0.5 * x * (1.0 + lax.erf(x * SQRT_HALF))


def gelu_slope(x):
    return 0.5 * (1.0 + lax.erf(x * SQRT_HALF)) + x * jnp.exp(-0.5 * x * x) * (2.0 * math.pi) ** -0.5


def rows_at(index, count=VISIBLE):
    return pl.ds(index * count, count)


class Links:
    def __init__(self, send_sem, recv_sem):
        self.send_sem, self.recv_sem, self.keys = send_sem, recv_sem, {}

    def copy(self, key, source, target, peer):
        index = self.keys.setdefault(key, len(self.keys))
        return pltpu.make_async_remote_copy(
            src_ref=source,
            dst_ref=target,
            send_sem=self.send_sem.at[index],
            recv_sem=self.recv_sem.at[index],
            device_id=peer,
            device_id_type=MESH_ID,
        )


LANDED = [W_QKV, W_OUT, W_UP, W_DOWN, E2D_W, VECS]
LANDED_SHAPES = [(768, 1152), (384, 768), (768, 1536), (1536, 768), (768, 384), (16, 768)]
STORED = [
    ((OWN, D), FLOAT),
    ((ALL, D), HALF),
    ((ALL, 3 * D // 2), HALF),
    ((ALL, D // 2), HALF),
    ((OWN, D), FLOAT),
    ((ALL, D), HALF),
    ((ALL, FF // 2), FLOAT),
    ((ALL, FF // 2), HALF),
    ((OWN, D), FLOAT),
    ((OWN, D), HALF),
]


def forward_kernel(shared, *refs):
    sent, refs = dict(zip(SENT, refs[: len(SENT)])), refs[len(SENT) :]
    shown, ids, far_places, near_places, refs = refs[0], refs[1], refs[2], refs[3], refs[4:]
    got, refs = dict(zip(LANDED, refs[: len(LANDED)])), refs[len(LANDED) :]
    got[HEAD], reduced, refs = refs[0], refs[1], refs[2:]
    own, refs = dict(zip(DEC_PARTS, refs[: len(DEC_PARTS)])), refs[len(DEC_PARTS) :]
    other, refs = dict(zip(DEC_PARTS, refs[: len(DEC_PARTS)])), refs[len(DEC_PARTS) :]
    stream, normed, joined, blended, attended, second, upward, activated, encoded, final_enc = refs[:10]
    got[PATCH_LOW], patch_mid, got[PATCH_HIGH], part_sent, part_got, reduced_own, places = refs[10:17]
    send_sem, recv_sem, local_sem = refs[17:]
    g, z, x = lax.axis_index("group"), lax.axis_index("dp"), lax.axis_index("tensor")
    odd = lax.rem(g, 2)
    mate = (g + 1 - 2 * odd, z, x)
    across = (g, z, 1 - x)
    links = Links(send_sem, recv_sem)
    copy = links.copy
    barrier = pltpu.get_barrier_semaphore()

    def at(row, column=None):
        return (g, row, x if column is None else column)

    def greet(peer):
        pl.semaphore_signal(barrier, inc=1, device_id=peer, device_id_type=MESH_ID)

    greet(across)
    if shared:
        greet(mate)
    near = {0: [1], 1: [0, 2, 3], 2: [1, 3], 3: [2, 1]}
    for row, peers in near.items():

        @pl.when(z == row)
        def _():
            for peer in peers:
                greet(at(peer))
            if row != HOST:

                @pl.when(x != row // 2)
                def _():
                    greet(at(HOST, row // 2))

                pl.semaphore_wait(barrier, len(peers) + (2 if shared else 1))

    for column in range(2):

        @pl.when((z == HOST) & (x == column))
        def _():
            pl.semaphore_wait(barrier, 3 + (2 if shared else 1) + 1 + column)

    def part(ref, start, count, half):
        if not half:
            return ref.at[pl.ds(start, count)]
        return ref.at[pl.ds(pl.multiple_of(start + odd * (count // 2), 16), count // 2)]

    keys = [(SEND_ENC, item[0], item[4]) for item in ENC_PARTS] + [(SEND_MATE, item[0], item[4]) for item in ENC_PARTS]
    for name in DEC_PARTS + [VECS, HEAD, HEAD_UP]:
        keys += [(label, name) for label in (CHAIN, CROSS, MATE_OWN, MATE_OTHER)]
    for key in keys + list(range(12)):
        links.keys[key] = len(links.keys)

    def enc_copy(item):
        name, count, owner, piece, first = item
        return copy(
            (SEND_ENC, name, first), part(sent[piece], 0, count, shared), part(got[name], first, count, shared), at(HOST)
        )

    def enc_mate(item):
        name, count, owner, piece, first = item
        half = part(got[name], first, count, True)
        return copy((SEND_MATE, name, first), half, half, mate)

    def local(index, source, target):
        return pltpu.make_async_copy(source, target, local_sem.at[index])

    def chain(name, source, peer):
        target = got[name] if name in got else own[name]
        rows = source.shape[0]
        half = shared and name in own
        return copy((CHAIN, name), part(source, 0, rows, half), part(target, 0, rows, half), at(peer))

    def cross(name, source):
        rows = source.shape[0]
        return copy((CROSS, name), part(source, 0, rows, shared), part(other[name], 0, rows, shared), across)

    def mates(name, ref, label):
        half = part(ref, 0, ref.shape[0], True)
        return copy((label, name), half, half, mate)

    def owned(row):
        return [item for item in ENC_PARTS if item[2] == row and row != HOST]

    def head_up():
        return copy((CHAIN, HEAD_UP), sent[HEAD], got[HEAD], at(LAST))

    def finish_dec(name, source, here):
        cross(name, source).start()
        if shared and not here:
            mates(name, own[name], MATE_OWN).start()

    def end_all(source_of, here):
        for name in DEC_PARTS:
            cross(name, source_of[name]).wait()
            if shared:
                mates(name, other[name], MATE_OTHER).start()
        for name in DEC_PARTS:
            if shared:
                if not here:
                    mates(name, own[name], MATE_OWN).wait()
                mates(name, other[name], MATE_OTHER).wait()

    def give(column, clip):
        row = 2 * column + clip
        return [
            copy(8 + 2 * clip + side, reduced_own.at[clip], reduced, at(row, side))
            for side in range(2)
            if (row, side) != (HOST, column)
        ]

    @pl.when(z == LAST)
    def _():
        chain(VECS, sent[VECS], 2).start()
        locals_ = [local(i, sent[name], own[name]) for i, name in enumerate(DEC_PARTS)]
        locals_.append(local(len(DEC_PARTS), sent[VECS], got[VECS]))
        for one in locals_:
            one.start()
        for item in owned(LAST):
            enc_copy(item).start()
            enc_copy(item).wait_send()
        for i, name in enumerate(DEC_PARTS):
            chain(name, sent[name], 2).start()
            finish_dec(name, sent[name], True)
            if i:
                chain(DEC_PARTS[i - 1], sent[DEC_PARTS[i - 1]], 2).wait_send()
        chain(DEC_PARTS[-1], sent[DEC_PARTS[-1]], 2).wait_send()
        chain(VECS, sent[VECS], 2).wait_send()
        end_all(sent, True)
        for one in locals_:
            one.wait()
        head_up().wait_recv()

    @pl.when(z == 2)
    def _():
        first = local(0, sent[HEAD], got[HEAD])
        first.start()
        chain(VECS, sent[VECS], 2).wait_recv()
        chain(VECS, got[VECS], HOST).start()
        late = [item for item in owned(2) if item[0] == E2D_W]
        for item in owned(2):
            if item not in late:
                enc_copy(item).start()
                enc_copy(item).wait_send()
        head_up().start()
        chain(HEAD, sent[HEAD], HOST).start()
        for i, name in enumerate(DEC_PARTS):
            chain(name, sent[name], 2).wait_recv()
            chain(name, own[name], HOST).start()
            finish_dec(name, own[name], False)
            if i:
                chain(DEC_PARTS[i - 1], own[DEC_PARTS[i - 1]], HOST).wait_send()
        for item in late:
            enc_copy(item).start()
            enc_copy(item).wait_send()
        chain(DEC_PARTS[-1], own[DEC_PARTS[-1]], HOST).wait_send()
        end_all(own, False)
        chain(VECS, got[VECS], HOST).wait_send()
        chain(HEAD, sent[HEAD], HOST).wait_send()
        head_up().wait_send()
        first.wait()

    @pl.when(z == 0)
    def _():
        for item in owned(0):
            enc_copy(item).start()
            enc_copy(item).wait_send()
        for name in DEC_PARTS:
            chain(name, sent[name], 0).wait_recv()
            finish_dec(name, own[name], False)
        end_all(own, False)
        chain(VECS, sent[VECS], 0).wait_recv()
        chain(HEAD, sent[HEAD], 0).wait_recv()

    @pl.when(z == HOST)
    def _():
        mine = [
            local(i, sent[piece].at[pl.ds(0, count)], got[name].at[pl.ds(first, count)])
            for i, (name, count, owner, piece, first) in enumerate(ENC_PARTS)
            if owner == HOST
        ]
        mine.append(local(len(ENC_PARTS), sent[PATCH_ROWS], patch_mid))
        for one in mine:
            one.start()
        chain(VECS, sent[VECS], HOST).wait_recv()
        chain(VECS, got[VECS], 0).start()
        vec = got[VECS][...].astype(FLOAT)
        for one in mine:
            one.wait()

        def await_parts(names):
            items = [item for item in ENC_PARTS if item[2] != HOST and item[0] in names]
            for item in items:
                enc_copy(item).wait_recv()
                if shared:
                    enc_mate(item).start()
            if shared:
                for item in items:
                    enc_mate(item).wait()

        def pump(name):
            chain(name, sent[name], HOST).wait_recv()
            chain(name, own[name], 0).start()
            finish_dec(name, own[name], False)

        def normed_copy(i):
            return copy(i, normed.at[rows_at(i)], normed.at[rows_at(2 + i)], across)

        def out_copy(i):
            return copy(2 + i, part_sent.at[rows_at(i)], part_got.at[rows_at(i)], across)

        def second_copy(i):
            return copy(4 + i, second.at[rows_at(i)], second.at[rows_at(2 + i)], across)

        def down_copy(i):
            return copy(6 + i, part_sent.at[rows_at(2 + i)], part_got.at[rows_at(2 + i)], across)

        spots = lax.broadcasted_iota(jnp.int32, (OWN, 64), 1)
        high = ((ids[...] // 32) == spots).astype(FLOAT).astype(HALF)
        low_hot = (lax.rem(ids[...], 32) == spots).astype(FLOAT).astype(HALF)
        far = mm(high, far_places[0]) + mm(high, far_places[1]) + mm(high, far_places[2])
        near = mm(low_hot, near_places[0]) + mm(low_hot, near_places[1]) + mm(low_hot, near_places[2])
        places[...] = far[:, :D] * near[:, :D] + far[:, D:] * near[:, D:]
        await_parts((PATCH_LOW, PATCH_HIGH))
        for i in range(2):
            rows = rows_at(i)
            emb = places[rows] + vec[0:1]
            for start, depth, weight in zip(SPAN, DEPTH, (got[PATCH_LOW], patch_mid, got[PATCH_HIGH])):
                emb = emb + mm(shown[rows, start : start + depth], weight[...])
            stream[rows] = emb
            normed[rows] = norm_to(emb, vec[1:2], vec[2:3]).astype(HALF)
            normed_copy(i).start()
        await_parts((W_QKV,))

        def attend(c):
            rows = rows_at(c)
            joined[rows] = mm(normed[rows], got[W_QKV][...]).astype(HALF)
            width = D // 2
            for h in range(width // HDIM):
                column = h * HDIM
                queries = joined[rows, column : column + HDIM]
                keys = joined[rows, width + column : width + column + HDIM]
                values = joined[rows, 2 * width + column : 2 * width + column + HDIM]
                scores = mm_nt(queries, keys) * HDIM**-0.5
                weights = jnp.exp(scores - jnp.max(scores, -1, keepdims=True))
                probs = weights * (1.0 / jnp.sum(weights, -1, keepdims=True))
                blended[rows, column : column + HDIM] = mm(probs.astype(HALF), values).astype(HALF)

        for i in range(2):
            attend(i)
            if i == 0:
                await_parts((W_OUT,))
            attended[rows_at(i)] = mm(blended[rows_at(i)], got[W_OUT][...]) + stream[rows_at(i)] + vec[3:4]
            normed_copy(i).wait_recv()
            attend(2 + i)
            part_sent[rows_at(i)] = mm(blended[rows_at(2 + i)], got[W_OUT][...]).astype(HALF)
            out_copy(i).start()

        def feed(c):
            rows = rows_at(c)
            up = mm(second[rows], got[W_UP][...])
            upward[rows] = up
            activated[rows] = gelu_to(up).astype(HALF)
            return mm(activated[rows], got[W_DOWN][...])

        for i in range(2):
            rows = rows_at(i)
            out_copy(i).wait_recv()
            after = attended[rows] + part_got[rows].astype(FLOAT)
            attended[rows] = after
            second[rows] = norm_to(after, vec[4:5], vec[5:6]).astype(HALF)
            second_copy(i).start()
        await_parts((W_UP, W_DOWN))
        chain(HEAD, sent[HEAD], HOST).wait_recv()
        chain(HEAD, got[HEAD], 0).start()
        pump(DEC_QKV)
        pump(DEC_OUT)
        for i in range(2):
            rows = rows_at(i)
            encoded[rows] = feed(i) + attended[rows] + vec[6:7]
            second_copy(i).wait_recv()
            part_sent[rows_at(2 + i)] = feed(2 + i).astype(HALF)
            down_copy(i).start()
            pump((DEC_UP, DEC_DOWN)[i])
        pump(HEAD_HALF)
        await_parts((E2D_W,))
        for i in range(2):
            rows = rows_at(i)
            down_copy(i).wait_recv()
            after = encoded[rows] + part_got[rows_at(2 + i)].astype(FLOAT)
            encoded[rows] = after
            low = norm_to(after, vec[7:8], vec[8:9]).astype(HALF)
            final_enc[rows] = low
            reduced_own[i] = mm(low, got[E2D_W][...])
            for column in range(2):

                @pl.when(x == column)
                def _():
                    for one in give(column, i):
                        one.start()

        for i in range(2):
            normed_copy(i).wait_send()
            out_copy(i).wait_send()
            second_copy(i).wait_send()
            down_copy(i).wait_send()
        for column in range(2):

            @pl.when(x == column)
            def _():
                for i in range(2):
                    for one in give(column, i):
                        one.wait_send()

        end_all(own, False)
        for name in DEC_PARTS:
            chain(name, own[name], 0).wait_send()
        chain(VECS, got[VECS], 0).wait_send()
        chain(HEAD, got[HEAD], 0).wait_send()

    @pl.when((z == HOST) & (x == 0))
    def _():
        mine = local(0, reduced_own.at[1], reduced)
        mine.start()
        mine.wait()

    for row in range(4):
        for side in range(2):
            if (row, side) != (HOST, 0):

                @pl.when((z == row) & (x == side))
                def _():
                    key = 8 + 2 * (row % 2) + side
                    copy(key, reduced_own.at[row % 2], reduced, at(HOST, row // 2)).wait_recv()


def encoder_forward(number, shared, pieces, shown_own, ids_and_places):
    side = lax.axis_index("tensor")
    vmem = pl.BlockSpec(memory_space=pltpu.VMEM)
    anywhere = pl.BlockSpec(memory_space=pl.ANY)
    dec_shapes = [(pieces[name].shape, HALF) for name in DEC_PARTS]
    shapes = [(one, HALF) for one in LANDED_SHAPES] + [((64, PATCH), HALF), ((VISIBLE, DD), FLOAT)]
    shapes = shapes + 2 * dec_shapes + STORED
    count = 2 * len(ENC_PARTS) + 4 * (len(DEC_PARTS) + 3) + 12
    scratch = [
        ((704, D), HALF),
        ((704, D), HALF),
        ((192, D), HALF),
        ((ALL, D), HALF),
        ((ALL, D), HALF),
        ((2, VISIBLE, DD), FLOAT),
        ((OWN, D), FLOAT),
    ]
    out = pl.pallas_call(
        functools.partial(forward_kernel, shared),
        name="encoder_forward",
        out_shape=[jax.ShapeDtypeStruct(*one) for one in shapes],
        in_specs=[anywhere] * len(SENT) + [vmem] * 4,
        out_specs=[vmem] * len(LANDED) + [anywhere, vmem] + [anywhere] * (2 * len(DEC_PARTS)) + [vmem] * len(STORED),
        scratch_shapes=[pltpu.VMEM(*one) for one in scratch]
        + [
            pltpu.SemaphoreType.DMA((count,)),
            pltpu.SemaphoreType.DMA((count,)),
            pltpu.SemaphoreType.DMA((len(ENC_PARTS) + 1,)),
        ],
        compiler_params=pltpu.CompilerParams(
            collective_id=number, has_side_effects=True, vmem_limit_bytes=56 << 20
        ),
    )(*[pieces[name] for name in SENT], shown_own, *ids_and_places)
    landed, out = out[: len(LANDED)], out[len(LANDED) :]
    head, reduced, out = out[0], out[1], out[2:]
    own, other, stored = out[: len(DEC_PARTS)], out[len(DEC_PARTS) : 2 * len(DEC_PARTS)], out[2 * len(DEC_PARTS) :]
    low, high = jnp.where(side == 0, own[4], other[4]), jnp.where(side == 0, other[4], own[4])
    head_w = jnp.concatenate([low, high], 1)
    head_w = jnp.concatenate([head_w[:64] + head, head_w[64:]], 0)
    enc_vec, dec_vec, head_b = split_flat(landed[5].astype(FLOAT).reshape(-1), [(9, D), (10, DD), (PATCH,)])
    enc_weights = (landed[:4], landed[4], jnp.pad(enc_vec, ((0, 7), (0, 0))))
    return reduced, stored, enc_weights, (own[:4], other[:4], head_w, dec_vec, head_b)


def encoder_backward_kernel(
    picked, shown, shown_other, w_qkv, w_out, w_up, w_down, e2d_w, vec,
    stream, normed, joined, blended, attended, second, upward, activated, encoded, final_enc,
    wide, tall, dec_qkv, small, normed_far, active_far, active_last,
    qkv_out, square_out, up_out, patch_out, e2d_out, vec_out,
    one_wide, one_tall, one_qkv, one_small, two_wide, two_tall, two_qkv, two_small,
    wide_sent, tall_sent, dec_qkv_sent, small_sent, wide_got, tall_got, dec_qkv_got, small_got,
    picks_got, low, grad_up_in, mid, grad_blend, grad_joined, part_sent, part_got, own_rows_grad, own_part,
    emb_low, emb_got, down_grad, up_grad, out_grad, qkv_grad, patch_low, patch_mid, patch_high, e2d_part, e2d_got, e2d_grad,
    vec_part, vec_got, send_sem, recv_sem, local_sem,
):
    g, z, x = lax.axis_index("group"), lax.axis_index("dp"), lax.axis_index("tensor")
    barrier = pltpu.get_barrier_semaphore()
    links = Links(send_sem, recv_sem)

    def at(row, column):
        return (g, row, column)

    def greet(peer):
        pl.semaphore_signal(barrier, inc=1, device_id=peer, device_id_type=MESH_ID)

    @pl.when(z != HOST)
    def _():
        greet(at(HOST, x))

    @pl.when(z == LAST)
    def _():
        greet(at(2, x))

    @pl.when((z == HOST) & (x == 0))
    def _():
        for peer in ((0, 0), (0, 1), (HOST, 1)):
            greet(at(*peer))

    @pl.when((z == HOST) & (x == 1))
    def _():
        for peer in ((2, 0), (2, 1), (3, 0), (3, 1), (0, 1), (HOST, 0)):
            greet(at(*peer))

    @pl.when(z == HOST)
    def _():
        pl.semaphore_wait(barrier, 4)

    @pl.when((z == 2) | ((z == 0) & (x == 1)))
    def _():
        pl.semaphore_wait(barrier, 2)

    @pl.when((z == LAST) | ((z == 0) & (x == 0)))
    def _():
        pl.semaphore_wait(barrier, 1)

    def pick_copy(row, side):
        return links.copy((row % 2) * 2 + side, picked, picks_got.at[row % 2, side], at(HOST, row // 2))

    for row in range(4):
        for side in range(2):
            if (row, side) != (HOST, 0):

                @pl.when((z == row) & (x == side))
                def _():
                    pick_copy(row, side).start()

    numbers = iter(range(4, 64))
    low_number = [next(numbers), next(numbers)]
    second_number = [next(numbers), next(numbers)]
    mid_number = [next(numbers), next(numbers)]
    normed_number = [next(numbers), next(numbers)]
    emb_number = [next(numbers), next(numbers)]
    e2d_number, vec_number = next(numbers), next(numbers)

    def row_copies(numbers_two, ref):
        return [
            links.copy(numbers_two[i], ref.at[rows_at(i)], ref.at[rows_at(2 + i)], at(HOST, 1 - x)) for i in range(2)
        ]

    def part_copies(numbers_two, first):
        return [
            links.copy(
                numbers_two[i], part_sent.at[rows_at(first + i)], part_got.at[rows_at(first + i)], at(HOST, 1 - x)
            )
            for i in range(2)
        ]

    out_rows, up_rows, down_rows = 288, 672, 1248
    next_row = jnp.minimum(z + 1, LAST)
    low_far = links.copy(next(numbers), low, low, at(next_row, x))
    joined_far = [
        links.copy(next(numbers), grad_joined.at[rows_at(c)], grad_joined.at[rows_at(c)], at(0, x)) for c in range(4)
    ]
    up_near = links.copy(next(numbers), up_grad.at[pl.ds(up_rows, 96)], up_out.at[pl.ds(0, 96)], at(2, x))
    out_near = links.copy(
        next(numbers), out_grad.at[pl.ds(0, out_rows)], square_out.at[pl.ds(0, out_rows)], at(0, x)
    )
    patch_one = links.copy(next(numbers), patch_low, patch_out, at(0, x))
    patch_two = links.copy(next(numbers), patch_high, patch_out.at[pl.ds(0, 192)], at(2, x))
    e2d_near = links.copy(next(numbers), e2d_grad, e2d_out, at(2, x))
    vec_far = links.copy(next(numbers), vec_part, vec_out, at(LAST, x))

    own_dec = (wide, tall, dec_qkv, small)
    sent_dec = (wide_sent, tall_sent, dec_qkv_sent, small_sent)
    got_dec = (wide_got, tall_got, dec_qkv_got, small_got)
    one_dec = (one_wide, one_tall, one_qkv, one_small)
    two_dec = (two_wide, two_tall, two_qkv, two_small)
    tree_one = [links.copy(next(numbers), sent_dec[i], got_dec[i], at(next_row, x)) for i in range(4)]
    tree_two = [links.copy(next(numbers), sent_dec[i], two_dec[i], at(LAST, x)) for i in range(4)]

    @pl.when((z == 0) | (z == 2))
    def _():
        for i in (3, 0, 1, 2):
            sent_dec[i][...] = own_dec[i][...].astype(sent_dec[i].dtype)
        for i in (3, 0, 1, 2):
            tree_one[i].start()
            if i != 3:
                tree_one[i].wait_send()

    def pass_on(*parts):
        for i in parts:
            tree_one[i].wait_recv()
            sent_dec[i][...] = (own_dec[i][...] + got_dec[i][...].astype(FLOAT)).astype(sent_dec[i].dtype)
            tree_two[i].start()

    def tall_product(left, right, target, step):
        def body(t, carry):
            columns = pl.ds(pl.multiple_of(t * step, step), step)
            target[columns] = mm_tn(left[:, columns], right[...]).astype(HALF)
            return carry

        lax.fori_loop(0, target.shape[0] // step, body, 0)

    @pl.when(z == HOST)
    def _():
        low_sent, mid_sent = row_copies(low_number, low), row_copies(mid_number, mid)
        second_sent, normed_sent = part_copies(second_number, 0), part_copies(normed_number, 2)
        emb_sent = [
            links.copy(
                emb_number[i],
                emb_low.at[1 - x, rows_at(i)],
                emb_got.at[rows_at(i)],
                at(HOST, 1 - x),
            )
            for i in range(2)
        ]
        e2d_sent = links.copy(e2d_number, e2d_part.at[1 - x], e2d_got, at(HOST, 1 - x))
        vec_sent = links.copy(vec_number, vec_part, vec_got, at(HOST, 1 - x))

        vec_part[...] = jnp.zeros_like(vec_part)

        def count(row, value):
            vec_part[row : row + 1] += value

        @pl.when(x == 0)
        def _():
            mine = pltpu.make_async_copy(picked, picks_got.at[1, 0], local_sem.at[0])
            mine.start()
            mine.wait()

        for clip in range(2):
            for side in range(2):
                waiting = links.copy(clip * 2 + side, picked, picks_got.at[clip, side], at(HOST, 0))
                if clip == HOST % 2 and side == 0:

                    @pl.when(x == 1)
                    def _():
                        waiting.wait_recv()

                else:
                    waiting.wait_recv()
        reduced_low = []
        for i in range(2):
            rows = rows_at(i)
            one = picks_got[i, 0] + picks_got[i, 1]
            reduced_low.append(one)
            grad, gain, bias = norm_from(encoded[rows], vec[7:8], mm_nt(one, e2d_w[...]))
            count(7, gain)
            count(8, bias)
            count(6, jnp.sum(grad, 0, keepdims=True))
            own_rows_grad[rows] = grad
            low[rows] = grad.astype(HALF)
            low_sent[i].start()
        whole_low = jnp.concatenate(reduced_low, 0)
        product = mm_tn(final_enc[...], whole_low).astype(HALF)
        e2d_part[0] = product[: D // 2]
        e2d_part[1] = product[D // 2 :]
        e2d_sent.start()

        def feed_back(c):
            rows = rows_at(c)
            grad_up_in[rows] = (mm_nt(low[rows], w_down[...]) * gelu_slope(upward[rows])).astype(HALF)
            return mm_nt(grad_up_in[rows], w_up[...])

        for i in range(2):
            own_part[rows_at(i)] = feed_back(i)
            low_sent[i].wait_recv()
            if i == 1:
                low_far.start()
            part_sent[rows_at(i)] = feed_back(2 + i).astype(HALF)
            second_sent[i].start()
        for i in range(2):
            rows = rows_at(i)
            second_sent[i].wait_recv()
            total = own_part[rows] + part_got[rows].astype(FLOAT)
            grad, gain, bias = norm_from(attended[rows], vec[4:5], total)
            count(4, gain)
            count(5, bias)
            grad = grad + own_rows_grad[rows]
            count(3, jnp.sum(grad, 0, keepdims=True))
            own_rows_grad[rows] = grad
            mid[rows] = grad.astype(HALF)
            mid_sent[i].start()
        e2d_sent.wait()
        e2d_grad[...] = (e2d_part[x].astype(FLOAT) + e2d_got[...].astype(FLOAT)).astype(HALF)
        e2d_near.start()

        def attend_back(c):
            rows = rows_at(c)
            width = D // 2
            grad_blend[...] = mm_nt(mid[rows], w_out[...]).astype(HALF)
            for h in range(width // HDIM):
                column = h * HDIM
                queries = joined[rows, column : column + HDIM]
                keys = joined[rows, width + column : width + column + HDIM]
                values = joined[rows, 2 * width + column : 2 * width + column + HDIM]
                grads = grad_blend[:, column : column + HDIM]
                scores = mm_nt(queries, keys) * HDIM**-0.5
                weights = jnp.exp(scores - jnp.max(scores, -1, keepdims=True))
                probs = weights * (1.0 / jnp.sum(weights, -1, keepdims=True))
                grad_values = mm_tn(probs.astype(HALF), grads)
                grad_probs = mm_nt(grads, values)
                grad_scores = (
                    probs * (grad_probs - jnp.sum(probs * grad_probs, -1, keepdims=True))
                ).astype(HALF)
                for third, value in enumerate(
                    (mm(grad_scores, keys) * HDIM**-0.5, mm_tn(grad_scores, queries) * HDIM**-0.5, grad_values)
                ):
                    start = third * width + column
                    grad_joined[rows, start : start + HDIM] = value.astype(HALF)
            return mm_nt(grad_joined[rows], w_qkv[...])

        for i in range(2):
            own_part[rows_at(i)] = attend_back(i)
            joined_far[i].start()
            pass_on(*((3, 0), (1,))[i])
            mid_sent[i].wait_recv()
            part_sent[rows_at(2 + i)] = attend_back(2 + i).astype(HALF)
            normed_sent[i].start()
            joined_far[2 + i].start()
        pass_on(2)
        tall_product(blended, mid, out_grad, 128)
        out_near.start()
        for i in range(2):
            rows = rows_at(i)
            normed_sent[i].wait_recv()
            total = own_part[rows] + part_got[rows_at(2 + i)].astype(FLOAT)
            grad, gain, bias = norm_from(stream[rows], vec[1:2], total)
            count(1, gain)
            count(2, bias)
            grad = grad + own_rows_grad[rows]
            count(0, jnp.sum(grad, 0, keepdims=True))
            grad_low = grad.astype(HALF)
            emb_low[0, rows] = grad_low[:, : D // 2]
            emb_low[1, rows] = grad_low[:, D // 2 :]
            emb_sent[i].start()
        vec_sent.start()
        tall_product(second, grad_up_in, up_grad, 256)
        up_near.start()
        for one in emb_sent:
            one.wait()
        for start, depth, target in zip(SPAN, DEPTH, (patch_low, patch_mid, patch_high)):
            columns = slice(start, start + depth)
            target[...] = (mm_tn(shown[:, columns], emb_low[x]) + mm_tn(shown_other[:, columns], emb_got[...])).astype(HALF)
        patch_one.start()
        patch_two.start()
        vec_sent.wait()
        vec_part[...] += vec_got[...]
        vec_far.start()
        mine = [
            pltpu.make_async_copy(out_grad.at[pl.ds(out_rows, 96)], square_out.at[pl.ds(0, 96)], local_sem.at[1]),
            pltpu.make_async_copy(up_grad.at[pl.ds(0, up_rows)], up_out, local_sem.at[2]),
            pltpu.make_async_copy(patch_mid, patch_out, local_sem.at[3]),
        ]
        for one in mine:
            one.start()
        for one in low_sent + mid_sent + second_sent + normed_sent:
            one.wait_send()
        for one in (low_far, *joined_far, up_near, out_near, patch_one, patch_two, e2d_near, vec_far):
            one.wait_send()
        for one in tree_two:
            one.wait_send()
        for one in mine:
            one.wait()

    for row in range(4):
        for side in range(2):
            if (row, side) != (HOST, 0):

                @pl.when((z == row) & (x == side))
                def _():
                    pick_copy(row, side).wait_send()

    for row, ones in ((0, (out_near, patch_one)), (2, (up_near, patch_two, e2d_near)), (LAST, (vec_far,))):

        @pl.when(z == row)
        def _():
            for one in ones:
                one.wait_recv()

    @pl.when((z == 0) | (z == 2))
    def _():
        tree_one[3].wait_send()

    @pl.when(z == 2)
    def _():
        low_far.wait_recv()
        low_far.start()
        tall_product(active_far, low, down_grad, 128)
        kept = pltpu.make_async_copy(down_grad.at[pl.ds(0, down_rows)], square_out, local_sem.at[0])
        kept.start()
        low_far.wait_send()
        kept.wait()

    @pl.when(z == LAST)
    def _():
        low_far.wait_recv()
        down_grad[pl.ds(0, 384)] = mm_tn(active_last[...], low[...]).astype(HALF)
        kept = pltpu.make_async_copy(down_grad.at[pl.ds(96, 288)], square_out.at[pl.ds(0, 288)], local_sem.at[0])
        kept.start()
        kept.wait()

    @pl.when(z == 0)
    def _():
        for one in joined_far:
            one.wait_recv()
        tall_product(normed_far, grad_joined, qkv_grad, 256)
        kept = pltpu.make_async_copy(qkv_grad, qkv_out, local_sem.at[0])
        kept.start()
        kept.wait()

    @pl.when(z == LAST)
    def _():
        kept = []
        for i in range(4):
            tree_one[i].wait_recv()
            kept.append(pltpu.make_async_copy(got_dec[i], one_dec[i], local_sem.at[i]))
            kept[i].start()
        for i in range(4):
            tree_two[i].wait_recv()
            kept[i].wait()


def encoder_backward(number, picked, shown, weights, stored, dec_grads, far):
    mats, e2d_w, vec = weights
    vmem = pl.BlockSpec(memory_space=pltpu.VMEM)
    anywhere = pl.BlockSpec(memory_space=pl.ANY)
    shapes = [
        ((D, 3 * D // 2), HALF),
        ((1248, D), HALF),
        ((672, FF // 2), HALF),
        ((704, D // 2), HALF),
        ((D // 2, DD), HALF),
        ((16, D), FLOAT),
    ]
    tree = [(one.shape, HALF) for one in dec_grads[:3]] + [(dec_grads[3].shape, FLOAT)]
    shapes = shapes + 2 * tree
    scratch = 2 * tree + [
        ((2, 2, VISIBLE, DD), HALF),
        ((ALL, D), HALF),
        ((ALL, FF // 2), HALF),
        ((ALL, D), HALF),
        ((VISIBLE, D // 2), HALF),
        ((ALL, 3 * D // 2), HALF),
        ((ALL, D), HALF),
        ((ALL, D), HALF),
        ((OWN, D), FLOAT),
        ((OWN, D), FLOAT),
        ((2, OWN, D // 2), HALF),
        ((OWN, D // 2), HALF),
        ((FF // 2, D), HALF),
        ((D, FF // 2), HALF),
        ((D // 2, D), HALF),
        ((D, 3 * D // 2), HALF),
        ((704, D // 2), HALF),
        ((704, D // 2), HALF),
        ((192, D // 2), HALF),
        ((2, D // 2, DD), HALF),
        ((D // 2, DD), HALF),
        ((D // 2, DD), HALF),
        ((16, D), FLOAT),
        ((16, D), FLOAT),
    ]
    return pl.pallas_call(
        encoder_backward_kernel,
        name="encoder_backward",
        out_shape=[jax.ShapeDtypeStruct(*one) for one in shapes],
        in_specs=[vmem] * 26,
        out_specs=[anywhere] * len(shapes),
        scratch_shapes=[pltpu.VMEM(*one) for one in scratch]
        + [pltpu.SemaphoreType.DMA((40,)), pltpu.SemaphoreType.DMA((40,)), pltpu.SemaphoreType.DMA((4,))],
        compiler_params=pltpu.CompilerParams(
            collective_id=number, has_side_effects=True, vmem_limit_bytes=60 << 20
        ),
    )(picked, *shown, *mats, e2d_w, vec, *stored, *dec_grads, *far)


LANES = 128
STEP_ROWS = 96
TEN_LANES = 8640
REP_LANES = 4056
LAID = [QKV, SQUARE, UP, PATCH_ROWS, E2D, HEAD, VECS, DEC_QKV, DEC_OUT, DEC_UP, DEC_DOWN, HEAD_HALF]
LAID_SHAPES = {**PIECES, HEAD_HALF: (384, 768)}
TEN_PLACES = [
    [(QKV, 768, 0), (SQUARE, 288, 6912)],
    [(SQUARE, 96, 0), (UP, 672, 576)],
    [(UP, 96, 0), (SQUARE, 1248, 1152)],
    [(SQUARE, 288, 0), (DEC_OUT, 192, 3456), (DEC_UP, 384, 4032), (DEC_DOWN, 768, 6336)],
]
DEC_QKV_PLACE = 1728
PATCH_COUNTS = (676, 676, 184)
E2D_PLACE = 1104
HEAD_PLACE = 3408
HEAD_TOP = 54
VEC_PLACE = 3960


def spread_rows(flat, place, blocks, count, read):
    def put(first, value):
        rows = value.shape[0]
        for j in range(blocks):
            flat[pl.ds(place + first * blocks + j, rows, stride=blocks), :] = value[:, j * LANES : (j + 1) * LANES]

    def body(t, carry):
        put(t * STEP_ROWS, read(pl.multiple_of(t * STEP_ROWS, 16), STEP_ROWS))
        return carry

    whole = count // STEP_ROWS
    if whole:
        lax.fori_loop(0, whole, body, 0)
    rest = count - whole * STEP_ROWS
    if rest:
        put(whole * STEP_ROWS, read(whole * STEP_ROWS, -(-rest // 16) * 16)[:rest])


def gather_rows(piece, flat, place, blocks, count):
    def put(first, rows, padded):
        for j in range(blocks):
            value = flat[pl.ds(place + first * blocks + j, rows, stride=blocks), :]
            if padded > rows:
                value = jnp.concatenate([value, jnp.zeros((padded - rows, LANES), FLOAT)], 0)
            piece[pl.ds(first, padded), j * LANES : (j + 1) * LANES] = value.astype(HALF)

    def body(t, carry):
        put(pl.multiple_of(t * STEP_ROWS, 16), STEP_ROWS, STEP_ROWS)
        return carry

    whole = count // STEP_ROWS
    if whole:
        lax.fori_loop(0, whole, body, 0)
    rest = count - whole * STEP_ROWS
    if rest:
        put(whole * STEP_ROWS, rest, -(-rest // 16) * 16)


def lay_out(z, x, ten, rep, pieces, wide_rows):
    for row in range(4):

        @pl.when(z == row)
        def _():
            for name, count, place in TEN_PLACES[row]:
                gather_rows(pieces[name], ten, place, PIECES[name][1] // LANES, count)
            if row < LAST:
                gather_rows(pieces[PATCH_ROWS], rep, 0, D // LANES, PATCH_COUNTS[row])
            if row < 2:
                pieces[PATCH_ROWS][pl.ds(688, 16)] = jnp.zeros((16, D), HALF)
            if row == 2:
                gather_rows(pieces[E2D], rep, E2D_PLACE, DD // LANES, D)
                gather_rows(pieces[HEAD], rep, HEAD_PLACE, PATCH // LANES, HEAD_TOP)
            if row == LAST:
                gather_rows(pieces[VECS], rep, VEC_PLACE, D // LANES, 16)
                for j in range(4):
                    wide_rows[j, pl.ds(0, 192, stride=2), :] = ten[pl.ds(DEC_QKV_PLACE + j, 192, stride=9), :]
                middle = ten[pl.ds(DEC_QKV_PLACE + 4, 192, stride=9), :]
                late = [middle[:, 64:]] + [ten[pl.ds(DEC_QKV_PLACE + 5 + j, 192, stride=9), :] for j in range(4)]
                late = jnp.concatenate(late + [jnp.zeros((192, 64), FLOAT)], 1)
                wide_rows[4, pl.ds(0, 192, stride=2), :] = middle
                for j in range(5):
                    columns = slice(j * LANES, (j + 1) * LANES)
                    wide_rows[j, pl.ds(1, 192, stride=2), :] = late[:, columns]
                for j in range(4):
                    columns = slice(j * LANES, (j + 1) * LANES)
                    pieces[DEC_QKV][:, columns] = wide_rows[j].astype(HALF)
                pieces[DEC_QKV][:, 512:576] = wide_rows[4][:, :64].astype(HALF)
                half = pieces[HEAD_HALF]
                blocks, offset = PATCH // LANES, x * 6
                half[pl.ds(0, 48)] = jnp.zeros((48, D), HALF)
                for j in range(6):
                    columns = slice(j * LANES, (j + 1) * LANES)
                    value = rep[pl.ds(offset + j, 42, stride=blocks), :]
                    half[pl.ds(48, 48), columns] = jnp.concatenate(
                        [jnp.zeros((6, LANES), FLOAT), value], 0
                    ).astype(HALF)
                    for t in range(1, 4):
                        value = rep[pl.ds((96 * t - HEAD_TOP) * blocks + offset + j, 96, stride=blocks), :]
                        half[pl.ds(96 * t, 96), columns] = value.astype(HALF)


def lay_out_kernel(ten, rep, *refs):
    pieces = dict(zip(LAID, refs))
    lay_out(lax.axis_index("dp"), lax.axis_index("tensor"), ten, rep, pieces, refs[len(LAID)])


def first_pieces(ten, rep):
    vmem = pl.BlockSpec(memory_space=pltpu.VMEM)
    out = pl.pallas_call(
        lay_out_kernel,
        name="lay_out",
        out_shape=[jax.ShapeDtypeStruct(LAID_SHAPES[name], HALF) for name in LAID],
        in_specs=[vmem] * 2,
        out_specs=[vmem] * len(LAID),
        scratch_shapes=[pltpu.VMEM((5, 384, LANES), FLOAT)],
        compiler_params=pltpu.CompilerParams(vmem_limit_bytes=61 << 20),
    )(ten, rep)
    return dict(zip(LAID, out))


def update_kernel(
    number, last,
    stats, qkv, square, up, patch, e2d, vec, wide, tall, dec_qkv, small,
    one_wide, one_tall, one_qkv, one_small, two_wide, two_tall, two_qkv, two_small,
    *refs,
):
    masters, refs = refs[:6], refs[6:]
    stats_out, outs, refs = refs[0], refs[1:7], refs[7:]
    pieces = {}
    if not last:
        pieces, refs = dict(zip(LAID, refs)), refs[len(LAID) :]
    held, refs = refs[:6], refs[6:]
    grad_ten, grad_rep, wide_rows, patch_other, e2d_other, head_own, head_other, slots, send_sem, recv_sem, local_sem = refs
    g, z, x = lax.axis_index("group"), lax.axis_index("dp"), lax.axis_index("tensor")
    me = 2 * z + x
    links = Links(send_sem, recv_sem)
    barrier = pltpu.get_barrier_semaphore()
    loads = [pltpu.make_async_copy(masters[i], held[i], local_sem.at[i]) for i in range(6)]
    for one in loads:
        one.start()

    def peer(shift):
        other = lax.rem(me + shift, 8)
        return (g, other // 2, lax.rem(other, 2))

    for shift in range(1, 8):
        pl.semaphore_signal(barrier, inc=1, device_id=peer(shift), device_id_type=MESH_ID)
    pl.semaphore_wait(barrier, 7)

    across = (g, z, 1 - x)
    patch_swap = links.copy(0, patch, patch_other, across)
    e2d_swap = links.copy(1, e2d, e2d_other, across)
    head_swap = links.copy(2, head_own, head_other, across)
    top_own = links.copy(3, head_own.at[pl.ds(0, 64)], head_own.at[pl.ds(0, 64)], (g, 2, x))
    top_other = links.copy(4, head_other.at[pl.ds(0, 64)], head_other.at[pl.ds(0, 64)], (g, 2, x))

    def plain(ref):
        return lambda first, rows: ref[pl.ds(first, rows)].astype(FLOAT)

    def joined(own, other):
        def read(first, rows):
            one, two = own[pl.ds(first, rows)].astype(FLOAT), other[pl.ds(first, rows)].astype(FLOAT)
            return jnp.concatenate([jnp.where(x == 0, one, two), jnp.where(x == 0, two, one)], 1)

        return read

    def total(own, one, two, top, columns):
        def read(first, rows):
            at = pl.ds(top + first, rows)
            return own[at, columns] + one[at, columns].astype(FLOAT) + two[at, columns].astype(FLOAT)

        return read

    @pl.when(z < LAST)
    def _():
        patch_swap.start()

    @pl.when(z == 2)
    def _():
        e2d_swap.start()

    fc = DFF // 2

    @pl.when(z == LAST)
    def _():
        head_own[...] = total(wide, one_wide, two_wide, 0, slice(fc, 2 * fc))(0, DD).astype(HALF)
        head_swap.start()
        top_own.start()
        whole = slice(0, DD)
        spread_rows(grad_ten, 0, 6, 288, plain(square))
        spread_rows(grad_ten, 3456, 3, 192, total(tall, one_tall, two_tall, fc, whole))
        spread_rows(grad_ten, 4032, 6, 384, total(wide, one_wide, two_wide, 0, slice(0, fc)))
        spread_rows(grad_ten, 6336, 3, 768, total(tall, one_tall, two_tall, 0, whole))
        for j in range(4):
            columns = slice(j * LANES, (j + 1) * LANES)
            wide_rows[j] = total(dec_qkv, one_qkv, two_qkv, 0, columns)(0, DD)
        tail = total(dec_qkv, one_qkv, two_qkv, 0, slice(512, 576))(0, DD)
        wide_rows[4] = jnp.concatenate([tail, jnp.zeros((DD, 64), FLOAT)], 1)
        for j in range(4):
            grad_ten[pl.ds(DEC_QKV_PLACE + j, 192, stride=9), :] = wide_rows[j, pl.ds(0, 192, stride=2), :]
        late = jnp.concatenate([wide_rows[j, pl.ds(1, 192, stride=2), :] for j in range(5)], 1)
        early = wide_rows[4, pl.ds(0, 192, stride=2), :]
        grad_ten[pl.ds(DEC_QKV_PLACE + 4, 192, stride=9), :] = jnp.concatenate([early[:, :64], late[:, :64]], 1)
        for j in range(4):
            start = 64 + j * LANES
            grad_ten[pl.ds(DEC_QKV_PLACE + 5 + j, 192, stride=9), :] = late[:, start : start + LANES]
        for j in range(6):
            columns = slice(j * LANES, (j + 1) * LANES)
            grad_rep[pl.ds(VEC_PLACE + j, 9, stride=6), :] = vec[0:9, columns]
        grad_rep[pl.ds(VEC_PLACE + 54, 42), :] = small[0:42] + one_small[0:42] + two_small[0:42]
        head_swap.wait_recv()
        top_other.start()
        read = joined(head_own, head_other)

        def put(first, value):
            rows = value.shape[0]
            for j in range(12):
                grad_rep[pl.ds(first * 12 + j, rows, stride=12), :] = value[:, j * LANES : (j + 1) * LANES]

        put(0, read(48, 48)[6:])
        for t in range(1, 4):
            put(96 * t - HEAD_TOP, read(96 * t, 96))

    for row in range(3):

        @pl.when(z == row)
        def _():
            refs_of = {QKV: qkv, SQUARE: square, UP: up}
            for name, count, place in TEN_PLACES[row]:
                spread_rows(grad_ten, place, PIECES[name][1] // LANES, count, plain(refs_of[name]))
            patch_swap.wait_recv()
            spread_rows(grad_rep, 0, 6, PATCH_COUNTS[row], joined(patch, patch_other))
            if row == 2:
                e2d_swap.wait_recv()
                for half in range(2):

                    def read(first, rows):
                        one, two = e2d[pl.ds(first, rows)].astype(FLOAT), e2d_other[pl.ds(first, rows)].astype(FLOAT)
                        return jnp.where(x == half, one, two)

                    spread_rows(grad_rep, E2D_PLACE + half * 1152, 3, 384, read)
                top_own.wait_recv()
                top_other.wait_recv()
                spread_rows(grad_rep, HEAD_PLACE, 12, HEAD_TOP, joined(head_own, head_other))

    def square_sum(flat, step):
        def body(t, carry):
            value = flat[pl.ds(pl.multiple_of(t * step, 8), step), :]
            return carry + jnp.sum((value * value).reshape(step // 8, 8, LANES), 0)

        return jnp.sum(lax.fori_loop(0, flat.shape[0] // step, body, jnp.zeros((8, LANES), FLOAT)))

    squares = square_sum(grad_ten, 360) + square_sum(grad_rep, 312) * 0.5
    line = lax.broadcasted_iota(jnp.int32, (8, LANES), 0)
    slots[me] = jnp.where(line == 0, squares, stats[...])
    shares = [links.copy(4 + shift, slots.at[me], slots.at[me], peer(shift)) for shift in range(1, 8)]
    for one in shares:
        one.start()
    for one in shares:
        one.wait()
    whole = slots[0]
    for i in range(1, 8):
        whole = whole + slots[i]
    square_all, loss_all, count_all = whole[0:1], whole[1:2], whole[2:3]
    norm = jnp.sqrt(square_all + 1e-30) / count_all
    factor = jnp.minimum(1.0, CLIP / norm) / count_all
    stats_out[...] = jnp.where(line == 0, norm, whole)
    for one in loads:
        one.wait()

    def adam(master, first, second, grad, step):
        def body(t, carry):
            at = pl.ds(pl.multiple_of(t * step, 8), step)
            new = adamw(master[at, :], first[at, :], second[at, :], grad[at, :] * factor, number)
            master[at, :], first[at, :], second[at, :] = new
            return carry

        lax.fori_loop(0, master.shape[0] // step, body, 0)

    stores = [pltpu.make_async_copy(held[i], outs[i], local_sem.at[i]) for i in range(6)]
    adam(*held[:3], grad_ten, 240)
    for one in stores[:3]:
        one.start()
    adam(*held[3:], grad_rep, 312)
    for one in stores[3:]:
        one.start()
    if not last:
        lay_out(z, x, held[0], held[3], pieces, wide_rows)

    @pl.when(z < LAST)
    def _():
        patch_swap.wait_send()

    @pl.when(z == 2)
    def _():
        e2d_swap.wait_send()

    @pl.when(z == LAST)
    def _():
        head_swap.wait_send()
        top_own.wait_send()
        top_other.wait_send()

    for one in stores:
        one.wait()


def update(identity, number, last, stats, gradients, states):
    vmem = pl.BlockSpec(memory_space=pltpu.VMEM)
    anywhere = pl.BlockSpec(memory_space=pl.ANY)
    laid = [] if last else LAID
    flat = [(TEN_LANES, LANES)] * 3 + [(REP_LANES, LANES)] * 3
    scratch = [(one, FLOAT) for one in flat + [(TEN_LANES, LANES), (REP_LANES, LANES), (5, 384, LANES)]] + [
        ((704, D // 2), HALF),
        ((D // 2, DD), HALF),
        ((DD, PATCH // 2), HALF),
        ((DD, PATCH // 2), HALF),
        ((8, 8, LANES), FLOAT),
    ]
    out = pl.pallas_call(
        functools.partial(update_kernel, number, last),
        name="update",
        out_shape=[jax.ShapeDtypeStruct((8, LANES), FLOAT)]
        + [jax.ShapeDtypeStruct(one, FLOAT) for one in flat]
        + [jax.ShapeDtypeStruct(LAID_SHAPES[name], HALF) for name in laid],
        in_specs=[vmem] * (1 + len(gradients)) + [anywhere] * 6,
        out_specs=[vmem] + [anywhere] * 6 + [vmem] * len(laid),
        scratch_shapes=[pltpu.VMEM(*one) for one in scratch]
        + [pltpu.SemaphoreType.DMA((12,)), pltpu.SemaphoreType.DMA((12,)), pltpu.SemaphoreType.DMA((6,))],
        compiler_params=pltpu.CompilerParams(
            collective_id=identity, has_side_effects=True, vmem_limit_bytes=61 << 20
        ),
    )(stats, *gradients, *states)
    return out[0], out[1:7], dict(zip(laid, out[7:]))


def decoder_round(tokens, pixels_low, counted, weights, far):
    own, other, head_w, vec, head_b = weights
    count = pixels_low.shape[0]
    width = DD // 2
    normed = layer_norm(tokens, vec[2], vec[3]).astype(HALF)
    joined = mm(normed, own[0]).astype(HALF)
    queries, keys, values = [joined[:, i * width : (i + 1) * width] for i in range(3)]
    blended, totals = attn_forward(queries, keys, values)
    blend_own = blended[:count]
    blend_other = swap(blended[count:])
    stream = tokens[:count]
    attended = mm(blend_own, own[1]) + mm(blend_other, other[1]) + stream + vec[4]
    second = layer_norm(attended, vec[5], vec[6]).astype(HALF)
    w_up = jnp.concatenate([own[2], other[2]], 1)
    w_down = jnp.concatenate([own[3], other[3]], 0)
    upward = mm(second, w_up)
    activated = gelu_exact(upward).astype(HALF)
    decoded = mm(activated, w_down) + attended + vec[7]
    final_low = layer_norm(decoded, vec[8], vec[9]).astype(HALF)
    predicted = mm(final_low, head_w) + head_b
    pixels = pixels_low.astype(FLOAT)
    center = jnp.mean(pixels, -1, keepdims=True)
    spread = jnp.mean((pixels - center) ** 2, -1, keepdims=True)
    differ = predicted - (pixels - center) * lax.rsqrt(spread + 1e-06)
    loss = jnp.sum(jnp.mean(differ**2, -1) * counted)
    grad_pred = 2.0 / PATCH * differ * counted[:, None]
    pred_low = grad_pred.astype(HALF)
    head_grad = mm_tn(final_low, pred_low)
    head_b_grad = jnp.sum(grad_pred, 0)
    grad_out, gain_end, bias_end = norm_back(decoded, vec[8], vec[9], mm_nt(pred_low, head_w))
    grad_low = grad_out.astype(HALF)
    down_grad = mm_tn(activated, grad_low)
    down_bias = jnp.sum(grad_out, 0)
    _, gelu_pull = jax.vjp(gelu_exact, upward)
    grad_up_in = gelu_pull(mm_nt(grad_low, w_down))[0].astype(HALF)
    up_grad = mm_tn(second, grad_up_in)
    grad_att, gain_two, bias_two = norm_back(attended, vec[5], vec[6], mm_nt(grad_up_in, w_up))
    grad_att = grad_att + grad_out
    out_bias = jnp.sum(grad_att, 0)
    mid = grad_att.astype(HALF)
    grad_other = swap(mm_nt(mid, other[1]).astype(HALF))
    grad_blend = jnp.concatenate([mm_nt(mid, own[1]).astype(HALF), grad_other], 0)
    out_own, out_other = mm_tn(blend_own, mid), mm_tn(blend_other, mid)
    side = lax.axis_index("tensor")
    head_cols = PATCH // 2
    wide_other = jnp.concatenate(
        [
            up_grad[:, DFF // 2 :].astype(HALF),
            lax.dynamic_slice_in_dim(head_grad, (1 - side) * head_cols, head_cols, 1).astype(HALF),
        ],
        1,
    )
    tall_other = jnp.concatenate([down_grad[DFF // 2 :], out_other], 0).astype(HALF)
    wide = jnp.concatenate(
        [up_grad[:, : DFF // 2], lax.dynamic_slice_in_dim(head_grad, side * head_cols, head_cols, 1)], 1
    ) + swap(wide_other)
    tall = jnp.concatenate([down_grad[: DFF // 2], out_own], 0) + swap(tall_other)
    grad_blend, far = lax.optimization_barrier((grad_blend, far))
    grad_joined = attn_backward(queries, keys, values, grad_blend, totals)
    joined_other = swap(grad_joined[count:])
    qkv_grad = mm_tn(normed, grad_joined)
    grad_normed = mm_nt(grad_joined[:count], own[0]) + mm_nt(joined_other, other[0])
    grad_in, gain_one, bias_one = norm_back(stream, vec[2], vec[3], grad_normed)
    grad_in = grad_in + grad_att
    vec_rows = [gain_one, bias_one, out_bias, gain_two, bias_two, down_bias, gain_end, bias_end]
    return loss, grad_in, (wide, tall, qkv_grad), vec_rows, head_b_grad, far


def hosted_round(
    patches,
    visible,
    frames_valid,
    clip_valid,
    rep_weights,
    ten_weights,
    rep_m,
    rep_v,
    ten_m,
    ten_v,
    rep_outer,
    ten_outer,
):
    side = lax.axis_index("tensor")
    z = lax.axis_index("dp")
    half_rows = TUBES // 2
    tube_ids = (jnp.arange(TUBES) + side * half_rows) % TUBES
    ids_one = hop(visible[:, 0, 0], ((0, 0), (HOST, 0)), ((2, 1), (HOST, 1)))
    ids_two = hop(visible[:, 0, 0], ((3, 1), (HOST, 1)))
    ids_two = jnp.where(side == 0, visible[:, 0, 0], ids_two)
    dec_table = sinus_all(DD)
    places = []
    for part in sinus_parts(D):
        part = jnp.pad(part, ((0, -part.shape[0] % 64), (0, 0)))
        places.append(jnp.stack(thirds_of(part)))
    dec_places = jnp.where(side == 0, dec_table, jnp.roll(dec_table, -half_rows, 0))
    states = [one.reshape(TEN_LANES, LANES) for one in (ten_weights, ten_m, ten_v)]
    states = states + [one.reshape(REP_LANES, LANES) for one in (rep_weights, rep_m, rep_v)]
    starts = states[0], states[3]
    pieces = first_pieces(*starts)
    rep_quarter = rep_weights.shape[0]
    shown_steps = []
    for s in range(STEPS):
        picks = (visible[s, 0, 0][:, None] == jnp.arange(TUBES)[None, :]).astype(HALF)
        rows = mm(picks, patches[s, 0, 0]).astype(HALF)
        cuts = (0, rep_quarter // D, 2 * (rep_quarter // D), PATCH)
        rows = jnp.concatenate(
            [
                jnp.pad(rows[:, cuts[i] : cuts[i + 1]], ((0, 0), (0, room - cuts[i + 1] + cuts[i])))
                for i, room in enumerate((768, 768, 256))
            ],
            1,
        )
        one = hop(rows, ((0, 0), (HOST, 0)), ((2, 1), (HOST, 1)))
        two = hop(rows, ((3, 1), (HOST, 1)))
        own = jnp.concatenate([one, jnp.where(side == 0, rows, two)], 0)
        shown_steps.append((own, swap(own, HOST)))
    loss_list, count_list, norm_list = [], [], []
    for s in range(STEPS):
        ids = visible[s, 0, 0]
        picks = tube_ids[:, None] == ids[None, :]
        shown_here = jnp.any(picks, 1)
        counted = (
            jnp.where(shown_here, 0.0, 1.0)
            * (tube_ids // (TUBES // FRAMES) < frames_valid[s, 0, 0])
            * (clip_valid[s, 0, 0] == 1)
        ).astype(FLOAT)[:half_rows]
        shown = shown_steps[s]
        vis = ids.shape[0]
        ids_own = jnp.concatenate([ids_one[s], ids_two[s]])
        reduced_clip, enc_stored, enc_weights, dec_weights = encoder_forward(
            3 + s, s == 0, pieces, shown[0], (ids_own[:, None], *places)
        )
        normed, activated = enc_stored[1], enc_stored[7]
        far = (
            hop_both(normed, (HOST, 0)),
            hop_both(activated, (HOST, 2)),
            hop_both(activated[:, 1152:], (HOST, LAST)),
        )
        dec_vec = dec_weights[3]
        thirds = thirds_of(reduced_clip + dec_vec[0])
        hot = picks.astype(HALF)
        placed = mm(jnp.concatenate([hot, hot, hot], 1), jnp.concatenate(thirds, 0))
        tokens = jnp.where(shown_here[:, None], placed, dec_vec[1]) + dec_places
        pixels_low = lax.dynamic_slice_in_dim(patches[s, 0, 0], side * half_rows, half_rows, 0)
        loss, grad_tokens, (wide, tall, qkv_grad), vec_rows, head_b_grad, far = decoder_round(
            tokens, pixels_low, counted, dec_weights, far
        )
        shown_own = shown_here[:half_rows, None]
        e2d_b_grad = jnp.sum(jnp.where(shown_own, grad_tokens, 0.0), 0)
        mask_grad = jnp.sum(jnp.where(shown_own, 0.0, grad_tokens), 0)
        picked = mm_tn(picks[:half_rows].astype(HALF), grad_tokens.astype(HALF)).astype(HALF)
        small = jnp.concatenate(
            [jnp.stack([e2d_b_grad, mask_grad] + vec_rows).reshape(-1), head_b_grad]
        )
        small = small + swap(small)
        small = jnp.pad(small.reshape(-1, LANES), ((0, 6), (0, 0)))
        back = encoder_backward(5 + s, picked, shown, enc_weights, enc_stored, (wide, tall, qkv_grad, small), far)
        line = jnp.arange(8)[:, None]
        stats = jnp.where(line == 1, loss, jnp.where(line == 2, jnp.sum(counted), 0.0))
        stats = jnp.broadcast_to(stats, (8, LANES))
        stats, states, pieces = update(
            7 + s, STEP_BEFORE + s + 1, s == STEPS - 1, stats, (*back[:6], wide, tall, qkv_grad, small, *back[6:]), states
        )
        norm_list.append(stats[0, 0])
        loss_list.append(stats[1, 0])
        count_list.append(stats[2, 0])
    ten_first, ten_second, rep_first, rep_second = [one.reshape(-1) for one in (*states[1:3], *states[4:])]
    ten_diff, rep_diff = [group_mean(starts[i] - states[3 * i]).reshape(-1) for i in range(2)]
    rep_momentum = MOMENTUM * rep_outer + rep_diff
    ten_momentum = MOMENTUM * ten_outer[0] + ten_diff
    rep_new = rep_weights - LR_OUT * (rep_diff + MOMENTUM * rep_momentum)
    ten_new = ten_weights[0] - LR_OUT * (ten_diff + MOMENTUM * ten_momentum)
    return (
        jnp.stack(loss_list)[:, None],
        jnp.stack(count_list)[:, None],
        jnp.stack(norm_list)[:, None],
        rep_first[None],
        rep_second[None],
        ten_first[None, None],
        ten_second[None, None],
        rep_diff,
        ten_diff[None],
        rep_momentum,
        ten_momentum[None],
        rep_new,
        ten_new[None],
    )


def group_mean(diff):
    if lax.axis_size("group") != 4:
        return lax.psum(diff, "group") / lax.axis_size("group")
    odd = lax.axis_index("group") % 2 == 1
    half = diff.shape[0] // 2
    low, high = diff[:half], diff[half:]
    part = jnp.where(odd, high, low) + partner(jnp.where(odd, low, high))
    part_low = lax.optimization_barrier(part.astype(HALF))
    far = lax.ppermute(part_low, "group", [(g, g ^ 2) for g in range(4)])
    total = (part_low.astype(FLOAT) + far.astype(FLOAT)) * 0.25
    other = partner(total)
    return jnp.concatenate([jnp.where(odd, other, total), jnp.where(odd, total, other)])


def solution(mesh):
    placed = (
        P(None, "group", "dp", None, None),
        P(None, "group", "dp", None),
        P(None, "group", "dp"),
        P(None, "group", "dp"),
        P("dp"),
        P("tensor", "dp"),
        P("group", "dp"),
        P("group", "dp"),
        P("group", "tensor", "dp"),
        P("group", "tensor", "dp"),
        P("dp"),
        P("tensor", "dp"),
    )
    return jax.shard_map(
        hosted_round if mesh.shape["dp"] == 4 and mesh.shape["tensor"] == 2 and mesh.shape["group"] % 2 == 0 else on_device,
        mesh=mesh,
        in_specs=placed,
        out_specs=(
            P(None, "group"),
            P(None, "group"),
            P(None, "group"),
            P("group", "dp"),
            P("group", "dp"),
            P("group", "tensor", "dp"),
            P("group", "tensor", "dp"),
            P("dp"),
            P("tensor", "dp"),
            P("dp"),
            P("tensor", "dp"),
            P("dp"),
            P("tensor", "dp"),
        ),
        check_vma=False,
    )
```

```python
import functools
import math

import jax
import jax.numpy as jnp
from jax import lax
from jax.experimental import pallas as pl
from jax.experimental.pallas import tpu as pltpu
from jax.sharding import PartitionSpec as P

D = 768
HDIM = 64
FF = 3072
DD = 384
DFF = 1536
PATCH = 1536
TUBES = 1568
FRAMES = 8
STEPS = 2
STEP_BEFORE = 6


CLIP = 0.001
LR_IN = 0.01
BETA1 = 0.9
BETA2 = 0.95
EPS = 1e-08
DECAY = 0.05
LR_OUT = 0.7
MOMENTUM = 0.9
FLOAT = jnp.float32
HALF = jnp.bfloat16


def sinus(count, width):
    places = jnp.arange(count).astype(jnp.float32)[:, None]
    column = jnp.arange(width)
    decays = jnp.power(10000.0, -2.0 * (column // 2).astype(jnp.float32) / width)
    angles = places * decays[None, :]
    return jnp.where(column % 2 == 0, jnp.sin(angles), jnp.cos(angles))


def layer_norm(stream, gain, bias):
    center = jnp.mean(stream, -1, keepdims=True)
    spread = jnp.mean((stream - center) ** 2, -1, keepdims=True)
    return (stream - center) * lax.rsqrt(spread + 1e-06) * gain + bias


def norm_back(stream, gain, bias, cotangent):
    _, pull = jax.vjp(layer_norm, stream, gain, bias)
    return pull(cotangent)


def gelu_exact(values):
    return jax.nn.gelu(values, approximate=False)


def split_flat(flat, shapes):
    pieces = []
    offset = 0
    for shapes_one in shapes:
        length = math.prod(shapes_one)
        pieces.append(flat[offset : offset + length].reshape(shapes_one))
        offset += length
    return pieces


def own_rows(stream, axis_dim):
    count = stream.shape[axis_dim] // lax.axis_size("tensor")
    return lax.dynamic_slice_in_dim(stream, lax.axis_index("tensor") * count, count, axis_dim)


def rows_sum(partial_rows):
    return lax.psum_scatter(partial_rows, "tensor", scatter_dimension=1, tiled=True)


def rows_full(own_part):
    return lax.all_gather(own_part, "tensor", axis=1, tiled=True)


def block_forward(stream, mats, vecs):
    w_qkv, w_out, w_up, w_down = mats
    gain_one, bias_one, out_bias, gain_two, bias_two, down_bias = vecs
    nclips, length, _ = stream.shape
    head_cols = w_out.shape[0]
    nheads = head_cols // HDIM
    normed = layer_norm(stream, gain_one, bias_one).astype(HALF)
    joined = jnp.dot(normed, w_qkv, preferred_element_type=FLOAT).astype(HALF)
    queries, key_rows, values = [
        joined[:, :, third_id * head_cols : (third_id + 1) * head_cols].reshape(
            nclips, length, nheads, HDIM
        )
        for third_id in range(3)
    ]
    scores = jnp.einsum(
        "cqhd,ckhd->chqk", queries, key_rows, preferred_element_type=FLOAT
    ) * HDIM ** (-0.5)
    highest = jnp.max(scores, -1, keepdims=True)
    totals = jnp.log(jnp.sum(jnp.exp(scores - highest), -1, keepdims=True)) + highest
    probs_low = jnp.exp(scores - totals).astype(HALF)
    blended = (
        jnp.einsum("chqk,ckhd->cqhd", probs_low, values, preferred_element_type=FLOAT)
        .astype(HALF)
        .reshape(nclips, length, head_cols)
    )
    attended = (
        rows_sum(jnp.dot(blended, w_out, preferred_element_type=FLOAT))
        + own_rows(stream, 1)
        + out_bias
    )
    second = layer_norm(attended, gain_two, bias_two).astype(HALF)
    second_all = lax.all_gather(second, "tensor", axis=1, tiled=True)
    upward = jnp.dot(second_all, w_up, preferred_element_type=FLOAT)
    activated = gelu_exact(upward).astype(HALF)
    result = (
        rows_sum(jnp.dot(activated, w_down, preferred_element_type=FLOAT)) + attended + down_bias
    )
    stored = (
        stream,
        normed,
        queries,
        key_rows,
        values,
        totals,
        blended,
        attended,
        second_all,
        upward,
        activated,
    )
    return (rows_full(result), stored)


def block_backward(grad_out, mats, vecs, stored):
    w_qkv, w_out, w_up, w_down = mats
    gain_one, bias_one, out_bias, gain_two, bias_two, down_bias = vecs
    (
        stream,
        normed,
        queries,
        key_rows,
        values,
        totals,
        blended,
        attended,
        second_all,
        upward,
        activated,
    ) = stored
    nclips, length, _ = stream.shape
    head_cols = w_out.shape[0]
    grad_low = grad_out.astype(HALF)
    grad_down = jnp.einsum("ctf,ctd->fd", activated, grad_low, preferred_element_type=FLOAT)
    down_bias_grad = jnp.sum(own_rows(grad_out, 1), (0, 1))
    grad_act = jnp.dot(grad_low, w_down.T, preferred_element_type=FLOAT)
    _, gelu_pull = jax.vjp(gelu_exact, upward)
    grad_up_in = gelu_pull(grad_act)[0].astype(HALF)
    grad_up = jnp.einsum("ctd,ctf->df", second_all, grad_up_in, preferred_element_type=FLOAT)
    grad_second = rows_sum(jnp.dot(grad_up_in, w_up.T, preferred_element_type=FLOAT))
    grad_att, gain_two_grad, bias_two_grad = norm_back(attended, gain_two, bias_two, grad_second)
    grad_att = grad_att + own_rows(grad_out, 1)
    out_bias_grad = jnp.sum(grad_att, (0, 1))
    grad_mid = rows_full(grad_att)
    mid_low = grad_mid.astype(HALF)
    grad_wout = jnp.einsum("cth,ctd->hd", blended, mid_low, preferred_element_type=FLOAT)
    nheads = head_cols // HDIM
    grad_blend = (
        jnp.dot(mid_low, w_out.T, preferred_element_type=FLOAT)
        .astype(HALF)
        .reshape(nclips, length, nheads, HDIM)
    )
    scores = jnp.einsum(
        "cqhd,ckhd->chqk", queries, key_rows, preferred_element_type=FLOAT
    ) * HDIM ** (-0.5)
    probs_full = jnp.exp(scores - totals)
    probs_low = probs_full.astype(HALF)
    grad_values = jnp.einsum("chqk,cqhd->ckhd", probs_low, grad_blend, preferred_element_type=FLOAT)
    grad_probs = jnp.einsum("cqhd,ckhd->chqk", grad_blend, values, preferred_element_type=FLOAT)
    grad_scores = (
        probs_full * (grad_probs - jnp.sum(probs_full * grad_probs, -1, keepdims=True))
    ).astype(HALF)
    grad_queries = jnp.einsum(
        "chqk,ckhd->cqhd", grad_scores, key_rows, preferred_element_type=FLOAT
    ) * HDIM ** (-0.5)
    grad_keys = jnp.einsum(
        "chqk,cqhd->ckhd", grad_scores, queries, preferred_element_type=FLOAT
    ) * HDIM ** (-0.5)
    grad_joined = jnp.concatenate(
        [
            part_grad.reshape(nclips, length, head_cols)
            for part_grad in (grad_queries, grad_keys, grad_values)
        ],
        -1,
    ).astype(HALF)
    grad_qkv = jnp.einsum("ctd,cte->de", normed, grad_joined, preferred_element_type=FLOAT)
    grad_norm_in = rows_sum(jnp.dot(grad_joined, w_qkv.T, preferred_element_type=FLOAT))
    grad_in, gain_one_grad, bias_one_grad = norm_back(
        own_rows(stream, 1), gain_one, bias_one, grad_norm_in
    )
    grad_in = grad_in + grad_att
    vec_grads = jnp.stack(
        [gain_one_grad, bias_one_grad, out_bias_grad, gain_two_grad, bias_two_grad, down_bias_grad]
    )
    return (rows_full(grad_in), (grad_qkv, grad_wout, grad_up, grad_down), vec_grads)


def group_step(patch_rows, visible_ids, shown, weight_rows, rep_full, ten_full):
    splits = lax.axis_size("tensor")
    patch_w, e2d_w, head_w, enc_vec, dec_vec, head_b = split_flat(
        rep_full, [(PATCH, D), (D, DD), (DD, PATCH), (9, D), (10, DD), (PATCH,)]
    )
    enc_vec = enc_vec.astype(FLOAT)
    dec_vec = dec_vec.astype(FLOAT)
    head_b = head_b.astype(FLOAT)
    enc_cols = D // splits
    dec_cols = DD // splits
    ten_pieces = split_flat(
        ten_full,
        [
            (D, 3 * enc_cols),
            (enc_cols, D),
            (D, FF // splits),
            (FF // splits, D),
            (DD, 3 * dec_cols),
            (dec_cols, DD),
            (DD, DFF // splits),
            (DFF // splits, DD),
        ],
    )
    enc_mats = ten_pieces[0:4]
    dec_mats = ten_pieces[4:8]
    enc_vecs = [enc_vec[i] for i in range(1, 7)]
    dec_vecs = [dec_vec[i] for i in range(2, 8)]
    shown_rows = jnp.take_along_axis(patch_rows, visible_ids[:, :, None], 1)
    embedded = (
        jnp.dot(shown_rows, patch_w, preferred_element_type=FLOAT)
        + enc_vec[0]
        + sinus(TUBES, D)[visible_ids]
    )
    encoded, enc_stored = block_forward(embedded, enc_mats, enc_vecs)
    final_enc = layer_norm(encoded, enc_vec[7], enc_vec[8]).astype(HALF)
    reduced = jnp.dot(final_enc, e2d_w, preferred_element_type=FLOAT) + dec_vec[0]
    blank = jnp.broadcast_to(dec_vec[1], (TUBES, DD))
    tokens_in = jax.vmap(lambda clip_ids, clip_rows: blank.at[clip_ids].set(clip_rows))(
        visible_ids, reduced
    ) + sinus(TUBES, DD)
    decoded, dec_stored = block_forward(tokens_in, dec_mats, dec_vecs)
    own_dec = own_rows(decoded, 1)
    final_low = layer_norm(own_dec, dec_vec[8], dec_vec[9]).astype(HALF)
    predicted = jnp.dot(final_low, head_w, preferred_element_type=FLOAT) + head_b
    pixels = own_rows(patch_rows, 1).astype(FLOAT)
    center = jnp.mean(pixels, -1, keepdims=True)
    spread = jnp.mean((pixels - center) ** 2, -1, keepdims=True)
    target = (pixels - center) * lax.rsqrt(spread + 1e-06)
    differ = predicted - target
    counted = own_rows(weight_rows, 1)
    loss_part = jnp.sum(jnp.mean(differ**2, -1) * counted)
    grad_pred = 2.0 / PATCH * differ * counted[:, :, None]
    pred_low = grad_pred.astype(HALF)
    head_w_grad = jnp.einsum("ctd,ctp->dp", final_low, pred_low, preferred_element_type=FLOAT)
    head_b_grad = jnp.sum(grad_pred, (0, 1))
    grad_final = jnp.dot(pred_low, head_w.T, preferred_element_type=FLOAT)
    grad_dec_own, dec_gain_grad, dec_bias_grad = norm_back(
        own_dec, dec_vec[8], dec_vec[9], grad_final
    )
    grad_tokens, dec_mat_grads, dec_vec_grads = block_backward(
        rows_full(grad_dec_own), dec_mats, dec_vecs, dec_stored
    )
    masked_own = own_rows(1.0 - shown.astype(FLOAT), 1)
    mask_grad = jnp.sum(own_rows(grad_tokens, 1) * masked_own[:, :, None], (0, 1))
    grad_reduced = own_rows(jnp.take_along_axis(grad_tokens, visible_ids[:, :, None], 1), 1)
    reduced_low = grad_reduced.astype(HALF)
    e2d_grad = jnp.einsum(
        "ctd,cte->de", own_rows(final_enc, 1), reduced_low, preferred_element_type=FLOAT
    )
    e2d_b_grad = jnp.sum(grad_reduced, (0, 1))
    grad_enc_final = jnp.dot(reduced_low, e2d_w.T, preferred_element_type=FLOAT)
    grad_enc_own, enc_gain_grad, enc_bias_grad = norm_back(
        own_rows(encoded, 1), enc_vec[7], enc_vec[8], grad_enc_final
    )
    grad_embedded, enc_mat_grads, enc_vec_grads = block_backward(
        rows_full(grad_enc_own), enc_mats, enc_vecs, enc_stored
    )
    own_embedded = own_rows(grad_embedded, 1)
    patch_grad = jnp.einsum(
        "ctp,ctd->pd",
        own_rows(shown_rows, 1),
        own_embedded.astype(HALF),
        preferred_element_type=FLOAT,
    )
    patch_b_grad = jnp.sum(own_embedded, (0, 1))
    enc_vec_grad = jnp.concatenate(
        [patch_b_grad[None], enc_vec_grads, enc_gain_grad[None], enc_bias_grad[None]], 0
    )
    dec_vec_grad = jnp.concatenate(
        [
            e2d_b_grad[None],
            mask_grad[None],
            dec_vec_grads,
            dec_gain_grad[None],
            dec_bias_grad[None],
        ],
        0,
    )
    rep_grad = jnp.concatenate(
        [
            patch_grad.reshape(-1),
            e2d_grad.reshape(-1),
            head_w_grad.reshape(-1),
            enc_vec_grad.reshape(-1),
            dec_vec_grad.reshape(-1),
            head_b_grad,
        ]
    )
    ten_grad = jnp.concatenate(
        [mat_grad.reshape(-1) for mat_grad in list(enc_mat_grads) + list(dec_mat_grads)]
    )
    return (loss_part, rep_grad, ten_grad)


def adamw(master, first, second, clipped, number):
    first = BETA1 * first + (1 - BETA1) * clipped
    second = BETA2 * second + (1 - BETA2) * clipped * clipped
    first_hat = first / (1 - BETA1**number)
    second_hat = second / (1 - BETA2**number)
    master = master - LR_IN * (first_hat / (jnp.sqrt(second_hat) + EPS) + DECAY * master)
    return (master, first, second)


def on_device(
    patches,
    visible,
    frames_valid,
    clip_valid,
    rep_weights,
    ten_weights,
    rep_m,
    rep_v,
    ten_m,
    ten_v,
    rep_outer,
    ten_outer,
):
    splits = lax.axis_size("tensor")
    owners = lax.axis_size("dp")
    tube_ids = jnp.arange(TUBES)
    rep_master, ten_master = (rep_weights, ten_weights[0])
    rep_first, rep_second = (rep_m[0], rep_v[0])
    ten_first, ten_second = (ten_m[0, 0], ten_v[0, 0])
    loss_list, count_list, norm_list = ([], [], [])
    for inner_step in range(STEPS):
        rep_full, ten_full = (
            lax.all_gather(rep_master.astype(HALF), "dp", axis=0, tiled=True),
            lax.all_gather(ten_master.astype(HALF), "dp", axis=0, tiled=True),
        )
        visible_ids = visible[inner_step, 0]
        shown = jnp.any(visible_ids[:, :, None] == tube_ids[None, None, :], axis=1)
        weight_rows = (
            jnp.where(shown, 0.0, 1.0)
            * (tube_ids[None, :] // (TUBES // FRAMES) < frames_valid[inner_step, 0][:, None])
            * (clip_valid[inner_step, 0][:, None] == 1)
        ).astype(FLOAT)
        count_part = jnp.sum(own_rows(weight_rows, 1))
        loss_part, rep_grad, ten_grad = group_step(
            patches[inner_step, 0], visible_ids, shown, weight_rows, rep_full, ten_full
        )
        rep_recv, ten_recv = (
            lax.all_to_all(
                rep_grad.reshape(owners, -1), "dp", split_axis=0, concat_axis=0, tiled=True
            ),
            lax.all_to_all(
                ten_grad.reshape(owners, -1), "dp", split_axis=0, concat_axis=0, tiled=True
            ),
        )
        rep_part = lax.psum(jnp.sum(rep_recv, 0), "tensor")
        ten_part = jnp.sum(ten_recv, 0)
        squares = jnp.sum(ten_part * ten_part) + jnp.sum(rep_part * rep_part) / splits
        square_all, loss_all, count_all = lax.psum(
            (squares, loss_part, count_part), ("dp", "tensor")
        )
        norm_value = jnp.sqrt(square_all + 1e-30) / count_all
        factor = jnp.minimum(1.0, CLIP / norm_value) / count_all
        number = STEP_BEFORE + inner_step + 1
        rep_master, rep_first, rep_second = adamw(
            rep_master, rep_first, rep_second, rep_part * factor, number
        )
        ten_master, ten_first, ten_second = adamw(
            ten_master, ten_first, ten_second, ten_part * factor, number
        )
        loss_list.append(loss_all)
        count_list.append(count_all)
        norm_list.append(norm_value)
    rep_sum, ten_sum = lax.psum((rep_weights - rep_master, ten_weights[0] - ten_master), "group")
    groups_count = lax.axis_size("group")
    rep_diff = rep_sum / groups_count
    ten_diff = ten_sum / groups_count
    rep_momentum = MOMENTUM * rep_outer + rep_diff
    ten_momentum = MOMENTUM * ten_outer[0] + ten_diff
    rep_new = rep_weights - LR_OUT * (rep_diff + MOMENTUM * rep_momentum)
    ten_new = ten_weights[0] - LR_OUT * (ten_diff + MOMENTUM * ten_momentum)
    return (
        jnp.stack(loss_list)[:, None],
        jnp.stack(count_list)[:, None],
        jnp.stack(norm_list)[:, None],
        rep_first[None],
        rep_second[None],
        ten_first[None, None],
        ten_second[None, None],
        rep_diff,
        ten_diff[None],
        rep_momentum,
        ten_momentum[None],
        rep_new,
        ten_new[None],
    )


TILE = 224


HOST = 1
LAST = 3
SWAP = [(0, 1), (1, 0)]
ENC_SHAPES = [(D, 3 * D // 2), (D // 2, D), (D, FF // 2), (FF // 2, D)]
DEC_SHAPES = [(DD, 3 * DD // 2), (DD // 2, DD), (DD, DFF // 2), (DFF // 2, DD)]
ENC_SIZE = sum(math.prod(one) for one in ENC_SHAPES)
DEC_SIZE = sum(math.prod(one) for one in DEC_SHAPES)
PATCH_SIZE = PATCH * D
E2D_SIZE = D * DD
HEAD_SIZE = DD * PATCH
ENC_VECS = 9 * D
DEC_VECS = 10 * DD


def hop(value, *moves):
    pairs = [(2 * a + b, 2 * c + d) for (a, b), (c, d) in moves]
    return lax.ppermute(value, ("dp", "tensor"), pairs)


def hop_both(value, *moves):
    return hop(value, *[((a, side), (b, side)) for a, b in moves for side in range(2)])


def swap(value, *where):
    if where:
        return hop(value, *[((z, side), (z, 1 - side)) for z in where for side in range(2)])
    return lax.ppermute(value, "tensor", SWAP)


def partner(value):
    count = lax.axis_size("group")
    return lax.ppermute(value, "group", [(g, g ^ 1) for g in range(count)])


def mm(left, right):
    return jnp.dot(left, right, preferred_element_type=FLOAT)


def mm_nt(left, right):
    return lax.dot_general(left, right, (((1,), (1,)), ((), ())), preferred_element_type=FLOAT)


def mm_tn(left, right):
    return lax.dot_general(left, right, (((0,), (0,)), ((), ())), preferred_element_type=FLOAT)


def sinus_parts(width):
    column = jnp.arange(width)
    decays = jnp.power(10000.0, -2.0 * (column // 2).astype(FLOAT) / width)
    far = (32 * jnp.arange(-(-TUBES // 32))).astype(FLOAT)[:, None] * decays
    near = jnp.arange(32).astype(FLOAT)[:, None] * decays
    even = column % 2 == 0
    near_one = jnp.where(even, jnp.cos(near), -jnp.sin(near))
    near_two = jnp.where(even, jnp.sin(near), jnp.cos(near))
    return jnp.concatenate([jnp.sin(far), jnp.cos(far)], 1), jnp.concatenate([near_one, near_two], 1)


def sinus_all(width):
    far, near = sinus_parts(width)
    table = far[:, None, :width] * near[None, :, :width] + far[:, None, width:] * near[None, :, width:]
    return table.reshape(-1, width)[:TUBES]


def thirds_of(rows):
    thirds = []
    for _ in range(3):
        thirds.append(lax.optimization_barrier(rows.astype(HALF)))
        rows = rows - thirds[-1].astype(FLOAT)
    return thirds


(
    QKV,
    SQUARE,
    UP,
    PATCH_ROWS,
    E2D,
    HEAD,
    VECS,
    DEC_QKV,
    DEC_OUT,
    DEC_UP,
    DEC_DOWN,
    HEAD_HALF,
    PATCH_LOW,
    PATCH_HIGH,
    W_QKV,
    W_OUT,
    W_UP,
    W_DOWN,
    E2D_W,
    HEAD_UP,
    SEND_ENC,
    SEND_MATE,
    CHAIN,
    CROSS,
    MATE_OWN,
    MATE_OTHER,
) = range(26)
PIECES = {
    QKV: (768, 1152),
    SQUARE: (1248, 768),
    UP: (672, 1536),
    PATCH_ROWS: (704, 768),
    E2D: (768, 384),
    HEAD: (64, 1536),
    VECS: (16, 768),
    DEC_QKV: (384, 576),
    DEC_OUT: (192, 384),
    DEC_UP: (384, 768),
    DEC_DOWN: (768, 384),
}


DEC_PARTS = [DEC_QKV, DEC_OUT, DEC_UP, DEC_DOWN, HEAD_HALF]
SENT = [QKV, SQUARE, UP, PATCH_ROWS, E2D, HEAD, VECS] + DEC_PARTS
ENC_PARTS = [
    (PATCH_LOW, 704, 0, PATCH_ROWS, 0),
    (W_QKV, 768, 0, QKV, 0),
    (W_OUT, 288, 0, SQUARE, 0),
    (W_OUT, 96, 1, SQUARE, 288),
    (PATCH_HIGH, 192, 2, PATCH_ROWS, 0),
    (W_UP, 672, 1, UP, 0),
    (W_UP, 96, 2, UP, 672),
    (W_DOWN, 1248, 2, SQUARE, 0),
    (W_DOWN, 288, 3, SQUARE, 1248),
    (E2D_W, 768, 2, E2D, 0),
]
MESH_ID = pl.DeviceIdType.MESH


VISIBLE = 160
OWN = 2 * VISIBLE
ALL = 4 * VISIBLE
SPAN = (0, 768, 1536)
DEPTH = (704, 704, 192)
WIDE = 1792
SQRT_HALF = 0.5**0.5


def norm_parts(x):
    center = jnp.mean(x, -1, keepdims=True)
    moved = x - center
    scale = lax.rsqrt(jnp.mean(moved * moved, -1, keepdims=True) + 1e-06)
    return moved * scale, scale


def norm_to(x, gain, bias):
    return norm_parts(x)[0] * gain + bias


def norm_from(x, gain, cotangent):
    hat, scale = norm_parts(x)
    inner = cotangent * gain
    grad = scale * (
        inner - jnp.mean(inner, -1, keepdims=True) - hat * jnp.mean(inner * hat, -1, keepdims=True)
    )
    return grad, jnp.sum(cotangent * hat, 0, keepdims=True), jnp.sum(cotangent, 0, keepdims=True)


def gelu_to(x):
    return 0.5 * x * (1.0 + lax.erf(x * SQRT_HALF))


def gelu_slope(x):
    return 0.5 * (1.0 + lax.erf(x * SQRT_HALF)) + x * jnp.exp(-0.5 * x * x) * (2.0 * math.pi) ** -0.5


def rows_at(index, count=VISIBLE):
    return pl.ds(index * count, count)


class Links:
    def __init__(self, send_sem, recv_sem):
        self.send_sem, self.recv_sem, self.keys = send_sem, recv_sem, {}

    def copy(self, key, source, target, peer):
        index = self.keys.setdefault(key, len(self.keys))
        return pltpu.make_async_remote_copy(
            src_ref=source,
            dst_ref=target,
            send_sem=self.send_sem.at[index],
            recv_sem=self.recv_sem.at[index],
            device_id=peer,
            device_id_type=MESH_ID,
        )


LANDED = [W_QKV, W_OUT, W_UP, W_DOWN, E2D_W, VECS]
LANDED_SHAPES = [(768, 1152), (384, 768), (768, 1536), (1536, 768), (768, 384), (16, 768)]
STORED = [
    ((OWN, D), FLOAT),
    ((ALL, D), HALF),
    ((ALL, 3 * D // 2), HALF),
    ((ALL, D // 2), HALF),
    ((OWN, D), FLOAT),
    ((ALL, D), HALF),
    ((ALL, FF // 2), FLOAT),
    ((ALL, FF // 2), HALF),
    ((OWN, D), FLOAT),
    ((OWN, D), HALF),
]


def forward_kernel(shared, *refs):
    sent, refs = dict(zip(SENT, refs[: len(SENT)])), refs[len(SENT) :]
    shown, ids, far_places, near_places, refs = refs[0], refs[1], refs[2], refs[3], refs[4:]
    got, refs = dict(zip(LANDED, refs[: len(LANDED)])), refs[len(LANDED) :]
    got[HEAD], reduced, refs = refs[0], refs[1], refs[2:]
    own, refs = dict(zip(DEC_PARTS, refs[: len(DEC_PARTS)])), refs[len(DEC_PARTS) :]
    other, refs = dict(zip(DEC_PARTS, refs[: len(DEC_PARTS)])), refs[len(DEC_PARTS) :]
    stream, normed, joined, blended, attended, second, upward, activated, encoded, final_enc = refs[:10]
    got[PATCH_LOW], patch_mid, got[PATCH_HIGH], part_sent, part_got, reduced_own, places = refs[10:17]
    send_sem, recv_sem, local_sem = refs[17:]
    g, z, x = lax.axis_index("group"), lax.axis_index("dp"), lax.axis_index("tensor")
    odd = lax.rem(g, 2)
    mate = (g + 1 - 2 * odd, z, x)
    across = (g, z, 1 - x)
    links = Links(send_sem, recv_sem)
    copy = links.copy
    barrier = pltpu.get_barrier_semaphore()

    def at(row, column=None):
        return (g, row, x if column is None else column)

    def greet(peer):
        pl.semaphore_signal(barrier, inc=1, device_id=peer, device_id_type=MESH_ID)

    greet(across)
    if shared:
        greet(mate)
    near = {0: [1], 1: [0, 2, 3], 2: [1, 3], 3: [2, 1]}
    for row, peers in near.items():

        @pl.when(z == row)
        def _():
            for peer in peers:
                greet(at(peer))
            if row != HOST:

                @pl.when(x != row // 2)
                def _():
                    greet(at(HOST, row // 2))

                pl.semaphore_wait(barrier, len(peers) + (2 if shared else 1))

    for column in range(2):

        @pl.when((z == HOST) & (x == column))
        def _():
            pl.semaphore_wait(barrier, 3 + (2 if shared else 1) + 1 + column)

    def part(ref, start, count, half):
        if not half:
            return ref.at[pl.ds(start, count)]
        return ref.at[pl.ds(pl.multiple_of(start + odd * (count // 2), 16), count // 2)]

    keys = [(SEND_ENC, item[0], item[4]) for item in ENC_PARTS] + [(SEND_MATE, item[0], item[4]) for item in ENC_PARTS]
    for name in DEC_PARTS + [VECS, HEAD, HEAD_UP]:
        keys += [(label, name) for label in (CHAIN, CROSS, MATE_OWN, MATE_OTHER)]
    for key in keys + list(range(12)):
        links.keys[key] = len(links.keys)

    def enc_copy(item):
        name, count, owner, piece, first = item
        return copy(
            (SEND_ENC, name, first), part(sent[piece], 0, count, shared), part(got[name], first, count, shared), at(HOST)
        )

    def enc_mate(item):
        name, count, owner, piece, first = item
        half = part(got[name], first, count, True)
        return copy((SEND_MATE, name, first), half, half, mate)

    def local(index, source, target):
        return pltpu.make_async_copy(source, target, local_sem.at[index])

    def chain(name, source, peer):
        target = got[name] if name in got else own[name]
        rows = source.shape[0]
        half = shared and name in own
        return copy((CHAIN, name), part(source, 0, rows, half), part(target, 0, rows, half), at(peer))

    def cross(name, source):
        rows = source.shape[0]
        return copy((CROSS, name), part(source, 0, rows, shared), part(other[name], 0, rows, shared), across)

    def mates(name, ref, label):
        half = part(ref, 0, ref.shape[0], True)
        return copy((label, name), half, half, mate)

    def owned(row):
        return [item for item in ENC_PARTS if item[2] == row and row != HOST]

    def head_up():
        return copy((CHAIN, HEAD_UP), sent[HEAD], got[HEAD], at(LAST))

    def finish_dec(name, source, here):
        cross(name, source).start()
        if shared and not here:
            mates(name, own[name], MATE_OWN).start()

    def end_all(source_of, here):
        for name in DEC_PARTS:
            cross(name, source_of[name]).wait()
            if shared:
                mates(name, other[name], MATE_OTHER).start()
        for name in DEC_PARTS:
            if shared:
                if not here:
                    mates(name, own[name], MATE_OWN).wait()
                mates(name, other[name], MATE_OTHER).wait()

    def give(column, clip):
        row = 2 * column + clip
        return [
            copy(8 + 2 * clip + side, reduced_own.at[clip], reduced, at(row, side))
            for side in range(2)
            if (row, side) != (HOST, column)
        ]

    @pl.when(z == LAST)
    def _():
        chain(VECS, sent[VECS], 2).start()
        locals_ = [local(i, sent[name], own[name]) for i, name in enumerate(DEC_PARTS)]
        locals_.append(local(len(DEC_PARTS), sent[VECS], got[VECS]))
        for one in locals_:
            one.start()
        for item in owned(LAST):
            enc_copy(item).start()
            enc_copy(item).wait_send()
        for i, name in enumerate(DEC_PARTS):
            chain(name, sent[name], 2).start()
            finish_dec(name, sent[name], True)
            if i:
                chain(DEC_PARTS[i - 1], sent[DEC_PARTS[i - 1]], 2).wait_send()
        chain(DEC_PARTS[-1], sent[DEC_PARTS[-1]], 2).wait_send()
        chain(VECS, sent[VECS], 2).wait_send()
        end_all(sent, True)
        for one in locals_:
            one.wait()
        head_up().wait_recv()

    @pl.when(z == 2)
    def _():
        first = local(0, sent[HEAD], got[HEAD])
        first.start()
        chain(VECS, sent[VECS], 2).wait_recv()
        chain(VECS, got[VECS], HOST).start()
        late = [item for item in owned(2) if item[0] == E2D_W]
        for item in owned(2):
            if item not in late:
                enc_copy(item).start()
                enc_copy(item).wait_send()
        head_up().start()
        chain(HEAD, sent[HEAD], HOST).start()
        for i, name in enumerate(DEC_PARTS):
            chain(name, sent[name], 2).wait_recv()
            chain(name, own[name], HOST).start()
            finish_dec(name, own[name], False)
            if i:
                chain(DEC_PARTS[i - 1], own[DEC_PARTS[i - 1]], HOST).wait_send()
        for item in late:
            enc_copy(item).start()
            enc_copy(item).wait_send()
        chain(DEC_PARTS[-1], own[DEC_PARTS[-1]], HOST).wait_send()
        end_all(own, False)
        chain(VECS, got[VECS], HOST).wait_send()
        chain(HEAD, sent[HEAD], HOST).wait_send()
        head_up().wait_send()
        first.wait()

    @pl.when(z == 0)
    def _():
        for item in owned(0):
            enc_copy(item).start()
            enc_copy(item).wait_send()
        for name in DEC_PARTS:
            chain(name, sent[name], 0).wait_recv()
            finish_dec(name, own[name], False)
        end_all(own, False)
        chain(VECS, sent[VECS], 0).wait_recv()
        chain(HEAD, sent[HEAD], 0).wait_recv()

    @pl.when(z == HOST)
    def _():
        mine = [
            local(i, sent[piece].at[pl.ds(0, count)], got[name].at[pl.ds(first, count)])
            for i, (name, count, owner, piece, first) in enumerate(ENC_PARTS)
            if owner == HOST
        ]
        mine.append(local(len(ENC_PARTS), sent[PATCH_ROWS], patch_mid))
        for one in mine:
            one.start()
        chain(VECS, sent[VECS], HOST).wait_recv()
        chain(VECS, got[VECS], 0).start()
        vec = got[VECS][...].astype(FLOAT)
        for one in mine:
            one.wait()

        def await_parts(names):
            items = [item for item in ENC_PARTS if item[2] != HOST and item[0] in names]
            for item in items:
                enc_copy(item).wait_recv()
                if shared:
                    enc_mate(item).start()
            if shared:
                for item in items:
                    enc_mate(item).wait()

        def pump(name):
            chain(name, sent[name], HOST).wait_recv()
            chain(name, own[name], 0).start()
            finish_dec(name, own[name], False)

        def normed_copy(i):
            return copy(i, normed.at[rows_at(i)], normed.at[rows_at(2 + i)], across)

        def out_copy(i):
            return copy(2 + i, part_sent.at[rows_at(i)], part_got.at[rows_at(i)], across)

        def second_copy(i):
            return copy(4 + i, second.at[rows_at(i)], second.at[rows_at(2 + i)], across)

        def down_copy(i):
            return copy(6 + i, part_sent.at[rows_at(2 + i)], part_got.at[rows_at(2 + i)], across)

        spots = lax.broadcasted_iota(jnp.int32, (OWN, 64), 1)
        high = ((ids[...] // 32) == spots).astype(FLOAT).astype(HALF)
        low_hot = (lax.rem(ids[...], 32) == spots).astype(FLOAT).astype(HALF)
        far = mm(high, far_places[0]) + mm(high, far_places[1]) + mm(high, far_places[2])
        near = mm(low_hot, near_places[0]) + mm(low_hot, near_places[1]) + mm(low_hot, near_places[2])
        places[...] = far[:, :D] * near[:, :D] + far[:, D:] * near[:, D:]
        await_parts((PATCH_LOW, PATCH_HIGH))
        for i in range(2):
            rows = rows_at(i)
            emb = places[rows] + vec[0:1]
            for start, depth, weight in zip(SPAN, DEPTH, (got[PATCH_LOW], patch_mid, got[PATCH_HIGH])):
                emb = emb + mm(shown[rows, start : start + depth], weight[...])
            stream[rows] = emb
            normed[rows] = norm_to(emb, vec[1:2], vec[2:3]).astype(HALF)
            normed_copy(i).start()
        await_parts((W_QKV,))

        def attend(c):
            rows = rows_at(c)
            joined[rows] = mm(normed[rows], got[W_QKV][...]).astype(HALF)
            width = D // 2
            for h in range(width // HDIM):
                column = h * HDIM
                queries = joined[rows, column : column + HDIM]
                keys = joined[rows, width + column : width + column + HDIM]
                values = joined[rows, 2 * width + column : 2 * width + column + HDIM]
                scores = mm_nt(queries, keys) * HDIM**-0.5
                weights = jnp.exp(scores - jnp.max(scores, -1, keepdims=True))
                probs = weights * (1.0 / jnp.sum(weights, -1, keepdims=True))
                blended[rows, column : column + HDIM] = mm(probs.astype(HALF), values).astype(HALF)

        for i in range(2):
            attend(i)
            if i == 0:
                await_parts((W_OUT,))
            attended[rows_at(i)] = mm(blended[rows_at(i)], got[W_OUT][...]) + stream[rows_at(i)] + vec[3:4]
            normed_copy(i).wait_recv()
            attend(2 + i)
            part_sent[rows_at(i)] = mm(blended[rows_at(2 + i)], got[W_OUT][...]).astype(HALF)
            out_copy(i).start()

        def feed(c):
            rows = rows_at(c)
            up = mm(second[rows], got[W_UP][...])
            upward[rows] = up
            activated[rows] = gelu_to(up).astype(HALF)
            return mm(activated[rows], got[W_DOWN][...])

        for i in range(2):
            rows = rows_at(i)
            out_copy(i).wait_recv()
            after = attended[rows] + part_got[rows].astype(FLOAT)
            attended[rows] = after
            second[rows] = norm_to(after, vec[4:5], vec[5:6]).astype(HALF)
            second_copy(i).start()
        await_parts((W_UP, W_DOWN))
        chain(HEAD, sent[HEAD], HOST).wait_recv()
        chain(HEAD, got[HEAD], 0).start()
        pump(DEC_QKV)
        pump(DEC_OUT)
        for i in range(2):
            rows = rows_at(i)
            encoded[rows] = feed(i) + attended[rows] + vec[6:7]
            second_copy(i).wait_recv()
            part_sent[rows_at(2 + i)] = feed(2 + i).astype(HALF)
            down_copy(i).start()
            pump((DEC_UP, DEC_DOWN)[i])
        pump(HEAD_HALF)
        await_parts((E2D_W,))
        for i in range(2):
            rows = rows_at(i)
            down_copy(i).wait_recv()
            after = encoded[rows] + part_got[rows_at(2 + i)].astype(FLOAT)
            encoded[rows] = after
            low = norm_to(after, vec[7:8], vec[8:9]).astype(HALF)
            final_enc[rows] = low
            reduced_own[i] = mm(low, got[E2D_W][...])
            for column in range(2):

                @pl.when(x == column)
                def _():
                    for one in give(column, i):
                        one.start()

        for i in range(2):
            normed_copy(i).wait_send()
            out_copy(i).wait_send()
            second_copy(i).wait_send()
            down_copy(i).wait_send()
        for column in range(2):

            @pl.when(x == column)
            def _():
                for i in range(2):
                    for one in give(column, i):
                        one.wait_send()

        end_all(own, False)
        for name in DEC_PARTS:
            chain(name, own[name], 0).wait_send()
        chain(VECS, got[VECS], 0).wait_send()
        chain(HEAD, got[HEAD], 0).wait_send()

    @pl.when((z == HOST) & (x == 0))
    def _():
        mine = local(0, reduced_own.at[1], reduced)
        mine.start()
        mine.wait()

    for row in range(4):
        for side in range(2):
            if (row, side) != (HOST, 0):

                @pl.when((z == row) & (x == side))
                def _():
                    key = 8 + 2 * (row % 2) + side
                    copy(key, reduced_own.at[row % 2], reduced, at(HOST, row // 2)).wait_recv()


def encoder_forward(number, shared, pieces, shown_own, ids_and_places):
    side = lax.axis_index("tensor")
    vmem = pl.BlockSpec(memory_space=pltpu.VMEM)
    anywhere = pl.BlockSpec(memory_space=pl.ANY)
    dec_shapes = [(pieces[name].shape, HALF) for name in DEC_PARTS]
    shapes = [(one, HALF) for one in LANDED_SHAPES] + [((64, PATCH), HALF), ((VISIBLE, DD), FLOAT)]
    shapes = shapes + 2 * dec_shapes + STORED
    count = 2 * len(ENC_PARTS) + 4 * (len(DEC_PARTS) + 3) + 12
    scratch = [
        ((704, D), HALF),
        ((704, D), HALF),
        ((192, D), HALF),
        ((ALL, D), HALF),
        ((ALL, D), HALF),
        ((2, VISIBLE, DD), FLOAT),
        ((OWN, D), FLOAT),
    ]
    out = pl.pallas_call(
        functools.partial(forward_kernel, shared),
        name="encoder_forward",
        out_shape=[jax.ShapeDtypeStruct(*one) for one in shapes],
        in_specs=[anywhere] * len(SENT) + [vmem] * 4,
        out_specs=[vmem] * len(LANDED) + [anywhere, vmem] + [anywhere] * (2 * len(DEC_PARTS)) + [vmem] * len(STORED),
        scratch_shapes=[pltpu.VMEM(*one) for one in scratch]
        + [
            pltpu.SemaphoreType.DMA((count,)),
            pltpu.SemaphoreType.DMA((count,)),
            pltpu.SemaphoreType.DMA((len(ENC_PARTS) + 1,)),
        ],
        compiler_params=pltpu.CompilerParams(
            collective_id=number, has_side_effects=True, vmem_limit_bytes=56 << 20
        ),
    )(*[pieces[name] for name in SENT], shown_own, *ids_and_places)
    landed, out = out[: len(LANDED)], out[len(LANDED) :]
    head, reduced, out = out[0], out[1], out[2:]
    own, other, stored = out[: len(DEC_PARTS)], out[len(DEC_PARTS) : 2 * len(DEC_PARTS)], out[2 * len(DEC_PARTS) :]
    low, high = jnp.where(side == 0, own[4], other[4]), jnp.where(side == 0, other[4], own[4])
    head_w = jnp.concatenate([low, high], 1)
    head_w = jnp.concatenate([head_w[:64] + head, head_w[64:]], 0)
    enc_vec, dec_vec, head_b = split_flat(landed[5].astype(FLOAT).reshape(-1), [(9, D), (10, DD), (PATCH,)])
    enc_weights = (landed[:4], landed[4], jnp.pad(enc_vec, ((0, 7), (0, 0))))
    return reduced, stored, enc_weights, (own[:4], other[:4], head_w, dec_vec, head_b)


def encoder_backward_kernel(
    picked, shown, shown_other, w_qkv, w_out, w_up, w_down, e2d_w, vec,
    stream, normed, joined, blended, attended, second, upward, activated, encoded, final_enc,
    wide, tall, dec_qkv, small, normed_far, active_far, active_last,
    qkv_out, square_out, up_out, patch_out, e2d_out, vec_out,
    one_wide, one_tall, one_qkv, one_small, two_wide, two_tall, two_qkv, two_small,
    wide_sent, tall_sent, dec_qkv_sent, small_sent, wide_got, tall_got, dec_qkv_got, small_got,
    picks_got, low, grad_up_in, mid, grad_blend, grad_joined, part_sent, part_got, own_rows_grad, own_part,
    emb_low, emb_got, down_grad, up_grad, out_grad, qkv_grad, patch_low, patch_mid, patch_high, e2d_part, e2d_got, e2d_grad,
    vec_part, vec_got, send_sem, recv_sem, local_sem,
):
    g, z, x = lax.axis_index("group"), lax.axis_index("dp"), lax.axis_index("tensor")
    barrier = pltpu.get_barrier_semaphore()
    links = Links(send_sem, recv_sem)

    def at(row, column):
        return (g, row, column)

    def greet(peer):
        pl.semaphore_signal(barrier, inc=1, device_id=peer, device_id_type=MESH_ID)

    @pl.when(z != HOST)
    def _():
        greet(at(HOST, x))

    @pl.when(z == LAST)
    def _():
        greet(at(2, x))

    @pl.when((z == HOST) & (x == 0))
    def _():
        for peer in ((0, 0), (0, 1), (HOST, 1)):
            greet(at(*peer))

    @pl.when((z == HOST) & (x == 1))
    def _():
        for peer in ((2, 0), (2, 1), (3, 0), (3, 1), (0, 1), (HOST, 0)):
            greet(at(*peer))

    @pl.when(z == HOST)
    def _():
        pl.semaphore_wait(barrier, 4)

    @pl.when((z == 2) | ((z == 0) & (x == 1)))
    def _():
        pl.semaphore_wait(barrier, 2)

    @pl.when((z == LAST) | ((z == 0) & (x == 0)))
    def _():
        pl.semaphore_wait(barrier, 1)

    def pick_copy(row, side):
        return links.copy((row % 2) * 2 + side, picked, picks_got.at[row % 2, side], at(HOST, row // 2))

    for row in range(4):
        for side in range(2):
            if (row, side) != (HOST, 0):

                @pl.when((z == row) & (x == side))
                def _():
                    pick_copy(row, side).start()

    numbers = iter(range(4, 64))
    low_number = [next(numbers), next(numbers)]
    second_number = [next(numbers), next(numbers)]
    mid_number = [next(numbers), next(numbers)]
    normed_number = [next(numbers), next(numbers)]
    emb_number = [next(numbers), next(numbers)]
    e2d_number, vec_number = next(numbers), next(numbers)

    def row_copies(numbers_two, ref):
        return [
            links.copy(numbers_two[i], ref.at[rows_at(i)], ref.at[rows_at(2 + i)], at(HOST, 1 - x)) for i in range(2)
        ]

    def part_copies(numbers_two, first):
        return [
            links.copy(
                numbers_two[i], part_sent.at[rows_at(first + i)], part_got.at[rows_at(first + i)], at(HOST, 1 - x)
            )
            for i in range(2)
        ]

    out_rows, up_rows, down_rows = 288, 672, 1248
    next_row = jnp.minimum(z + 1, LAST)
    low_far = links.copy(next(numbers), low, low, at(next_row, x))
    joined_far = [
        links.copy(next(numbers), grad_joined.at[rows_at(c)], grad_joined.at[rows_at(c)], at(0, x)) for c in range(4)
    ]
    up_near = links.copy(next(numbers), up_grad.at[pl.ds(up_rows, 96)], up_out.at[pl.ds(0, 96)], at(2, x))
    out_near = links.copy(
        next(numbers), out_grad.at[pl.ds(0, out_rows)], square_out.at[pl.ds(0, out_rows)], at(0, x)
    )
    patch_one = links.copy(next(numbers), patch_low, patch_out, at(0, x))
    patch_two = links.copy(next(numbers), patch_high, patch_out.at[pl.ds(0, 192)], at(2, x))
    e2d_near = links.copy(next(numbers), e2d_grad, e2d_out, at(2, x))
    vec_far = links.copy(next(numbers), vec_part, vec_out, at(LAST, x))

    own_dec = (wide, tall, dec_qkv, small)
    sent_dec = (wide_sent, tall_sent, dec_qkv_sent, small_sent)
    got_dec = (wide_got, tall_got, dec_qkv_got, small_got)
    one_dec = (one_wide, one_tall, one_qkv, one_small)
    two_dec = (two_wide, two_tall, two_qkv, two_small)
    tree_one = [links.copy(next(numbers), sent_dec[i], got_dec[i], at(next_row, x)) for i in range(4)]
    tree_two = [links.copy(next(numbers), sent_dec[i], two_dec[i], at(LAST, x)) for i in range(4)]

    @pl.when((z == 0) | (z == 2))
    def _():
        for i in (3, 0, 1, 2):
            sent_dec[i][...] = own_dec[i][...].astype(sent_dec[i].dtype)
        for i in (3, 0, 1, 2):
            tree_one[i].start()
            if i != 3:
                tree_one[i].wait_send()

    def pass_on(*parts):
        for i in parts:
            tree_one[i].wait_recv()
            sent_dec[i][...] = (own_dec[i][...] + got_dec[i][...].astype(FLOAT)).astype(sent_dec[i].dtype)
            tree_two[i].start()

    def tall_product(left, right, target, step):
        def body(t, carry):
            columns = pl.ds(pl.multiple_of(t * step, step), step)
            target[columns] = mm_tn(left[:, columns], right[...]).astype(HALF)
            return carry

        lax.fori_loop(0, target.shape[0] // step, body, 0)

    @pl.when(z == HOST)
    def _():
        low_sent, mid_sent = row_copies(low_number, low), row_copies(mid_number, mid)
        second_sent, normed_sent = part_copies(second_number, 0), part_copies(normed_number, 2)
        emb_sent = [
            links.copy(
                emb_number[i],
                emb_low.at[1 - x, rows_at(i)],
                emb_got.at[rows_at(i)],
                at(HOST, 1 - x),
            )
            for i in range(2)
        ]
        e2d_sent = links.copy(e2d_number, e2d_part.at[1 - x], e2d_got, at(HOST, 1 - x))
        vec_sent = links.copy(vec_number, vec_part, vec_got, at(HOST, 1 - x))

        vec_part[...] = jnp.zeros_like(vec_part)

        def count(row, value):
            vec_part[row : row + 1] += value

        @pl.when(x == 0)
        def _():
            mine = pltpu.make_async_copy(picked, picks_got.at[1, 0], local_sem.at[0])
            mine.start()
            mine.wait()

        for clip in range(2):
            for side in range(2):
                waiting = links.copy(clip * 2 + side, picked, picks_got.at[clip, side], at(HOST, 0))
                if clip == HOST % 2 and side == 0:

                    @pl.when(x == 1)
                    def _():
                        waiting.wait_recv()

                else:
                    waiting.wait_recv()
        reduced_low = []
        for i in range(2):
            rows = rows_at(i)
            one = picks_got[i, 0] + picks_got[i, 1]
            reduced_low.append(one)
            grad, gain, bias = norm_from(encoded[rows], vec[7:8], mm_nt(one, e2d_w[...]))
            count(7, gain)
            count(8, bias)
            count(6, jnp.sum(grad, 0, keepdims=True))
            own_rows_grad[rows] = grad
            low[rows] = grad.astype(HALF)
            low_sent[i].start()
        whole_low = jnp.concatenate(reduced_low, 0)
        product = mm_tn(final_enc[...], whole_low).astype(HALF)
        e2d_part[0] = product[: D // 2]
        e2d_part[1] = product[D // 2 :]
        e2d_sent.start()

        def feed_back(c):
            rows = rows_at(c)
            grad_up_in[rows] = (mm_nt(low[rows], w_down[...]) * gelu_slope(upward[rows])).astype(HALF)
            return mm_nt(grad_up_in[rows], w_up[...])

        for i in range(2):
            own_part[rows_at(i)] = feed_back(i)
            low_sent[i].wait_recv()
            if i == 1:
                low_far.start()
            part_sent[rows_at(i)] = feed_back(2 + i).astype(HALF)
            second_sent[i].start()
        for i in range(2):
            rows = rows_at(i)
            second_sent[i].wait_recv()
            total = own_part[rows] + part_got[rows].astype(FLOAT)
            grad, gain, bias = norm_from(attended[rows], vec[4:5], total)
            count(4, gain)
            count(5, bias)
            grad = grad + own_rows_grad[rows]
            count(3, jnp.sum(grad, 0, keepdims=True))
            own_rows_grad[rows] = grad
            mid[rows] = grad.astype(HALF)
            mid_sent[i].start()
        e2d_sent.wait()
        e2d_grad[...] = (e2d_part[x].astype(FLOAT) + e2d_got[...].astype(FLOAT)).astype(HALF)
        e2d_near.start()

        def attend_back(c):
            rows = rows_at(c)
            width = D // 2
            grad_blend[...] = mm_nt(mid[rows], w_out[...]).astype(HALF)
            for h in range(width // HDIM):
                column = h * HDIM
                queries = joined[rows, column : column + HDIM]
                keys = joined[rows, width + column : width + column + HDIM]
                values = joined[rows, 2 * width + column : 2 * width + column + HDIM]
                grads = grad_blend[:, column : column + HDIM]
                scores = mm_nt(queries, keys) * HDIM**-0.5
                weights = jnp.exp(scores - jnp.max(scores, -1, keepdims=True))
                probs = weights * (1.0 / jnp.sum(weights, -1, keepdims=True))
                grad_values = mm_tn(probs.astype(HALF), grads)
                grad_probs = mm_nt(grads, values)
                grad_scores = (
                    probs * (grad_probs - jnp.sum(probs * grad_probs, -1, keepdims=True))
                ).astype(HALF)
                for third, value in enumerate(
                    (mm(grad_scores, keys) * HDIM**-0.5, mm_tn(grad_scores, queries) * HDIM**-0.5, grad_values)
                ):
                    start = third * width + column
                    grad_joined[rows, start : start + HDIM] = value.astype(HALF)
            return mm_nt(grad_joined[rows], w_qkv[...])

        for i in range(2):
            own_part[rows_at(i)] = attend_back(i)
            joined_far[i].start()
            pass_on(*((3, 0), (1,))[i])
            mid_sent[i].wait_recv()
            part_sent[rows_at(2 + i)] = attend_back(2 + i).astype(HALF)
            normed_sent[i].start()
            joined_far[2 + i].start()
        pass_on(2)
        tall_product(blended, mid, out_grad, 128)
        out_near.start()
        for i in range(2):
            rows = rows_at(i)
            normed_sent[i].wait_recv()
            total = own_part[rows] + part_got[rows_at(2 + i)].astype(FLOAT)
            grad, gain, bias = norm_from(stream[rows], vec[1:2], total)
            count(1, gain)
            count(2, bias)
            grad = grad + own_rows_grad[rows]
            count(0, jnp.sum(grad, 0, keepdims=True))
            grad_low = grad.astype(HALF)
            emb_low[0, rows] = grad_low[:, : D // 2]
            emb_low[1, rows] = grad_low[:, D // 2 :]
            emb_sent[i].start()
        vec_sent.start()
        tall_product(second, grad_up_in, up_grad, 256)
        up_near.start()
        for one in emb_sent:
            one.wait()
        for start, depth, target in zip(SPAN, DEPTH, (patch_low, patch_mid, patch_high)):
            columns = slice(start, start + depth)
            target[...] = (mm_tn(shown[:, columns], emb_low[x]) + mm_tn(shown_other[:, columns], emb_got[...])).astype(HALF)
        patch_one.start()
        patch_two.start()
        vec_sent.wait()
        vec_part[...] += vec_got[...]
        vec_far.start()
        mine = [
            pltpu.make_async_copy(out_grad.at[pl.ds(out_rows, 96)], square_out.at[pl.ds(0, 96)], local_sem.at[1]),
            pltpu.make_async_copy(up_grad.at[pl.ds(0, up_rows)], up_out, local_sem.at[2]),
            pltpu.make_async_copy(patch_mid, patch_out, local_sem.at[3]),
        ]
        for one in mine:
            one.start()
        for one in low_sent + mid_sent + second_sent + normed_sent:
            one.wait_send()
        for one in (low_far, *joined_far, up_near, out_near, patch_one, patch_two, e2d_near, vec_far):
            one.wait_send()
        for one in tree_two:
            one.wait_send()
        for one in mine:
            one.wait()

    for row in range(4):
        for side in range(2):
            if (row, side) != (HOST, 0):

                @pl.when((z == row) & (x == side))
                def _():
                    pick_copy(row, side).wait_send()

    for row, ones in ((0, (out_near, patch_one)), (2, (up_near, patch_two, e2d_near)), (LAST, (vec_far,))):

        @pl.when(z == row)
        def _():
            for one in ones:
                one.wait_recv()

    @pl.when((z == 0) | (z == 2))
    def _():
        tree_one[3].wait_send()

    @pl.when(z == 2)
    def _():
        low_far.wait_recv()
        low_far.start()
        tall_product(active_far, low, down_grad, 128)
        kept = pltpu.make_async_copy(down_grad.at[pl.ds(0, down_rows)], square_out, local_sem.at[0])
        kept.start()
        low_far.wait_send()
        kept.wait()

    @pl.when(z == LAST)
    def _():
        low_far.wait_recv()
        down_grad[pl.ds(0, 384)] = mm_tn(active_last[...], low[...]).astype(HALF)
        kept = pltpu.make_async_copy(down_grad.at[pl.ds(96, 288)], square_out.at[pl.ds(0, 288)], local_sem.at[0])
        kept.start()
        kept.wait()

    @pl.when(z == 0)
    def _():
        for one in joined_far:
            one.wait_recv()
        tall_product(normed_far, grad_joined, qkv_grad, 256)
        kept = pltpu.make_async_copy(qkv_grad, qkv_out, local_sem.at[0])
        kept.start()
        kept.wait()

    @pl.when(z == LAST)
    def _():
        kept = []
        for i in range(4):
            tree_one[i].wait_recv()
            kept.append(pltpu.make_async_copy(got_dec[i], one_dec[i], local_sem.at[i]))
            kept[i].start()
        for i in range(4):
            tree_two[i].wait_recv()
            kept[i].wait()


def encoder_backward(number, picked, shown, weights, stored, dec_grads, far):
    mats, e2d_w, vec = weights
    vmem = pl.BlockSpec(memory_space=pltpu.VMEM)
    anywhere = pl.BlockSpec(memory_space=pl.ANY)
    shapes = [
        ((D, 3 * D // 2), HALF),
        ((1248, D), HALF),
        ((672, FF // 2), HALF),
        ((704, D // 2), HALF),
        ((D // 2, DD), HALF),
        ((16, D), FLOAT),
    ]
    tree = [(one.shape, HALF) for one in dec_grads[:3]] + [(dec_grads[3].shape, FLOAT)]
    shapes = shapes + 2 * tree
    scratch = 2 * tree + [
        ((2, 2, VISIBLE, DD), HALF),
        ((ALL, D), HALF),
        ((ALL, FF // 2), HALF),
        ((ALL, D), HALF),
        ((VISIBLE, D // 2), HALF),
        ((ALL, 3 * D // 2), HALF),
        ((ALL, D), HALF),
        ((ALL, D), HALF),
        ((OWN, D), FLOAT),
        ((OWN, D), FLOAT),
        ((2, OWN, D // 2), HALF),
        ((OWN, D // 2), HALF),
        ((FF // 2, D), HALF),
        ((D, FF // 2), HALF),
        ((D // 2, D), HALF),
        ((D, 3 * D // 2), HALF),
        ((704, D // 2), HALF),
        ((704, D // 2), HALF),
        ((192, D // 2), HALF),
        ((2, D // 2, DD), HALF),
        ((D // 2, DD), HALF),
        ((D // 2, DD), HALF),
        ((16, D), FLOAT),
        ((16, D), FLOAT),
    ]
    return pl.pallas_call(
        encoder_backward_kernel,
        name="encoder_backward",
        out_shape=[jax.ShapeDtypeStruct(*one) for one in shapes],
        in_specs=[vmem] * 26,
        out_specs=[anywhere] * len(shapes),
        scratch_shapes=[pltpu.VMEM(*one) for one in scratch]
        + [pltpu.SemaphoreType.DMA((40,)), pltpu.SemaphoreType.DMA((40,)), pltpu.SemaphoreType.DMA((4,))],
        compiler_params=pltpu.CompilerParams(
            collective_id=number, has_side_effects=True, vmem_limit_bytes=60 << 20
        ),
    )(picked, *shown, *mats, e2d_w, vec, *stored, *dec_grads, *far)


LANES = 128
STEP_ROWS = 96
TEN_LANES = 8640
REP_LANES = 4056
LAID = [QKV, SQUARE, UP, PATCH_ROWS, E2D, HEAD, VECS, DEC_QKV, DEC_OUT, DEC_UP, DEC_DOWN, HEAD_HALF]
LAID_SHAPES = {**PIECES, HEAD_HALF: (384, 768)}
TEN_PLACES = [
    [(QKV, 768, 0), (SQUARE, 288, 6912)],
    [(SQUARE, 96, 0), (UP, 672, 576)],
    [(UP, 96, 0), (SQUARE, 1248, 1152)],
    [(SQUARE, 288, 0), (DEC_OUT, 192, 3456), (DEC_UP, 384, 4032), (DEC_DOWN, 768, 6336)],
]
DEC_QKV_PLACE = 1728
PATCH_COUNTS = (676, 676, 184)
E2D_PLACE = 1104
HEAD_PLACE = 3408
HEAD_TOP = 54
VEC_PLACE = 3960


def spread_rows(flat, place, blocks, count, read):
    def put(first, value):
        rows = value.shape[0]
        for j in range(blocks):
            flat[pl.ds(place + first * blocks + j, rows, stride=blocks), :] = value[:, j * LANES : (j + 1) * LANES]

    def body(t, carry):
        put(t * STEP_ROWS, read(pl.multiple_of(t * STEP_ROWS, 16), STEP_ROWS))
        return carry

    whole = count // STEP_ROWS
    if whole:
        lax.fori_loop(0, whole, body, 0)
    rest = count - whole * STEP_ROWS
    if rest:
        put(whole * STEP_ROWS, read(whole * STEP_ROWS, -(-rest // 16) * 16)[:rest])


def gather_rows(piece, flat, place, blocks, count):
    def put(first, rows, padded):
        for j in range(blocks):
            value = flat[pl.ds(place + first * blocks + j, rows, stride=blocks), :]
            if padded > rows:
                value = jnp.concatenate([value, jnp.zeros((padded - rows, LANES), FLOAT)], 0)
            piece[pl.ds(first, padded), j * LANES : (j + 1) * LANES] = value.astype(HALF)

    def body(t, carry):
        put(pl.multiple_of(t * STEP_ROWS, 16), STEP_ROWS, STEP_ROWS)
        return carry

    whole = count // STEP_ROWS
    if whole:
        lax.fori_loop(0, whole, body, 0)
    rest = count - whole * STEP_ROWS
    if rest:
        put(whole * STEP_ROWS, rest, -(-rest // 16) * 16)


def lay_out(z, x, ten, rep, pieces, wide_rows):
    for row in range(4):

        @pl.when(z == row)
        def _():
            for name, count, place in TEN_PLACES[row]:
                gather_rows(pieces[name], ten, place, PIECES[name][1] // LANES, count)
            if row < LAST:
                gather_rows(pieces[PATCH_ROWS], rep, 0, D // LANES, PATCH_COUNTS[row])
            if row < 2:
                pieces[PATCH_ROWS][pl.ds(688, 16)] = jnp.zeros((16, D), HALF)
            if row == 2:
                gather_rows(pieces[E2D], rep, E2D_PLACE, DD // LANES, D)
                gather_rows(pieces[HEAD], rep, HEAD_PLACE, PATCH // LANES, HEAD_TOP)
            if row == LAST:
                gather_rows(pieces[VECS], rep, VEC_PLACE, D // LANES, 16)
                for j in range(4):
                    wide_rows[j, pl.ds(0, 192, stride=2), :] = ten[pl.ds(DEC_QKV_PLACE + j, 192, stride=9), :]
                middle = ten[pl.ds(DEC_QKV_PLACE + 4, 192, stride=9), :]
                late = [middle[:, 64:]] + [ten[pl.ds(DEC_QKV_PLACE + 5 + j, 192, stride=9), :] for j in range(4)]
                late = jnp.concatenate(late + [jnp.zeros((192, 64), FLOAT)], 1)
                wide_rows[4, pl.ds(0, 192, stride=2), :] = middle
                for j in range(5):
                    columns = slice(j * LANES, (j + 1) * LANES)
                    wide_rows[j, pl.ds(1, 192, stride=2), :] = late[:, columns]
                for j in range(4):
                    columns = slice(j * LANES, (j + 1) * LANES)
                    pieces[DEC_QKV][:, columns] = wide_rows[j].astype(HALF)
                pieces[DEC_QKV][:, 512:576] = wide_rows[4][:, :64].astype(HALF)
                half = pieces[HEAD_HALF]
                blocks, offset = PATCH // LANES, x * 6
                half[pl.ds(0, 48)] = jnp.zeros((48, D), HALF)
                for j in range(6):
                    columns = slice(j * LANES, (j + 1) * LANES)
                    value = rep[pl.ds(offset + j, 42, stride=blocks), :]
                    half[pl.ds(48, 48), columns] = jnp.concatenate(
                        [jnp.zeros((6, LANES), FLOAT), value], 0
                    ).astype(HALF)
                    for t in range(1, 4):
                        value = rep[pl.ds((96 * t - HEAD_TOP) * blocks + offset + j, 96, stride=blocks), :]
                        half[pl.ds(96 * t, 96), columns] = value.astype(HALF)


def lay_out_kernel(ten, rep, *refs):
    pieces = dict(zip(LAID, refs))
    lay_out(lax.axis_index("dp"), lax.axis_index("tensor"), ten, rep, pieces, refs[len(LAID)])


def first_pieces(ten, rep):
    vmem = pl.BlockSpec(memory_space=pltpu.VMEM)
    out = pl.pallas_call(
        lay_out_kernel,
        name="lay_out",
        out_shape=[jax.ShapeDtypeStruct(LAID_SHAPES[name], HALF) for name in LAID],
        in_specs=[vmem] * 2,
        out_specs=[vmem] * len(LAID),
        scratch_shapes=[pltpu.VMEM((5, 384, LANES), FLOAT)],
        compiler_params=pltpu.CompilerParams(vmem_limit_bytes=61 << 20),
    )(ten, rep)
    return dict(zip(LAID, out))


def update_kernel(
    number, last,
    stats, qkv, square, up, patch, e2d, vec, wide, tall, dec_qkv, small,
    one_wide, one_tall, one_qkv, one_small, two_wide, two_tall, two_qkv, two_small,
    *refs,
):
    masters, refs = refs[:6], refs[6:]
    stats_out, outs, refs = refs[0], refs[1:7], refs[7:]
    pieces = {}
    if not last:
        pieces, refs = dict(zip(LAID, refs)), refs[len(LAID) :]
    held, refs = refs[:6], refs[6:]
    grad_ten, grad_rep, wide_rows, patch_other, e2d_other, head_own, head_other, slots, send_sem, recv_sem, local_sem = refs
    g, z, x = lax.axis_index("group"), lax.axis_index("dp"), lax.axis_index("tensor")
    me = 2 * z + x
    links = Links(send_sem, recv_sem)
    barrier = pltpu.get_barrier_semaphore()
    loads = [pltpu.make_async_copy(masters[i], held[i], local_sem.at[i]) for i in range(6)]
    for one in loads:
        one.start()

    def peer(shift):
        other = lax.rem(me + shift, 8)
        return (g, other // 2, lax.rem(other, 2))

    for shift in range(1, 8):
        pl.semaphore_signal(barrier, inc=1, device_id=peer(shift), device_id_type=MESH_ID)
    pl.semaphore_wait(barrier, 7)

    across = (g, z, 1 - x)
    patch_swap = links.copy(0, patch, patch_other, across)
    e2d_swap = links.copy(1, e2d, e2d_other, across)
    head_swap = links.copy(2, head_own, head_other, across)
    top_own = links.copy(3, head_own.at[pl.ds(0, 64)], head_own.at[pl.ds(0, 64)], (g, 2, x))
    top_other = links.copy(4, head_other.at[pl.ds(0, 64)], head_other.at[pl.ds(0, 64)], (g, 2, x))

    def plain(ref):
        return lambda first, rows: ref[pl.ds(first, rows)].astype(FLOAT)

    def joined(own, other):
        def read(first, rows):
            one, two = own[pl.ds(first, rows)].astype(FLOAT), other[pl.ds(first, rows)].astype(FLOAT)
            return jnp.concatenate([jnp.where(x == 0, one, two), jnp.where(x == 0, two, one)], 1)

        return read

    def total(own, one, two, top, columns):
        def read(first, rows):
            at = pl.ds(top + first, rows)
            return own[at, columns] + one[at, columns].astype(FLOAT) + two[at, columns].astype(FLOAT)

        return read

    @pl.when(z < LAST)
    def _():
        patch_swap.start()

    @pl.when(z == 2)
    def _():
        e2d_swap.start()

    fc = DFF // 2

    @pl.when(z == LAST)
    def _():
        head_own[...] = total(wide, one_wide, two_wide, 0, slice(fc, 2 * fc))(0, DD).astype(HALF)
        head_swap.start()
        top_own.start()
        whole = slice(0, DD)
        spread_rows(grad_ten, 0, 6, 288, plain(square))
        spread_rows(grad_ten, 3456, 3, 192, total(tall, one_tall, two_tall, fc, whole))
        spread_rows(grad_ten, 4032, 6, 384, total(wide, one_wide, two_wide, 0, slice(0, fc)))
        spread_rows(grad_ten, 6336, 3, 768, total(tall, one_tall, two_tall, 0, whole))
        for j in range(4):
            columns = slice(j * LANES, (j + 1) * LANES)
            wide_rows[j] = total(dec_qkv, one_qkv, two_qkv, 0, columns)(0, DD)
        tail = total(dec_qkv, one_qkv, two_qkv, 0, slice(512, 576))(0, DD)
        wide_rows[4] = jnp.concatenate([tail, jnp.zeros((DD, 64), FLOAT)], 1)
        for j in range(4):
            grad_ten[pl.ds(DEC_QKV_PLACE + j, 192, stride=9), :] = wide_rows[j, pl.ds(0, 192, stride=2), :]
        late = jnp.concatenate([wide_rows[j, pl.ds(1, 192, stride=2), :] for j in range(5)], 1)
        early = wide_rows[4, pl.ds(0, 192, stride=2), :]
        grad_ten[pl.ds(DEC_QKV_PLACE + 4, 192, stride=9), :] = jnp.concatenate([early[:, :64], late[:, :64]], 1)
        for j in range(4):
            start = 64 + j * LANES
            grad_ten[pl.ds(DEC_QKV_PLACE + 5 + j, 192, stride=9), :] = late[:, start : start + LANES]
        for j in range(6):
            columns = slice(j * LANES, (j + 1) * LANES)
            grad_rep[pl.ds(VEC_PLACE + j, 9, stride=6), :] = vec[0:9, columns]
        grad_rep[pl.ds(VEC_PLACE + 54, 42), :] = small[0:42] + one_small[0:42] + two_small[0:42]
        head_swap.wait_recv()
        top_other.start()
        read = joined(head_own, head_other)

        def put(first, value):
            rows = value.shape[0]
            for j in range(12):
                grad_rep[pl.ds(first * 12 + j, rows, stride=12), :] = value[:, j * LANES : (j + 1) * LANES]

        put(0, read(48, 48)[6:])
        for t in range(1, 4):
            put(96 * t - HEAD_TOP, read(96 * t, 96))

    for row in range(3):

        @pl.when(z == row)
        def _():
            refs_of = {QKV: qkv, SQUARE: square, UP: up}
            for name, count, place in TEN_PLACES[row]:
                spread_rows(grad_ten, place, PIECES[name][1] // LANES, count, plain(refs_of[name]))
            patch_swap.wait_recv()
            spread_rows(grad_rep, 0, 6, PATCH_COUNTS[row], joined(patch, patch_other))
            if row == 2:
                e2d_swap.wait_recv()
                for half in range(2):

                    def read(first, rows):
                        one, two = e2d[pl.ds(first, rows)].astype(FLOAT), e2d_other[pl.ds(first, rows)].astype(FLOAT)
                        return jnp.where(x == half, one, two)

                    spread_rows(grad_rep, E2D_PLACE + half * 1152, 3, 384, read)
                top_own.wait_recv()
                top_other.wait_recv()
                spread_rows(grad_rep, HEAD_PLACE, 12, HEAD_TOP, joined(head_own, head_other))

    def square_sum(flat, step):
        def body(t, carry):
            value = flat[pl.ds(pl.multiple_of(t * step, 8), step), :]
            return carry + jnp.sum((value * value).reshape(step // 8, 8, LANES), 0)

        return jnp.sum(lax.fori_loop(0, flat.shape[0] // step, body, jnp.zeros((8, LANES), FLOAT)))

    squares = square_sum(grad_ten, 360) + square_sum(grad_rep, 312) * 0.5
    line = lax.broadcasted_iota(jnp.int32, (8, LANES), 0)
    slots[me] = jnp.where(line == 0, squares, stats[...])
    shares = [links.copy(4 + shift, slots.at[me], slots.at[me], peer(shift)) for shift in range(1, 8)]
    for one in shares:
        one.start()
    for one in shares:
        one.wait()
    whole = slots[0]
    for i in range(1, 8):
        whole = whole + slots[i]
    square_all, loss_all, count_all = whole[0:1], whole[1:2], whole[2:3]
    norm = jnp.sqrt(square_all + 1e-30) / count_all
    factor = jnp.minimum(1.0, CLIP / norm) / count_all
    stats_out[...] = jnp.where(line == 0, norm, whole)
    for one in loads:
        one.wait()

    def adam(master, first, second, grad, step):
        def body(t, carry):
            at = pl.ds(pl.multiple_of(t * step, 8), step)
            new = adamw(master[at, :], first[at, :], second[at, :], grad[at, :] * factor, number)
            master[at, :], first[at, :], second[at, :] = new
            return carry

        lax.fori_loop(0, master.shape[0] // step, body, 0)

    stores = [pltpu.make_async_copy(held[i], outs[i], local_sem.at[i]) for i in range(6)]
    adam(*held[:3], grad_ten, 240)
    for one in stores[:3]:
        one.start()
    adam(*held[3:], grad_rep, 312)
    for one in stores[3:]:
        one.start()
    if not last:
        lay_out(z, x, held[0], held[3], pieces, wide_rows)

    @pl.when(z < LAST)
    def _():
        patch_swap.wait_send()

    @pl.when(z == 2)
    def _():
        e2d_swap.wait_send()

    @pl.when(z == LAST)
    def _():
        head_swap.wait_send()
        top_own.wait_send()
        top_other.wait_send()

    for one in stores:
        one.wait()


def update(identity, number, last, stats, gradients, states):
    vmem = pl.BlockSpec(memory_space=pltpu.VMEM)
    anywhere = pl.BlockSpec(memory_space=pl.ANY)
    laid = [] if last else LAID
    flat = [(TEN_LANES, LANES)] * 3 + [(REP_LANES, LANES)] * 3
    scratch = [(one, FLOAT) for one in flat + [(TEN_LANES, LANES), (REP_LANES, LANES), (5, 384, LANES)]] + [
        ((704, D // 2), HALF),
        ((D // 2, DD), HALF),
        ((DD, PATCH // 2), HALF),
        ((DD, PATCH // 2), HALF),
        ((8, 8, LANES), FLOAT),
    ]
    out = pl.pallas_call(
        functools.partial(update_kernel, number, last),
        name="update",
        out_shape=[jax.ShapeDtypeStruct((8, LANES), FLOAT)]
        + [jax.ShapeDtypeStruct(one, FLOAT) for one in flat]
        + [jax.ShapeDtypeStruct(LAID_SHAPES[name], HALF) for name in laid],
        in_specs=[vmem] * (1 + len(gradients)) + [anywhere] * 6,
        out_specs=[vmem] + [anywhere] * 6 + [vmem] * len(laid),
        scratch_shapes=[pltpu.VMEM(*one) for one in scratch]
        + [pltpu.SemaphoreType.DMA((12,)), pltpu.SemaphoreType.DMA((12,)), pltpu.SemaphoreType.DMA((6,))],
        compiler_params=pltpu.CompilerParams(
            collective_id=identity, has_side_effects=True, vmem_limit_bytes=61 << 20
        ),
    )(stats, *gradients, *states)
    return out[0], out[1:7], dict(zip(laid, out[7:]))


def decoder_kernel(
    q_ref, k_ref, v_ref, tokens, pixels, counted, out_own, out_oth, up_own, up_oth, down_own, down_oth, head_w, vec, head_b,
    grad_joined, grad_att, wide, tall, vec_grad, head_b_grad, loss,
    blended, blend_other, totals, upward, activated, second, final_low, pred_low, low, grad_up_in, mid, grad_blend,
    blend_sent, wide_sent, wide_got, tall_sent, tall_got, dk_ref, dv_ref, send_sem, recv_sem,
):
    g, z, x = lax.axis_index("group"), lax.axis_index("dp"), lax.axis_index("tensor")
    across = (g, z, 1 - x)
    links = Links(send_sem, recv_sem)
    barrier = pltpu.get_barrier_semaphore()
    pl.semaphore_signal(barrier, inc=1, device_id=across, device_id_type=MESH_ID)
    half = tokens.shape[0]
    width = q_ref.shape[1]
    heads = width // HDIM
    tiles = q_ref.shape[0] // TILE
    fc = DFF // 2

    def attend(first, last):
        for h in range(heads):
            cols = slice(h * HDIM, (h + 1) * HDIM)
            keys = k_ref[:, cols] * HALF(HDIM**-0.5)
            turned = v_ref[:, cols].T

            def step(t, carry):
                rows = pl.ds(pl.multiple_of(t * TILE, TILE), TILE)
                scores = mm_nt(keys, q_ref[rows, cols])
                highest = jnp.max(scores, 0, keepdims=True)
                weights = jnp.exp(scores - highest)
                total = jnp.sum(weights, 0, keepdims=True)
                probs = (weights * (1.0 / total)).astype(HALF)
                blended[rows, cols] = mm(turned, probs).T.astype(HALF)
                totals[h, pl.ds(t, 1), :] = highest + jnp.log(total)
                return carry

            lax.fori_loop(first, last, step, 0)

    whole = half // TILE
    attend(whole, tiles)
    pl.semaphore_wait(barrier, 1)
    blend_swap = links.copy(0, blended.at[pl.ds(half, half)], blend_other, across)
    blend_swap.start()
    attend(0, whole)
    vec_grad[...] = jnp.zeros_like(vec_grad)
    head_b_grad[...] = jnp.zeros_like(head_b_grad)
    loss[...] = jnp.zeros_like(loss)
    blend_swap.wait_recv()

    def count(row, value):
        vec_grad[row : row + 1] += value

    grad_swaps = []
    start = 0
    for step, size in enumerate((400, 384)):
        rows = pl.ds(start, size)
        start += size
        attended = mm(blended[rows], out_own[...]) + mm(blend_other[rows], out_oth[...]) + tokens[rows] + vec[4:5]
        second[rows] = norm_to(attended, vec[5:6], vec[6:7]).astype(HALF)
        decoded = attended + vec[7:8]
        for side, (into, back) in enumerate(((up_own, down_own), (up_oth, down_oth))):
            cols = slice(side * fc, (side + 1) * fc)
            up = mm(second[rows], into[...])
            upward[rows, cols] = up
            activated[rows, cols] = gelu_to(up).astype(HALF)
            decoded = decoded + mm(activated[rows, cols], back[...])
        final_low[rows] = norm_to(decoded, vec[8:9], vec[9:10]).astype(HALF)
        differ = mm(final_low[rows], head_w[...]) + head_b[...]
        differ = differ - norm_parts(pixels[rows].astype(FLOAT))[0]
        share = counted[rows]
        loss[...] += jnp.sum(jnp.mean(differ * differ, -1, keepdims=True) * share)
        grad = (2.0 / PATCH) * differ * share
        head_b_grad[...] += jnp.sum(grad, 0, keepdims=True)
        pred_low[rows] = grad.astype(HALF)
        grad_out, gain, bias = norm_from(decoded, vec[8:9], mm_nt(pred_low[rows], head_w[...]))
        count(8, gain)
        count(9, bias)
        count(7, jnp.sum(grad_out, 0, keepdims=True))
        low[rows] = grad_out.astype(HALF)
        grad_second = jnp.zeros((size, DD), FLOAT)
        for side, (into, back) in enumerate(((up_own, down_own), (up_oth, down_oth))):
            cols = slice(side * fc, (side + 1) * fc)
            slope = gelu_slope(upward[rows, cols])
            grad_up_in[rows, cols] = (mm_nt(low[rows], back[...]) * slope).astype(HALF)
            grad_second = grad_second + mm_nt(grad_up_in[rows, cols], into[...])
        grad, gain, bias = norm_from(attended, vec[5:6], grad_second)
        count(5, gain)
        count(6, bias)
        grad = grad + grad_out
        count(4, jnp.sum(grad, 0, keepdims=True))
        grad_att[rows] = grad
        mid[rows] = grad.astype(HALF)
        grad_blend[rows] = mm_nt(mid[rows], out_own[...]).astype(HALF)
        blend_sent[rows] = mm_nt(mid[rows], out_oth[...]).astype(HALF)
        swap_rows = pl.ds(half + start - size, size)
        grad_swaps.append(links.copy(1 + step, blend_sent.at[rows], grad_blend.at[swap_rows], across))
        grad_swaps[-1].start()
    mine = pl.ds(pl.multiple_of(x * fc, LANES), fc)
    theirs = pl.ds(pl.multiple_of((1 - x) * fc, LANES), fc)
    wide_sent[:, :fc] = mm_tn(second[...], grad_up_in[:, fc:]).astype(HALF)
    wide_sent[:, fc:] = mm_tn(final_low[...], pred_low[:, theirs]).astype(HALF)
    wide_swap = links.copy(3, wide_sent, wide_got, across)
    wide_swap.start()
    tall_sent[:fc] = mm_tn(activated[:, fc:], low[...]).astype(HALF)
    tall_sent[fc:] = mm_tn(blend_other[...], mid[...]).astype(HALF)
    tall_swap = links.copy(4, tall_sent, tall_got, across)
    tall_swap.start()
    wide[:, :fc] = mm_tn(second[...], grad_up_in[:, :fc])
    wide[:, fc:] = mm_tn(final_low[...], pred_low[:, mine])
    tall[:fc] = mm_tn(activated[:, :fc], low[...])
    tall[fc:] = mm_tn(blended[pl.ds(0, half)], mid[...])
    for one in grad_swaps:
        one.wait_recv()
    for h in range(heads):
        cols = slice(h * HDIM, (h + 1) * HDIM)
        keys = k_ref[:, cols] * HALF(HDIM**-0.5)
        values = v_ref[:, cols]
        turned = keys.T
        dk_ref[...] = jnp.zeros_like(dk_ref)
        dv_ref[...] = jnp.zeros_like(dv_ref)

        def back_step(t, carry):
            rows = pl.ds(pl.multiple_of(t * TILE, TILE), TILE)
            queries, grads = q_ref[rows, cols], grad_blend[rows, cols]
            probs = jnp.exp(mm_nt(keys, queries) - totals[h, pl.ds(t, 1), :])
            dv_ref[...] += mm(probs.astype(HALF), grads)
            grad_probs = mm_nt(values, grads)
            grad_scores = (probs * (grad_probs - jnp.sum(probs * grad_probs, 0, keepdims=True))).astype(HALF)
            dk_ref[...] += mm(grad_scores, queries)
            grad_joined[rows, cols] = mm(turned, grad_scores).T.astype(HALF)
            return carry

        lax.fori_loop(0, tiles, back_step, 0)
        grad_joined[:, width + h * HDIM : width + (h + 1) * HDIM] = (dk_ref[...] * HDIM**-0.5).astype(HALF)
        grad_joined[:, 2 * width + h * HDIM : 2 * width + (h + 1) * HDIM] = dv_ref[...].astype(HALF)
    wide_swap.wait_recv()
    wide[...] += wide_got[...].astype(FLOAT)
    tall_swap.wait_recv()
    tall[...] += tall_got[...].astype(FLOAT)
    for one in [blend_swap, wide_swap, tall_swap] + grad_swaps:
        one.wait_send()


def decoder_round(number, tokens, pixels_low, counted, weights):
    own, other, head_w, vec, head_b = weights
    count, rows, width = pixels_low.shape[0], tokens.shape[0], DD // 2
    normed = layer_norm(tokens, vec[2], vec[3]).astype(HALF)
    joined = mm(normed, own[0]).astype(HALF)
    queries, keys, values = [joined[:, i * width : (i + 1) * width] for i in range(3)]
    vmem = pl.BlockSpec(memory_space=pltpu.VMEM)
    shapes = [
        ((rows, 3 * width), HALF),
        ((count, DD), FLOAT),
        ((DD, DFF // 2 + PATCH // 2), FLOAT),
        ((DFF // 2 + width, DD), FLOAT),
        ((16, DD), FLOAT),
        ((1, PATCH), FLOAT),
        ((8, LANES), FLOAT),
    ]
    scratch = [
        ((rows, width), HALF),
        ((count, width), HALF),
        ((width // HDIM, rows // TILE, TILE), FLOAT),
        ((count, DFF), FLOAT),
        ((count, DFF), HALF),
        ((count, DD), HALF),
        ((count, DD), HALF),
        ((count, PATCH), HALF),
        ((count, DD), HALF),
        ((count, DFF), HALF),
        ((count, DD), HALF),
        ((rows, width), HALF),
        ((count, width), HALF),
        ((DD, DFF // 2 + PATCH // 2), HALF),
        ((DD, DFF // 2 + PATCH // 2), HALF),
        ((DFF // 2 + width, DD), HALF),
        ((DFF // 2 + width, DD), HALF),
        ((rows, HDIM), FLOAT),
        ((rows, HDIM), FLOAT),
    ]
    grad_joined, grad_att, wide, tall, vec_grad, head_b_grad, loss = pl.pallas_call(
        decoder_kernel,
        name="decoder",
        out_shape=[jax.ShapeDtypeStruct(*one) for one in shapes],
        in_specs=[vmem] * 15,
        out_specs=[vmem] * len(shapes),
        scratch_shapes=[pltpu.VMEM(*one) for one in scratch]
        + [pltpu.SemaphoreType.DMA((5,)), pltpu.SemaphoreType.DMA((5,))],
        compiler_params=pltpu.CompilerParams(
            collective_id=number, has_side_effects=True, vmem_limit_bytes=60 << 20
        ),
    )(
        queries,
        keys,
        values,
        tokens[:count],
        pixels_low,
        counted[:, None],
        own[1],
        other[1],
        own[2],
        other[2],
        own[3],
        other[3],
        head_w,
        jnp.pad(vec, ((0, 6), (0, 0))),
        head_b[None],
    )
    joined_other = swap(grad_joined[count:])
    qkv_grad = mm_tn(normed, grad_joined)
    grad_normed = mm_nt(grad_joined[:count], own[0]) + mm_nt(joined_other, other[0])
    grad_in, gain_one, bias_one = norm_back(tokens[:count], vec[2], vec[3], grad_normed)
    grad_in = grad_in + grad_att
    vec_rows = [gain_one, bias_one] + [vec_grad[i] for i in range(4, 10)]
    return loss[0, 0], grad_in, (wide, tall, qkv_grad), vec_rows, head_b_grad[0]


def hosted_round(
    patches,
    visible,
    frames_valid,
    clip_valid,
    rep_weights,
    ten_weights,
    rep_m,
    rep_v,
    ten_m,
    ten_v,
    rep_outer,
    ten_outer,
):
    side = lax.axis_index("tensor")
    z = lax.axis_index("dp")
    half_rows = TUBES // 2
    tube_ids = (jnp.arange(TUBES) + side * half_rows) % TUBES
    ids_one = hop(visible[:, 0, 0], ((0, 0), (HOST, 0)), ((2, 1), (HOST, 1)))
    ids_two = hop(visible[:, 0, 0], ((3, 1), (HOST, 1)))
    ids_two = jnp.where(side == 0, visible[:, 0, 0], ids_two)
    dec_table = sinus_all(DD)
    places = []
    for part in sinus_parts(D):
        part = jnp.pad(part, ((0, -part.shape[0] % 64), (0, 0)))
        places.append(jnp.stack(thirds_of(part)))
    dec_places = jnp.where(side == 0, dec_table, jnp.roll(dec_table, -half_rows, 0))
    states = [one.reshape(TEN_LANES, LANES) for one in (ten_weights, ten_m, ten_v)]
    states = states + [one.reshape(REP_LANES, LANES) for one in (rep_weights, rep_m, rep_v)]
    starts = states[0], states[3]
    pieces = first_pieces(*starts)
    rep_quarter = rep_weights.shape[0]
    shown_steps = []
    for s in range(STEPS):
        picks = (visible[s, 0, 0][:, None] == jnp.arange(TUBES)[None, :]).astype(HALF)
        rows = mm(picks, patches[s, 0, 0]).astype(HALF)
        cuts = (0, rep_quarter // D, 2 * (rep_quarter // D), PATCH)
        rows = jnp.concatenate(
            [
                jnp.pad(rows[:, cuts[i] : cuts[i + 1]], ((0, 0), (0, room - cuts[i + 1] + cuts[i])))
                for i, room in enumerate((768, 768, 256))
            ],
            1,
        )
        one = hop(rows, ((0, 0), (HOST, 0)), ((2, 1), (HOST, 1)))
        two = hop(rows, ((3, 1), (HOST, 1)))
        own = jnp.concatenate([one, jnp.where(side == 0, rows, two)], 0)
        shown_steps.append((own, swap(own, HOST)))
    loss_list, count_list, norm_list = [], [], []
    for s in range(STEPS):
        ids = visible[s, 0, 0]
        picks = tube_ids[:, None] == ids[None, :]
        shown_here = jnp.any(picks, 1)
        counted = (
            jnp.where(shown_here, 0.0, 1.0)
            * (tube_ids // (TUBES // FRAMES) < frames_valid[s, 0, 0])
            * (clip_valid[s, 0, 0] == 1)
        ).astype(FLOAT)[:half_rows]
        shown = shown_steps[s]
        vis = ids.shape[0]
        ids_own = jnp.concatenate([ids_one[s], ids_two[s]])
        reduced_clip, enc_stored, enc_weights, dec_weights = encoder_forward(
            3 + s, s == 0, pieces, shown[0], (ids_own[:, None], *places)
        )
        normed, activated = enc_stored[1], enc_stored[7]
        far = (
            hop_both(normed, (HOST, 0)),
            hop_both(activated, (HOST, 2)),
            hop_both(activated[:, 1152:], (HOST, LAST)),
        )
        dec_vec = dec_weights[3]
        thirds = thirds_of(reduced_clip + dec_vec[0])
        hot = picks.astype(HALF)
        placed = mm(jnp.concatenate([hot, hot, hot], 1), jnp.concatenate(thirds, 0))
        tokens = jnp.where(shown_here[:, None], placed, dec_vec[1]) + dec_places
        pixels_low = lax.dynamic_slice_in_dim(patches[s, 0, 0], side * half_rows, half_rows, 0)
        loss, grad_tokens, (wide, tall, qkv_grad), vec_rows, head_b_grad = decoder_round(
            9 + s, tokens, pixels_low, counted, dec_weights
        )
        shown_own = shown_here[:half_rows, None]
        e2d_b_grad = jnp.sum(jnp.where(shown_own, grad_tokens, 0.0), 0)
        mask_grad = jnp.sum(jnp.where(shown_own, 0.0, grad_tokens), 0)
        picked = mm_tn(picks[:half_rows].astype(HALF), grad_tokens.astype(HALF)).astype(HALF)
        small = jnp.concatenate(
            [jnp.stack([e2d_b_grad, mask_grad] + vec_rows).reshape(-1), head_b_grad]
        )
        small = small + swap(small)
        small = jnp.pad(small.reshape(-1, LANES), ((0, 6), (0, 0)))
        back = encoder_backward(5 + s, picked, shown, enc_weights, enc_stored, (wide, tall, qkv_grad, small), far)
        line = jnp.arange(8)[:, None]
        stats = jnp.where(line == 1, loss, jnp.where(line == 2, jnp.sum(counted), 0.0))
        stats = jnp.broadcast_to(stats, (8, LANES))
        stats, states, pieces = update(
            7 + s, STEP_BEFORE + s + 1, s == STEPS - 1, stats, (*back[:6], wide, tall, qkv_grad, small, *back[6:]), states
        )
        norm_list.append(stats[0, 0])
        loss_list.append(stats[1, 0])
        count_list.append(stats[2, 0])
    ten_first, ten_second, rep_first, rep_second = [one.reshape(-1) for one in (*states[1:3], *states[4:])]
    ten_diff, rep_diff = [group_mean(starts[i] - states[3 * i]).reshape(-1) for i in range(2)]
    rep_momentum = MOMENTUM * rep_outer + rep_diff
    ten_momentum = MOMENTUM * ten_outer[0] + ten_diff
    rep_new = rep_weights - LR_OUT * (rep_diff + MOMENTUM * rep_momentum)
    ten_new = ten_weights[0] - LR_OUT * (ten_diff + MOMENTUM * ten_momentum)
    return (
        jnp.stack(loss_list)[:, None],
        jnp.stack(count_list)[:, None],
        jnp.stack(norm_list)[:, None],
        rep_first[None],
        rep_second[None],
        ten_first[None, None],
        ten_second[None, None],
        rep_diff,
        ten_diff[None],
        rep_momentum,
        ten_momentum[None],
        rep_new,
        ten_new[None],
    )


def group_mean(diff):
    if lax.axis_size("group") != 4:
        return lax.psum(diff, "group") / lax.axis_size("group")
    odd = lax.axis_index("group") % 2 == 1
    half = diff.shape[0] // 2
    low, high = diff[:half], diff[half:]
    part = jnp.where(odd, high, low) + partner(jnp.where(odd, low, high))
    part_low = lax.optimization_barrier(part.astype(HALF))
    far = lax.ppermute(part_low, "group", [(g, g ^ 2) for g in range(4)])
    total = (part_low.astype(FLOAT) + far.astype(FLOAT)) * 0.25
    other = partner(total)
    return jnp.concatenate([jnp.where(odd, other, total), jnp.where(odd, total, other)])


def solution(mesh):
    placed = (
        P(None, "group", "dp", None, None),
        P(None, "group", "dp", None),
        P(None, "group", "dp"),
        P(None, "group", "dp"),
        P("dp"),
        P("tensor", "dp"),
        P("group", "dp"),
        P("group", "dp"),
        P("group", "tensor", "dp"),
        P("group", "tensor", "dp"),
        P("dp"),
        P("tensor", "dp"),
    )
    return jax.shard_map(
        hosted_round if mesh.shape["dp"] == 4 and mesh.shape["tensor"] == 2 and mesh.shape["group"] % 2 == 0 else on_device,
        mesh=mesh,
        in_specs=placed,
        out_specs=(
            P(None, "group"),
            P(None, "group"),
            P(None, "group"),
            P("group", "dp"),
            P("group", "dp"),
            P("group", "tensor", "dp"),
            P("group", "tensor", "dp"),
            P("dp"),
            P("tensor", "dp"),
            P("dp"),
            P("tensor", "dp"),
            P("dp"),
            P("tensor", "dp"),
        ),
        check_vma=False,
    )
```

```python
import functools
import math

import jax
import jax.numpy as jnp
from jax import lax
from jax.experimental import pallas as pl
from jax.experimental.pallas import tpu as pltpu
from jax.sharding import PartitionSpec as P

D = 768
HDIM = 64
FF = 3072
DD = 384
DFF = 1536
PATCH = 1536
TUBES = 1568
FRAMES = 8
STEPS = 2
STEP_BEFORE = 6


CLIP = 0.001
LR_IN = 0.01
BETA1 = 0.9
BETA2 = 0.95
EPS = 1e-08
DECAY = 0.05
LR_OUT = 0.7
MOMENTUM = 0.9
FLOAT = jnp.float32
HALF = jnp.bfloat16


def sinus(count, width):
    places = jnp.arange(count).astype(jnp.float32)[:, None]
    column = jnp.arange(width)
    decays = jnp.power(10000.0, -2.0 * (column // 2).astype(jnp.float32) / width)
    angles = places * decays[None, :]
    return jnp.where(column % 2 == 0, jnp.sin(angles), jnp.cos(angles))


def layer_norm(stream, gain, bias):
    center = jnp.mean(stream, -1, keepdims=True)
    spread = jnp.mean((stream - center) ** 2, -1, keepdims=True)
    return (stream - center) * lax.rsqrt(spread + 1e-06) * gain + bias


def norm_back(stream, gain, bias, cotangent):
    _, pull = jax.vjp(layer_norm, stream, gain, bias)
    return pull(cotangent)


def gelu_exact(values):
    return jax.nn.gelu(values, approximate=False)


def split_flat(flat, shapes):
    pieces = []
    offset = 0
    for shapes_one in shapes:
        length = math.prod(shapes_one)
        pieces.append(flat[offset : offset + length].reshape(shapes_one))
        offset += length
    return pieces


def own_rows(stream, axis_dim):
    count = stream.shape[axis_dim] // lax.axis_size("tensor")
    return lax.dynamic_slice_in_dim(stream, lax.axis_index("tensor") * count, count, axis_dim)


def rows_sum(partial_rows):
    return lax.psum_scatter(partial_rows, "tensor", scatter_dimension=1, tiled=True)


def rows_full(own_part):
    return lax.all_gather(own_part, "tensor", axis=1, tiled=True)


def block_forward(stream, mats, vecs):
    w_qkv, w_out, w_up, w_down = mats
    gain_one, bias_one, out_bias, gain_two, bias_two, down_bias = vecs
    nclips, length, _ = stream.shape
    head_cols = w_out.shape[0]
    nheads = head_cols // HDIM
    normed = layer_norm(stream, gain_one, bias_one).astype(HALF)
    joined = jnp.dot(normed, w_qkv, preferred_element_type=FLOAT).astype(HALF)
    queries, key_rows, values = [
        joined[:, :, third_id * head_cols : (third_id + 1) * head_cols].reshape(
            nclips, length, nheads, HDIM
        )
        for third_id in range(3)
    ]
    scores = jnp.einsum(
        "cqhd,ckhd->chqk", queries, key_rows, preferred_element_type=FLOAT
    ) * HDIM ** (-0.5)
    highest = jnp.max(scores, -1, keepdims=True)
    totals = jnp.log(jnp.sum(jnp.exp(scores - highest), -1, keepdims=True)) + highest
    probs_low = jnp.exp(scores - totals).astype(HALF)
    blended = (
        jnp.einsum("chqk,ckhd->cqhd", probs_low, values, preferred_element_type=FLOAT)
        .astype(HALF)
        .reshape(nclips, length, head_cols)
    )
    attended = (
        rows_sum(jnp.dot(blended, w_out, preferred_element_type=FLOAT))
        + own_rows(stream, 1)
        + out_bias
    )
    second = layer_norm(attended, gain_two, bias_two).astype(HALF)
    second_all = lax.all_gather(second, "tensor", axis=1, tiled=True)
    upward = jnp.dot(second_all, w_up, preferred_element_type=FLOAT)
    activated = gelu_exact(upward).astype(HALF)
    result = (
        rows_sum(jnp.dot(activated, w_down, preferred_element_type=FLOAT)) + attended + down_bias
    )
    stored = (
        stream,
        normed,
        queries,
        key_rows,
        values,
        totals,
        blended,
        attended,
        second_all,
        upward,
        activated,
    )
    return (rows_full(result), stored)


def block_backward(grad_out, mats, vecs, stored):
    w_qkv, w_out, w_up, w_down = mats
    gain_one, bias_one, out_bias, gain_two, bias_two, down_bias = vecs
    (
        stream,
        normed,
        queries,
        key_rows,
        values,
        totals,
        blended,
        attended,
        second_all,
        upward,
        activated,
    ) = stored
    nclips, length, _ = stream.shape
    head_cols = w_out.shape[0]
    grad_low = grad_out.astype(HALF)
    grad_down = jnp.einsum("ctf,ctd->fd", activated, grad_low, preferred_element_type=FLOAT)
    down_bias_grad = jnp.sum(own_rows(grad_out, 1), (0, 1))
    grad_act = jnp.dot(grad_low, w_down.T, preferred_element_type=FLOAT)
    _, gelu_pull = jax.vjp(gelu_exact, upward)
    grad_up_in = gelu_pull(grad_act)[0].astype(HALF)
    grad_up = jnp.einsum("ctd,ctf->df", second_all, grad_up_in, preferred_element_type=FLOAT)
    grad_second = rows_sum(jnp.dot(grad_up_in, w_up.T, preferred_element_type=FLOAT))
    grad_att, gain_two_grad, bias_two_grad = norm_back(attended, gain_two, bias_two, grad_second)
    grad_att = grad_att + own_rows(grad_out, 1)
    out_bias_grad = jnp.sum(grad_att, (0, 1))
    grad_mid = rows_full(grad_att)
    mid_low = grad_mid.astype(HALF)
    grad_wout = jnp.einsum("cth,ctd->hd", blended, mid_low, preferred_element_type=FLOAT)
    nheads = head_cols // HDIM
    grad_blend = (
        jnp.dot(mid_low, w_out.T, preferred_element_type=FLOAT)
        .astype(HALF)
        .reshape(nclips, length, nheads, HDIM)
    )
    scores = jnp.einsum(
        "cqhd,ckhd->chqk", queries, key_rows, preferred_element_type=FLOAT
    ) * HDIM ** (-0.5)
    probs_full = jnp.exp(scores - totals)
    probs_low = probs_full.astype(HALF)
    grad_values = jnp.einsum("chqk,cqhd->ckhd", probs_low, grad_blend, preferred_element_type=FLOAT)
    grad_probs = jnp.einsum("cqhd,ckhd->chqk", grad_blend, values, preferred_element_type=FLOAT)
    grad_scores = (
        probs_full * (grad_probs - jnp.sum(probs_full * grad_probs, -1, keepdims=True))
    ).astype(HALF)
    grad_queries = jnp.einsum(
        "chqk,ckhd->cqhd", grad_scores, key_rows, preferred_element_type=FLOAT
    ) * HDIM ** (-0.5)
    grad_keys = jnp.einsum(
        "chqk,cqhd->ckhd", grad_scores, queries, preferred_element_type=FLOAT
    ) * HDIM ** (-0.5)
    grad_joined = jnp.concatenate(
        [
            part_grad.reshape(nclips, length, head_cols)
            for part_grad in (grad_queries, grad_keys, grad_values)
        ],
        -1,
    ).astype(HALF)
    grad_qkv = jnp.einsum("ctd,cte->de", normed, grad_joined, preferred_element_type=FLOAT)
    grad_norm_in = rows_sum(jnp.dot(grad_joined, w_qkv.T, preferred_element_type=FLOAT))
    grad_in, gain_one_grad, bias_one_grad = norm_back(
        own_rows(stream, 1), gain_one, bias_one, grad_norm_in
    )
    grad_in = grad_in + grad_att
    vec_grads = jnp.stack(
        [gain_one_grad, bias_one_grad, out_bias_grad, gain_two_grad, bias_two_grad, down_bias_grad]
    )
    return (rows_full(grad_in), (grad_qkv, grad_wout, grad_up, grad_down), vec_grads)


def group_step(patch_rows, visible_ids, shown, weight_rows, rep_full, ten_full):
    splits = lax.axis_size("tensor")
    patch_w, e2d_w, head_w, enc_vec, dec_vec, head_b = split_flat(
        rep_full, [(PATCH, D), (D, DD), (DD, PATCH), (9, D), (10, DD), (PATCH,)]
    )
    enc_vec = enc_vec.astype(FLOAT)
    dec_vec = dec_vec.astype(FLOAT)
    head_b = head_b.astype(FLOAT)
    enc_cols = D // splits
    dec_cols = DD // splits
    ten_pieces = split_flat(
        ten_full,
        [
            (D, 3 * enc_cols),
            (enc_cols, D),
            (D, FF // splits),
            (FF // splits, D),
            (DD, 3 * dec_cols),
            (dec_cols, DD),
            (DD, DFF // splits),
            (DFF // splits, DD),
        ],
    )
    enc_mats = ten_pieces[0:4]
    dec_mats = ten_pieces[4:8]
    enc_vecs = [enc_vec[i] for i in range(1, 7)]
    dec_vecs = [dec_vec[i] for i in range(2, 8)]
    shown_rows = jnp.take_along_axis(patch_rows, visible_ids[:, :, None], 1)
    embedded = (
        jnp.dot(shown_rows, patch_w, preferred_element_type=FLOAT)
        + enc_vec[0]
        + sinus(TUBES, D)[visible_ids]
    )
    encoded, enc_stored = block_forward(embedded, enc_mats, enc_vecs)
    final_enc = layer_norm(encoded, enc_vec[7], enc_vec[8]).astype(HALF)
    reduced = jnp.dot(final_enc, e2d_w, preferred_element_type=FLOAT) + dec_vec[0]
    blank = jnp.broadcast_to(dec_vec[1], (TUBES, DD))
    tokens_in = jax.vmap(lambda clip_ids, clip_rows: blank.at[clip_ids].set(clip_rows))(
        visible_ids, reduced
    ) + sinus(TUBES, DD)
    decoded, dec_stored = block_forward(tokens_in, dec_mats, dec_vecs)
    own_dec = own_rows(decoded, 1)
    final_low = layer_norm(own_dec, dec_vec[8], dec_vec[9]).astype(HALF)
    predicted = jnp.dot(final_low, head_w, preferred_element_type=FLOAT) + head_b
    pixels = own_rows(patch_rows, 1).astype(FLOAT)
    center = jnp.mean(pixels, -1, keepdims=True)
    spread = jnp.mean((pixels - center) ** 2, -1, keepdims=True)
    target = (pixels - center) * lax.rsqrt(spread + 1e-06)
    differ = predicted - target
    counted = own_rows(weight_rows, 1)
    loss_part = jnp.sum(jnp.mean(differ**2, -1) * counted)
    grad_pred = 2.0 / PATCH * differ * counted[:, :, None]
    pred_low = grad_pred.astype(HALF)
    head_w_grad = jnp.einsum("ctd,ctp->dp", final_low, pred_low, preferred_element_type=FLOAT)
    head_b_grad = jnp.sum(grad_pred, (0, 1))
    grad_final = jnp.dot(pred_low, head_w.T, preferred_element_type=FLOAT)
    grad_dec_own, dec_gain_grad, dec_bias_grad = norm_back(
        own_dec, dec_vec[8], dec_vec[9], grad_final
    )
    grad_tokens, dec_mat_grads, dec_vec_grads = block_backward(
        rows_full(grad_dec_own), dec_mats, dec_vecs, dec_stored
    )
    masked_own = own_rows(1.0 - shown.astype(FLOAT), 1)
    mask_grad = jnp.sum(own_rows(grad_tokens, 1) * masked_own[:, :, None], (0, 1))
    grad_reduced = own_rows(jnp.take_along_axis(grad_tokens, visible_ids[:, :, None], 1), 1)
    reduced_low = grad_reduced.astype(HALF)
    e2d_grad = jnp.einsum(
        "ctd,cte->de", own_rows(final_enc, 1), reduced_low, preferred_element_type=FLOAT
    )
    e2d_b_grad = jnp.sum(grad_reduced, (0, 1))
    grad_enc_final = jnp.dot(reduced_low, e2d_w.T, preferred_element_type=FLOAT)
    grad_enc_own, enc_gain_grad, enc_bias_grad = norm_back(
        own_rows(encoded, 1), enc_vec[7], enc_vec[8], grad_enc_final
    )
    grad_embedded, enc_mat_grads, enc_vec_grads = block_backward(
        rows_full(grad_enc_own), enc_mats, enc_vecs, enc_stored
    )
    own_embedded = own_rows(grad_embedded, 1)
    patch_grad = jnp.einsum(
        "ctp,ctd->pd",
        own_rows(shown_rows, 1),
        own_embedded.astype(HALF),
        preferred_element_type=FLOAT,
    )
    patch_b_grad = jnp.sum(own_embedded, (0, 1))
    enc_vec_grad = jnp.concatenate(
        [patch_b_grad[None], enc_vec_grads, enc_gain_grad[None], enc_bias_grad[None]], 0
    )
    dec_vec_grad = jnp.concatenate(
        [
            e2d_b_grad[None],
            mask_grad[None],
            dec_vec_grads,
            dec_gain_grad[None],
            dec_bias_grad[None],
        ],
        0,
    )
    rep_grad = jnp.concatenate(
        [
            patch_grad.reshape(-1),
            e2d_grad.reshape(-1),
            head_w_grad.reshape(-1),
            enc_vec_grad.reshape(-1),
            dec_vec_grad.reshape(-1),
            head_b_grad,
        ]
    )
    ten_grad = jnp.concatenate(
        [mat_grad.reshape(-1) for mat_grad in list(enc_mat_grads) + list(dec_mat_grads)]
    )
    return (loss_part, rep_grad, ten_grad)


def adamw(master, first, second, clipped, number):
    first = BETA1 * first + (1 - BETA1) * clipped
    second = BETA2 * second + (1 - BETA2) * clipped * clipped
    first_hat = first / (1 - BETA1**number)
    second_hat = second / (1 - BETA2**number)
    master = master - LR_IN * (first_hat / (jnp.sqrt(second_hat) + EPS) + DECAY * master)
    return (master, first, second)


def on_device(
    patches,
    visible,
    frames_valid,
    clip_valid,
    rep_weights,
    ten_weights,
    rep_m,
    rep_v,
    ten_m,
    ten_v,
    rep_outer,
    ten_outer,
):
    splits = lax.axis_size("tensor")
    owners = lax.axis_size("dp")
    tube_ids = jnp.arange(TUBES)
    rep_master, ten_master = (rep_weights, ten_weights[0])
    rep_first, rep_second = (rep_m[0], rep_v[0])
    ten_first, ten_second = (ten_m[0, 0], ten_v[0, 0])
    loss_list, count_list, norm_list = ([], [], [])
    for inner_step in range(STEPS):
        rep_full, ten_full = (
            lax.all_gather(rep_master.astype(HALF), "dp", axis=0, tiled=True),
            lax.all_gather(ten_master.astype(HALF), "dp", axis=0, tiled=True),
        )
        visible_ids = visible[inner_step, 0]
        shown = jnp.any(visible_ids[:, :, None] == tube_ids[None, None, :], axis=1)
        weight_rows = (
            jnp.where(shown, 0.0, 1.0)
            * (tube_ids[None, :] // (TUBES // FRAMES) < frames_valid[inner_step, 0][:, None])
            * (clip_valid[inner_step, 0][:, None] == 1)
        ).astype(FLOAT)
        count_part = jnp.sum(own_rows(weight_rows, 1))
        loss_part, rep_grad, ten_grad = group_step(
            patches[inner_step, 0], visible_ids, shown, weight_rows, rep_full, ten_full
        )
        rep_recv, ten_recv = (
            lax.all_to_all(
                rep_grad.reshape(owners, -1), "dp", split_axis=0, concat_axis=0, tiled=True
            ),
            lax.all_to_all(
                ten_grad.reshape(owners, -1), "dp", split_axis=0, concat_axis=0, tiled=True
            ),
        )
        rep_part = lax.psum(jnp.sum(rep_recv, 0), "tensor")
        ten_part = jnp.sum(ten_recv, 0)
        squares = jnp.sum(ten_part * ten_part) + jnp.sum(rep_part * rep_part) / splits
        square_all, loss_all, count_all = lax.psum(
            (squares, loss_part, count_part), ("dp", "tensor")
        )
        norm_value = jnp.sqrt(square_all + 1e-30) / count_all
        factor = jnp.minimum(1.0, CLIP / norm_value) / count_all
        number = STEP_BEFORE + inner_step + 1
        rep_master, rep_first, rep_second = adamw(
            rep_master, rep_first, rep_second, rep_part * factor, number
        )
        ten_master, ten_first, ten_second = adamw(
            ten_master, ten_first, ten_second, ten_part * factor, number
        )
        loss_list.append(loss_all)
        count_list.append(count_all)
        norm_list.append(norm_value)
    rep_sum, ten_sum = lax.psum((rep_weights - rep_master, ten_weights[0] - ten_master), "group")
    groups_count = lax.axis_size("group")
    rep_diff = rep_sum / groups_count
    ten_diff = ten_sum / groups_count
    rep_momentum = MOMENTUM * rep_outer + rep_diff
    ten_momentum = MOMENTUM * ten_outer[0] + ten_diff
    rep_new = rep_weights - LR_OUT * (rep_diff + MOMENTUM * rep_momentum)
    ten_new = ten_weights[0] - LR_OUT * (ten_diff + MOMENTUM * ten_momentum)
    return (
        jnp.stack(loss_list)[:, None],
        jnp.stack(count_list)[:, None],
        jnp.stack(norm_list)[:, None],
        rep_first[None],
        rep_second[None],
        ten_first[None, None],
        ten_second[None, None],
        rep_diff,
        ten_diff[None],
        rep_momentum,
        ten_momentum[None],
        rep_new,
        ten_new[None],
    )


TILE = 224


HOST = 1
LAST = 3
SWAP = [(0, 1), (1, 0)]
ENC_SHAPES = [(D, 3 * D // 2), (D // 2, D), (D, FF // 2), (FF // 2, D)]
DEC_SHAPES = [(DD, 3 * DD // 2), (DD // 2, DD), (DD, DFF // 2), (DFF // 2, DD)]
ENC_SIZE = sum(math.prod(one) for one in ENC_SHAPES)
DEC_SIZE = sum(math.prod(one) for one in DEC_SHAPES)
PATCH_SIZE = PATCH * D
E2D_SIZE = D * DD
HEAD_SIZE = DD * PATCH
ENC_VECS = 9 * D
DEC_VECS = 10 * DD


def hop(value, *moves):
    pairs = [(2 * a + b, 2 * c + d) for (a, b), (c, d) in moves]
    return lax.ppermute(value, ("dp", "tensor"), pairs)


def hop_both(value, *moves):
    return hop(value, *[((a, side), (b, side)) for a, b in moves for side in range(2)])


def swap(value, *where):
    if where:
        return hop(value, *[((z, side), (z, 1 - side)) for z in where for side in range(2)])
    return lax.ppermute(value, "tensor", SWAP)


def partner(value):
    count = lax.axis_size("group")
    return lax.ppermute(value, "group", [(g, g ^ 1) for g in range(count)])


def mm(left, right):
    return jnp.dot(left, right, preferred_element_type=FLOAT)


def mm_nt(left, right):
    return lax.dot_general(left, right, (((1,), (1,)), ((), ())), preferred_element_type=FLOAT)


def mm_tn(left, right):
    return lax.dot_general(left, right, (((0,), (0,)), ((), ())), preferred_element_type=FLOAT)


def sinus_parts(width):
    column = jnp.arange(width)
    decays = jnp.power(10000.0, -2.0 * (column // 2).astype(FLOAT) / width)
    far = (32 * jnp.arange(-(-TUBES // 32))).astype(FLOAT)[:, None] * decays
    near = jnp.arange(32).astype(FLOAT)[:, None] * decays
    even = column % 2 == 0
    near_one = jnp.where(even, jnp.cos(near), -jnp.sin(near))
    near_two = jnp.where(even, jnp.sin(near), jnp.cos(near))
    return jnp.concatenate([jnp.sin(far), jnp.cos(far)], 1), jnp.concatenate([near_one, near_two], 1)


def sinus_all(width):
    far, near = sinus_parts(width)
    table = far[:, None, :width] * near[None, :, :width] + far[:, None, width:] * near[None, :, width:]
    return table.reshape(-1, width)[:TUBES]


def thirds_of(rows):
    thirds = []
    for _ in range(3):
        thirds.append(lax.optimization_barrier(rows.astype(HALF)))
        rows = rows - thirds[-1].astype(FLOAT)
    return thirds


(
    QKV,
    SQUARE,
    UP,
    PATCH_ROWS,
    E2D,
    HEAD,
    VECS,
    DEC_QKV,
    DEC_OUT,
    DEC_UP,
    DEC_DOWN,
    HEAD_HALF,
    PATCH_LOW,
    PATCH_HIGH,
    W_QKV,
    W_OUT,
    W_UP,
    W_DOWN,
    E2D_W,
    HEAD_UP,
    SEND_ENC,
    SEND_MATE,
    CHAIN,
    CROSS,
    MATE_OWN,
    MATE_OTHER,
) = range(26)
PIECES = {
    QKV: (768, 1152),
    SQUARE: (1248, 768),
    UP: (672, 1536),
    PATCH_ROWS: (704, 768),
    E2D: (768, 384),
    HEAD: (64, 1536),
    VECS: (16, 768),
    DEC_QKV: (384, 576),
    DEC_OUT: (192, 384),
    DEC_UP: (384, 768),
    DEC_DOWN: (768, 384),
}


DEC_PARTS = [DEC_QKV, DEC_OUT, DEC_UP, DEC_DOWN, HEAD_HALF]
SENT = [QKV, SQUARE, UP, PATCH_ROWS, E2D, HEAD, VECS] + DEC_PARTS
ENC_PARTS = [
    (PATCH_LOW, 704, 0, PATCH_ROWS, 0),
    (W_QKV, 768, 0, QKV, 0),
    (W_OUT, 288, 0, SQUARE, 0),
    (W_OUT, 96, 1, SQUARE, 288),
    (PATCH_HIGH, 192, 2, PATCH_ROWS, 0),
    (W_UP, 672, 1, UP, 0),
    (W_UP, 96, 2, UP, 672),
    (W_DOWN, 1248, 2, SQUARE, 0),
    (W_DOWN, 288, 3, SQUARE, 1248),
    (E2D_W, 768, 2, E2D, 0),
]
MESH_ID = pl.DeviceIdType.MESH


VISIBLE = 160
OWN = 2 * VISIBLE
ALL = 4 * VISIBLE
SPAN = (0, 768, 1536)
DEPTH = (704, 704, 192)
WIDE = 1792
SQRT_HALF = 0.5**0.5


def norm_parts(x):
    center = jnp.mean(x, -1, keepdims=True)
    moved = x - center
    scale = lax.rsqrt(jnp.mean(moved * moved, -1, keepdims=True) + 1e-06)
    return moved * scale, scale


def norm_to(x, gain, bias):
    return norm_parts(x)[0] * gain + bias


def norm_from(x, gain, cotangent):
    hat, scale = norm_parts(x)
    inner = cotangent * gain
    grad = scale * (
        inner - jnp.mean(inner, -1, keepdims=True) - hat * jnp.mean(inner * hat, -1, keepdims=True)
    )
    return grad, jnp.sum(cotangent * hat, 0, keepdims=True), jnp.sum(cotangent, 0, keepdims=True)


def gelu_to(x):
    return 0.5 * x * (1.0 + lax.erf(x * SQRT_HALF))


def gelu_slope(x):
    return 0.5 * (1.0 + lax.erf(x * SQRT_HALF)) + x * jnp.exp(-0.5 * x * x) * (2.0 * math.pi) ** -0.5


def rows_at(index, count=VISIBLE):
    return pl.ds(index * count, count)


class Links:
    def __init__(self, send_sem, recv_sem):
        self.send_sem, self.recv_sem, self.keys = send_sem, recv_sem, {}

    def copy(self, key, source, target, peer):
        index = self.keys.setdefault(key, len(self.keys))
        return pltpu.make_async_remote_copy(
            src_ref=source,
            dst_ref=target,
            send_sem=self.send_sem.at[index],
            recv_sem=self.recv_sem.at[index],
            device_id=peer,
            device_id_type=MESH_ID,
        )


LANDED = [W_QKV, W_OUT, W_UP, W_DOWN, E2D_W, VECS]
LANDED_SHAPES = [(768, 1152), (384, 768), (768, 1536), (1536, 768), (768, 384), (16, 768)]
STORED = [
    ((OWN, D), FLOAT),
    ((ALL, D), HALF),
    ((ALL, 3 * D // 2), HALF),
    ((ALL, D // 2), HALF),
    ((OWN, D), FLOAT),
    ((ALL, D), HALF),
    ((ALL, FF // 2), FLOAT),
    ((ALL, FF // 2), HALF),
    ((OWN, D), FLOAT),
    ((OWN, D), HALF),
]


def forward_kernel(shared, *refs):
    sent, refs = dict(zip(SENT, refs[: len(SENT)])), refs[len(SENT) :]
    shown, ids, far_places, near_places, refs = refs[0], refs[1], refs[2], refs[3], refs[4:]
    got, refs = dict(zip(LANDED, refs[: len(LANDED)])), refs[len(LANDED) :]
    got[HEAD], reduced, refs = refs[0], refs[1], refs[2:]
    own, refs = dict(zip(DEC_PARTS, refs[: len(DEC_PARTS)])), refs[len(DEC_PARTS) :]
    other, refs = dict(zip(DEC_PARTS, refs[: len(DEC_PARTS)])), refs[len(DEC_PARTS) :]
    stream, normed, joined, blended, attended, second, upward, activated, encoded, final_enc = refs[:10]
    got[PATCH_LOW], patch_mid, got[PATCH_HIGH], part_sent, part_got, reduced_own, places = refs[10:17]
    send_sem, recv_sem, local_sem = refs[17:]
    g, z, x = lax.axis_index("group"), lax.axis_index("dp"), lax.axis_index("tensor")
    odd = lax.rem(g, 2)
    mate = (g + 1 - 2 * odd, z, x)
    across = (g, z, 1 - x)
    links = Links(send_sem, recv_sem)
    copy = links.copy
    barrier = pltpu.get_barrier_semaphore()

    def at(row, column=None):
        return (g, row, x if column is None else column)

    def greet(peer):
        pl.semaphore_signal(barrier, inc=1, device_id=peer, device_id_type=MESH_ID)

    greet(across)
    if shared:
        greet(mate)
    near = {0: [1], 1: [0, 2, 3], 2: [1, 3], 3: [2, 1]}
    for row, peers in near.items():

        @pl.when(z == row)
        def _():
            for peer in peers:
                greet(at(peer))
            if row != HOST:

                @pl.when(x != row // 2)
                def _():
                    greet(at(HOST, row // 2))

                pl.semaphore_wait(barrier, len(peers) + (2 if shared else 1))

    for column in range(2):

        @pl.when((z == HOST) & (x == column))
        def _():
            pl.semaphore_wait(barrier, 3 + (2 if shared else 1) + 1 + column)

    def part(ref, start, count, half, index=odd):
        if not half:
            return ref.at[pl.ds(start, count)]
        return ref.at[pl.ds(pl.multiple_of(start + index * (count // 2), 16), count // 2)]

    def twice(name):
        return not shared and name in (PATCH_LOW, PATCH_HIGH, E2D_W)

    keys = [(SEND_ENC, item[0], item[4]) for item in ENC_PARTS] + [(SEND_MATE, item[0], item[4]) for item in ENC_PARTS]
    for name in DEC_PARTS + [VECS, HEAD, HEAD_UP]:
        keys += [(label, name) for label in (CHAIN, CROSS, MATE_OWN, MATE_OTHER)]
    for key in keys + list(range(12)):
        links.keys[key] = len(links.keys)

    def enc_copy(item):
        name, count, owner, piece, first = item
        half, index = shared or twice(name), x if twice(name) else odd
        return copy(
            (SEND_ENC, name, first),
            part(sent[piece], 0, count, half, index),
            part(got[name], first, count, half, index),
            at(HOST),
        )

    def enc_mate(item):
        name, count, owner, piece, first = item
        half = part(got[name], first, count, True, x if twice(name) else odd)
        return copy((SEND_MATE, name, first), half, half, across if twice(name) else mate)

    def local(index, source, target):
        return pltpu.make_async_copy(source, target, local_sem.at[index])

    def chain(name, source, peer):
        target = got[name] if name in got else own[name]
        rows = source.shape[0]
        half = shared and name in own
        return copy((CHAIN, name), part(source, 0, rows, half), part(target, 0, rows, half), at(peer))

    def cross(name, source):
        rows = source.shape[0]
        return copy((CROSS, name), part(source, 0, rows, shared), part(other[name], 0, rows, shared), across)

    def mates(name, ref, label):
        half = part(ref, 0, ref.shape[0], True)
        return copy((label, name), half, half, mate)

    def owned(row):
        return [item for item in ENC_PARTS if item[2] == row and row != HOST]

    def head_up():
        return copy((CHAIN, HEAD_UP), sent[HEAD], got[HEAD], at(LAST))

    def finish_dec(name, source, here):
        cross(name, source).start()
        if shared and not here:
            mates(name, own[name], MATE_OWN).start()

    def end_all(source_of, here):
        for name in DEC_PARTS:
            cross(name, source_of[name]).wait()
            if shared:
                mates(name, other[name], MATE_OTHER).start()
        for name in DEC_PARTS:
            if shared:
                if not here:
                    mates(name, own[name], MATE_OWN).wait()
                mates(name, other[name], MATE_OTHER).wait()

    def give(column, clip):
        row = 2 * column + clip
        return [
            copy(8 + 2 * clip + side, reduced_own.at[clip], reduced, at(row, side))
            for side in range(2)
            if (row, side) != (HOST, column)
        ]

    @pl.when(z == LAST)
    def _():
        chain(VECS, sent[VECS], 2).start()
        locals_ = [local(i, sent[name], own[name]) for i, name in enumerate(DEC_PARTS)]
        locals_.append(local(len(DEC_PARTS), sent[VECS], got[VECS]))
        for one in locals_:
            one.start()
        for item in owned(LAST):
            enc_copy(item).start()
            enc_copy(item).wait_send()
        for i, name in enumerate(DEC_PARTS):
            chain(name, sent[name], 2).start()
            finish_dec(name, sent[name], True)
            if i:
                chain(DEC_PARTS[i - 1], sent[DEC_PARTS[i - 1]], 2).wait_send()
        chain(DEC_PARTS[-1], sent[DEC_PARTS[-1]], 2).wait_send()
        chain(VECS, sent[VECS], 2).wait_send()
        end_all(sent, True)
        for one in locals_:
            one.wait()
        head_up().wait_recv()

    @pl.when(z == 2)
    def _():
        first = local(0, sent[HEAD], got[HEAD])
        first.start()
        chain(VECS, sent[VECS], 2).wait_recv()
        chain(VECS, got[VECS], HOST).start()
        late = [item for item in owned(2) if item[0] == E2D_W]
        for item in owned(2):
            if item not in late:
                enc_copy(item).start()
                enc_copy(item).wait_send()
        head_up().start()
        chain(HEAD, sent[HEAD], HOST).start()
        for i, name in enumerate(DEC_PARTS):
            chain(name, sent[name], 2).wait_recv()
            chain(name, own[name], HOST).start()
            finish_dec(name, own[name], False)
            if i:
                chain(DEC_PARTS[i - 1], own[DEC_PARTS[i - 1]], HOST).wait_send()
        for item in late:
            enc_copy(item).start()
            enc_copy(item).wait_send()
        chain(DEC_PARTS[-1], own[DEC_PARTS[-1]], HOST).wait_send()
        end_all(own, False)
        chain(VECS, got[VECS], HOST).wait_send()
        chain(HEAD, sent[HEAD], HOST).wait_send()
        head_up().wait_send()
        first.wait()

    @pl.when(z == 0)
    def _():
        for item in owned(0):
            enc_copy(item).start()
            enc_copy(item).wait_send()
        for name in DEC_PARTS:
            chain(name, sent[name], 0).wait_recv()
            finish_dec(name, own[name], False)
        end_all(own, False)
        chain(VECS, sent[VECS], 0).wait_recv()
        chain(HEAD, sent[HEAD], 0).wait_recv()

    @pl.when(z == HOST)
    def _():
        mine = [
            local(i, sent[piece].at[pl.ds(0, count)], got[name].at[pl.ds(first, count)])
            for i, (name, count, owner, piece, first) in enumerate(ENC_PARTS)
            if owner == HOST
        ]
        mine.append(local(len(ENC_PARTS), sent[PATCH_ROWS], patch_mid))
        for one in mine:
            one.start()
        chain(VECS, sent[VECS], HOST).wait_recv()
        chain(VECS, got[VECS], 0).start()
        vec = got[VECS][...].astype(FLOAT)
        for one in mine:
            one.wait()

        def await_parts(names):
            items = [item for item in ENC_PARTS if item[2] != HOST and item[0] in names]
            for item in items:
                enc_copy(item).wait_recv()
                if shared or twice(item[0]):
                    enc_mate(item).start()
            for item in items:
                if shared or twice(item[0]):
                    enc_mate(item).wait()

        def pump(name):
            chain(name, sent[name], HOST).wait_recv()
            chain(name, own[name], 0).start()
            finish_dec(name, own[name], False)

        def normed_copy(i):
            return copy(i, normed.at[rows_at(i)], normed.at[rows_at(2 + i)], across)

        def out_copy(i):
            return copy(2 + i, part_sent.at[rows_at(i)], part_got.at[rows_at(i)], across)

        def second_copy(i):
            return copy(4 + i, second.at[rows_at(i)], second.at[rows_at(2 + i)], across)

        def down_copy(i):
            return copy(6 + i, part_sent.at[rows_at(2 + i)], part_got.at[rows_at(2 + i)], across)

        spots = lax.broadcasted_iota(jnp.int32, (OWN, 64), 1)
        high = ((ids[...] // 32) == spots).astype(FLOAT).astype(HALF)
        low_hot = (lax.rem(ids[...], 32) == spots).astype(FLOAT).astype(HALF)
        far = mm(high, far_places[0]) + mm(high, far_places[1]) + mm(high, far_places[2])
        near = mm(low_hot, near_places[0]) + mm(low_hot, near_places[1]) + mm(low_hot, near_places[2])
        places[...] = far[:, :D] * near[:, :D] + far[:, D:] * near[:, D:]
        await_parts((PATCH_LOW, PATCH_HIGH))
        for i in range(2):
            rows = rows_at(i)
            emb = places[rows] + vec[0:1]
            for start, depth, weight in zip(SPAN, DEPTH, (got[PATCH_LOW], patch_mid, got[PATCH_HIGH])):
                emb = emb + mm(shown[rows, start : start + depth], weight[...])
            stream[rows] = emb
            normed[rows] = norm_to(emb, vec[1:2], vec[2:3]).astype(HALF)
            normed_copy(i).start()
        await_parts((W_QKV,))

        def attend(c):
            rows = rows_at(c)
            joined[rows] = mm(normed[rows], got[W_QKV][...]).astype(HALF)
            width = D // 2
            for h in range(width // HDIM):
                column = h * HDIM
                queries = joined[rows, column : column + HDIM]
                keys = joined[rows, width + column : width + column + HDIM]
                values = joined[rows, 2 * width + column : 2 * width + column + HDIM]
                scores = mm_nt(queries, keys) * HDIM**-0.5
                weights = jnp.exp(scores - jnp.max(scores, -1, keepdims=True))
                probs = weights * (1.0 / jnp.sum(weights, -1, keepdims=True))
                blended[rows, column : column + HDIM] = mm(probs.astype(HALF), values).astype(HALF)

        for i in range(2):
            attend(i)
            if i == 0:
                await_parts((W_OUT,))
            attended[rows_at(i)] = mm(blended[rows_at(i)], got[W_OUT][...]) + stream[rows_at(i)] + vec[3:4]
            normed_copy(i).wait_recv()
            attend(2 + i)
            part_sent[rows_at(i)] = mm(blended[rows_at(2 + i)], got[W_OUT][...]).astype(HALF)
            out_copy(i).start()

        def feed(c):
            rows = rows_at(c)
            up = mm(second[rows], got[W_UP][...])
            upward[rows] = up
            activated[rows] = gelu_to(up).astype(HALF)
            return mm(activated[rows], got[W_DOWN][...])

        for i in range(2):
            rows = rows_at(i)
            out_copy(i).wait_recv()
            after = attended[rows] + part_got[rows].astype(FLOAT)
            attended[rows] = after
            second[rows] = norm_to(after, vec[4:5], vec[5:6]).astype(HALF)
            second_copy(i).start()
        await_parts((W_UP, W_DOWN))
        chain(HEAD, sent[HEAD], HOST).wait_recv()
        chain(HEAD, got[HEAD], 0).start()
        pump(DEC_QKV)
        pump(DEC_OUT)
        for i in range(2):
            rows = rows_at(i)
            encoded[rows] = feed(i) + attended[rows] + vec[6:7]
            second_copy(i).wait_recv()
            part_sent[rows_at(2 + i)] = feed(2 + i).astype(HALF)
            down_copy(i).start()
            pump((DEC_UP, DEC_DOWN)[i])
        pump(HEAD_HALF)
        await_parts((E2D_W,))
        for i in range(2):
            rows = rows_at(i)
            down_copy(i).wait_recv()
            after = encoded[rows] + part_got[rows_at(2 + i)].astype(FLOAT)
            encoded[rows] = after
            low = norm_to(after, vec[7:8], vec[8:9]).astype(HALF)
            final_enc[rows] = low
            reduced_own[i] = mm(low, got[E2D_W][...])
            for column in range(2):

                @pl.when(x == column)
                def _():
                    for one in give(column, i):
                        one.start()

        for i in range(2):
            normed_copy(i).wait_send()
            out_copy(i).wait_send()
            second_copy(i).wait_send()
            down_copy(i).wait_send()
        for column in range(2):

            @pl.when(x == column)
            def _():
                for i in range(2):
                    for one in give(column, i):
                        one.wait_send()

        end_all(own, False)
        for name in DEC_PARTS:
            chain(name, own[name], 0).wait_send()
        chain(VECS, got[VECS], 0).wait_send()
        chain(HEAD, got[HEAD], 0).wait_send()

    @pl.when((z == HOST) & (x == 0))
    def _():
        mine = local(0, reduced_own.at[1], reduced)
        mine.start()
        mine.wait()

    for row in range(4):
        for side in range(2):
            if (row, side) != (HOST, 0):

                @pl.when((z == row) & (x == side))
                def _():
                    key = 8 + 2 * (row % 2) + side
                    copy(key, reduced_own.at[row % 2], reduced, at(HOST, row // 2)).wait_recv()


def encoder_forward(number, shared, pieces, shown_own, ids_and_places):
    side = lax.axis_index("tensor")
    vmem = pl.BlockSpec(memory_space=pltpu.VMEM)
    anywhere = pl.BlockSpec(memory_space=pl.ANY)
    dec_shapes = [(pieces[name].shape, HALF) for name in DEC_PARTS]
    shapes = [(one, HALF) for one in LANDED_SHAPES] + [((64, PATCH), HALF), ((VISIBLE, DD), FLOAT)]
    shapes = shapes + 2 * dec_shapes + STORED
    count = 2 * len(ENC_PARTS) + 4 * (len(DEC_PARTS) + 3) + 12
    scratch = [
        ((704, D), HALF),
        ((704, D), HALF),
        ((192, D), HALF),
        ((ALL, D), HALF),
        ((ALL, D), HALF),
        ((2, VISIBLE, DD), FLOAT),
        ((OWN, D), FLOAT),
    ]
    out = pl.pallas_call(
        functools.partial(forward_kernel, shared),
        name="encoder_forward",
        out_shape=[jax.ShapeDtypeStruct(*one) for one in shapes],
        in_specs=[anywhere] * len(SENT) + [vmem] * 4,
        out_specs=[vmem] * len(LANDED) + [anywhere, vmem] + [anywhere] * (2 * len(DEC_PARTS)) + [vmem] * len(STORED),
        scratch_shapes=[pltpu.VMEM(*one) for one in scratch]
        + [
            pltpu.SemaphoreType.DMA((count,)),
            pltpu.SemaphoreType.DMA((count,)),
            pltpu.SemaphoreType.DMA((len(ENC_PARTS) + 1,)),
        ],
        compiler_params=pltpu.CompilerParams(
            collective_id=number, has_side_effects=True, vmem_limit_bytes=56 << 20
        ),
    )(*[pieces[name] for name in SENT], shown_own, *ids_and_places)
    landed, out = out[: len(LANDED)], out[len(LANDED) :]
    head, reduced, out = out[0], out[1], out[2:]
    own, other, stored = out[: len(DEC_PARTS)], out[len(DEC_PARTS) : 2 * len(DEC_PARTS)], out[2 * len(DEC_PARTS) :]
    low, high = jnp.where(side == 0, own[4], other[4]), jnp.where(side == 0, other[4], own[4])
    head_w = jnp.concatenate([low, high], 1)
    head_w = jnp.concatenate([head_w[:64] + head, head_w[64:]], 0)
    enc_vec, dec_vec, head_b = split_flat(landed[5].astype(FLOAT).reshape(-1), [(9, D), (10, DD), (PATCH,)])
    enc_weights = (landed[:4], landed[4], jnp.pad(enc_vec, ((0, 7), (0, 0))))
    return reduced, stored, enc_weights, (own[:4], other[:4], head_w, dec_vec, head_b)


def encoder_backward_kernel(
    picked, shown, shown_other, w_qkv, w_out, w_up, w_down, e2d_w, vec,
    stream, normed, joined, blended, attended, second, upward, activated, encoded, final_enc,
    wide, tall, dec_qkv, small, normed_far, active_far, active_last,
    qkv_out, square_out, up_out, patch_out, e2d_out, vec_out,
    one_wide, one_tall, one_qkv, one_small, two_wide, two_tall, two_qkv, two_small,
    wide_sent, tall_sent, dec_qkv_sent, small_sent, wide_got, tall_got, dec_qkv_got, small_got,
    picks_got, low, grad_up_in, mid, grad_blend, grad_joined, part_sent, part_got, own_rows_grad, own_part,
    emb_low, emb_got, down_grad, up_grad, out_grad, qkv_grad, patch_low, patch_mid, patch_high, e2d_part, e2d_got, e2d_grad,
    vec_part, vec_got, send_sem, recv_sem, local_sem,
):
    g, z, x = lax.axis_index("group"), lax.axis_index("dp"), lax.axis_index("tensor")
    barrier = pltpu.get_barrier_semaphore()
    links = Links(send_sem, recv_sem)

    def at(row, column):
        return (g, row, column)

    def greet(peer):
        pl.semaphore_signal(barrier, inc=1, device_id=peer, device_id_type=MESH_ID)

    @pl.when(z != HOST)
    def _():
        greet(at(HOST, x))

    @pl.when(z == LAST)
    def _():
        greet(at(2, x))

    @pl.when((z == HOST) & (x == 0))
    def _():
        for peer in ((0, 0), (0, 1), (HOST, 1)):
            greet(at(*peer))

    @pl.when((z == HOST) & (x == 1))
    def _():
        for peer in ((2, 0), (2, 1), (3, 0), (3, 1), (0, 1), (HOST, 0)):
            greet(at(*peer))

    @pl.when(z == HOST)
    def _():
        pl.semaphore_wait(barrier, 4)

    @pl.when((z == 2) | ((z == 0) & (x == 1)))
    def _():
        pl.semaphore_wait(barrier, 2)

    @pl.when((z == LAST) | ((z == 0) & (x == 0)))
    def _():
        pl.semaphore_wait(barrier, 1)

    def pick_copy(row, side):
        return links.copy((row % 2) * 2 + side, picked, picks_got.at[row % 2, side], at(HOST, row // 2))

    for row in range(4):
        for side in range(2):
            if (row, side) != (HOST, 0):

                @pl.when((z == row) & (x == side))
                def _():
                    pick_copy(row, side).start()

    numbers = iter(range(4, 64))
    low_number = [next(numbers), next(numbers)]
    second_number = [next(numbers), next(numbers)]
    mid_number = [next(numbers), next(numbers)]
    normed_number = [next(numbers), next(numbers)]
    emb_number = [next(numbers), next(numbers)]
    e2d_number, vec_number = next(numbers), next(numbers)

    def row_copies(numbers_two, ref):
        return [
            links.copy(numbers_two[i], ref.at[rows_at(i)], ref.at[rows_at(2 + i)], at(HOST, 1 - x)) for i in range(2)
        ]

    def part_copies(numbers_two, first):
        return [
            links.copy(
                numbers_two[i], part_sent.at[rows_at(first + i)], part_got.at[rows_at(first + i)], at(HOST, 1 - x)
            )
            for i in range(2)
        ]

    out_rows, up_rows, down_rows = 288, 672, 1248
    next_row = jnp.minimum(z + 1, LAST)
    low_far = [links.copy(next(numbers), low.at[rows_at(c)], low.at[rows_at(c)], at(next_row, x)) for c in range(4)]
    joined_far = [
        links.copy(next(numbers), grad_joined.at[rows_at(c)], grad_joined.at[rows_at(c)], at(0, x)) for c in range(4)
    ]
    up_near = links.copy(next(numbers), up_grad.at[pl.ds(up_rows, 96)], up_out.at[pl.ds(0, 96)], at(2, x))
    out_near = links.copy(
        next(numbers), out_grad.at[pl.ds(0, out_rows)], square_out.at[pl.ds(0, out_rows)], at(0, x)
    )
    patch_one = links.copy(next(numbers), patch_low, patch_out, at(0, x))
    patch_two = links.copy(next(numbers), patch_high, patch_out.at[pl.ds(0, 192)], at(2, x))
    e2d_near = links.copy(next(numbers), e2d_grad, e2d_out, at(2, x))
    vec_far = links.copy(next(numbers), vec_part, vec_out, at(LAST, x))

    own_dec = (wide, tall, dec_qkv, small)
    sent_dec = (wide_sent, tall_sent, dec_qkv_sent, small_sent)
    got_dec = (wide_got, tall_got, dec_qkv_got, small_got)
    one_dec = (one_wide, one_tall, one_qkv, one_small)
    two_dec = (two_wide, two_tall, two_qkv, two_small)
    tree_one = [links.copy(next(numbers), sent_dec[i], got_dec[i], at(next_row, x)) for i in range(4)]
    tree_two = [links.copy(next(numbers), sent_dec[i], two_dec[i], at(LAST, x)) for i in range(4)]

    @pl.when((z == 0) | (z == 2))
    def _():
        for i in (3, 0, 1, 2):
            sent_dec[i][...] = own_dec[i][...].astype(sent_dec[i].dtype)
        for i in (3, 0, 1, 2):
            tree_one[i].start()
            if i != 3:
                tree_one[i].wait_send()

    def pass_on(*parts):
        for i in parts:
            tree_one[i].wait_recv()
            sent_dec[i][...] = (own_dec[i][...] + got_dec[i][...].astype(FLOAT)).astype(sent_dec[i].dtype)
            tree_two[i].start()

    def tall_product(left, right, target, step):
        def body(t, carry):
            columns = pl.ds(pl.multiple_of(t * step, step), step)
            target[columns] = mm_tn(left[:, columns], right[...]).astype(HALF)
            return carry

        lax.fori_loop(0, target.shape[0] // step, body, 0)

    @pl.when(z == HOST)
    def _():
        low_sent, mid_sent = row_copies(low_number, low), row_copies(mid_number, mid)
        second_sent, normed_sent = part_copies(second_number, 0), part_copies(normed_number, 2)
        emb_sent = [
            links.copy(
                emb_number[i],
                emb_low.at[1 - x, rows_at(i)],
                emb_got.at[rows_at(i)],
                at(HOST, 1 - x),
            )
            for i in range(2)
        ]
        e2d_sent = links.copy(e2d_number, e2d_part.at[1 - x], e2d_got, at(HOST, 1 - x))
        vec_sent = links.copy(vec_number, vec_part, vec_got, at(HOST, 1 - x))

        vec_part[...] = jnp.zeros_like(vec_part)

        def count(row, value):
            vec_part[row : row + 1] += value

        @pl.when(x == 0)
        def _():
            mine = pltpu.make_async_copy(picked, picks_got.at[1, 0], local_sem.at[0])
            mine.start()
            mine.wait()

        for clip in range(2):
            for side in range(2):
                waiting = links.copy(clip * 2 + side, picked, picks_got.at[clip, side], at(HOST, 0))
                if clip == HOST % 2 and side == 0:

                    @pl.when(x == 1)
                    def _():
                        waiting.wait_recv()

                else:
                    waiting.wait_recv()
        reduced_low = []
        for i in range(2):
            rows = rows_at(i)
            one = picks_got[i, 0] + picks_got[i, 1]
            reduced_low.append(one)
            grad, gain, bias = norm_from(encoded[rows], vec[7:8], mm_nt(one, e2d_w[...]))
            count(7, gain)
            count(8, bias)
            count(6, jnp.sum(grad, 0, keepdims=True))
            own_rows_grad[rows] = grad
            low[rows] = grad.astype(HALF)
            low_sent[i].start()
            low_far[i].start()
        whole_low = jnp.concatenate(reduced_low, 0)
        product = mm_tn(final_enc[...], whole_low).astype(HALF)
        e2d_part[0] = product[: D // 2]
        e2d_part[1] = product[D // 2 :]
        e2d_sent.start()

        def feed_back(c):
            rows = rows_at(c)
            grad_up_in[rows] = (mm_nt(low[rows], w_down[...]) * gelu_slope(upward[rows])).astype(HALF)
            return mm_nt(grad_up_in[rows], w_up[...])

        for i in range(2):
            own_part[rows_at(i)] = feed_back(i)
            low_sent[i].wait_recv()
            low_far[2 + i].start()
            part_sent[rows_at(i)] = feed_back(2 + i).astype(HALF)
            second_sent[i].start()
        for i in range(2):
            rows = rows_at(i)
            second_sent[i].wait_recv()
            total = own_part[rows] + part_got[rows].astype(FLOAT)
            grad, gain, bias = norm_from(attended[rows], vec[4:5], total)
            count(4, gain)
            count(5, bias)
            grad = grad + own_rows_grad[rows]
            count(3, jnp.sum(grad, 0, keepdims=True))
            own_rows_grad[rows] = grad
            mid[rows] = grad.astype(HALF)
            mid_sent[i].start()
        e2d_sent.wait()
        e2d_grad[...] = (e2d_part[x].astype(FLOAT) + e2d_got[...].astype(FLOAT)).astype(HALF)
        e2d_near.start()

        def attend_back(c):
            rows = rows_at(c)
            width = D // 2
            grad_blend[...] = mm_nt(mid[rows], w_out[...]).astype(HALF)
            for h in range(width // HDIM):
                column = h * HDIM
                queries = joined[rows, column : column + HDIM]
                keys = joined[rows, width + column : width + column + HDIM]
                values = joined[rows, 2 * width + column : 2 * width + column + HDIM]
                grads = grad_blend[:, column : column + HDIM]
                scores = mm_nt(queries, keys) * HDIM**-0.5
                weights = jnp.exp(scores - jnp.max(scores, -1, keepdims=True))
                probs = weights * (1.0 / jnp.sum(weights, -1, keepdims=True))
                grad_values = mm_tn(probs.astype(HALF), grads)
                grad_probs = mm_nt(grads, values)
                grad_scores = (
                    probs * (grad_probs - jnp.sum(probs * grad_probs, -1, keepdims=True))
                ).astype(HALF)
                for third, value in enumerate(
                    (mm(grad_scores, keys) * HDIM**-0.5, mm_tn(grad_scores, queries) * HDIM**-0.5, grad_values)
                ):
                    start = third * width + column
                    grad_joined[rows, start : start + HDIM] = value.astype(HALF)
            return mm_nt(grad_joined[rows], w_qkv[...])

        for i in range(2):
            own_part[rows_at(i)] = attend_back(i)
            joined_far[i].start()
            pass_on(*((3, 0), (1,))[i])
            mid_sent[i].wait_recv()
            part_sent[rows_at(2 + i)] = attend_back(2 + i).astype(HALF)
            normed_sent[i].start()
            joined_far[2 + i].start()
        pass_on(2)
        tall_product(blended, mid, out_grad, 384)
        out_near.start()
        for i in range(2):
            rows = rows_at(i)
            normed_sent[i].wait_recv()
            total = own_part[rows] + part_got[rows_at(2 + i)].astype(FLOAT)
            grad, gain, bias = norm_from(stream[rows], vec[1:2], total)
            count(1, gain)
            count(2, bias)
            grad = grad + own_rows_grad[rows]
            count(0, jnp.sum(grad, 0, keepdims=True))
            grad_low = grad.astype(HALF)
            emb_low[0, rows] = grad_low[:, : D // 2]
            emb_low[1, rows] = grad_low[:, D // 2 :]
            emb_sent[i].start()
        vec_sent.start()
        tall_product(second, grad_up_in, up_grad, 384)
        up_near.start()
        for one in emb_sent:
            one.wait()
        for start, depth, target in zip(SPAN, DEPTH, (patch_low, patch_mid, patch_high)):
            columns = slice(start, start + depth)
            target[...] = (mm_tn(shown[:, columns], emb_low[x]) + mm_tn(shown_other[:, columns], emb_got[...])).astype(HALF)
        patch_one.start()
        patch_two.start()
        vec_sent.wait()
        vec_part[...] += vec_got[...]
        vec_far.start()
        mine = [
            pltpu.make_async_copy(out_grad.at[pl.ds(out_rows, 96)], square_out.at[pl.ds(0, 96)], local_sem.at[1]),
            pltpu.make_async_copy(up_grad.at[pl.ds(0, up_rows)], up_out, local_sem.at[2]),
            pltpu.make_async_copy(patch_mid, patch_out, local_sem.at[3]),
        ]
        for one in mine:
            one.start()
        for one in low_sent + mid_sent + second_sent + normed_sent:
            one.wait_send()
        for one in (*low_far, *joined_far, up_near, out_near, patch_one, patch_two, e2d_near, vec_far):
            one.wait_send()
        for one in tree_two:
            one.wait_send()
        for one in mine:
            one.wait()

    for row in range(4):
        for side in range(2):
            if (row, side) != (HOST, 0):

                @pl.when((z == row) & (x == side))
                def _():
                    pick_copy(row, side).wait_send()

    for row, ones in ((0, (out_near, patch_one)), (2, (up_near, patch_two, e2d_near)), (LAST, (vec_far,))):

        @pl.when(z == row)
        def _():
            for one in ones:
                one.wait_recv()

    @pl.when((z == 0) | (z == 2))
    def _():
        tree_one[3].wait_send()

    @pl.when(z == 2)
    def _():
        for one in low_far:
            one.wait_recv()
            one.start()
        tall_product(active_far, low, down_grad, 384)
        kept = pltpu.make_async_copy(down_grad.at[pl.ds(0, down_rows)], square_out, local_sem.at[0])
        kept.start()
        for one in low_far:
            one.wait_send()
        kept.wait()

    @pl.when(z == LAST)
    def _():
        for one in low_far:
            one.wait_recv()
        down_grad[pl.ds(0, 384)] = mm_tn(active_last[...], low[...]).astype(HALF)
        kept = pltpu.make_async_copy(down_grad.at[pl.ds(96, 288)], square_out.at[pl.ds(0, 288)], local_sem.at[0])
        kept.start()
        kept.wait()

    @pl.when(z == 0)
    def _():
        for one in joined_far:
            one.wait_recv()
        tall_product(normed_far, grad_joined, qkv_grad, 384)
        kept = pltpu.make_async_copy(qkv_grad, qkv_out, local_sem.at[0])
        kept.start()
        kept.wait()

    @pl.when(z == LAST)
    def _():
        kept = []
        for i in range(4):
            tree_one[i].wait_recv()
            kept.append(pltpu.make_async_copy(got_dec[i], one_dec[i], local_sem.at[i]))
            kept[i].start()
        for i in range(4):
            tree_two[i].wait_recv()
            kept[i].wait()


def encoder_backward(number, picked, shown, weights, stored, dec_grads, far):
    mats, e2d_w, vec = weights
    vmem = pl.BlockSpec(memory_space=pltpu.VMEM)
    anywhere = pl.BlockSpec(memory_space=pl.ANY)
    shapes = [
        ((D, 3 * D // 2), HALF),
        ((1248, D), HALF),
        ((672, FF // 2), HALF),
        ((704, D // 2), HALF),
        ((D // 2, DD), HALF),
        ((16, D), FLOAT),
    ]
    tree = [(one.shape, HALF) for one in dec_grads[:3]] + [(dec_grads[3].shape, FLOAT)]
    shapes = shapes + 2 * tree
    scratch = 2 * tree + [
        ((2, 2, VISIBLE, DD), HALF),
        ((ALL, D), HALF),
        ((ALL, FF // 2), HALF),
        ((ALL, D), HALF),
        ((VISIBLE, D // 2), HALF),
        ((ALL, 3 * D // 2), HALF),
        ((ALL, D), HALF),
        ((ALL, D), HALF),
        ((OWN, D), FLOAT),
        ((OWN, D), FLOAT),
        ((2, OWN, D // 2), HALF),
        ((OWN, D // 2), HALF),
        ((FF // 2, D), HALF),
        ((D, FF // 2), HALF),
        ((D // 2, D), HALF),
        ((D, 3 * D // 2), HALF),
        ((704, D // 2), HALF),
        ((704, D // 2), HALF),
        ((192, D // 2), HALF),
        ((2, D // 2, DD), HALF),
        ((D // 2, DD), HALF),
        ((D // 2, DD), HALF),
        ((16, D), FLOAT),
        ((16, D), FLOAT),
    ]
    return pl.pallas_call(
        encoder_backward_kernel,
        name="encoder_backward",
        out_shape=[jax.ShapeDtypeStruct(*one) for one in shapes],
        in_specs=[vmem] * 26,
        out_specs=[anywhere] * len(shapes),
        scratch_shapes=[pltpu.VMEM(*one) for one in scratch]
        + [pltpu.SemaphoreType.DMA((44,)), pltpu.SemaphoreType.DMA((44,)), pltpu.SemaphoreType.DMA((4,))],
        compiler_params=pltpu.CompilerParams(
            collective_id=number, has_side_effects=True, vmem_limit_bytes=60 << 20
        ),
    )(picked, *shown, *mats, e2d_w, vec, *stored, *dec_grads, *far)


LANES = 128
STEP_ROWS = 96
TEN_LANES = 8640
REP_LANES = 4056
LAID = [QKV, SQUARE, UP, PATCH_ROWS, E2D, HEAD, VECS, DEC_QKV, DEC_OUT, DEC_UP, DEC_DOWN, HEAD_HALF]
LAID_SHAPES = {**PIECES, HEAD_HALF: (384, 768)}
TEN_PLACES = [
    [(QKV, 768, 0), (SQUARE, 288, 6912)],
    [(SQUARE, 96, 0), (UP, 672, 576)],
    [(UP, 96, 0), (SQUARE, 1248, 1152)],
    [(SQUARE, 288, 0), (DEC_OUT, 192, 3456), (DEC_UP, 384, 4032), (DEC_DOWN, 768, 6336)],
]
DEC_QKV_PLACE = 1728
PATCH_COUNTS = (676, 676, 184)
E2D_PLACE = 1104
HEAD_PLACE = 3408
HEAD_TOP = 54
VEC_PLACE = 3960


def spread_rows(flat, place, blocks, count, read):
    def put(first, value):
        rows = value.shape[0]
        for j in range(blocks):
            flat[pl.ds(place + first * blocks + j, rows, stride=blocks), :] = value[:, j * LANES : (j + 1) * LANES]

    def body(t, carry):
        put(t * STEP_ROWS, read(pl.multiple_of(t * STEP_ROWS, 16), STEP_ROWS))
        return carry

    whole = count // STEP_ROWS
    if whole:
        lax.fori_loop(0, whole, body, 0)
    rest = count - whole * STEP_ROWS
    if rest:
        put(whole * STEP_ROWS, read(whole * STEP_ROWS, -(-rest // 16) * 16)[:rest])


def gather_rows(piece, flat, place, blocks, count):
    def put(first, rows, padded):
        for j in range(blocks):
            value = flat[pl.ds(place + first * blocks + j, rows, stride=blocks), :]
            if padded > rows:
                value = jnp.concatenate([value, jnp.zeros((padded - rows, LANES), FLOAT)], 0)
            piece[pl.ds(first, padded), j * LANES : (j + 1) * LANES] = value.astype(HALF)

    def body(t, carry):
        put(pl.multiple_of(t * STEP_ROWS, 16), STEP_ROWS, STEP_ROWS)
        return carry

    whole = count // STEP_ROWS
    if whole:
        lax.fori_loop(0, whole, body, 0)
    rest = count - whole * STEP_ROWS
    if rest:
        put(whole * STEP_ROWS, rest, -(-rest // 16) * 16)


def lay_out(z, x, ten, rep, pieces, wide_rows):
    for row in range(4):

        @pl.when(z == row)
        def _():
            for name, count, place in TEN_PLACES[row]:
                gather_rows(pieces[name], ten, place, PIECES[name][1] // LANES, count)
            if row < LAST:
                gather_rows(pieces[PATCH_ROWS], rep, 0, D // LANES, PATCH_COUNTS[row])
            if row < 2:
                pieces[PATCH_ROWS][pl.ds(688, 16)] = jnp.zeros((16, D), HALF)
            if row == 2:
                gather_rows(pieces[E2D], rep, E2D_PLACE, DD // LANES, D)
                gather_rows(pieces[HEAD], rep, HEAD_PLACE, PATCH // LANES, HEAD_TOP)
            if row == LAST:
                gather_rows(pieces[VECS], rep, VEC_PLACE, D // LANES, 16)
                for j in range(4):
                    wide_rows[j, pl.ds(0, 192, stride=2), :] = ten[pl.ds(DEC_QKV_PLACE + j, 192, stride=9), :]
                middle = ten[pl.ds(DEC_QKV_PLACE + 4, 192, stride=9), :]
                late = [middle[:, 64:]] + [ten[pl.ds(DEC_QKV_PLACE + 5 + j, 192, stride=9), :] for j in range(4)]
                late = jnp.concatenate(late + [jnp.zeros((192, 64), FLOAT)], 1)
                wide_rows[4, pl.ds(0, 192, stride=2), :] = middle
                for j in range(5):
                    columns = slice(j * LANES, (j + 1) * LANES)
                    wide_rows[j, pl.ds(1, 192, stride=2), :] = late[:, columns]
                for j in range(4):
                    columns = slice(j * LANES, (j + 1) * LANES)
                    pieces[DEC_QKV][:, columns] = wide_rows[j].astype(HALF)
                pieces[DEC_QKV][:, 512:576] = wide_rows[4][:, :64].astype(HALF)
                half = pieces[HEAD_HALF]
                blocks, offset = PATCH // LANES, x * 6
                half[pl.ds(0, 48)] = jnp.zeros((48, D), HALF)
                for j in range(6):
                    columns = slice(j * LANES, (j + 1) * LANES)
                    value = rep[pl.ds(offset + j, 42, stride=blocks), :]
                    half[pl.ds(48, 48), columns] = jnp.concatenate(
                        [jnp.zeros((6, LANES), FLOAT), value], 0
                    ).astype(HALF)
                    for t in range(1, 4):
                        value = rep[pl.ds((96 * t - HEAD_TOP) * blocks + offset + j, 96, stride=blocks), :]
                        half[pl.ds(96 * t, 96), columns] = value.astype(HALF)


def lay_out_kernel(ten, rep, *refs):
    pieces = dict(zip(LAID, refs))
    lay_out(lax.axis_index("dp"), lax.axis_index("tensor"), ten, rep, pieces, refs[len(LAID)])


def first_pieces(ten, rep):
    vmem = pl.BlockSpec(memory_space=pltpu.VMEM)
    out = pl.pallas_call(
        lay_out_kernel,
        name="lay_out",
        out_shape=[jax.ShapeDtypeStruct(LAID_SHAPES[name], HALF) for name in LAID],
        in_specs=[vmem] * 2,
        out_specs=[vmem] * len(LAID),
        scratch_shapes=[pltpu.VMEM((5, 384, LANES), FLOAT)],
        compiler_params=pltpu.CompilerParams(vmem_limit_bytes=61 << 20),
    )(ten, rep)
    return dict(zip(LAID, out))


def update_kernel(
    number, last,
    stats, qkv, square, up, patch, e2d, vec, wide, tall, dec_qkv, small,
    one_wide, one_tall, one_qkv, one_small, two_wide, two_tall, two_qkv, two_small,
    *refs,
):
    masters, refs = refs[:6], refs[6:]
    stats_out, outs, refs = refs[0], refs[1:7], refs[7:]
    pieces = {}
    if not last:
        pieces, refs = dict(zip(LAID, refs)), refs[len(LAID) :]
    held, refs = refs[:6], refs[6:]
    grad_ten, grad_rep, wide_rows, patch_other, e2d_other, head_own, head_other, slots, send_sem, recv_sem, local_sem = refs
    g, z, x = lax.axis_index("group"), lax.axis_index("dp"), lax.axis_index("tensor")
    me = 2 * z + x
    links = Links(send_sem, recv_sem)
    barrier = pltpu.get_barrier_semaphore()
    loads = [pltpu.make_async_copy(masters[i], held[i], local_sem.at[i]) for i in range(6)]
    for one in loads:
        one.start()

    def peer(shift):
        other = lax.rem(me + shift, 8)
        return (g, other // 2, lax.rem(other, 2))

    for shift in range(1, 8):
        pl.semaphore_signal(barrier, inc=1, device_id=peer(shift), device_id_type=MESH_ID)
    pl.semaphore_wait(barrier, 7)

    across = (g, z, 1 - x)
    patch_swap = links.copy(0, patch, patch_other, across)
    e2d_swap = links.copy(1, e2d, e2d_other, across)
    head_swap = links.copy(2, head_own, head_other, across)
    top_own = links.copy(3, head_own.at[pl.ds(0, 64)], head_own.at[pl.ds(0, 64)], (g, 2, x))
    top_other = links.copy(4, head_other.at[pl.ds(0, 64)], head_other.at[pl.ds(0, 64)], (g, 2, x))

    def plain(ref):
        return lambda first, rows: ref[pl.ds(first, rows)].astype(FLOAT)

    def joined(own, other):
        def read(first, rows):
            one, two = own[pl.ds(first, rows)].astype(FLOAT), other[pl.ds(first, rows)].astype(FLOAT)
            return jnp.concatenate([jnp.where(x == 0, one, two), jnp.where(x == 0, two, one)], 1)

        return read

    def total(own, one, two, top, columns):
        def read(first, rows):
            at = pl.ds(top + first, rows)
            return own[at, columns] + one[at, columns].astype(FLOAT) + two[at, columns].astype(FLOAT)

        return read

    @pl.when(z < LAST)
    def _():
        patch_swap.start()

    @pl.when(z == 2)
    def _():
        e2d_swap.start()

    fc = DFF // 2

    @pl.when(z == LAST)
    def _():
        head_own[...] = total(wide, one_wide, two_wide, 0, slice(fc, 2 * fc))(0, DD).astype(HALF)
        head_swap.start()
        top_own.start()
        whole = slice(0, DD)
        spread_rows(grad_ten, 0, 6, 288, plain(square))
        spread_rows(grad_ten, 3456, 3, 192, total(tall, one_tall, two_tall, fc, whole))
        spread_rows(grad_ten, 4032, 6, 384, total(wide, one_wide, two_wide, 0, slice(0, fc)))
        spread_rows(grad_ten, 6336, 3, 768, total(tall, one_tall, two_tall, 0, whole))
        for j in range(4):
            columns = slice(j * LANES, (j + 1) * LANES)
            wide_rows[j] = total(dec_qkv, one_qkv, two_qkv, 0, columns)(0, DD)
        tail = total(dec_qkv, one_qkv, two_qkv, 0, slice(512, 576))(0, DD)
        wide_rows[4] = jnp.concatenate([tail, jnp.zeros((DD, 64), FLOAT)], 1)
        for j in range(4):
            grad_ten[pl.ds(DEC_QKV_PLACE + j, 192, stride=9), :] = wide_rows[j, pl.ds(0, 192, stride=2), :]
        late = jnp.concatenate([wide_rows[j, pl.ds(1, 192, stride=2), :] for j in range(5)], 1)
        early = wide_rows[4, pl.ds(0, 192, stride=2), :]
        grad_ten[pl.ds(DEC_QKV_PLACE + 4, 192, stride=9), :] = jnp.concatenate([early[:, :64], late[:, :64]], 1)
        for j in range(4):
            start = 64 + j * LANES
            grad_ten[pl.ds(DEC_QKV_PLACE + 5 + j, 192, stride=9), :] = late[:, start : start + LANES]
        for j in range(6):
            columns = slice(j * LANES, (j + 1) * LANES)
            grad_rep[pl.ds(VEC_PLACE + j, 9, stride=6), :] = vec[0:9, columns]
        rest = small[...] + one_small[...] + two_small[...]
        for j in range(3):
            grad_rep[pl.ds(VEC_PLACE + 54 + j, 14, stride=3), :] = rest[0:14, j * LANES : (j + 1) * LANES]
        head_swap.wait_recv()
        top_other.start()
        read = joined(head_own, head_other)

        def put(first, value):
            rows = value.shape[0]
            for j in range(12):
                grad_rep[pl.ds(first * 12 + j, rows, stride=12), :] = value[:, j * LANES : (j + 1) * LANES]

        put(0, read(48, 48)[6:])
        for t in range(1, 4):
            put(96 * t - HEAD_TOP, read(96 * t, 96))

    for row in range(3):

        @pl.when(z == row)
        def _():
            refs_of = {QKV: qkv, SQUARE: square, UP: up}
            for name, count, place in TEN_PLACES[row]:
                spread_rows(grad_ten, place, PIECES[name][1] // LANES, count, plain(refs_of[name]))
            patch_swap.wait_recv()
            spread_rows(grad_rep, 0, 6, PATCH_COUNTS[row], joined(patch, patch_other))
            if row == 2:
                e2d_swap.wait_recv()
                for half in range(2):

                    def read(first, rows):
                        one, two = e2d[pl.ds(first, rows)].astype(FLOAT), e2d_other[pl.ds(first, rows)].astype(FLOAT)
                        return jnp.where(x == half, one, two)

                    spread_rows(grad_rep, E2D_PLACE + half * 1152, 3, 384, read)
                top_own.wait_recv()
                top_other.wait_recv()
                spread_rows(grad_rep, HEAD_PLACE, 12, HEAD_TOP, joined(head_own, head_other))

    def square_sum(flat, step):
        def body(t, carry):
            value = flat[pl.ds(pl.multiple_of(t * step, 8), step), :]
            return carry + jnp.sum((value * value).reshape(step // 8, 8, LANES), 0)

        return jnp.sum(lax.fori_loop(0, flat.shape[0] // step, body, jnp.zeros((8, LANES), FLOAT)))

    squares = square_sum(grad_ten, 360) + square_sum(grad_rep, 312) * 0.5
    line = lax.broadcasted_iota(jnp.int32, (8, LANES), 0)
    slots[me] = jnp.where(line == 0, squares, stats[...])
    shares = [links.copy(4 + shift, slots.at[me], slots.at[me], peer(shift)) for shift in range(1, 8)]
    for one in shares:
        one.start()
    for one in shares:
        one.wait()
    whole = slots[0]
    for i in range(1, 8):
        whole = whole + slots[i]
    square_all, loss_all, count_all = whole[0:1], whole[1:2], whole[2:3]
    norm = jnp.sqrt(square_all + 1e-30) / count_all
    factor = jnp.minimum(1.0, CLIP / norm) / count_all
    stats_out[...] = jnp.where(line == 0, norm, whole)
    for one in loads:
        one.wait()

    def adam(master, first, second, grad, step):
        def body(t, carry):
            at = pl.ds(pl.multiple_of(t * step, 8), step)
            new = adamw(master[at, :], first[at, :], second[at, :], grad[at, :] * factor, number)
            master[at, :], first[at, :], second[at, :] = new
            return carry

        lax.fori_loop(0, master.shape[0] // step, body, 0)

    stores = [pltpu.make_async_copy(held[i], outs[i], local_sem.at[i]) for i in range(6)]
    adam(*held[:3], grad_ten, 240)
    for one in stores[:3]:
        one.start()
    adam(*held[3:], grad_rep, 312)
    for one in stores[3:]:
        one.start()
    if not last:
        lay_out(z, x, held[0], held[3], pieces, wide_rows)

    @pl.when(z < LAST)
    def _():
        patch_swap.wait_send()

    @pl.when(z == 2)
    def _():
        e2d_swap.wait_send()

    @pl.when(z == LAST)
    def _():
        head_swap.wait_send()
        top_own.wait_send()
        top_other.wait_send()

    for one in stores:
        one.wait()


def update(identity, number, last, stats, gradients, states):
    vmem = pl.BlockSpec(memory_space=pltpu.VMEM)
    anywhere = pl.BlockSpec(memory_space=pl.ANY)
    laid = [] if last else LAID
    flat = [(TEN_LANES, LANES)] * 3 + [(REP_LANES, LANES)] * 3
    scratch = [(one, FLOAT) for one in flat + [(TEN_LANES, LANES), (REP_LANES, LANES), (5, 384, LANES)]] + [
        ((704, D // 2), HALF),
        ((D // 2, DD), HALF),
        ((DD, PATCH // 2), HALF),
        ((DD, PATCH // 2), HALF),
        ((8, 8, LANES), FLOAT),
    ]
    out = pl.pallas_call(
        functools.partial(update_kernel, number, last),
        name="update",
        out_shape=[jax.ShapeDtypeStruct((8, LANES), FLOAT)]
        + [jax.ShapeDtypeStruct(one, FLOAT) for one in flat]
        + [jax.ShapeDtypeStruct(LAID_SHAPES[name], HALF) for name in laid],
        in_specs=[vmem] * (1 + len(gradients)) + [anywhere] * 6,
        out_specs=[vmem] + [anywhere] * 6 + [vmem] * len(laid),
        scratch_shapes=[pltpu.VMEM(*one) for one in scratch]
        + [pltpu.SemaphoreType.DMA((12,)), pltpu.SemaphoreType.DMA((12,)), pltpu.SemaphoreType.DMA((6,))],
        compiler_params=pltpu.CompilerParams(
            collective_id=identity, has_side_effects=True, vmem_limit_bytes=61 << 20
        ),
    )(stats, *gradients, *states)
    return out[0], out[1:7], dict(zip(laid, out[7:]))


def decoder_kernel(
    reduced, hot, shown, places, pixels, counted, qkv_own, qkv_oth,
    out_own, out_oth, up_own, up_oth, down_own, down_oth, head_w, vec, head_b,
    picked, wide, tall, qkv_grad, small, loss,
    normed, tokens, q_ref, k_ref, v_ref, parts, parts_got, grad_att, vec_grad, vec_got, head_b_grad,
    blended, blend_other, totals, upward, activated, second, final_low, pred_low, low, grad_up_in, mid, grad_blend,
    blend_sent, wide_sent, wide_got, tall_sent, tall_got, dk_ref, dv_ref, send_sem, recv_sem,
):
    g, z, x = lax.axis_index("group"), lax.axis_index("dp"), lax.axis_index("tensor")
    across = (g, z, 1 - x)
    links = Links(send_sem, recv_sem)
    barrier = pltpu.get_barrier_semaphore()
    pl.semaphore_signal(barrier, inc=1, device_id=across, device_id_type=MESH_ID)
    half = pixels.shape[0]
    width = q_ref.shape[1]
    heads = width // HDIM
    tiles = q_ref.shape[0] // TILE
    fc = DFF // 2
    left = reduced[...] + vec[0:1]
    thirds = []
    for _ in range(3):
        thirds.append(left.astype(HALF))
        left = left - thirds[-1].astype(FLOAT)

    def embed(t, carry):
        rows = pl.ds(pl.multiple_of(t * TILE, TILE), TILE)
        placed = mm(hot[rows], thirds[0]) + mm(hot[rows], thirds[1]) + mm(hot[rows], thirds[2])
        values = jnp.where(shown[rows] > 0.5, placed, vec[1:2]) + places[rows]
        tokens[rows] = values
        low_rows = norm_to(values, vec[2:3], vec[3:4]).astype(HALF)
        normed[rows] = low_rows
        joined = mm(low_rows, qkv_own[...]).astype(HALF)
        q_ref[rows] = joined[:, :width]
        k_ref[rows] = joined[:, width : 2 * width]
        v_ref[rows] = joined[:, 2 * width :]
        return carry

    lax.fori_loop(0, tiles, embed, 0)
    parts[...] = jnp.zeros_like(parts)

    def attend(first, last):
        for h in range(heads):
            cols = slice(h * HDIM, (h + 1) * HDIM)
            keys = k_ref[:, cols] * HALF(HDIM**-0.5)
            turned = v_ref[:, cols].T

            def step(t, carry):
                rows = pl.ds(pl.multiple_of(t * TILE, TILE), TILE)
                scores = mm_nt(keys, q_ref[rows, cols])
                highest = jnp.max(scores, 0, keepdims=True)
                weights = jnp.exp(scores - highest)
                total = jnp.sum(weights, 0, keepdims=True)
                probs = (weights * (1.0 / total)).astype(HALF)
                blended[rows, cols] = mm(turned, probs).T.astype(HALF)
                totals[h, pl.ds(t, 1), :] = highest + jnp.log(total)
                return carry

            lax.fori_loop(first, last, step, 0)

    whole = half // TILE
    attend(whole, tiles)
    pl.semaphore_wait(barrier, 1)
    blend_swap = links.copy(0, blended.at[pl.ds(half, half)], blend_other, across)
    blend_swap.start()
    attend(0, whole)
    vec_grad[...] = jnp.zeros_like(vec_grad)
    head_b_grad[...] = jnp.zeros_like(head_b_grad)
    loss[...] = jnp.zeros_like(loss)
    blend_swap.wait_recv()

    def count(row, value):
        vec_grad[row : row + 1] += value

    grad_swaps = []
    start = 0
    for step, size in enumerate((400, 384)):
        rows = pl.ds(start, size)
        start += size
        attended = mm(blended[rows], out_own[...]) + mm(blend_other[rows], out_oth[...]) + tokens[rows] + vec[4:5]
        second[rows] = norm_to(attended, vec[5:6], vec[6:7]).astype(HALF)
        decoded = attended + vec[7:8]
        for side, (into, back) in enumerate(((up_own, down_own), (up_oth, down_oth))):
            cols = slice(side * fc, (side + 1) * fc)
            up = mm(second[rows], into[...])
            upward[rows, cols] = up
            activated[rows, cols] = gelu_to(up).astype(HALF)
            decoded = decoded + mm(activated[rows, cols], back[...])
        final_low[rows] = norm_to(decoded, vec[8:9], vec[9:10]).astype(HALF)
        differ = mm(final_low[rows], head_w[...]) + head_b[...]
        differ = differ - norm_parts(pixels[rows].astype(FLOAT))[0]
        share = counted[rows]
        loss[...] += jnp.sum(jnp.mean(differ * differ, -1, keepdims=True) * share)
        grad = (2.0 / PATCH) * differ * share
        head_b_grad[...] += jnp.sum(grad, 0, keepdims=True)
        pred_low[rows] = grad.astype(HALF)
        grad_out, gain, bias = norm_from(decoded, vec[8:9], mm_nt(pred_low[rows], head_w[...]))
        count(8, gain)
        count(9, bias)
        count(7, jnp.sum(grad_out, 0, keepdims=True))
        low[rows] = grad_out.astype(HALF)
        grad_second = jnp.zeros((size, DD), FLOAT)
        for side, (into, back) in enumerate(((up_own, down_own), (up_oth, down_oth))):
            cols = slice(side * fc, (side + 1) * fc)
            slope = gelu_slope(upward[rows, cols])
            grad_up_in[rows, cols] = (mm_nt(low[rows], back[...]) * slope).astype(HALF)
            grad_second = grad_second + mm_nt(grad_up_in[rows, cols], into[...])
        grad, gain, bias = norm_from(attended, vec[5:6], grad_second)
        count(5, gain)
        count(6, bias)
        grad = grad + grad_out
        count(4, jnp.sum(grad, 0, keepdims=True))
        grad_att[rows] = grad
        mid[rows] = grad.astype(HALF)
        grad_blend[rows] = mm_nt(mid[rows], out_own[...]).astype(HALF)
        blend_sent[rows] = mm_nt(mid[rows], out_oth[...]).astype(HALF)
        swap_rows = pl.ds(half + start - size, size)
        grad_swaps.append(links.copy(1 + step, blend_sent.at[rows], grad_blend.at[swap_rows], across))
        grad_swaps[-1].start()
    mine = pl.ds(pl.multiple_of(x * fc, LANES), fc)
    theirs = pl.ds(pl.multiple_of((1 - x) * fc, LANES), fc)
    wide_sent[:, :fc] = mm_tn(second[...], grad_up_in[:, fc:]).astype(HALF)
    wide_sent[:, fc:] = mm_tn(final_low[...], pred_low[:, theirs]).astype(HALF)
    wide_swap = links.copy(3, wide_sent, wide_got, across)
    wide_swap.start()
    tall_sent[:fc] = mm_tn(activated[:, fc:], low[...]).astype(HALF)
    tall_sent[fc:] = mm_tn(blend_other[...], mid[...]).astype(HALF)
    tall_swap = links.copy(4, tall_sent, tall_got, across)
    tall_swap.start()
    wide[:, :fc] = mm_tn(second[...], grad_up_in[:, :fc])
    wide[:, fc:] = mm_tn(final_low[...], pred_low[:, mine])
    tall[:fc] = mm_tn(activated[:, :fc], low[...])
    tall[fc:] = mm_tn(blended[pl.ds(0, half)], mid[...])
    for one in grad_swaps:
        one.wait_recv()
    part_swaps = []

    def send_parts(block):
        for third in range(3):
            cols = pl.ds(256 * third + 128 * block, 128)
            one = links.copy(5 + 3 * block + third, parts.at[pl.ds(half, half), cols], parts_got.at[:, cols], across)
            one.start()
            part_swaps.append(one)

    for h in range(heads):
        cols = slice(h * HDIM, (h + 1) * HDIM)
        keys = k_ref[:, cols] * HALF(HDIM**-0.5)
        values = v_ref[:, cols]
        turned = keys.T
        dk_ref[...] = jnp.zeros_like(dk_ref)
        dv_ref[...] = jnp.zeros_like(dv_ref)

        def back_step(t, carry):
            rows = pl.ds(pl.multiple_of(t * TILE, TILE), TILE)
            queries, grads = q_ref[rows, cols], grad_blend[rows, cols]
            probs = jnp.exp(mm_nt(keys, queries) - totals[h, pl.ds(t, 1), :])
            dv_ref[...] += mm(probs.astype(HALF), grads)
            grad_probs = mm_nt(values, grads)
            grad_scores = (probs * (grad_probs - jnp.sum(probs * grad_probs, 0, keepdims=True))).astype(HALF)
            dk_ref[...] += mm(grad_scores, queries)
            parts[rows, cols] = mm(turned, grad_scores).T.astype(HALF)
            return carry

        lax.fori_loop(0, tiles, back_step, 0)
        parts[:, 256 + h * HDIM : 256 + (h + 1) * HDIM] = (dk_ref[...] * HDIM**-0.5).astype(HALF)
        parts[:, 512 + h * HDIM : 512 + (h + 1) * HDIM] = dv_ref[...].astype(HALF)
        if h == 1:
            send_parts(0)
    send_parts(1)

    def back(ref, rows, weights):
        total = jnp.zeros((half, DD), FLOAT)
        for third in range(3):
            columns = ref[rows, 256 * third : 256 * third + width]
            total = total + mm_nt(columns, weights[:, third * width : (third + 1) * width])
        return total

    own_rows_ = pl.ds(0, half)
    grad_normed = back(parts, own_rows_, qkv_own)
    product = mm_tn(normed[...], parts[...])
    for third in range(3):
        qkv_grad[:, third * width : (third + 1) * width] = product[:, 256 * third : 256 * third + width]
    wide_swap.wait_recv()
    wide[...] += wide_got[...].astype(FLOAT)
    tall_swap.wait_recv()
    tall[...] += tall_got[...].astype(FLOAT)
    for one in part_swaps:
        one.wait_recv()
    grad_normed = grad_normed + back(parts_got, own_rows_, qkv_oth)
    grad, gain, bias = norm_from(tokens[own_rows_], vec[2:3], grad_normed)
    count(2, gain)
    count(3, bias)
    grad = grad + grad_att[...]
    seen = jnp.where(shown[own_rows_] > 0.5, grad, 0.0)
    count(0, jnp.sum(seen, 0, keepdims=True))
    count(1, jnp.sum(grad - seen, 0, keepdims=True))
    for i in range(PATCH // DD):
        count(10 + i, head_b_grad[:, i * DD : (i + 1) * DD])
    vec_swap = links.copy(11, vec_grad, vec_got, across)
    vec_swap.start()
    picked[...] = mm_tn(hot[own_rows_], grad.astype(HALF)).astype(HALF)
    vec_swap.wait_recv()
    small[...] = vec_grad[...] + vec_got[...]
    for one in [blend_swap, wide_swap, tall_swap, vec_swap] + grad_swaps + part_swaps:
        one.wait_send()


def decoder_round(number, reduced, hot, shown, places, pixels_low, counted, weights):
    own, other, head_w, vec, head_b = weights
    count, rows, width = pixels_low.shape[0], hot.shape[0], DD // 2
    vmem = pl.BlockSpec(memory_space=pltpu.VMEM)
    shapes = [
        ((VISIBLE, DD), HALF),
        ((DD, DFF // 2 + PATCH // 2), FLOAT),
        ((DFF // 2 + width, DD), FLOAT),
        ((DD, 3 * width), FLOAT),
        ((16, DD), FLOAT),
        ((8, LANES), FLOAT),
    ]
    scratch = [
        ((rows, DD), HALF),
        ((rows, DD), FLOAT),
        ((rows, width), HALF),
        ((rows, width), HALF),
        ((rows, width), HALF),
        ((rows, 768), HALF),
        ((count, 768), HALF),
        ((count, DD), FLOAT),
        ((16, DD), FLOAT),
        ((16, DD), FLOAT),
        ((1, PATCH), FLOAT),
        ((rows, width), HALF),
        ((count, width), HALF),
        ((width // HDIM, rows // TILE, TILE), FLOAT),
        ((count, DFF), FLOAT),
        ((count, DFF), HALF),
        ((count, DD), HALF),
        ((count, DD), HALF),
        ((count, PATCH), HALF),
        ((count, DD), HALF),
        ((count, DFF), HALF),
        ((count, DD), HALF),
        ((rows, width), HALF),
        ((count, width), HALF),
        ((DD, DFF // 2 + PATCH // 2), HALF),
        ((DD, DFF // 2 + PATCH // 2), HALF),
        ((DFF // 2 + width, DD), HALF),
        ((DFF // 2 + width, DD), HALF),
        ((rows, HDIM), FLOAT),
        ((rows, HDIM), FLOAT),
    ]
    return pl.pallas_call(
        decoder_kernel,
        name="decoder",
        out_shape=[jax.ShapeDtypeStruct(*one) for one in shapes],
        in_specs=[vmem] * 17,
        out_specs=[vmem] * len(shapes),
        scratch_shapes=[pltpu.VMEM(*one) for one in scratch]
        + [pltpu.SemaphoreType.DMA((12,)), pltpu.SemaphoreType.DMA((12,))],
        compiler_params=pltpu.CompilerParams(
            collective_id=number, has_side_effects=True, vmem_limit_bytes=60 << 20
        ),
    )(
        reduced,
        hot,
        shown,
        places,
        pixels_low,
        counted[:, None],
        own[0],
        other[0],
        own[1],
        other[1],
        own[2],
        other[2],
        own[3],
        other[3],
        head_w,
        jnp.pad(vec, ((0, 6), (0, 0))),
        head_b[None],
    )


def hosted_round(
    patches,
    visible,
    frames_valid,
    clip_valid,
    rep_weights,
    ten_weights,
    rep_m,
    rep_v,
    ten_m,
    ten_v,
    rep_outer,
    ten_outer,
):
    side = lax.axis_index("tensor")
    z = lax.axis_index("dp")
    half_rows = TUBES // 2
    tube_ids = (jnp.arange(TUBES) + side * half_rows) % TUBES
    ids_one = hop(visible[:, 0, 0], ((0, 0), (HOST, 0)), ((2, 1), (HOST, 1)))
    ids_two = hop(visible[:, 0, 0], ((3, 1), (HOST, 1)))
    ids_two = jnp.where(side == 0, visible[:, 0, 0], ids_two)
    dec_table = sinus_all(DD)
    places = []
    for part in sinus_parts(D):
        part = jnp.pad(part, ((0, -part.shape[0] % 64), (0, 0)))
        places.append(jnp.stack(thirds_of(part)))
    dec_places = jnp.where(side == 0, dec_table, jnp.roll(dec_table, -half_rows, 0))
    states = [one.reshape(TEN_LANES, LANES) for one in (ten_weights, ten_m, ten_v)]
    states = states + [one.reshape(REP_LANES, LANES) for one in (rep_weights, rep_m, rep_v)]
    starts = states[0], states[3]
    pieces = first_pieces(*starts)
    rep_quarter = rep_weights.shape[0]
    source, target = jnp.arange(PATCH)[:, None], jnp.arange(WIDE)[None, :]
    cut = rep_quarter // D
    layout = (target == source + (SPAN[1] - cut) * (source // cut)).astype(HALF)
    shown_steps = []
    for s in range(STEPS):
        picks = (visible[s, 0, 0][:, None] == jnp.arange(TUBES)[None, :]).astype(HALF)
        rows = mm(picks, patches[s, 0, 0]).astype(HALF)
        rows = mm(rows, layout).astype(HALF)
        one = hop(rows, ((0, 0), (HOST, 0)), ((2, 1), (HOST, 1)))
        two = hop(rows, ((3, 1), (HOST, 1)))
        own = jnp.concatenate([one, jnp.where(side == 0, rows, two)], 0)
        shown_steps.append((own, swap(own, HOST)))
    loss_list, count_list, norm_list = [], [], []
    for s in range(STEPS):
        ids = visible[s, 0, 0]
        picks = tube_ids[:, None] == ids[None, :]
        shown_here = jnp.any(picks, 1)
        counted = (
            jnp.where(shown_here, 0.0, 1.0)
            * (tube_ids // (TUBES // FRAMES) < frames_valid[s, 0, 0])
            * (clip_valid[s, 0, 0] == 1)
        ).astype(FLOAT)[:half_rows]
        shown = shown_steps[s]
        vis = ids.shape[0]
        ids_own = jnp.concatenate([ids_one[s], ids_two[s]])
        reduced_clip, enc_stored, enc_weights, dec_weights = encoder_forward(
            3 + s, s == 0, pieces, shown[0], (ids_own[:, None], *places)
        )
        normed, activated = enc_stored[1], enc_stored[7]
        far = (
            hop_both(normed, (HOST, 0)),
            hop_both(activated, (HOST, 2)),
            hop_both(activated[:, 1152:], (HOST, LAST)),
        )
        pixels_low = lax.dynamic_slice_in_dim(patches[s, 0, 0], side * half_rows, half_rows, 0)
        picked, wide, tall, qkv_grad, small, loss = decoder_round(
            9 + s,
            reduced_clip,
            picks.astype(HALF),
            shown_here[:, None].astype(FLOAT),
            dec_places,
            pixels_low,
            counted,
            dec_weights,
        )
        back = encoder_backward(5 + s, picked, shown, enc_weights, enc_stored, (wide, tall, qkv_grad, small), far)
        line = jnp.arange(8)[:, None]
        stats = jnp.where(line == 1, loss[0, 0], jnp.where(line == 2, jnp.sum(counted), 0.0))
        stats = jnp.broadcast_to(stats, (8, LANES))
        stats, states, pieces = update(
            7 + s, STEP_BEFORE + s + 1, s == STEPS - 1, stats, (*back[:6], wide, tall, qkv_grad, small, *back[6:]), states
        )
        norm_list.append(stats[0, 0])
        loss_list.append(stats[1, 0])
        count_list.append(stats[2, 0])
    ten_first, ten_second, rep_first, rep_second = [one.reshape(-1) for one in (*states[1:3], *states[4:])]
    ten_diff, rep_diff = [group_mean(starts[i] - states[3 * i]).reshape(-1) for i in range(2)]
    rep_momentum = MOMENTUM * rep_outer + rep_diff
    ten_momentum = MOMENTUM * ten_outer[0] + ten_diff
    rep_new = rep_weights - LR_OUT * (rep_diff + MOMENTUM * rep_momentum)
    ten_new = ten_weights[0] - LR_OUT * (ten_diff + MOMENTUM * ten_momentum)
    return (
        jnp.stack(loss_list)[:, None],
        jnp.stack(count_list)[:, None],
        jnp.stack(norm_list)[:, None],
        rep_first[None],
        rep_second[None],
        ten_first[None, None],
        ten_second[None, None],
        rep_diff,
        ten_diff[None],
        rep_momentum,
        ten_momentum[None],
        rep_new,
        ten_new[None],
    )


def group_mean(diff):
    if lax.axis_size("group") != 4:
        return lax.psum(diff, "group") / lax.axis_size("group")
    odd = lax.axis_index("group") % 2 == 1
    half = diff.shape[0] // 2
    low, high = diff[:half], diff[half:]
    part = jnp.where(odd, high, low) + partner(jnp.where(odd, low, high))
    part_low = lax.optimization_barrier(part.astype(HALF))
    far = lax.ppermute(part_low, "group", [(g, g ^ 2) for g in range(4)])
    total = (part_low.astype(FLOAT) + far.astype(FLOAT)) * 0.25
    other = partner(total)
    return jnp.concatenate([jnp.where(odd, other, total), jnp.where(odd, total, other)])


def solution(mesh):
    placed = (
        P(None, "group", "dp", None, None),
        P(None, "group", "dp", None),
        P(None, "group", "dp"),
        P(None, "group", "dp"),
        P("dp"),
        P("tensor", "dp"),
        P("group", "dp"),
        P("group", "dp"),
        P("group", "tensor", "dp"),
        P("group", "tensor", "dp"),
        P("dp"),
        P("tensor", "dp"),
    )
    return jax.shard_map(
        hosted_round if mesh.shape["dp"] == 4 and mesh.shape["tensor"] == 2 and mesh.shape["group"] % 2 == 0 else on_device,
        mesh=mesh,
        in_specs=placed,
        out_specs=(
            P(None, "group"),
            P(None, "group"),
            P(None, "group"),
            P("group", "dp"),
            P("group", "dp"),
            P("group", "tensor", "dp"),
            P("group", "tensor", "dp"),
            P("dp"),
            P("tensor", "dp"),
            P("dp"),
            P("tensor", "dp"),
            P("dp"),
            P("tensor", "dp"),
        ),
        check_vma=False,
    )
```

```python
import functools
import math

import jax
import jax.numpy as jnp
from jax import lax
from jax.experimental import pallas as pl
from jax.experimental.pallas import tpu as pltpu
from jax.sharding import PartitionSpec as P

D = 768
HDIM = 64
FF = 3072
DD = 384
DFF = 1536
PATCH = 1536
TUBES = 1568
FRAMES = 8
STEPS = 2
STEP_BEFORE = 6


CLIP = 0.001
LR_IN = 0.01
BETA1 = 0.9
BETA2 = 0.95
EPS = 1e-08
DECAY = 0.05
LR_OUT = 0.7
MOMENTUM = 0.9
FLOAT = jnp.float32
HALF = jnp.bfloat16


def sinus(count, width):
    places = jnp.arange(count).astype(jnp.float32)[:, None]
    column = jnp.arange(width)
    decays = jnp.power(10000.0, -2.0 * (column // 2).astype(jnp.float32) / width)
    angles = places * decays[None, :]
    return jnp.where(column % 2 == 0, jnp.sin(angles), jnp.cos(angles))


def layer_norm(stream, gain, bias):
    center = jnp.mean(stream, -1, keepdims=True)
    spread = jnp.mean((stream - center) ** 2, -1, keepdims=True)
    return (stream - center) * lax.rsqrt(spread + 1e-06) * gain + bias


def norm_back(stream, gain, bias, cotangent):
    _, pull = jax.vjp(layer_norm, stream, gain, bias)
    return pull(cotangent)


def gelu_exact(values):
    return jax.nn.gelu(values, approximate=False)


def split_flat(flat, shapes):
    pieces = []
    offset = 0
    for shapes_one in shapes:
        length = math.prod(shapes_one)
        pieces.append(flat[offset : offset + length].reshape(shapes_one))
        offset += length
    return pieces


def own_rows(stream, axis_dim):
    count = stream.shape[axis_dim] // lax.axis_size("tensor")
    return lax.dynamic_slice_in_dim(stream, lax.axis_index("tensor") * count, count, axis_dim)


def rows_sum(partial_rows):
    return lax.psum_scatter(partial_rows, "tensor", scatter_dimension=1, tiled=True)


def rows_full(own_part):
    return lax.all_gather(own_part, "tensor", axis=1, tiled=True)


def block_forward(stream, mats, vecs):
    w_qkv, w_out, w_up, w_down = mats
    gain_one, bias_one, out_bias, gain_two, bias_two, down_bias = vecs
    nclips, length, _ = stream.shape
    head_cols = w_out.shape[0]
    nheads = head_cols // HDIM
    normed = layer_norm(stream, gain_one, bias_one).astype(HALF)
    joined = jnp.dot(normed, w_qkv, preferred_element_type=FLOAT).astype(HALF)
    queries, key_rows, values = [
        joined[:, :, third_id * head_cols : (third_id + 1) * head_cols].reshape(
            nclips, length, nheads, HDIM
        )
        for third_id in range(3)
    ]
    scores = jnp.einsum(
        "cqhd,ckhd->chqk", queries, key_rows, preferred_element_type=FLOAT
    ) * HDIM ** (-0.5)
    highest = jnp.max(scores, -1, keepdims=True)
    totals = jnp.log(jnp.sum(jnp.exp(scores - highest), -1, keepdims=True)) + highest
    probs_low = jnp.exp(scores - totals).astype(HALF)
    blended = (
        jnp.einsum("chqk,ckhd->cqhd", probs_low, values, preferred_element_type=FLOAT)
        .astype(HALF)
        .reshape(nclips, length, head_cols)
    )
    attended = (
        rows_sum(jnp.dot(blended, w_out, preferred_element_type=FLOAT))
        + own_rows(stream, 1)
        + out_bias
    )
    second = layer_norm(attended, gain_two, bias_two).astype(HALF)
    second_all = lax.all_gather(second, "tensor", axis=1, tiled=True)
    upward = jnp.dot(second_all, w_up, preferred_element_type=FLOAT)
    activated = gelu_exact(upward).astype(HALF)
    result = (
        rows_sum(jnp.dot(activated, w_down, preferred_element_type=FLOAT)) + attended + down_bias
    )
    stored = (
        stream,
        normed,
        queries,
        key_rows,
        values,
        totals,
        blended,
        attended,
        second_all,
        upward,
        activated,
    )
    return (rows_full(result), stored)


def block_backward(grad_out, mats, vecs, stored):
    w_qkv, w_out, w_up, w_down = mats
    gain_one, bias_one, out_bias, gain_two, bias_two, down_bias = vecs
    (
        stream,
        normed,
        queries,
        key_rows,
        values,
        totals,
        blended,
        attended,
        second_all,
        upward,
        activated,
    ) = stored
    nclips, length, _ = stream.shape
    head_cols = w_out.shape[0]
    grad_low = grad_out.astype(HALF)
    grad_down = jnp.einsum("ctf,ctd->fd", activated, grad_low, preferred_element_type=FLOAT)
    down_bias_grad = jnp.sum(own_rows(grad_out, 1), (0, 1))
    grad_act = jnp.dot(grad_low, w_down.T, preferred_element_type=FLOAT)
    _, gelu_pull = jax.vjp(gelu_exact, upward)
    grad_up_in = gelu_pull(grad_act)[0].astype(HALF)
    grad_up = jnp.einsum("ctd,ctf->df", second_all, grad_up_in, preferred_element_type=FLOAT)
    grad_second = rows_sum(jnp.dot(grad_up_in, w_up.T, preferred_element_type=FLOAT))
    grad_att, gain_two_grad, bias_two_grad = norm_back(attended, gain_two, bias_two, grad_second)
    grad_att = grad_att + own_rows(grad_out, 1)
    out_bias_grad = jnp.sum(grad_att, (0, 1))
    grad_mid = rows_full(grad_att)
    mid_low = grad_mid.astype(HALF)
    grad_wout = jnp.einsum("cth,ctd->hd", blended, mid_low, preferred_element_type=FLOAT)
    nheads = head_cols // HDIM
    grad_blend = (
        jnp.dot(mid_low, w_out.T, preferred_element_type=FLOAT)
        .astype(HALF)
        .reshape(nclips, length, nheads, HDIM)
    )
    scores = jnp.einsum(
        "cqhd,ckhd->chqk", queries, key_rows, preferred_element_type=FLOAT
    ) * HDIM ** (-0.5)
    probs_full = jnp.exp(scores - totals)
    probs_low = probs_full.astype(HALF)
    grad_values = jnp.einsum("chqk,cqhd->ckhd", probs_low, grad_blend, preferred_element_type=FLOAT)
    grad_probs = jnp.einsum("cqhd,ckhd->chqk", grad_blend, values, preferred_element_type=FLOAT)
    grad_scores = (
        probs_full * (grad_probs - jnp.sum(probs_full * grad_probs, -1, keepdims=True))
    ).astype(HALF)
    grad_queries = jnp.einsum(
        "chqk,ckhd->cqhd", grad_scores, key_rows, preferred_element_type=FLOAT
    ) * HDIM ** (-0.5)
    grad_keys = jnp.einsum(
        "chqk,cqhd->ckhd", grad_scores, queries, preferred_element_type=FLOAT
    ) * HDIM ** (-0.5)
    grad_joined = jnp.concatenate(
        [
            part_grad.reshape(nclips, length, head_cols)
            for part_grad in (grad_queries, grad_keys, grad_values)
        ],
        -1,
    ).astype(HALF)
    grad_qkv = jnp.einsum("ctd,cte->de", normed, grad_joined, preferred_element_type=FLOAT)
    grad_norm_in = rows_sum(jnp.dot(grad_joined, w_qkv.T, preferred_element_type=FLOAT))
    grad_in, gain_one_grad, bias_one_grad = norm_back(
        own_rows(stream, 1), gain_one, bias_one, grad_norm_in
    )
    grad_in = grad_in + grad_att
    vec_grads = jnp.stack(
        [gain_one_grad, bias_one_grad, out_bias_grad, gain_two_grad, bias_two_grad, down_bias_grad]
    )
    return (rows_full(grad_in), (grad_qkv, grad_wout, grad_up, grad_down), vec_grads)


def group_step(patch_rows, visible_ids, shown, weight_rows, rep_full, ten_full):
    splits = lax.axis_size("tensor")
    patch_w, e2d_w, head_w, enc_vec, dec_vec, head_b = split_flat(
        rep_full, [(PATCH, D), (D, DD), (DD, PATCH), (9, D), (10, DD), (PATCH,)]
    )
    enc_vec = enc_vec.astype(FLOAT)
    dec_vec = dec_vec.astype(FLOAT)
    head_b = head_b.astype(FLOAT)
    enc_cols = D // splits
    dec_cols = DD // splits
    ten_pieces = split_flat(
        ten_full,
        [
            (D, 3 * enc_cols),
            (enc_cols, D),
            (D, FF // splits),
            (FF // splits, D),
            (DD, 3 * dec_cols),
            (dec_cols, DD),
            (DD, DFF // splits),
            (DFF // splits, DD),
        ],
    )
    enc_mats = ten_pieces[0:4]
    dec_mats = ten_pieces[4:8]
    enc_vecs = [enc_vec[i] for i in range(1, 7)]
    dec_vecs = [dec_vec[i] for i in range(2, 8)]
    shown_rows = jnp.take_along_axis(patch_rows, visible_ids[:, :, None], 1)
    embedded = (
        jnp.dot(shown_rows, patch_w, preferred_element_type=FLOAT)
        + enc_vec[0]
        + sinus(TUBES, D)[visible_ids]
    )
    encoded, enc_stored = block_forward(embedded, enc_mats, enc_vecs)
    final_enc = layer_norm(encoded, enc_vec[7], enc_vec[8]).astype(HALF)
    reduced = jnp.dot(final_enc, e2d_w, preferred_element_type=FLOAT) + dec_vec[0]
    blank = jnp.broadcast_to(dec_vec[1], (TUBES, DD))
    tokens_in = jax.vmap(lambda clip_ids, clip_rows: blank.at[clip_ids].set(clip_rows))(
        visible_ids, reduced
    ) + sinus(TUBES, DD)
    decoded, dec_stored = block_forward(tokens_in, dec_mats, dec_vecs)
    own_dec = own_rows(decoded, 1)
    final_low = layer_norm(own_dec, dec_vec[8], dec_vec[9]).astype(HALF)
    predicted = jnp.dot(final_low, head_w, preferred_element_type=FLOAT) + head_b
    pixels = own_rows(patch_rows, 1).astype(FLOAT)
    center = jnp.mean(pixels, -1, keepdims=True)
    spread = jnp.mean((pixels - center) ** 2, -1, keepdims=True)
    target = (pixels - center) * lax.rsqrt(spread + 1e-06)
    differ = predicted - target
    counted = own_rows(weight_rows, 1)
    loss_part = jnp.sum(jnp.mean(differ**2, -1) * counted)
    grad_pred = 2.0 / PATCH * differ * counted[:, :, None]
    pred_low = grad_pred.astype(HALF)
    head_w_grad = jnp.einsum("ctd,ctp->dp", final_low, pred_low, preferred_element_type=FLOAT)
    head_b_grad = jnp.sum(grad_pred, (0, 1))
    grad_final = jnp.dot(pred_low, head_w.T, preferred_element_type=FLOAT)
    grad_dec_own, dec_gain_grad, dec_bias_grad = norm_back(
        own_dec, dec_vec[8], dec_vec[9], grad_final
    )
    grad_tokens, dec_mat_grads, dec_vec_grads = block_backward(
        rows_full(grad_dec_own), dec_mats, dec_vecs, dec_stored
    )
    masked_own = own_rows(1.0 - shown.astype(FLOAT), 1)
    mask_grad = jnp.sum(own_rows(grad_tokens, 1) * masked_own[:, :, None], (0, 1))
    grad_reduced = own_rows(jnp.take_along_axis(grad_tokens, visible_ids[:, :, None], 1), 1)
    reduced_low = grad_reduced.astype(HALF)
    e2d_grad = jnp.einsum(
        "ctd,cte->de", own_rows(final_enc, 1), reduced_low, preferred_element_type=FLOAT
    )
    e2d_b_grad = jnp.sum(grad_reduced, (0, 1))
    grad_enc_final = jnp.dot(reduced_low, e2d_w.T, preferred_element_type=FLOAT)
    grad_enc_own, enc_gain_grad, enc_bias_grad = norm_back(
        own_rows(encoded, 1), enc_vec[7], enc_vec[8], grad_enc_final
    )
    grad_embedded, enc_mat_grads, enc_vec_grads = block_backward(
        rows_full(grad_enc_own), enc_mats, enc_vecs, enc_stored
    )
    own_embedded = own_rows(grad_embedded, 1)
    patch_grad = jnp.einsum(
        "ctp,ctd->pd",
        own_rows(shown_rows, 1),
        own_embedded.astype(HALF),
        preferred_element_type=FLOAT,
    )
    patch_b_grad = jnp.sum(own_embedded, (0, 1))
    enc_vec_grad = jnp.concatenate(
        [patch_b_grad[None], enc_vec_grads, enc_gain_grad[None], enc_bias_grad[None]], 0
    )
    dec_vec_grad = jnp.concatenate(
        [
            e2d_b_grad[None],
            mask_grad[None],
            dec_vec_grads,
            dec_gain_grad[None],
            dec_bias_grad[None],
        ],
        0,
    )
    rep_grad = jnp.concatenate(
        [
            patch_grad.reshape(-1),
            e2d_grad.reshape(-1),
            head_w_grad.reshape(-1),
            enc_vec_grad.reshape(-1),
            dec_vec_grad.reshape(-1),
            head_b_grad,
        ]
    )
    ten_grad = jnp.concatenate(
        [mat_grad.reshape(-1) for mat_grad in list(enc_mat_grads) + list(dec_mat_grads)]
    )
    return (loss_part, rep_grad, ten_grad)


def adamw(master, first, second, clipped, number):
    first = BETA1 * first + (1 - BETA1) * clipped
    second = BETA2 * second + (1 - BETA2) * clipped * clipped
    first_hat = first / (1 - BETA1**number)
    second_hat = second / (1 - BETA2**number)
    master = master - LR_IN * (first_hat / (jnp.sqrt(second_hat) + EPS) + DECAY * master)
    return (master, first, second)


def on_device(
    patches,
    visible,
    frames_valid,
    clip_valid,
    rep_weights,
    ten_weights,
    rep_m,
    rep_v,
    ten_m,
    ten_v,
    rep_outer,
    ten_outer,
):
    splits = lax.axis_size("tensor")
    owners = lax.axis_size("dp")
    tube_ids = jnp.arange(TUBES)
    rep_master, ten_master = (rep_weights, ten_weights[0])
    rep_first, rep_second = (rep_m[0], rep_v[0])
    ten_first, ten_second = (ten_m[0, 0], ten_v[0, 0])
    loss_list, count_list, norm_list = ([], [], [])
    for inner_step in range(STEPS):
        rep_full, ten_full = (
            lax.all_gather(rep_master.astype(HALF), "dp", axis=0, tiled=True),
            lax.all_gather(ten_master.astype(HALF), "dp", axis=0, tiled=True),
        )
        visible_ids = visible[inner_step, 0]
        shown = jnp.any(visible_ids[:, :, None] == tube_ids[None, None, :], axis=1)
        weight_rows = (
            jnp.where(shown, 0.0, 1.0)
            * (tube_ids[None, :] // (TUBES // FRAMES) < frames_valid[inner_step, 0][:, None])
            * (clip_valid[inner_step, 0][:, None] == 1)
        ).astype(FLOAT)
        count_part = jnp.sum(own_rows(weight_rows, 1))
        loss_part, rep_grad, ten_grad = group_step(
            patches[inner_step, 0], visible_ids, shown, weight_rows, rep_full, ten_full
        )
        rep_recv, ten_recv = (
            lax.all_to_all(
                rep_grad.reshape(owners, -1), "dp", split_axis=0, concat_axis=0, tiled=True
            ),
            lax.all_to_all(
                ten_grad.reshape(owners, -1), "dp", split_axis=0, concat_axis=0, tiled=True
            ),
        )
        rep_part = lax.psum(jnp.sum(rep_recv, 0), "tensor")
        ten_part = jnp.sum(ten_recv, 0)
        squares = jnp.sum(ten_part * ten_part) + jnp.sum(rep_part * rep_part) / splits
        square_all, loss_all, count_all = lax.psum(
            (squares, loss_part, count_part), ("dp", "tensor")
        )
        norm_value = jnp.sqrt(square_all + 1e-30) / count_all
        factor = jnp.minimum(1.0, CLIP / norm_value) / count_all
        number = STEP_BEFORE + inner_step + 1
        rep_master, rep_first, rep_second = adamw(
            rep_master, rep_first, rep_second, rep_part * factor, number
        )
        ten_master, ten_first, ten_second = adamw(
            ten_master, ten_first, ten_second, ten_part * factor, number
        )
        loss_list.append(loss_all)
        count_list.append(count_all)
        norm_list.append(norm_value)
    rep_sum, ten_sum = lax.psum((rep_weights - rep_master, ten_weights[0] - ten_master), "group")
    groups_count = lax.axis_size("group")
    rep_diff = rep_sum / groups_count
    ten_diff = ten_sum / groups_count
    rep_momentum = MOMENTUM * rep_outer + rep_diff
    ten_momentum = MOMENTUM * ten_outer[0] + ten_diff
    rep_new = rep_weights - LR_OUT * (rep_diff + MOMENTUM * rep_momentum)
    ten_new = ten_weights[0] - LR_OUT * (ten_diff + MOMENTUM * ten_momentum)
    return (
        jnp.stack(loss_list)[:, None],
        jnp.stack(count_list)[:, None],
        jnp.stack(norm_list)[:, None],
        rep_first[None],
        rep_second[None],
        ten_first[None, None],
        ten_second[None, None],
        rep_diff,
        ten_diff[None],
        rep_momentum,
        ten_momentum[None],
        rep_new,
        ten_new[None],
    )


TILE = 224


HOST = 1
LAST = 3
SWAP = [(0, 1), (1, 0)]
ENC_SHAPES = [(D, 3 * D // 2), (D // 2, D), (D, FF // 2), (FF // 2, D)]
DEC_SHAPES = [(DD, 3 * DD // 2), (DD // 2, DD), (DD, DFF // 2), (DFF // 2, DD)]
ENC_SIZE = sum(math.prod(one) for one in ENC_SHAPES)
DEC_SIZE = sum(math.prod(one) for one in DEC_SHAPES)
PATCH_SIZE = PATCH * D
E2D_SIZE = D * DD
HEAD_SIZE = DD * PATCH
ENC_VECS = 9 * D
DEC_VECS = 10 * DD


def hop(value, *moves):
    pairs = [(2 * a + b, 2 * c + d) for (a, b), (c, d) in moves]
    return lax.ppermute(value, ("dp", "tensor"), pairs)


def hop_both(value, *moves):
    return hop(value, *[((a, side), (b, side)) for a, b in moves for side in range(2)])


def swap(value, *where):
    if where:
        return hop(value, *[((z, side), (z, 1 - side)) for z in where for side in range(2)])
    return lax.ppermute(value, "tensor", SWAP)


def partner(value):
    count = lax.axis_size("group")
    return lax.ppermute(value, "group", [(g, g ^ 1) for g in range(count)])


def mm(left, right):
    return jnp.dot(left, right, preferred_element_type=FLOAT)


def mm_nt(left, right):
    return lax.dot_general(left, right, (((1,), (1,)), ((), ())), preferred_element_type=FLOAT)


def mm_tn(left, right):
    return lax.dot_general(left, right, (((0,), (0,)), ((), ())), preferred_element_type=FLOAT)


def sinus_parts(width):
    column = jnp.arange(width)
    decays = jnp.power(10000.0, -2.0 * (column // 2).astype(FLOAT) / width)
    far = (32 * jnp.arange(-(-TUBES // 32))).astype(FLOAT)[:, None] * decays
    near = jnp.arange(32).astype(FLOAT)[:, None] * decays
    even = column % 2 == 0
    near_one = jnp.where(even, jnp.cos(near), -jnp.sin(near))
    near_two = jnp.where(even, jnp.sin(near), jnp.cos(near))
    return jnp.concatenate([jnp.sin(far), jnp.cos(far)], 1), jnp.concatenate([near_one, near_two], 1)


def sinus_all(width):
    far, near = sinus_parts(width)
    table = far[:, None, :width] * near[None, :, :width] + far[:, None, width:] * near[None, :, width:]
    return table.reshape(-1, width)[:TUBES]


def thirds_of(rows):
    thirds = []
    for _ in range(3):
        thirds.append(lax.optimization_barrier(rows.astype(HALF)))
        rows = rows - thirds[-1].astype(FLOAT)
    return thirds


(
    QKV,
    SQUARE,
    UP,
    PATCH_ROWS,
    E2D,
    HEAD,
    VECS,
    DEC_QKV,
    DEC_OUT,
    DEC_UP,
    DEC_DOWN,
    HEAD_HALF,
    PATCH_LOW,
    PATCH_HIGH,
    W_QKV,
    W_OUT,
    W_UP,
    W_DOWN,
    E2D_W,
    HEAD_UP,
    SEND_ENC,
    SEND_MATE,
    CHAIN,
    CROSS,
    MATE_OWN,
    MATE_OTHER,
) = range(26)
PIECES = {
    QKV: (768, 1152),
    SQUARE: (1248, 768),
    UP: (672, 1536),
    PATCH_ROWS: (704, 768),
    E2D: (768, 384),
    HEAD: (64, 1536),
    VECS: (16, 768),
    DEC_QKV: (384, 576),
    DEC_OUT: (192, 384),
    DEC_UP: (384, 768),
    DEC_DOWN: (768, 384),
}


DEC_PARTS = [DEC_QKV, DEC_OUT, DEC_UP, DEC_DOWN, HEAD_HALF]
SENT = [QKV, SQUARE, UP, PATCH_ROWS, E2D, HEAD, VECS] + DEC_PARTS
ENC_PARTS = [
    (PATCH_LOW, 704, 0, PATCH_ROWS, 0),
    (W_QKV, 768, 0, QKV, 0),
    (W_OUT, 288, 0, SQUARE, 0),
    (W_OUT, 96, 1, SQUARE, 288),
    (PATCH_HIGH, 192, 2, PATCH_ROWS, 0),
    (W_UP, 672, 1, UP, 0),
    (W_UP, 96, 2, UP, 672),
    (W_DOWN, 1248, 2, SQUARE, 0),
    (W_DOWN, 288, 3, SQUARE, 1248),
    (E2D_W, 768, 2, E2D, 0),
]
MESH_ID = pl.DeviceIdType.MESH


VISIBLE = 160
OWN = 2 * VISIBLE
ALL = 4 * VISIBLE
SPAN = (0, 768, 1536)
DEPTH = (704, 704, 192)
WIDE = 1792
SQRT_HALF = 0.5**0.5


def norm_parts(x):
    center = jnp.mean(x, -1, keepdims=True)
    moved = x - center
    scale = lax.rsqrt(jnp.mean(moved * moved, -1, keepdims=True) + 1e-06)
    return moved * scale, scale


def norm_to(x, gain, bias):
    return norm_parts(x)[0] * gain + bias


def norm_from(x, gain, cotangent):
    hat, scale = norm_parts(x)
    inner = cotangent * gain
    grad = scale * (
        inner - jnp.mean(inner, -1, keepdims=True) - hat * jnp.mean(inner * hat, -1, keepdims=True)
    )
    return grad, jnp.sum(cotangent * hat, 0, keepdims=True), jnp.sum(cotangent, 0, keepdims=True)


def gelu_to(x):
    return 0.5 * x * (1.0 + lax.erf(x * SQRT_HALF))


def gelu_slope(x):
    return 0.5 * (1.0 + lax.erf(x * SQRT_HALF)) + x * jnp.exp(-0.5 * x * x) * (2.0 * math.pi) ** -0.5


def rows_at(index, count=VISIBLE):
    return pl.ds(index * count, count)


class Links:
    def __init__(self, send_sem, recv_sem):
        self.send_sem, self.recv_sem, self.keys = send_sem, recv_sem, {}

    def copy(self, key, source, target, peer):
        index = self.keys.setdefault(key, len(self.keys))
        return pltpu.make_async_remote_copy(
            src_ref=source,
            dst_ref=target,
            send_sem=self.send_sem.at[index],
            recv_sem=self.recv_sem.at[index],
            device_id=peer,
            device_id_type=MESH_ID,
        )


LANDED = [W_QKV, W_OUT, W_UP, W_DOWN, E2D_W, VECS]
LANDED_SHAPES = [(768, 1152), (384, 768), (768, 1536), (1536, 768), (768, 384), (16, 768)]
STORED = [
    ((OWN, D), FLOAT),
    ((ALL, D), HALF),
    ((ALL, 3 * D // 2), HALF),
    ((ALL, D // 2), HALF),
    ((OWN, D), FLOAT),
    ((ALL, D), HALF),
    ((ALL, FF // 2), FLOAT),
    ((ALL, FF // 2), HALF),
    ((OWN, D), FLOAT),
    ((OWN, D), HALF),
]


def forward_kernel(shared, *refs):
    sent, refs = dict(zip(SENT, refs[: len(SENT)])), refs[len(SENT) :]
    shown, ids, far_places, near_places, refs = refs[0], refs[1], refs[2], refs[3], refs[4:]
    got, refs = dict(zip(LANDED, refs[: len(LANDED)])), refs[len(LANDED) :]
    got[HEAD], reduced, refs = refs[0], refs[1], refs[2:]
    own, refs = dict(zip(DEC_PARTS, refs[: len(DEC_PARTS)])), refs[len(DEC_PARTS) :]
    other, refs = dict(zip(DEC_PARTS, refs[: len(DEC_PARTS)])), refs[len(DEC_PARTS) :]
    stream, normed, joined, blended, attended, second, upward, activated, encoded, final_enc = refs[:10]
    got[PATCH_LOW], patch_mid, got[PATCH_HIGH], part_sent, part_got, reduced_own, places = refs[10:17]
    send_sem, recv_sem, local_sem = refs[17:]
    g, z, x = lax.axis_index("group"), lax.axis_index("dp"), lax.axis_index("tensor")
    odd = lax.rem(g, 2)
    mate = (g + 1 - 2 * odd, z, x)
    across = (g, z, 1 - x)
    links = Links(send_sem, recv_sem)
    copy = links.copy
    barrier = pltpu.get_barrier_semaphore()

    def at(row, column=None):
        return (g, row, x if column is None else column)

    def greet(peer):
        pl.semaphore_signal(barrier, inc=1, device_id=peer, device_id_type=MESH_ID)

    greet(across)
    if shared:
        greet(mate)
    near = {0: [1], 1: [0, 2, 3], 2: [1, 3], 3: [2, 1]}
    for row, peers in near.items():

        @pl.when(z == row)
        def _():
            for peer in peers:
                greet(at(peer))
            if row != HOST:

                @pl.when(x != row // 2)
                def _():
                    greet(at(HOST, row // 2))

                pl.semaphore_wait(barrier, len(peers) + (2 if shared else 1))

    for column in range(2):

        @pl.when((z == HOST) & (x == column))
        def _():
            pl.semaphore_wait(barrier, 3 + (2 if shared else 1) + 1 + column)

    def part(ref, start, count, half, index=odd):
        if not half:
            return ref.at[pl.ds(start, count)]
        return ref.at[pl.ds(pl.multiple_of(start + index * (count // 2), 16), count // 2)]

    def twice(name):
        return not shared and name in (PATCH_LOW, PATCH_HIGH, E2D_W)

    keys = [(SEND_ENC, item[0], item[4]) for item in ENC_PARTS] + [(SEND_MATE, item[0], item[4]) for item in ENC_PARTS]
    for name in DEC_PARTS + [VECS, HEAD, HEAD_UP]:
        keys += [(label, name) for label in (CHAIN, CROSS, MATE_OWN, MATE_OTHER)]
    for key in keys + list(range(12)):
        links.keys[key] = len(links.keys)

    def enc_copy(item):
        name, count, owner, piece, first = item
        half, index = shared or twice(name), x if twice(name) else odd
        return copy(
            (SEND_ENC, name, first),
            part(sent[piece], 0, count, half, index),
            part(got[name], first, count, half, index),
            at(HOST),
        )

    def enc_mate(item):
        name, count, owner, piece, first = item
        half = part(got[name], first, count, True, x if twice(name) else odd)
        return copy((SEND_MATE, name, first), half, half, across if twice(name) else mate)

    def local(index, source, target):
        return pltpu.make_async_copy(source, target, local_sem.at[index])

    def chain(name, source, peer):
        target = got[name] if name in got else own[name]
        rows = source.shape[0]
        half = shared and name in own
        return copy((CHAIN, name), part(source, 0, rows, half), part(target, 0, rows, half), at(peer))

    def cross(name, source):
        rows = source.shape[0]
        return copy((CROSS, name), part(source, 0, rows, shared), part(other[name], 0, rows, shared), across)

    def mates(name, ref, label):
        half = part(ref, 0, ref.shape[0], True)
        return copy((label, name), half, half, mate)

    def owned(row):
        return [item for item in ENC_PARTS if item[2] == row and row != HOST]

    def head_up():
        return copy((CHAIN, HEAD_UP), sent[HEAD], got[HEAD], at(LAST))

    def finish_dec(name, source, here):
        cross(name, source).start()
        if shared and not here:
            mates(name, own[name], MATE_OWN).start()

    def end_all(source_of, here):
        for name in DEC_PARTS:
            cross(name, source_of[name]).wait()
            if shared:
                mates(name, other[name], MATE_OTHER).start()
        for name in DEC_PARTS:
            if shared:
                if not here:
                    mates(name, own[name], MATE_OWN).wait()
                mates(name, other[name], MATE_OTHER).wait()

    def give(column, clip):
        row = 2 * column + clip
        return [
            copy(8 + 2 * clip + side, reduced_own.at[clip], reduced, at(row, side))
            for side in range(2)
            if (row, side) != (HOST, column)
        ]

    @pl.when(z == LAST)
    def _():
        chain(VECS, sent[VECS], 2).start()
        locals_ = [local(i, sent[name], own[name]) for i, name in enumerate(DEC_PARTS)]
        locals_.append(local(len(DEC_PARTS), sent[VECS], got[VECS]))
        for one in locals_:
            one.start()
        for item in owned(LAST):
            enc_copy(item).start()
            enc_copy(item).wait_send()
        for i, name in enumerate(DEC_PARTS):
            chain(name, sent[name], 2).start()
            finish_dec(name, sent[name], True)
            if i:
                chain(DEC_PARTS[i - 1], sent[DEC_PARTS[i - 1]], 2).wait_send()
        chain(DEC_PARTS[-1], sent[DEC_PARTS[-1]], 2).wait_send()
        chain(VECS, sent[VECS], 2).wait_send()
        end_all(sent, True)
        for one in locals_:
            one.wait()
        head_up().wait_recv()

    @pl.when(z == 2)
    def _():
        first = local(0, sent[HEAD], got[HEAD])
        first.start()
        chain(VECS, sent[VECS], 2).wait_recv()
        chain(VECS, got[VECS], HOST).start()
        late = [item for item in owned(2) if item[0] == E2D_W]
        for item in owned(2):
            if item not in late:
                enc_copy(item).start()
                enc_copy(item).wait_send()
        head_up().start()
        chain(HEAD, sent[HEAD], HOST).start()
        for i, name in enumerate(DEC_PARTS):
            chain(name, sent[name], 2).wait_recv()
            chain(name, own[name], HOST).start()
            finish_dec(name, own[name], False)
            if i:
                chain(DEC_PARTS[i - 1], own[DEC_PARTS[i - 1]], HOST).wait_send()
        for item in late:
            enc_copy(item).start()
            enc_copy(item).wait_send()
        chain(DEC_PARTS[-1], own[DEC_PARTS[-1]], HOST).wait_send()
        end_all(own, False)
        chain(VECS, got[VECS], HOST).wait_send()
        chain(HEAD, sent[HEAD], HOST).wait_send()
        head_up().wait_send()
        first.wait()

    @pl.when(z == 0)
    def _():
        for item in owned(0):
            enc_copy(item).start()
            enc_copy(item).wait_send()
        for name in DEC_PARTS:
            chain(name, sent[name], 0).wait_recv()
            finish_dec(name, own[name], False)
        end_all(own, False)
        chain(VECS, sent[VECS], 0).wait_recv()
        chain(HEAD, sent[HEAD], 0).wait_recv()

    @pl.when(z == HOST)
    def _():
        mine = [
            local(i, sent[piece].at[pl.ds(0, count)], got[name].at[pl.ds(first, count)])
            for i, (name, count, owner, piece, first) in enumerate(ENC_PARTS)
            if owner == HOST
        ]
        mine.append(local(len(ENC_PARTS), sent[PATCH_ROWS], patch_mid))
        for one in mine:
            one.start()
        chain(VECS, sent[VECS], HOST).wait_recv()
        chain(VECS, got[VECS], 0).start()
        vec = got[VECS][...].astype(FLOAT)
        for one in mine:
            one.wait()

        def await_parts(names):
            items = [item for item in ENC_PARTS if item[2] != HOST and item[0] in names]
            for item in items:
                enc_copy(item).wait_recv()
                if shared or twice(item[0]):
                    enc_mate(item).start()
            for item in items:
                if shared or twice(item[0]):
                    enc_mate(item).wait()

        def pump(name):
            chain(name, sent[name], HOST).wait_recv()
            chain(name, own[name], 0).start()
            finish_dec(name, own[name], False)

        def normed_copy(i):
            return copy(i, normed.at[rows_at(i)], normed.at[rows_at(2 + i)], across)

        def out_copy(i):
            return copy(2 + i, part_sent.at[rows_at(i)], part_got.at[rows_at(i)], across)

        def second_copy(i):
            return copy(4 + i, second.at[rows_at(i)], second.at[rows_at(2 + i)], across)

        def down_copy(i):
            return copy(6 + i, part_sent.at[rows_at(2 + i)], part_got.at[rows_at(2 + i)], across)

        spots = lax.broadcasted_iota(jnp.int32, (OWN, 64), 1)
        high = ((ids[...] // 32) == spots).astype(FLOAT).astype(HALF)
        low_hot = (lax.rem(ids[...], 32) == spots).astype(FLOAT).astype(HALF)
        far = mm(high, far_places[0]) + mm(high, far_places[1]) + mm(high, far_places[2])
        near = mm(low_hot, near_places[0]) + mm(low_hot, near_places[1]) + mm(low_hot, near_places[2])
        places[...] = far[:, :D] * near[:, :D] + far[:, D:] * near[:, D:]
        await_parts((PATCH_LOW, PATCH_HIGH))
        for i in range(2):
            rows = rows_at(i)
            emb = places[rows] + vec[0:1]
            for start, depth, weight in zip(SPAN, DEPTH, (got[PATCH_LOW], patch_mid, got[PATCH_HIGH])):
                emb = emb + mm(shown[rows, start : start + depth], weight[...])
            stream[rows] = emb
            normed[rows] = norm_to(emb, vec[1:2], vec[2:3]).astype(HALF)
            normed_copy(i).start()
        await_parts((W_QKV,))

        def attend(c):
            rows = rows_at(c)
            joined[rows] = mm(normed[rows], got[W_QKV][...]).astype(HALF)
            width = D // 2
            for h in range(width // HDIM):
                column = h * HDIM
                queries = joined[rows, column : column + HDIM]
                keys = joined[rows, width + column : width + column + HDIM]
                values = joined[rows, 2 * width + column : 2 * width + column + HDIM]
                scores = mm_nt(queries, keys) * HDIM**-0.5
                weights = jnp.exp(scores - jnp.max(scores, -1, keepdims=True))
                probs = weights * (1.0 / jnp.sum(weights, -1, keepdims=True))
                blended[rows, column : column + HDIM] = mm(probs.astype(HALF), values).astype(HALF)

        for i in range(2):
            attend(i)
            if i == 0:
                await_parts((W_OUT,))
            attended[rows_at(i)] = mm(blended[rows_at(i)], got[W_OUT][...]) + stream[rows_at(i)] + vec[3:4]
            normed_copy(i).wait_recv()
            attend(2 + i)
            part_sent[rows_at(i)] = mm(blended[rows_at(2 + i)], got[W_OUT][...]).astype(HALF)
            out_copy(i).start()

        def feed(c):
            rows = rows_at(c)
            up = mm(second[rows], got[W_UP][...])
            upward[rows] = up
            activated[rows] = gelu_to(up).astype(HALF)
            return mm(activated[rows], got[W_DOWN][...])

        for i in range(2):
            rows = rows_at(i)
            out_copy(i).wait_recv()
            after = attended[rows] + part_got[rows].astype(FLOAT)
            attended[rows] = after
            second[rows] = norm_to(after, vec[4:5], vec[5:6]).astype(HALF)
            second_copy(i).start()
        await_parts((W_UP, W_DOWN))
        chain(HEAD, sent[HEAD], HOST).wait_recv()
        chain(HEAD, got[HEAD], 0).start()
        pump(DEC_QKV)
        pump(DEC_OUT)
        for i in range(2):
            rows = rows_at(i)
            encoded[rows] = feed(i) + attended[rows] + vec[6:7]
            second_copy(i).wait_recv()
            part_sent[rows_at(2 + i)] = feed(2 + i).astype(HALF)
            down_copy(i).start()
            pump((DEC_UP, DEC_DOWN)[i])
        pump(HEAD_HALF)
        await_parts((E2D_W,))
        for i in range(2):
            rows = rows_at(i)
            down_copy(i).wait_recv()
            after = encoded[rows] + part_got[rows_at(2 + i)].astype(FLOAT)
            encoded[rows] = after
            low = norm_to(after, vec[7:8], vec[8:9]).astype(HALF)
            final_enc[rows] = low
            reduced_own[i] = mm(low, got[E2D_W][...])
            for column in range(2):

                @pl.when(x == column)
                def _():
                    for one in give(column, i):
                        one.start()

        for i in range(2):
            normed_copy(i).wait_send()
            out_copy(i).wait_send()
            second_copy(i).wait_send()
            down_copy(i).wait_send()
        for column in range(2):

            @pl.when(x == column)
            def _():
                for i in range(2):
                    for one in give(column, i):
                        one.wait_send()

        end_all(own, False)
        for name in DEC_PARTS:
            chain(name, own[name], 0).wait_send()
        chain(VECS, got[VECS], 0).wait_send()
        chain(HEAD, got[HEAD], 0).wait_send()

    @pl.when((z == HOST) & (x == 0))
    def _():
        mine = local(0, reduced_own.at[1], reduced)
        mine.start()
        mine.wait()

    for row in range(4):
        for side in range(2):
            if (row, side) != (HOST, 0):

                @pl.when((z == row) & (x == side))
                def _():
                    key = 8 + 2 * (row % 2) + side
                    copy(key, reduced_own.at[row % 2], reduced, at(HOST, row // 2)).wait_recv()


def encoder_forward(number, shared, pieces, shown_own, ids_and_places):
    side = lax.axis_index("tensor")
    vmem = pl.BlockSpec(memory_space=pltpu.VMEM)
    anywhere = pl.BlockSpec(memory_space=pl.ANY)
    dec_shapes = [(pieces[name].shape, HALF) for name in DEC_PARTS]
    shapes = [(one, HALF) for one in LANDED_SHAPES] + [((64, PATCH), HALF), ((VISIBLE, DD), FLOAT)]
    shapes = shapes + 2 * dec_shapes + STORED
    count = 2 * len(ENC_PARTS) + 4 * (len(DEC_PARTS) + 3) + 12
    scratch = [
        ((704, D), HALF),
        ((704, D), HALF),
        ((192, D), HALF),
        ((ALL, D), HALF),
        ((ALL, D), HALF),
        ((2, VISIBLE, DD), FLOAT),
        ((OWN, D), FLOAT),
    ]
    out = pl.pallas_call(
        functools.partial(forward_kernel, shared),
        name="encoder_forward",
        out_shape=[jax.ShapeDtypeStruct(*one) for one in shapes],
        in_specs=[anywhere] * len(SENT) + [vmem] * 4,
        out_specs=[vmem] * len(LANDED) + [anywhere, vmem] + [anywhere] * (2 * len(DEC_PARTS)) + [vmem] * len(STORED),
        scratch_shapes=[pltpu.VMEM(*one) for one in scratch]
        + [
            pltpu.SemaphoreType.DMA((count,)),
            pltpu.SemaphoreType.DMA((count,)),
            pltpu.SemaphoreType.DMA((len(ENC_PARTS) + 1,)),
        ],
        compiler_params=pltpu.CompilerParams(
            collective_id=number, has_side_effects=True, vmem_limit_bytes=56 << 20
        ),
    )(*[pieces[name] for name in SENT], shown_own, *ids_and_places)
    landed, out = out[: len(LANDED)], out[len(LANDED) :]
    head, reduced, out = out[0], out[1], out[2:]
    own, other, stored = out[: len(DEC_PARTS)], out[len(DEC_PARTS) : 2 * len(DEC_PARTS)], out[2 * len(DEC_PARTS) :]
    low, high = jnp.where(side == 0, own[4], other[4]), jnp.where(side == 0, other[4], own[4])
    head_w = jnp.concatenate([low, high], 1)
    head_w = jnp.concatenate([head_w[:64] + head, head_w[64:]], 0)
    enc_vec, dec_vec, head_b = split_flat(landed[5].astype(FLOAT).reshape(-1), [(9, D), (10, DD), (PATCH,)])
    enc_weights = (landed[:4], landed[4], jnp.pad(enc_vec, ((0, 7), (0, 0))))
    return reduced, stored, enc_weights, (own[:4], other[:4], head_w, dec_vec, head_b)


def encoder_backward_kernel(
    picked, shown, shown_other, w_qkv, w_out, w_up, w_down, e2d_w, vec,
    stream, normed, joined, blended, attended, second, upward, activated, encoded, final_enc,
    wide, tall, dec_qkv, small, normed_far, active_far,
    qkv_out, square_out, up_out, patch_out, e2d_out, vec_out,
    one_wide, one_tall, one_qkv, one_small, two_wide, two_tall, two_qkv, two_small,
    wide_sent, tall_sent, dec_qkv_sent, small_sent, wide_got, tall_got, dec_qkv_got, small_got,
    picks_got, low, grad_up_in, mid, grad_blend, grad_joined, part_sent, part_got, own_rows_grad, own_part,
    emb_low, emb_got, down_grad, up_grad, out_grad, qkv_grad, patch_low, patch_mid, patch_high, e2d_part, e2d_got, e2d_grad,
    vec_part, vec_got, send_sem, recv_sem, local_sem,
):
    g, z, x = lax.axis_index("group"), lax.axis_index("dp"), lax.axis_index("tensor")
    barrier = pltpu.get_barrier_semaphore()
    links = Links(send_sem, recv_sem)

    def at(row, column):
        return (g, row, column)

    def greet(peer):
        pl.semaphore_signal(barrier, inc=1, device_id=peer, device_id_type=MESH_ID)

    @pl.when(z != HOST)
    def _():
        greet(at(HOST, x))

    @pl.when(z == LAST)
    def _():
        greet(at(2, x))

    @pl.when((z == HOST) & (x == 0))
    def _():
        for peer in ((0, 0), (0, 1), (HOST, 1)):
            greet(at(*peer))

    @pl.when((z == HOST) & (x == 1))
    def _():
        for peer in ((2, 0), (2, 1), (3, 0), (3, 1), (0, 1), (HOST, 0)):
            greet(at(*peer))

    @pl.when(z == HOST)
    def _():
        pl.semaphore_wait(barrier, 4)

    @pl.when((z == 2) | ((z == 0) & (x == 1)))
    def _():
        pl.semaphore_wait(barrier, 2)

    @pl.when((z == LAST) | ((z == 0) & (x == 0)))
    def _():
        pl.semaphore_wait(barrier, 1)

    def pick_copy(row, side):
        return links.copy((row % 2) * 2 + side, picked, picks_got.at[row % 2, side], at(HOST, row // 2))

    for row in range(4):
        for side in range(2):
            if (row, side) != (HOST, 0):

                @pl.when((z == row) & (x == side))
                def _():
                    pick_copy(row, side).start()

    numbers = iter(range(4, 64))
    low_number = [next(numbers), next(numbers)]
    second_number = [next(numbers), next(numbers)]
    mid_number = [next(numbers), next(numbers)]
    normed_number = [next(numbers), next(numbers)]
    emb_number = [next(numbers), next(numbers)]
    e2d_number, vec_number = next(numbers), next(numbers)

    def row_copies(numbers_two, ref):
        return [
            links.copy(numbers_two[i], ref.at[rows_at(i)], ref.at[rows_at(2 + i)], at(HOST, 1 - x)) for i in range(2)
        ]

    def part_copies(numbers_two, first):
        return [
            links.copy(
                numbers_two[i], part_sent.at[rows_at(first + i)], part_got.at[rows_at(first + i)], at(HOST, 1 - x)
            )
            for i in range(2)
        ]

    out_rows, up_rows, down_rows = 288, 672, 1248
    next_row = jnp.minimum(z + 1, LAST)
    low_far = [links.copy(next(numbers), low.at[rows_at(c)], low.at[rows_at(c)], at(2, x)) for c in range(4)]
    down_far = links.copy(next(numbers), down_grad.at[pl.ds(96, 288)], square_out.at[pl.ds(0, 288)], at(LAST, x))
    joined_far = [
        links.copy(next(numbers), grad_joined.at[rows_at(c)], grad_joined.at[rows_at(c)], at(0, x)) for c in range(4)
    ]
    up_near = links.copy(next(numbers), up_grad.at[pl.ds(up_rows, 96)], up_out.at[pl.ds(0, 96)], at(2, x))
    out_near = links.copy(
        next(numbers), out_grad.at[pl.ds(0, out_rows)], square_out.at[pl.ds(0, out_rows)], at(0, x)
    )
    patch_one = links.copy(next(numbers), patch_low, patch_out, at(0, x))
    patch_two = links.copy(next(numbers), patch_high, patch_out.at[pl.ds(0, 192)], at(2, x))
    e2d_near = links.copy(next(numbers), e2d_grad, e2d_out, at(2, x))
    vec_far = links.copy(next(numbers), vec_part, vec_out, at(LAST, x))

    own_dec = (wide, tall, dec_qkv, small)
    sent_dec = (wide_sent, tall_sent, dec_qkv_sent, small_sent)
    got_dec = (wide_got, tall_got, dec_qkv_got, small_got)
    one_dec = (one_wide, one_tall, one_qkv, one_small)
    two_dec = (two_wide, two_tall, two_qkv, two_small)
    tree_one = [links.copy(next(numbers), sent_dec[i], got_dec[i], at(next_row, x)) for i in range(4)]
    tree_two = [links.copy(next(numbers), sent_dec[i], two_dec[i], at(LAST, x)) for i in range(4)]

    @pl.when((z == 0) | (z == 2))
    def _():
        for i in (3, 0, 1, 2):
            sent_dec[i][...] = own_dec[i][...].astype(sent_dec[i].dtype)
        for i in (3, 0, 1, 2):
            tree_one[i].start()
            if i != 3:
                tree_one[i].wait_send()

    def pass_on(*parts):
        for i in parts:
            tree_one[i].wait_recv()
            sent_dec[i][...] = (own_dec[i][...] + got_dec[i][...].astype(FLOAT)).astype(sent_dec[i].dtype)
            tree_two[i].start()

    def tall_product(left, right, target, step):
        def body(t, carry):
            columns = pl.ds(pl.multiple_of(t * step, step), step)
            target[columns] = mm_tn(left[:, columns], right[...]).astype(HALF)
            return carry

        lax.fori_loop(0, target.shape[0] // step, body, 0)

    @pl.when(z == HOST)
    def _():
        low_sent, mid_sent = row_copies(low_number, low), row_copies(mid_number, mid)
        second_sent, normed_sent = part_copies(second_number, 0), part_copies(normed_number, 2)
        emb_sent = [
            links.copy(
                emb_number[i],
                emb_low.at[1 - x, rows_at(i)],
                emb_got.at[rows_at(i)],
                at(HOST, 1 - x),
            )
            for i in range(2)
        ]
        e2d_sent = links.copy(e2d_number, e2d_part.at[1 - x], e2d_got, at(HOST, 1 - x))
        vec_sent = links.copy(vec_number, vec_part, vec_got, at(HOST, 1 - x))

        vec_part[...] = jnp.zeros_like(vec_part)

        def count(row, value):
            vec_part[row : row + 1] += value

        @pl.when(x == 0)
        def _():
            mine = pltpu.make_async_copy(picked, picks_got.at[1, 0], local_sem.at[0])
            mine.start()
            mine.wait()

        for clip in range(2):
            for side in range(2):
                waiting = links.copy(clip * 2 + side, picked, picks_got.at[clip, side], at(HOST, 0))
                if clip == HOST % 2 and side == 0:

                    @pl.when(x == 1)
                    def _():
                        waiting.wait_recv()

                else:
                    waiting.wait_recv()
        reduced_low = []
        for i in range(2):
            rows = rows_at(i)
            one = picks_got[i, 0] + picks_got[i, 1]
            reduced_low.append(one)
            grad, gain, bias = norm_from(encoded[rows], vec[7:8], mm_nt(one, e2d_w[...]))
            count(7, gain)
            count(8, bias)
            count(6, jnp.sum(grad, 0, keepdims=True))
            own_rows_grad[rows] = grad
            low[rows] = grad.astype(HALF)
            low_sent[i].start()
            low_far[i].start()
        whole_low = jnp.concatenate(reduced_low, 0)
        product = mm_tn(final_enc[...], whole_low).astype(HALF)
        e2d_part[0] = product[: D // 2]
        e2d_part[1] = product[D // 2 :]
        e2d_sent.start()

        def feed_back(c):
            rows = rows_at(c)
            grad_up_in[rows] = (mm_nt(low[rows], w_down[...]) * gelu_slope(upward[rows])).astype(HALF)
            return mm_nt(grad_up_in[rows], w_up[...])

        for i in range(2):
            own_part[rows_at(i)] = feed_back(i)
            low_sent[i].wait_recv()
            low_far[2 + i].start()
            part_sent[rows_at(i)] = feed_back(2 + i).astype(HALF)
            second_sent[i].start()
        down_grad[pl.ds(0, 384)] = mm_tn(activated[:, 1152:], low[...]).astype(HALF)
        down_far.start()
        for i in range(2):
            rows = rows_at(i)
            second_sent[i].wait_recv()
            total = own_part[rows] + part_got[rows].astype(FLOAT)
            grad, gain, bias = norm_from(attended[rows], vec[4:5], total)
            count(4, gain)
            count(5, bias)
            grad = grad + own_rows_grad[rows]
            count(3, jnp.sum(grad, 0, keepdims=True))
            own_rows_grad[rows] = grad
            mid[rows] = grad.astype(HALF)
            mid_sent[i].start()
        e2d_sent.wait()
        e2d_grad[...] = (e2d_part[x].astype(FLOAT) + e2d_got[...].astype(FLOAT)).astype(HALF)
        e2d_near.start()

        def attend_back(c):
            rows = rows_at(c)
            width = D // 2
            grad_blend[...] = mm_nt(mid[rows], w_out[...]).astype(HALF)
            for h in range(width // HDIM):
                column = h * HDIM
                queries = joined[rows, column : column + HDIM]
                keys = joined[rows, width + column : width + column + HDIM]
                values = joined[rows, 2 * width + column : 2 * width + column + HDIM]
                grads = grad_blend[:, column : column + HDIM]
                scores = mm_nt(queries, keys) * HDIM**-0.5
                weights = jnp.exp(scores - jnp.max(scores, -1, keepdims=True))
                probs = weights * (1.0 / jnp.sum(weights, -1, keepdims=True))
                grad_values = mm_tn(probs.astype(HALF), grads)
                grad_probs = mm_nt(grads, values)
                grad_scores = (
                    probs * (grad_probs - jnp.sum(probs * grad_probs, -1, keepdims=True))
                ).astype(HALF)
                for third, value in enumerate(
                    (mm(grad_scores, keys) * HDIM**-0.5, mm_tn(grad_scores, queries) * HDIM**-0.5, grad_values)
                ):
                    start = third * width + column
                    grad_joined[rows, start : start + HDIM] = value.astype(HALF)
            return mm_nt(grad_joined[rows], w_qkv[...])

        for i in range(2):
            own_part[rows_at(i)] = attend_back(i)
            joined_far[i].start()
            pass_on(*((3, 0), (1,))[i])
            mid_sent[i].wait_recv()
            part_sent[rows_at(2 + i)] = attend_back(2 + i).astype(HALF)
            normed_sent[i].start()
            joined_far[2 + i].start()
        pass_on(2)
        tall_product(blended, mid, out_grad, 384)
        out_near.start()
        for i in range(2):
            rows = rows_at(i)
            normed_sent[i].wait_recv()
            total = own_part[rows] + part_got[rows_at(2 + i)].astype(FLOAT)
            grad, gain, bias = norm_from(stream[rows], vec[1:2], total)
            count(1, gain)
            count(2, bias)
            grad = grad + own_rows_grad[rows]
            count(0, jnp.sum(grad, 0, keepdims=True))
            grad_low = grad.astype(HALF)
            emb_low[0, rows] = grad_low[:, : D // 2]
            emb_low[1, rows] = grad_low[:, D // 2 :]
            emb_sent[i].start()
        vec_sent.start()
        tall_product(second, grad_up_in, up_grad, 384)
        up_near.start()
        for one in emb_sent:
            one.wait()
        for start, depth, target in zip(SPAN, DEPTH, (patch_low, patch_mid, patch_high)):
            columns = slice(start, start + depth)
            target[...] = (mm_tn(shown[:, columns], emb_low[x]) + mm_tn(shown_other[:, columns], emb_got[...])).astype(HALF)
        patch_one.start()
        patch_two.start()
        vec_sent.wait()
        vec_part[...] += vec_got[...]
        vec_far.start()
        mine = [
            pltpu.make_async_copy(out_grad.at[pl.ds(out_rows, 96)], square_out.at[pl.ds(0, 96)], local_sem.at[1]),
            pltpu.make_async_copy(up_grad.at[pl.ds(0, up_rows)], up_out, local_sem.at[2]),
            pltpu.make_async_copy(patch_mid, patch_out, local_sem.at[3]),
        ]
        for one in mine:
            one.start()
        for one in low_sent + mid_sent + second_sent + normed_sent:
            one.wait_send()
        for one in (*low_far, down_far, *joined_far, up_near, out_near, patch_one, patch_two, e2d_near, vec_far):
            one.wait_send()
        for one in tree_two:
            one.wait_send()
        for one in mine:
            one.wait()

    for row in range(4):
        for side in range(2):
            if (row, side) != (HOST, 0):

                @pl.when((z == row) & (x == side))
                def _():
                    pick_copy(row, side).wait_send()

    for row, ones in ((0, (out_near, patch_one)), (2, (up_near, patch_two, e2d_near)), (LAST, (down_far, vec_far))):

        @pl.when(z == row)
        def _():
            for one in ones:
                one.wait_recv()

    @pl.when((z == 0) | (z == 2))
    def _():
        tree_one[3].wait_send()

    @pl.when(z == 2)
    def _():
        for one in low_far:
            one.wait_recv()
        tall_product(active_far, low, down_grad, 384)
        kept = pltpu.make_async_copy(down_grad.at[pl.ds(0, down_rows)], square_out, local_sem.at[0])
        kept.start()
        kept.wait()

    @pl.when(z == 0)
    def _():
        for one in joined_far:
            one.wait_recv()
        tall_product(normed_far, grad_joined, qkv_grad, 384)
        kept = pltpu.make_async_copy(qkv_grad, qkv_out, local_sem.at[0])
        kept.start()
        kept.wait()

    @pl.when(z == LAST)
    def _():
        kept = []
        for i in range(4):
            tree_one[i].wait_recv()
            kept.append(pltpu.make_async_copy(got_dec[i], one_dec[i], local_sem.at[i]))
            kept[i].start()
        for i in range(4):
            tree_two[i].wait_recv()
            kept[i].wait()


def encoder_backward(number, picked, shown, weights, stored, dec_grads, far):
    mats, e2d_w, vec = weights
    vmem = pl.BlockSpec(memory_space=pltpu.VMEM)
    anywhere = pl.BlockSpec(memory_space=pl.ANY)
    shapes = [
        ((D, 3 * D // 2), HALF),
        ((1248, D), HALF),
        ((672, FF // 2), HALF),
        ((704, D // 2), HALF),
        ((D // 2, DD), HALF),
        ((16, D), FLOAT),
    ]
    tree = [(one.shape, HALF) for one in dec_grads[:3]] + [(dec_grads[3].shape, FLOAT)]
    shapes = shapes + 2 * tree
    scratch = 2 * tree + [
        ((2, 2, VISIBLE, DD), HALF),
        ((ALL, D), HALF),
        ((ALL, FF // 2), HALF),
        ((ALL, D), HALF),
        ((VISIBLE, D // 2), HALF),
        ((ALL, 3 * D // 2), HALF),
        ((ALL, D), HALF),
        ((ALL, D), HALF),
        ((OWN, D), FLOAT),
        ((OWN, D), FLOAT),
        ((2, OWN, D // 2), HALF),
        ((OWN, D // 2), HALF),
        ((FF // 2, D), HALF),
        ((D, FF // 2), HALF),
        ((D // 2, D), HALF),
        ((D, 3 * D // 2), HALF),
        ((704, D // 2), HALF),
        ((704, D // 2), HALF),
        ((192, D // 2), HALF),
        ((2, D // 2, DD), HALF),
        ((D // 2, DD), HALF),
        ((D // 2, DD), HALF),
        ((16, D), FLOAT),
        ((16, D), FLOAT),
    ]
    return pl.pallas_call(
        encoder_backward_kernel,
        name="encoder_backward",
        out_shape=[jax.ShapeDtypeStruct(*one) for one in shapes],
        in_specs=[vmem] * 25,
        out_specs=[anywhere] * len(shapes),
        scratch_shapes=[pltpu.VMEM(*one) for one in scratch]
        + [pltpu.SemaphoreType.DMA((44,)), pltpu.SemaphoreType.DMA((44,)), pltpu.SemaphoreType.DMA((4,))],
        compiler_params=pltpu.CompilerParams(
            collective_id=number, has_side_effects=True, vmem_limit_bytes=60 << 20
        ),
    )(picked, *shown, *mats, e2d_w, vec, *stored, *dec_grads, *far)


LANES = 128
STEP_ROWS = 96
TEN_LANES = 8640
REP_LANES = 4056
LAID = [QKV, SQUARE, UP, PATCH_ROWS, E2D, HEAD, VECS, DEC_QKV, DEC_OUT, DEC_UP, DEC_DOWN, HEAD_HALF]
LAID_SHAPES = {**PIECES, HEAD_HALF: (384, 768)}
TEN_PLACES = [
    [(QKV, 768, 0), (SQUARE, 288, 6912)],
    [(SQUARE, 96, 0), (UP, 672, 576)],
    [(UP, 96, 0), (SQUARE, 1248, 1152)],
    [(SQUARE, 288, 0), (DEC_OUT, 192, 3456), (DEC_UP, 384, 4032), (DEC_DOWN, 768, 6336)],
]
DEC_QKV_PLACE = 1728
PATCH_COUNTS = (676, 676, 184)
E2D_PLACE = 1104
HEAD_PLACE = 3408
HEAD_TOP = 54
VEC_PLACE = 3960


def spread_rows(flat, place, blocks, count, read):
    def put(first, value):
        rows = value.shape[0]
        for j in range(blocks):
            flat[pl.ds(place + first * blocks + j, rows, stride=blocks), :] = value[:, j * LANES : (j + 1) * LANES]

    def body(t, carry):
        put(t * STEP_ROWS, read(pl.multiple_of(t * STEP_ROWS, 16), STEP_ROWS))
        return carry

    whole = count // STEP_ROWS
    if whole:
        lax.fori_loop(0, whole, body, 0)
    rest = count - whole * STEP_ROWS
    if rest:
        put(whole * STEP_ROWS, read(whole * STEP_ROWS, -(-rest // 16) * 16)[:rest])


def gather_rows(piece, flat, place, blocks, count):
    def put(first, rows, padded):
        for j in range(blocks):
            value = flat[pl.ds(place + first * blocks + j, rows, stride=blocks), :]
            if padded > rows:
                value = jnp.concatenate([value, jnp.zeros((padded - rows, LANES), FLOAT)], 0)
            piece[pl.ds(first, padded), j * LANES : (j + 1) * LANES] = value.astype(HALF)

    def body(t, carry):
        put(pl.multiple_of(t * STEP_ROWS, 16), STEP_ROWS, STEP_ROWS)
        return carry

    whole = count // STEP_ROWS
    if whole:
        lax.fori_loop(0, whole, body, 0)
    rest = count - whole * STEP_ROWS
    if rest:
        put(whole * STEP_ROWS, rest, -(-rest // 16) * 16)


def lay_out(z, x, ten, rep, pieces, wide_rows):
    for row in range(4):

        @pl.when(z == row)
        def _():
            for name, count, place in TEN_PLACES[row]:
                gather_rows(pieces[name], ten, place, PIECES[name][1] // LANES, count)
            if row < LAST:
                gather_rows(pieces[PATCH_ROWS], rep, 0, D // LANES, PATCH_COUNTS[row])
            if row < 2:
                pieces[PATCH_ROWS][pl.ds(688, 16)] = jnp.zeros((16, D), HALF)
            if row == 2:
                gather_rows(pieces[E2D], rep, E2D_PLACE, DD // LANES, D)
                gather_rows(pieces[HEAD], rep, HEAD_PLACE, PATCH // LANES, HEAD_TOP)
            if row == LAST:
                gather_rows(pieces[VECS], rep, VEC_PLACE, D // LANES, 16)
                for j in range(4):
                    wide_rows[j, pl.ds(0, 192, stride=2), :] = ten[pl.ds(DEC_QKV_PLACE + j, 192, stride=9), :]
                middle = ten[pl.ds(DEC_QKV_PLACE + 4, 192, stride=9), :]
                late = [middle[:, 64:]] + [ten[pl.ds(DEC_QKV_PLACE + 5 + j, 192, stride=9), :] for j in range(4)]
                late = jnp.concatenate(late + [jnp.zeros((192, 64), FLOAT)], 1)
                wide_rows[4, pl.ds(0, 192, stride=2), :] = middle
                for j in range(5):
                    columns = slice(j * LANES, (j + 1) * LANES)
                    wide_rows[j, pl.ds(1, 192, stride=2), :] = late[:, columns]
                for j in range(4):
                    columns = slice(j * LANES, (j + 1) * LANES)
                    pieces[DEC_QKV][:, columns] = wide_rows[j].astype(HALF)
                pieces[DEC_QKV][:, 512:576] = wide_rows[4][:, :64].astype(HALF)
                half = pieces[HEAD_HALF]
                blocks, offset = PATCH // LANES, x * 6
                half[pl.ds(0, 48)] = jnp.zeros((48, D), HALF)
                for j in range(6):
                    columns = slice(j * LANES, (j + 1) * LANES)
                    value = rep[pl.ds(offset + j, 42, stride=blocks), :]
                    half[pl.ds(48, 48), columns] = jnp.concatenate(
                        [jnp.zeros((6, LANES), FLOAT), value], 0
                    ).astype(HALF)
                    for t in range(1, 4):
                        value = rep[pl.ds((96 * t - HEAD_TOP) * blocks + offset + j, 96, stride=blocks), :]
                        half[pl.ds(96 * t, 96), columns] = value.astype(HALF)


def lay_out_kernel(ten, rep, *refs):
    pieces = dict(zip(LAID, refs))
    lay_out(lax.axis_index("dp"), lax.axis_index("tensor"), ten, rep, pieces, refs[len(LAID)])


def first_pieces(ten, rep):
    vmem = pl.BlockSpec(memory_space=pltpu.VMEM)
    out = pl.pallas_call(
        lay_out_kernel,
        name="lay_out",
        out_shape=[jax.ShapeDtypeStruct(LAID_SHAPES[name], HALF) for name in LAID],
        in_specs=[vmem] * 2,
        out_specs=[vmem] * len(LAID),
        scratch_shapes=[pltpu.VMEM((5, 384, LANES), FLOAT)],
        compiler_params=pltpu.CompilerParams(vmem_limit_bytes=61 << 20),
    )(ten, rep)
    return dict(zip(LAID, out))


def update_kernel(
    number, last,
    stats, qkv, square, up, patch, e2d, vec, wide, tall, dec_qkv, small,
    one_wide, one_tall, one_qkv, one_small, two_wide, two_tall, two_qkv, two_small,
    *refs,
):
    masters, refs = refs[:6], refs[6:]
    stats_out, outs, refs = refs[0], refs[1:7], refs[7:]
    pieces = {}
    if not last:
        pieces, refs = dict(zip(LAID, refs)), refs[len(LAID) :]
    held, refs = refs[:6], refs[6:]
    grad_ten, grad_rep, wide_rows, patch_other, e2d_other, head_own, head_other, slots, send_sem, recv_sem, local_sem = refs
    g, z, x = lax.axis_index("group"), lax.axis_index("dp"), lax.axis_index("tensor")
    me = 2 * z + x
    links = Links(send_sem, recv_sem)
    barrier = pltpu.get_barrier_semaphore()
    loads = [pltpu.make_async_copy(masters[i], held[i], local_sem.at[i]) for i in range(6)]
    for one in loads:
        one.start()

    def peer(shift):
        other = lax.rem(me + shift, 8)
        return (g, other // 2, lax.rem(other, 2))

    for shift in range(1, 8):
        pl.semaphore_signal(barrier, inc=1, device_id=peer(shift), device_id_type=MESH_ID)
    pl.semaphore_wait(barrier, 7)

    across = (g, z, 1 - x)
    patch_swap = links.copy(0, patch, patch_other, across)
    e2d_swap = links.copy(1, e2d, e2d_other, across)
    head_swap = links.copy(2, head_own, head_other, across)
    top_own = links.copy(3, head_own.at[pl.ds(0, 64)], head_own.at[pl.ds(0, 64)], (g, 2, x))
    top_other = links.copy(4, head_other.at[pl.ds(0, 64)], head_other.at[pl.ds(0, 64)], (g, 2, x))

    def plain(ref):
        return lambda first, rows: ref[pl.ds(first, rows)].astype(FLOAT)

    def joined(own, other):
        def read(first, rows):
            one, two = own[pl.ds(first, rows)].astype(FLOAT), other[pl.ds(first, rows)].astype(FLOAT)
            return jnp.concatenate([jnp.where(x == 0, one, two), jnp.where(x == 0, two, one)], 1)

        return read

    def total(own, one, two, top, columns):
        def read(first, rows):
            at = pl.ds(top + first, rows)
            return own[at, columns] + one[at, columns].astype(FLOAT) + two[at, columns].astype(FLOAT)

        return read

    @pl.when(z < LAST)
    def _():
        patch_swap.start()

    @pl.when(z == 2)
    def _():
        e2d_swap.start()

    fc = DFF // 2

    @pl.when(z == LAST)
    def _():
        head_own[...] = total(wide, one_wide, two_wide, 0, slice(fc, 2 * fc))(0, DD).astype(HALF)
        head_swap.start()
        top_own.start()
        whole = slice(0, DD)
        spread_rows(grad_ten, 0, 6, 288, plain(square))
        spread_rows(grad_ten, 3456, 3, 192, total(tall, one_tall, two_tall, fc, whole))
        spread_rows(grad_ten, 4032, 6, 384, total(wide, one_wide, two_wide, 0, slice(0, fc)))
        spread_rows(grad_ten, 6336, 3, 768, total(tall, one_tall, two_tall, 0, whole))
        for j in range(4):
            columns = slice(j * LANES, (j + 1) * LANES)
            wide_rows[j] = total(dec_qkv, one_qkv, two_qkv, 0, columns)(0, DD)
        tail = total(dec_qkv, one_qkv, two_qkv, 0, slice(512, 576))(0, DD)
        wide_rows[4] = jnp.concatenate([tail, jnp.zeros((DD, 64), FLOAT)], 1)
        for j in range(4):
            grad_ten[pl.ds(DEC_QKV_PLACE + j, 192, stride=9), :] = wide_rows[j, pl.ds(0, 192, stride=2), :]
        late = jnp.concatenate([wide_rows[j, pl.ds(1, 192, stride=2), :] for j in range(5)], 1)
        early = wide_rows[4, pl.ds(0, 192, stride=2), :]
        grad_ten[pl.ds(DEC_QKV_PLACE + 4, 192, stride=9), :] = jnp.concatenate([early[:, :64], late[:, :64]], 1)
        for j in range(4):
            start = 64 + j * LANES
            grad_ten[pl.ds(DEC_QKV_PLACE + 5 + j, 192, stride=9), :] = late[:, start : start + LANES]
        for j in range(6):
            columns = slice(j * LANES, (j + 1) * LANES)
            grad_rep[pl.ds(VEC_PLACE + j, 9, stride=6), :] = vec[0:9, columns]
        rest = small[...] + one_small[...] + two_small[...]
        for j in range(3):
            grad_rep[pl.ds(VEC_PLACE + 54 + j, 14, stride=3), :] = rest[0:14, j * LANES : (j + 1) * LANES]
        head_swap.wait_recv()
        top_other.start()
        read = joined(head_own, head_other)

        def put(first, value):
            rows = value.shape[0]
            for j in range(12):
                grad_rep[pl.ds(first * 12 + j, rows, stride=12), :] = value[:, j * LANES : (j + 1) * LANES]

        put(0, read(48, 48)[6:])
        for t in range(1, 4):
            put(96 * t - HEAD_TOP, read(96 * t, 96))

    for row in range(3):

        @pl.when(z == row)
        def _():
            refs_of = {QKV: qkv, SQUARE: square, UP: up}
            for name, count, place in TEN_PLACES[row]:
                spread_rows(grad_ten, place, PIECES[name][1] // LANES, count, plain(refs_of[name]))
            patch_swap.wait_recv()
            spread_rows(grad_rep, 0, 6, PATCH_COUNTS[row], joined(patch, patch_other))
            if row == 2:
                e2d_swap.wait_recv()
                for half in range(2):

                    def read(first, rows):
                        one, two = e2d[pl.ds(first, rows)].astype(FLOAT), e2d_other[pl.ds(first, rows)].astype(FLOAT)
                        return jnp.where(x == half, one, two)

                    spread_rows(grad_rep, E2D_PLACE + half * 1152, 3, 384, read)
                top_own.wait_recv()
                top_other.wait_recv()
                spread_rows(grad_rep, HEAD_PLACE, 12, HEAD_TOP, joined(head_own, head_other))

    def square_sum(flat, step):
        def body(t, carry):
            value = flat[pl.ds(pl.multiple_of(t * step, 8), step), :]
            return carry + jnp.sum((value * value).reshape(step // 8, 8, LANES), 0)

        return jnp.sum(lax.fori_loop(0, flat.shape[0] // step, body, jnp.zeros((8, LANES), FLOAT)))

    squares = square_sum(grad_ten, 360) + square_sum(grad_rep, 312) * 0.5
    line = lax.broadcasted_iota(jnp.int32, (8, LANES), 0)
    slots[me] = jnp.where(line == 0, squares, stats[...])
    shares = [links.copy(4 + shift, slots.at[me], slots.at[me], peer(shift)) for shift in range(1, 8)]
    for one in shares:
        one.start()
    for one in shares:
        one.wait()
    whole = slots[0]
    for i in range(1, 8):
        whole = whole + slots[i]
    square_all, loss_all, count_all = whole[0:1], whole[1:2], whole[2:3]
    norm = jnp.sqrt(square_all + 1e-30) / count_all
    factor = jnp.minimum(1.0, CLIP / norm) / count_all
    stats_out[...] = jnp.where(line == 0, norm, whole)
    for one in loads:
        one.wait()

    def adam(master, first, second, grad, step):
        def body(t, carry):
            at = pl.ds(pl.multiple_of(t * step, 8), step)
            new = adamw(master[at, :], first[at, :], second[at, :], grad[at, :] * factor, number)
            master[at, :], first[at, :], second[at, :] = new
            return carry

        lax.fori_loop(0, master.shape[0] // step, body, 0)

    stores = [pltpu.make_async_copy(held[i], outs[i], local_sem.at[i]) for i in range(6)]
    adam(*held[:3], grad_ten, 240)
    for one in stores[:3]:
        one.start()
    adam(*held[3:], grad_rep, 312)
    for one in stores[3:]:
        one.start()
    if not last:
        lay_out(z, x, held[0], held[3], pieces, wide_rows)

    @pl.when(z < LAST)
    def _():
        patch_swap.wait_send()

    @pl.when(z == 2)
    def _():
        e2d_swap.wait_send()

    @pl.when(z == LAST)
    def _():
        head_swap.wait_send()
        top_own.wait_send()
        top_other.wait_send()

    for one in stores:
        one.wait()


def update(identity, number, last, stats, gradients, states):
    vmem = pl.BlockSpec(memory_space=pltpu.VMEM)
    anywhere = pl.BlockSpec(memory_space=pl.ANY)
    laid = [] if last else LAID
    flat = [(TEN_LANES, LANES)] * 3 + [(REP_LANES, LANES)] * 3
    scratch = [(one, FLOAT) for one in flat + [(TEN_LANES, LANES), (REP_LANES, LANES), (5, 384, LANES)]] + [
        ((704, D // 2), HALF),
        ((D // 2, DD), HALF),
        ((DD, PATCH // 2), HALF),
        ((DD, PATCH // 2), HALF),
        ((8, 8, LANES), FLOAT),
    ]
    out = pl.pallas_call(
        functools.partial(update_kernel, number, last),
        name="update",
        out_shape=[jax.ShapeDtypeStruct((8, LANES), FLOAT)]
        + [jax.ShapeDtypeStruct(one, FLOAT) for one in flat]
        + [jax.ShapeDtypeStruct(LAID_SHAPES[name], HALF) for name in laid],
        in_specs=[vmem] * (1 + len(gradients)) + [anywhere] * 6,
        out_specs=[vmem] + [anywhere] * 6 + [vmem] * len(laid),
        scratch_shapes=[pltpu.VMEM(*one) for one in scratch]
        + [pltpu.SemaphoreType.DMA((12,)), pltpu.SemaphoreType.DMA((12,)), pltpu.SemaphoreType.DMA((6,))],
        compiler_params=pltpu.CompilerParams(
            collective_id=identity, has_side_effects=True, vmem_limit_bytes=61 << 20
        ),
    )(stats, *gradients, *states)
    return out[0], out[1:7], dict(zip(laid, out[7:]))


def decoder_kernel(
    reduced, hot, shown, places, pixels, counted, qkv_own, qkv_oth,
    out_own, out_oth, up_own, up_oth, down_own, down_oth, head_w, vec, head_b,
    picked, wide, tall, qkv_grad, small, loss,
    normed, tokens, q_ref, k_ref, v_ref, parts, parts_got, grad_att, vec_grad, vec_got, head_b_grad,
    blended, blend_other, totals, upward, activated, second, final_low, pred_low, low, grad_up_in, mid, grad_blend,
    blend_sent, wide_sent, wide_got, tall_sent, tall_got, dk_ref, dv_ref, send_sem, recv_sem,
):
    g, z, x = lax.axis_index("group"), lax.axis_index("dp"), lax.axis_index("tensor")
    across = (g, z, 1 - x)
    links = Links(send_sem, recv_sem)
    barrier = pltpu.get_barrier_semaphore()
    pl.semaphore_signal(barrier, inc=1, device_id=across, device_id_type=MESH_ID)
    half = pixels.shape[0]
    width = q_ref.shape[1]
    heads = width // HDIM
    tiles = q_ref.shape[0] // TILE
    fc = DFF // 2
    left = reduced[...] + vec[0:1]
    thirds = []
    for _ in range(3):
        thirds.append(left.astype(HALF))
        left = left - thirds[-1].astype(FLOAT)

    def embed(t, carry):
        rows = pl.ds(pl.multiple_of(t * TILE, TILE), TILE)
        placed = mm(hot[rows], thirds[0]) + mm(hot[rows], thirds[1]) + mm(hot[rows], thirds[2])
        values = jnp.where(shown[rows] > 0.5, placed, vec[1:2]) + places[rows]
        tokens[rows] = values
        low_rows = norm_to(values, vec[2:3], vec[3:4]).astype(HALF)
        normed[rows] = low_rows
        joined = mm(low_rows, qkv_own[...]).astype(HALF)
        q_ref[rows] = joined[:, :width]
        k_ref[rows] = joined[:, width : 2 * width]
        v_ref[rows] = joined[:, 2 * width :]
        return carry

    lax.fori_loop(0, tiles, embed, 0)
    parts[...] = jnp.zeros_like(parts)

    def attend(first, last):
        for h in range(heads):
            cols = slice(h * HDIM, (h + 1) * HDIM)
            keys = k_ref[:, cols] * HALF(HDIM**-0.5)
            turned = v_ref[:, cols].T

            def step(t, carry):
                rows = pl.ds(pl.multiple_of(t * TILE, TILE), TILE)
                scores = mm_nt(keys, q_ref[rows, cols])
                highest = jnp.max(scores, 0, keepdims=True)
                weights = jnp.exp(scores - highest)
                total = jnp.sum(weights, 0, keepdims=True)
                probs = (weights * (1.0 / total)).astype(HALF)
                blended[rows, cols] = mm(turned, probs).T.astype(HALF)
                totals[h, pl.ds(t, 1), :] = highest + jnp.log(total)
                return carry

            lax.fori_loop(first, last, step, 0)

    whole = half // TILE
    attend(whole, tiles)
    pl.semaphore_wait(barrier, 1)
    blend_swap = links.copy(0, blended.at[pl.ds(half, half)], blend_other, across)
    blend_swap.start()
    attend(0, whole)
    vec_grad[...] = jnp.zeros_like(vec_grad)
    head_b_grad[...] = jnp.zeros_like(head_b_grad)
    loss[...] = jnp.zeros_like(loss)
    blend_swap.wait_recv()

    def count(row, value):
        vec_grad[row : row + 1] += value

    grad_swaps = []
    start = 0
    for step, size in enumerate((400, 384)):
        rows = pl.ds(start, size)
        start += size
        attended = mm(blended[rows], out_own[...]) + mm(blend_other[rows], out_oth[...]) + tokens[rows] + vec[4:5]
        second[rows] = norm_to(attended, vec[5:6], vec[6:7]).astype(HALF)
        decoded = attended + vec[7:8]
        for side, (into, back) in enumerate(((up_own, down_own), (up_oth, down_oth))):
            cols = slice(side * fc, (side + 1) * fc)
            up = mm(second[rows], into[...])
            upward[rows, cols] = up
            activated[rows, cols] = gelu_to(up).astype(HALF)
            decoded = decoded + mm(activated[rows, cols], back[...])
        final_low[rows] = norm_to(decoded, vec[8:9], vec[9:10]).astype(HALF)
        differ = mm(final_low[rows], head_w[...]) + head_b[...]
        differ = differ - norm_parts(pixels[rows].astype(FLOAT))[0]
        share = counted[rows]
        loss[...] += jnp.sum(jnp.mean(differ * differ, -1, keepdims=True) * share)
        grad = (2.0 / PATCH) * differ * share
        head_b_grad[...] += jnp.sum(grad, 0, keepdims=True)
        pred_low[rows] = grad.astype(HALF)
        grad_out, gain, bias = norm_from(decoded, vec[8:9], mm_nt(pred_low[rows], head_w[...]))
        count(8, gain)
        count(9, bias)
        count(7, jnp.sum(grad_out, 0, keepdims=True))
        low[rows] = grad_out.astype(HALF)
        grad_second = jnp.zeros((size, DD), FLOAT)
        for side, (into, back) in enumerate(((up_own, down_own), (up_oth, down_oth))):
            cols = slice(side * fc, (side + 1) * fc)
            slope = gelu_slope(upward[rows, cols])
            grad_up_in[rows, cols] = (mm_nt(low[rows], back[...]) * slope).astype(HALF)
            grad_second = grad_second + mm_nt(grad_up_in[rows, cols], into[...])
        grad, gain, bias = norm_from(attended, vec[5:6], grad_second)
        count(5, gain)
        count(6, bias)
        grad = grad + grad_out
        count(4, jnp.sum(grad, 0, keepdims=True))
        grad_att[rows] = grad
        mid[rows] = grad.astype(HALF)
        grad_blend[rows] = mm_nt(mid[rows], out_own[...]).astype(HALF)
        blend_sent[rows] = mm_nt(mid[rows], out_oth[...]).astype(HALF)
        swap_rows = pl.ds(half + start - size, size)
        grad_swaps.append(links.copy(1 + step, blend_sent.at[rows], grad_blend.at[swap_rows], across))
        grad_swaps[-1].start()
    mine = pl.ds(pl.multiple_of(x * fc, LANES), fc)
    theirs = pl.ds(pl.multiple_of((1 - x) * fc, LANES), fc)
    wide_sent[:, :fc] = mm_tn(second[...], grad_up_in[:, fc:]).astype(HALF)
    wide_sent[:, fc:] = mm_tn(final_low[...], pred_low[:, theirs]).astype(HALF)
    wide_swap = links.copy(3, wide_sent, wide_got, across)
    wide_swap.start()
    tall_sent[:fc] = mm_tn(activated[:, fc:], low[...]).astype(HALF)
    tall_sent[fc:] = mm_tn(blend_other[...], mid[...]).astype(HALF)
    tall_swap = links.copy(4, tall_sent, tall_got, across)
    tall_swap.start()
    wide[:, :fc] = mm_tn(second[...], grad_up_in[:, :fc])
    wide[:, fc:] = mm_tn(final_low[...], pred_low[:, mine])
    tall[:fc] = mm_tn(activated[:, :fc], low[...])
    tall[fc:] = mm_tn(blended[pl.ds(0, half)], mid[...])
    for one in grad_swaps:
        one.wait_recv()
    part_swaps = []

    def send_parts(block):
        for third in range(3):
            cols = pl.ds(256 * third + 128 * block, 128)
            one = links.copy(5 + 3 * block + third, parts.at[pl.ds(half, half), cols], parts_got.at[:, cols], across)
            one.start()
            part_swaps.append(one)

    for h in range(heads):
        cols = slice(h * HDIM, (h + 1) * HDIM)
        keys = k_ref[:, cols] * HALF(HDIM**-0.5)
        values = v_ref[:, cols]
        turned = keys.T
        dk_ref[...] = jnp.zeros_like(dk_ref)
        dv_ref[...] = jnp.zeros_like(dv_ref)

        def back_step(t, carry):
            rows = pl.ds(pl.multiple_of(t * TILE, TILE), TILE)
            queries, grads = q_ref[rows, cols], grad_blend[rows, cols]
            probs = jnp.exp(mm_nt(keys, queries) - totals[h, pl.ds(t, 1), :])
            dv_ref[...] += mm(probs.astype(HALF), grads)
            grad_probs = mm_nt(values, grads)
            grad_scores = (probs * (grad_probs - jnp.sum(probs * grad_probs, 0, keepdims=True))).astype(HALF)
            dk_ref[...] += mm(grad_scores, queries)
            parts[rows, cols] = mm(turned, grad_scores).T.astype(HALF)
            return carry

        lax.fori_loop(0, tiles, back_step, 0)
        parts[:, 256 + h * HDIM : 256 + (h + 1) * HDIM] = (dk_ref[...] * HDIM**-0.5).astype(HALF)
        parts[:, 512 + h * HDIM : 512 + (h + 1) * HDIM] = dv_ref[...].astype(HALF)
        if h == 1:
            send_parts(0)
    send_parts(1)

    def back(ref, rows, weights):
        total = jnp.zeros((half, DD), FLOAT)
        for third in range(3):
            columns = ref[rows, 256 * third : 256 * third + width]
            total = total + mm_nt(columns, weights[:, third * width : (third + 1) * width])
        return total

    own_rows_ = pl.ds(0, half)
    grad_normed = back(parts, own_rows_, qkv_own)
    product = mm_tn(normed[...], parts[...])
    for third in range(3):
        qkv_grad[:, third * width : (third + 1) * width] = product[:, 256 * third : 256 * third + width]
    wide_swap.wait_recv()
    wide[...] += wide_got[...].astype(FLOAT)
    tall_swap.wait_recv()
    tall[...] += tall_got[...].astype(FLOAT)
    for one in part_swaps:
        one.wait_recv()
    grad_normed = grad_normed + back(parts_got, own_rows_, qkv_oth)
    grad, gain, bias = norm_from(tokens[own_rows_], vec[2:3], grad_normed)
    count(2, gain)
    count(3, bias)
    grad = grad + grad_att[...]
    seen = jnp.where(shown[own_rows_] > 0.5, grad, 0.0)
    count(0, jnp.sum(seen, 0, keepdims=True))
    count(1, jnp.sum(grad - seen, 0, keepdims=True))
    for i in range(PATCH // DD):
        count(10 + i, head_b_grad[:, i * DD : (i + 1) * DD])
    vec_swap = links.copy(11, vec_grad, vec_got, across)
    vec_swap.start()
    picked[...] = mm_tn(hot[own_rows_], grad.astype(HALF)).astype(HALF)
    vec_swap.wait_recv()
    small[...] = vec_grad[...] + vec_got[...]
    for one in [blend_swap, wide_swap, tall_swap, vec_swap] + grad_swaps + part_swaps:
        one.wait_send()


def decoder_round(number, reduced, hot, shown, places, pixels_low, counted, weights):
    own, other, head_w, vec, head_b = weights
    count, rows, width = pixels_low.shape[0], hot.shape[0], DD // 2
    vmem = pl.BlockSpec(memory_space=pltpu.VMEM)
    shapes = [
        ((VISIBLE, DD), HALF),
        ((DD, DFF // 2 + PATCH // 2), FLOAT),
        ((DFF // 2 + width, DD), FLOAT),
        ((DD, 3 * width), FLOAT),
        ((16, DD), FLOAT),
        ((8, LANES), FLOAT),
    ]
    scratch = [
        ((rows, DD), HALF),
        ((rows, DD), FLOAT),
        ((rows, width), HALF),
        ((rows, width), HALF),
        ((rows, width), HALF),
        ((rows, 768), HALF),
        ((count, 768), HALF),
        ((count, DD), FLOAT),
        ((16, DD), FLOAT),
        ((16, DD), FLOAT),
        ((1, PATCH), FLOAT),
        ((rows, width), HALF),
        ((count, width), HALF),
        ((width // HDIM, rows // TILE, TILE), FLOAT),
        ((count, DFF), FLOAT),
        ((count, DFF), HALF),
        ((count, DD), HALF),
        ((count, DD), HALF),
        ((count, PATCH), HALF),
        ((count, DD), HALF),
        ((count, DFF), HALF),
        ((count, DD), HALF),
        ((rows, width), HALF),
        ((count, width), HALF),
        ((DD, DFF // 2 + PATCH // 2), HALF),
        ((DD, DFF // 2 + PATCH // 2), HALF),
        ((DFF // 2 + width, DD), HALF),
        ((DFF // 2 + width, DD), HALF),
        ((rows, HDIM), FLOAT),
        ((rows, HDIM), FLOAT),
    ]
    return pl.pallas_call(
        decoder_kernel,
        name="decoder",
        out_shape=[jax.ShapeDtypeStruct(*one) for one in shapes],
        in_specs=[vmem] * 17,
        out_specs=[vmem] * len(shapes),
        scratch_shapes=[pltpu.VMEM(*one) for one in scratch]
        + [pltpu.SemaphoreType.DMA((12,)), pltpu.SemaphoreType.DMA((12,))],
        compiler_params=pltpu.CompilerParams(
            collective_id=number, has_side_effects=True, vmem_limit_bytes=60 << 20
        ),
    )(
        reduced,
        hot,
        shown,
        places,
        pixels_low,
        counted[:, None],
        own[0],
        other[0],
        own[1],
        other[1],
        own[2],
        other[2],
        own[3],
        other[3],
        head_w,
        jnp.pad(vec, ((0, 6), (0, 0))),
        head_b[None],
    )


def hosted_round(
    patches,
    visible,
    frames_valid,
    clip_valid,
    rep_weights,
    ten_weights,
    rep_m,
    rep_v,
    ten_m,
    ten_v,
    rep_outer,
    ten_outer,
):
    side = lax.axis_index("tensor")
    z = lax.axis_index("dp")
    half_rows = TUBES // 2
    tube_ids = (jnp.arange(TUBES) + side * half_rows) % TUBES
    ids_one = hop(visible[:, 0, 0], ((0, 0), (HOST, 0)), ((2, 1), (HOST, 1)))
    ids_two = hop(visible[:, 0, 0], ((3, 1), (HOST, 1)))
    ids_two = jnp.where(side == 0, visible[:, 0, 0], ids_two)
    dec_table = sinus_all(DD)
    places = []
    for part in sinus_parts(D):
        part = jnp.pad(part, ((0, -part.shape[0] % 64), (0, 0)))
        places.append(jnp.stack(thirds_of(part)))
    dec_places = jnp.where(side == 0, dec_table, jnp.roll(dec_table, -half_rows, 0))
    states = [one.reshape(TEN_LANES, LANES) for one in (ten_weights, ten_m, ten_v)]
    states = states + [one.reshape(REP_LANES, LANES) for one in (rep_weights, rep_m, rep_v)]
    starts = states[0], states[3]
    pieces = first_pieces(*starts)
    rep_quarter = rep_weights.shape[0]
    source, target = jnp.arange(PATCH)[:, None], jnp.arange(WIDE)[None, :]
    cut = rep_quarter // D
    moved = lax.optimization_barrier(source + (SPAN[1] - cut) * (source // cut))
    layout = (target == moved).astype(HALF)
    shown_steps = []
    for s in range(STEPS):
        picks = (visible[s, 0, 0][:, None] == jnp.arange(TUBES)[None, :]).astype(HALF)
        rows = mm(picks, patches[s, 0, 0]).astype(HALF)
        rows = mm(rows, layout).astype(HALF)
        one = hop(rows, ((0, 0), (HOST, 0)), ((2, 1), (HOST, 1)))
        two = hop(rows, ((3, 1), (HOST, 1)))
        own = jnp.concatenate([one, jnp.where(side == 0, rows, two)], 0)
        shown_steps.append((own, swap(own, HOST)))
    loss_list, count_list, norm_list = [], [], []
    for s in range(STEPS):
        ids = visible[s, 0, 0]
        picks = tube_ids[:, None] == ids[None, :]
        shown_here = jnp.any(picks, 1)
        counted = (
            jnp.where(shown_here, 0.0, 1.0)
            * (tube_ids // (TUBES // FRAMES) < frames_valid[s, 0, 0])
            * (clip_valid[s, 0, 0] == 1)
        ).astype(FLOAT)[:half_rows]
        shown = shown_steps[s]
        vis = ids.shape[0]
        ids_own = jnp.concatenate([ids_one[s], ids_two[s]])
        reduced_clip, enc_stored, enc_weights, dec_weights = encoder_forward(
            3 + s, s == 0, pieces, shown[0], (ids_own[:, None], *places)
        )
        normed, activated = enc_stored[1], enc_stored[7]
        far = (
            hop_both(normed, (HOST, 0)),
            hop_both(activated, (HOST, 2)),
        )
        pixels_low = lax.dynamic_slice_in_dim(patches[s, 0, 0], side * half_rows, half_rows, 0)
        picked, wide, tall, qkv_grad, small, loss = decoder_round(
            9 + s,
            reduced_clip,
            picks.astype(HALF),
            shown_here[:, None].astype(FLOAT),
            dec_places,
            pixels_low,
            counted,
            dec_weights,
        )
        back = encoder_backward(5 + s, picked, shown, enc_weights, enc_stored, (wide, tall, qkv_grad, small), far)
        line = jnp.arange(8)[:, None]
        stats = jnp.where(line == 1, loss[0, 0], jnp.where(line == 2, jnp.sum(counted), 0.0))
        stats = jnp.broadcast_to(stats, (8, LANES))
        stats, states, pieces = update(
            7 + s, STEP_BEFORE + s + 1, s == STEPS - 1, stats, (*back[:6], wide, tall, qkv_grad, small, *back[6:]), states
        )
        norm_list.append(stats[0, 0])
        loss_list.append(stats[1, 0])
        count_list.append(stats[2, 0])
    one = jnp.where(count_list[-1] >= 0, 1.0, 0.0)
    ten_first, ten_second, rep_first, rep_second = [(one * part).reshape(-1) for part in (*states[1:3], *states[4:])]
    ten_diff, rep_diff = [group_mean(starts[i] - states[3 * i]).reshape(-1) for i in range(2)]
    rep_momentum = MOMENTUM * rep_outer + rep_diff
    ten_momentum = MOMENTUM * ten_outer[0] + ten_diff
    rep_new = rep_weights - LR_OUT * (rep_diff + MOMENTUM * rep_momentum)
    ten_new = ten_weights[0] - LR_OUT * (ten_diff + MOMENTUM * ten_momentum)
    return (
        jnp.stack(loss_list)[:, None],
        jnp.stack(count_list)[:, None],
        jnp.stack(norm_list)[:, None],
        rep_first[None],
        rep_second[None],
        ten_first[None, None],
        ten_second[None, None],
        rep_diff,
        ten_diff[None],
        rep_momentum,
        ten_momentum[None],
        rep_new,
        ten_new[None],
    )


def group_mean(diff):
    if lax.axis_size("group") != 4:
        return lax.psum(diff, "group") / lax.axis_size("group")
    odd = lax.axis_index("group") % 2 == 1
    half = diff.shape[0] // 2
    low, high = diff[:half], diff[half:]
    part = jnp.where(odd, high, low) + partner(jnp.where(odd, low, high))
    part_low = lax.optimization_barrier(part.astype(HALF))
    far = lax.ppermute(part_low, "group", [(g, g ^ 2) for g in range(4)])
    total = (part_low.astype(FLOAT) + far.astype(FLOAT)) * 0.25
    other = partner(total)
    return jnp.concatenate([jnp.where(odd, other, total), jnp.where(odd, total, other)])


def solution(mesh):
    placed = (
        P(None, "group", "dp", None, None),
        P(None, "group", "dp", None),
        P(None, "group", "dp"),
        P(None, "group", "dp"),
        P("dp"),
        P("tensor", "dp"),
        P("group", "dp"),
        P("group", "dp"),
        P("group", "tensor", "dp"),
        P("group", "tensor", "dp"),
        P("dp"),
        P("tensor", "dp"),
    )
    return jax.shard_map(
        hosted_round if mesh.shape["dp"] == 4 and mesh.shape["tensor"] == 2 and mesh.shape["group"] % 2 == 0 else on_device,
        mesh=mesh,
        in_specs=placed,
        out_specs=(
            P(None, "group"),
            P(None, "group"),
            P(None, "group"),
            P("group", "dp"),
            P("group", "dp"),
            P("group", "tensor", "dp"),
            P("group", "tensor", "dp"),
            P("dp"),
            P("tensor", "dp"),
            P("dp"),
            P("tensor", "dp"),
            P("dp"),
            P("tensor", "dp"),
        ),
        check_vma=False,
    )
```

```python
import functools
import math

import jax
import jax.numpy as jnp
from jax import lax
from jax.experimental import pallas as pl
from jax.experimental.pallas import tpu as pltpu
from jax.sharding import PartitionSpec as P

D = 768
HDIM = 64
FF = 3072
DD = 384
DFF = 1536
PATCH = 1536
TUBES = 1568
FRAMES = 8
STEPS = 2
STEP_BEFORE = 6


CLIP = 0.001
LR_IN = 0.01
BETA1 = 0.9
BETA2 = 0.95
EPS = 1e-08
DECAY = 0.05
LR_OUT = 0.7
MOMENTUM = 0.9
FLOAT = jnp.float32
HALF = jnp.bfloat16


def sinus(count, width):
    places = jnp.arange(count).astype(jnp.float32)[:, None]
    column = jnp.arange(width)
    decays = jnp.power(10000.0, -2.0 * (column // 2).astype(jnp.float32) / width)
    angles = places * decays[None, :]
    return jnp.where(column % 2 == 0, jnp.sin(angles), jnp.cos(angles))


def layer_norm(stream, gain, bias):
    center = jnp.mean(stream, -1, keepdims=True)
    spread = jnp.mean((stream - center) ** 2, -1, keepdims=True)
    return (stream - center) * lax.rsqrt(spread + 1e-06) * gain + bias


def norm_back(stream, gain, bias, cotangent):
    _, pull = jax.vjp(layer_norm, stream, gain, bias)
    return pull(cotangent)


def gelu_exact(values):
    return jax.nn.gelu(values, approximate=False)


def split_flat(flat, shapes):
    pieces = []
    offset = 0
    for shapes_one in shapes:
        length = math.prod(shapes_one)
        pieces.append(flat[offset : offset + length].reshape(shapes_one))
        offset += length
    return pieces


def own_rows(stream, axis_dim):
    count = stream.shape[axis_dim] // lax.axis_size("tensor")
    return lax.dynamic_slice_in_dim(stream, lax.axis_index("tensor") * count, count, axis_dim)


def rows_sum(partial_rows):
    return lax.psum_scatter(partial_rows, "tensor", scatter_dimension=1, tiled=True)


def rows_full(own_part):
    return lax.all_gather(own_part, "tensor", axis=1, tiled=True)


def block_forward(stream, mats, vecs):
    w_qkv, w_out, w_up, w_down = mats
    gain_one, bias_one, out_bias, gain_two, bias_two, down_bias = vecs
    nclips, length, _ = stream.shape
    head_cols = w_out.shape[0]
    nheads = head_cols // HDIM
    normed = layer_norm(stream, gain_one, bias_one).astype(HALF)
    joined = jnp.dot(normed, w_qkv, preferred_element_type=FLOAT).astype(HALF)
    queries, key_rows, values = [
        joined[:, :, third_id * head_cols : (third_id + 1) * head_cols].reshape(
            nclips, length, nheads, HDIM
        )
        for third_id in range(3)
    ]
    scores = jnp.einsum(
        "cqhd,ckhd->chqk", queries, key_rows, preferred_element_type=FLOAT
    ) * HDIM ** (-0.5)
    highest = jnp.max(scores, -1, keepdims=True)
    totals = jnp.log(jnp.sum(jnp.exp(scores - highest), -1, keepdims=True)) + highest
    probs_low = jnp.exp(scores - totals).astype(HALF)
    blended = (
        jnp.einsum("chqk,ckhd->cqhd", probs_low, values, preferred_element_type=FLOAT)
        .astype(HALF)
        .reshape(nclips, length, head_cols)
    )
    attended = (
        rows_sum(jnp.dot(blended, w_out, preferred_element_type=FLOAT))
        + own_rows(stream, 1)
        + out_bias
    )
    second = layer_norm(attended, gain_two, bias_two).astype(HALF)
    second_all = lax.all_gather(second, "tensor", axis=1, tiled=True)
    upward = jnp.dot(second_all, w_up, preferred_element_type=FLOAT)
    activated = gelu_exact(upward).astype(HALF)
    result = (
        rows_sum(jnp.dot(activated, w_down, preferred_element_type=FLOAT)) + attended + down_bias
    )
    stored = (
        stream,
        normed,
        queries,
        key_rows,
        values,
        totals,
        blended,
        attended,
        second_all,
        upward,
        activated,
    )
    return (rows_full(result), stored)


def block_backward(grad_out, mats, vecs, stored):
    w_qkv, w_out, w_up, w_down = mats
    gain_one, bias_one, out_bias, gain_two, bias_two, down_bias = vecs
    (
        stream,
        normed,
        queries,
        key_rows,
        values,
        totals,
        blended,
        attended,
        second_all,
        upward,
        activated,
    ) = stored
    nclips, length, _ = stream.shape
    head_cols = w_out.shape[0]
    grad_low = grad_out.astype(HALF)
    grad_down = jnp.einsum("ctf,ctd->fd", activated, grad_low, preferred_element_type=FLOAT)
    down_bias_grad = jnp.sum(own_rows(grad_out, 1), (0, 1))
    grad_act = jnp.dot(grad_low, w_down.T, preferred_element_type=FLOAT)
    _, gelu_pull = jax.vjp(gelu_exact, upward)
    grad_up_in = gelu_pull(grad_act)[0].astype(HALF)
    grad_up = jnp.einsum("ctd,ctf->df", second_all, grad_up_in, preferred_element_type=FLOAT)
    grad_second = rows_sum(jnp.dot(grad_up_in, w_up.T, preferred_element_type=FLOAT))
    grad_att, gain_two_grad, bias_two_grad = norm_back(attended, gain_two, bias_two, grad_second)
    grad_att = grad_att + own_rows(grad_out, 1)
    out_bias_grad = jnp.sum(grad_att, (0, 1))
    grad_mid = rows_full(grad_att)
    mid_low = grad_mid.astype(HALF)
    grad_wout = jnp.einsum("cth,ctd->hd", blended, mid_low, preferred_element_type=FLOAT)
    nheads = head_cols // HDIM
    grad_blend = (
        jnp.dot(mid_low, w_out.T, preferred_element_type=FLOAT)
        .astype(HALF)
        .reshape(nclips, length, nheads, HDIM)
    )
    scores = jnp.einsum(
        "cqhd,ckhd->chqk", queries, key_rows, preferred_element_type=FLOAT
    ) * HDIM ** (-0.5)
    probs_full = jnp.exp(scores - totals)
    probs_low = probs_full.astype(HALF)
    grad_values = jnp.einsum("chqk,cqhd->ckhd", probs_low, grad_blend, preferred_element_type=FLOAT)
    grad_probs = jnp.einsum("cqhd,ckhd->chqk", grad_blend, values, preferred_element_type=FLOAT)
    grad_scores = (
        probs_full * (grad_probs - jnp.sum(probs_full * grad_probs, -1, keepdims=True))
    ).astype(HALF)
    grad_queries = jnp.einsum(
        "chqk,ckhd->cqhd", grad_scores, key_rows, preferred_element_type=FLOAT
    ) * HDIM ** (-0.5)
    grad_keys = jnp.einsum(
        "chqk,cqhd->ckhd", grad_scores, queries, preferred_element_type=FLOAT
    ) * HDIM ** (-0.5)
    grad_joined = jnp.concatenate(
        [
            part_grad.reshape(nclips, length, head_cols)
            for part_grad in (grad_queries, grad_keys, grad_values)
        ],
        -1,
    ).astype(HALF)
    grad_qkv = jnp.einsum("ctd,cte->de", normed, grad_joined, preferred_element_type=FLOAT)
    grad_norm_in = rows_sum(jnp.dot(grad_joined, w_qkv.T, preferred_element_type=FLOAT))
    grad_in, gain_one_grad, bias_one_grad = norm_back(
        own_rows(stream, 1), gain_one, bias_one, grad_norm_in
    )
    grad_in = grad_in + grad_att
    vec_grads = jnp.stack(
        [gain_one_grad, bias_one_grad, out_bias_grad, gain_two_grad, bias_two_grad, down_bias_grad]
    )
    return (rows_full(grad_in), (grad_qkv, grad_wout, grad_up, grad_down), vec_grads)


def group_step(patch_rows, visible_ids, shown, weight_rows, rep_full, ten_full):
    splits = lax.axis_size("tensor")
    patch_w, e2d_w, head_w, enc_vec, dec_vec, head_b = split_flat(
        rep_full, [(PATCH, D), (D, DD), (DD, PATCH), (9, D), (10, DD), (PATCH,)]
    )
    enc_vec = enc_vec.astype(FLOAT)
    dec_vec = dec_vec.astype(FLOAT)
    head_b = head_b.astype(FLOAT)
    enc_cols = D // splits
    dec_cols = DD // splits
    ten_pieces = split_flat(
        ten_full,
        [
            (D, 3 * enc_cols),
            (enc_cols, D),
            (D, FF // splits),
            (FF // splits, D),
            (DD, 3 * dec_cols),
            (dec_cols, DD),
            (DD, DFF // splits),
            (DFF // splits, DD),
        ],
    )
    enc_mats = ten_pieces[0:4]
    dec_mats = ten_pieces[4:8]
    enc_vecs = [enc_vec[i] for i in range(1, 7)]
    dec_vecs = [dec_vec[i] for i in range(2, 8)]
    shown_rows = jnp.take_along_axis(patch_rows, visible_ids[:, :, None], 1)
    embedded = (
        jnp.dot(shown_rows, patch_w, preferred_element_type=FLOAT)
        + enc_vec[0]
        + sinus(TUBES, D)[visible_ids]
    )
    encoded, enc_stored = block_forward(embedded, enc_mats, enc_vecs)
    final_enc = layer_norm(encoded, enc_vec[7], enc_vec[8]).astype(HALF)
    reduced = jnp.dot(final_enc, e2d_w, preferred_element_type=FLOAT) + dec_vec[0]
    blank = jnp.broadcast_to(dec_vec[1], (TUBES, DD))
    tokens_in = jax.vmap(lambda clip_ids, clip_rows: blank.at[clip_ids].set(clip_rows))(
        visible_ids, reduced
    ) + sinus(TUBES, DD)
    decoded, dec_stored = block_forward(tokens_in, dec_mats, dec_vecs)
    own_dec = own_rows(decoded, 1)
    final_low = layer_norm(own_dec, dec_vec[8], dec_vec[9]).astype(HALF)
    predicted = jnp.dot(final_low, head_w, preferred_element_type=FLOAT) + head_b
    pixels = own_rows(patch_rows, 1).astype(FLOAT)
    center = jnp.mean(pixels, -1, keepdims=True)
    spread = jnp.mean((pixels - center) ** 2, -1, keepdims=True)
    target = (pixels - center) * lax.rsqrt(spread + 1e-06)
    differ = predicted - target
    counted = own_rows(weight_rows, 1)
    loss_part = jnp.sum(jnp.mean(differ**2, -1) * counted)
    grad_pred = 2.0 / PATCH * differ * counted[:, :, None]
    pred_low = grad_pred.astype(HALF)
    head_w_grad = jnp.einsum("ctd,ctp->dp", final_low, pred_low, preferred_element_type=FLOAT)
    head_b_grad = jnp.sum(grad_pred, (0, 1))
    grad_final = jnp.dot(pred_low, head_w.T, preferred_element_type=FLOAT)
    grad_dec_own, dec_gain_grad, dec_bias_grad = norm_back(
        own_dec, dec_vec[8], dec_vec[9], grad_final
    )
    grad_tokens, dec_mat_grads, dec_vec_grads = block_backward(
        rows_full(grad_dec_own), dec_mats, dec_vecs, dec_stored
    )
    masked_own = own_rows(1.0 - shown.astype(FLOAT), 1)
    mask_grad = jnp.sum(own_rows(grad_tokens, 1) * masked_own[:, :, None], (0, 1))
    grad_reduced = own_rows(jnp.take_along_axis(grad_tokens, visible_ids[:, :, None], 1), 1)
    reduced_low = grad_reduced.astype(HALF)
    e2d_grad = jnp.einsum(
        "ctd,cte->de", own_rows(final_enc, 1), reduced_low, preferred_element_type=FLOAT
    )
    e2d_b_grad = jnp.sum(grad_reduced, (0, 1))
    grad_enc_final = jnp.dot(reduced_low, e2d_w.T, preferred_element_type=FLOAT)
    grad_enc_own, enc_gain_grad, enc_bias_grad = norm_back(
        own_rows(encoded, 1), enc_vec[7], enc_vec[8], grad_enc_final
    )
    grad_embedded, enc_mat_grads, enc_vec_grads = block_backward(
        rows_full(grad_enc_own), enc_mats, enc_vecs, enc_stored
    )
    own_embedded = own_rows(grad_embedded, 1)
    patch_grad = jnp.einsum(
        "ctp,ctd->pd",
        own_rows(shown_rows, 1),
        own_embedded.astype(HALF),
        preferred_element_type=FLOAT,
    )
    patch_b_grad = jnp.sum(own_embedded, (0, 1))
    enc_vec_grad = jnp.concatenate(
        [patch_b_grad[None], enc_vec_grads, enc_gain_grad[None], enc_bias_grad[None]], 0
    )
    dec_vec_grad = jnp.concatenate(
        [
            e2d_b_grad[None],
            mask_grad[None],
            dec_vec_grads,
            dec_gain_grad[None],
            dec_bias_grad[None],
        ],
        0,
    )
    rep_grad = jnp.concatenate(
        [
            patch_grad.reshape(-1),
            e2d_grad.reshape(-1),
            head_w_grad.reshape(-1),
            enc_vec_grad.reshape(-1),
            dec_vec_grad.reshape(-1),
            head_b_grad,
        ]
    )
    ten_grad = jnp.concatenate(
        [mat_grad.reshape(-1) for mat_grad in list(enc_mat_grads) + list(dec_mat_grads)]
    )
    return (loss_part, rep_grad, ten_grad)


def adamw(master, first, second, clipped, number):
    first = BETA1 * first + (1 - BETA1) * clipped
    second = BETA2 * second + (1 - BETA2) * clipped * clipped
    first_hat = first / (1 - BETA1**number)
    second_hat = second / (1 - BETA2**number)
    master = master - LR_IN * (first_hat / (jnp.sqrt(second_hat) + EPS) + DECAY * master)
    return (master, first, second)


def on_device(
    patches,
    visible,
    frames_valid,
    clip_valid,
    rep_weights,
    ten_weights,
    rep_m,
    rep_v,
    ten_m,
    ten_v,
    rep_outer,
    ten_outer,
):
    splits = lax.axis_size("tensor")
    owners = lax.axis_size("dp")
    tube_ids = jnp.arange(TUBES)
    rep_master, ten_master = (rep_weights, ten_weights[0])
    rep_first, rep_second = (rep_m[0], rep_v[0])
    ten_first, ten_second = (ten_m[0, 0], ten_v[0, 0])
    loss_list, count_list, norm_list = ([], [], [])
    for inner_step in range(STEPS):
        rep_full, ten_full = (
            lax.all_gather(rep_master.astype(HALF), "dp", axis=0, tiled=True),
            lax.all_gather(ten_master.astype(HALF), "dp", axis=0, tiled=True),
        )
        visible_ids = visible[inner_step, 0]
        shown = jnp.any(visible_ids[:, :, None] == tube_ids[None, None, :], axis=1)
        weight_rows = (
            jnp.where(shown, 0.0, 1.0)
            * (tube_ids[None, :] // (TUBES // FRAMES) < frames_valid[inner_step, 0][:, None])
            * (clip_valid[inner_step, 0][:, None] == 1)
        ).astype(FLOAT)
        count_part = jnp.sum(own_rows(weight_rows, 1))
        loss_part, rep_grad, ten_grad = group_step(
            patches[inner_step, 0], visible_ids, shown, weight_rows, rep_full, ten_full
        )
        rep_recv, ten_recv = (
            lax.all_to_all(
                rep_grad.reshape(owners, -1), "dp", split_axis=0, concat_axis=0, tiled=True
            ),
            lax.all_to_all(
                ten_grad.reshape(owners, -1), "dp", split_axis=0, concat_axis=0, tiled=True
            ),
        )
        rep_part = lax.psum(jnp.sum(rep_recv, 0), "tensor")
        ten_part = jnp.sum(ten_recv, 0)
        squares = jnp.sum(ten_part * ten_part) + jnp.sum(rep_part * rep_part) / splits
        square_all, loss_all, count_all = lax.psum(
            (squares, loss_part, count_part), ("dp", "tensor")
        )
        norm_value = jnp.sqrt(square_all + 1e-30) / count_all
        factor = jnp.minimum(1.0, CLIP / norm_value) / count_all
        number = STEP_BEFORE + inner_step + 1
        rep_master, rep_first, rep_second = adamw(
            rep_master, rep_first, rep_second, rep_part * factor, number
        )
        ten_master, ten_first, ten_second = adamw(
            ten_master, ten_first, ten_second, ten_part * factor, number
        )
        loss_list.append(loss_all)
        count_list.append(count_all)
        norm_list.append(norm_value)
    rep_sum, ten_sum = lax.psum((rep_weights - rep_master, ten_weights[0] - ten_master), "group")
    groups_count = lax.axis_size("group")
    rep_diff = rep_sum / groups_count
    ten_diff = ten_sum / groups_count
    rep_momentum = MOMENTUM * rep_outer + rep_diff
    ten_momentum = MOMENTUM * ten_outer[0] + ten_diff
    rep_new = rep_weights - LR_OUT * (rep_diff + MOMENTUM * rep_momentum)
    ten_new = ten_weights[0] - LR_OUT * (ten_diff + MOMENTUM * ten_momentum)
    return (
        jnp.stack(loss_list)[:, None],
        jnp.stack(count_list)[:, None],
        jnp.stack(norm_list)[:, None],
        rep_first[None],
        rep_second[None],
        ten_first[None, None],
        ten_second[None, None],
        rep_diff,
        ten_diff[None],
        rep_momentum,
        ten_momentum[None],
        rep_new,
        ten_new[None],
    )


TILE = 224


HOST = 1
LAST = 3
SWAP = [(0, 1), (1, 0)]
ENC_SHAPES = [(D, 3 * D // 2), (D // 2, D), (D, FF // 2), (FF // 2, D)]
DEC_SHAPES = [(DD, 3 * DD // 2), (DD // 2, DD), (DD, DFF // 2), (DFF // 2, DD)]
ENC_SIZE = sum(math.prod(one) for one in ENC_SHAPES)
DEC_SIZE = sum(math.prod(one) for one in DEC_SHAPES)
PATCH_SIZE = PATCH * D
E2D_SIZE = D * DD
HEAD_SIZE = DD * PATCH
ENC_VECS = 9 * D
DEC_VECS = 10 * DD


def hop(value, *moves):
    pairs = [(2 * a + b, 2 * c + d) for (a, b), (c, d) in moves]
    return lax.ppermute(value, ("dp", "tensor"), pairs)


def hop_both(value, *moves):
    return hop(value, *[((a, side), (b, side)) for a, b in moves for side in range(2)])


def swap(value, *where):
    if where:
        return hop(value, *[((z, side), (z, 1 - side)) for z in where for side in range(2)])
    return lax.ppermute(value, "tensor", SWAP)


def partner(value):
    count = lax.axis_size("group")
    return lax.ppermute(value, "group", [(g, g ^ 1) for g in range(count)])


def mm(left, right):
    return jnp.dot(left, right, preferred_element_type=FLOAT)


def mm_nt(left, right):
    return lax.dot_general(left, right, (((1,), (1,)), ((), ())), preferred_element_type=FLOAT)


def mm_tn(left, right):
    return lax.dot_general(left, right, (((0,), (0,)), ((), ())), preferred_element_type=FLOAT)


def sinus_parts(width):
    column = jnp.arange(width)
    decays = jnp.power(10000.0, -2.0 * (column // 2).astype(FLOAT) / width)
    far = (32 * jnp.arange(-(-TUBES // 32))).astype(FLOAT)[:, None] * decays
    near = jnp.arange(32).astype(FLOAT)[:, None] * decays
    even = column % 2 == 0
    near_one = jnp.where(even, jnp.cos(near), -jnp.sin(near))
    near_two = jnp.where(even, jnp.sin(near), jnp.cos(near))
    return jnp.concatenate([jnp.sin(far), jnp.cos(far)], 1), jnp.concatenate([near_one, near_two], 1)


def sinus_all(width):
    far, near = sinus_parts(width)
    table = far[:, None, :width] * near[None, :, :width] + far[:, None, width:] * near[None, :, width:]
    return table.reshape(-1, width)[:TUBES]


def thirds_of(rows):
    thirds = []
    for _ in range(3):
        thirds.append(lax.optimization_barrier(rows.astype(HALF)))
        rows = rows - thirds[-1].astype(FLOAT)
    return thirds


(
    QKV,
    SQUARE,
    UP,
    PATCH_ROWS,
    E2D,
    HEAD,
    VECS,
    DEC_QKV,
    DEC_OUT,
    DEC_UP,
    DEC_DOWN,
    HEAD_HALF,
    PATCH_LOW,
    PATCH_HIGH,
    W_QKV,
    W_OUT,
    W_UP,
    W_DOWN,
    E2D_W,
    HEAD_UP,
    SEND_ENC,
    SEND_MATE,
    CHAIN,
    CROSS,
    MATE_OWN,
    MATE_OTHER,
) = range(26)
PIECES = {
    QKV: (768, 1152),
    SQUARE: (1248, 768),
    UP: (672, 1536),
    PATCH_ROWS: (704, 768),
    E2D: (768, 384),
    HEAD: (64, 1536),
    VECS: (16, 768),
    DEC_QKV: (384, 576),
    DEC_OUT: (192, 384),
    DEC_UP: (384, 768),
    DEC_DOWN: (768, 384),
}


DEC_PARTS = [DEC_QKV, DEC_OUT, DEC_UP, DEC_DOWN, HEAD_HALF]
SENT = [QKV, SQUARE, UP, PATCH_ROWS, E2D, HEAD, VECS] + DEC_PARTS
ENC_PARTS = [
    (PATCH_LOW, 704, 0, PATCH_ROWS, 0),
    (W_QKV, 768, 0, QKV, 0),
    (W_OUT, 288, 0, SQUARE, 0),
    (W_OUT, 96, 1, SQUARE, 288),
    (PATCH_HIGH, 192, 2, PATCH_ROWS, 0),
    (W_UP, 672, 1, UP, 0),
    (W_UP, 96, 2, UP, 672),
    (W_DOWN, 1248, 2, SQUARE, 0),
    (W_DOWN, 288, 3, SQUARE, 1248),
    (E2D_W, 768, 2, E2D, 0),
]
MESH_ID = pl.DeviceIdType.MESH


VISIBLE = 160
OWN = 2 * VISIBLE
ALL = 4 * VISIBLE
SPAN = (0, 768, 1536)
DEPTH = (704, 704, 192)
WIDE = 1792
SQRT_HALF = 0.5**0.5


def norm_parts(x):
    center = jnp.mean(x, -1, keepdims=True)
    moved = x - center
    scale = lax.rsqrt(jnp.mean(moved * moved, -1, keepdims=True) + 1e-06)
    return moved * scale, scale


def norm_to(x, gain, bias):
    return norm_parts(x)[0] * gain + bias


def norm_from(x, gain, cotangent):
    hat, scale = norm_parts(x)
    inner = cotangent * gain
    grad = scale * (
        inner - jnp.mean(inner, -1, keepdims=True) - hat * jnp.mean(inner * hat, -1, keepdims=True)
    )
    return grad, jnp.sum(cotangent * hat, 0, keepdims=True), jnp.sum(cotangent, 0, keepdims=True)


def gelu_to(x):
    return 0.5 * x * (1.0 + lax.erf(x * SQRT_HALF))


def gelu_slope(x):
    return 0.5 * (1.0 + lax.erf(x * SQRT_HALF)) + x * jnp.exp(-0.5 * x * x) * (2.0 * math.pi) ** -0.5


def rows_at(index, count=VISIBLE):
    return pl.ds(index * count, count)


class Links:
    def __init__(self, send_sem, recv_sem):
        self.send_sem, self.recv_sem, self.keys = send_sem, recv_sem, {}

    def copy(self, key, source, target, peer):
        index = self.keys.setdefault(key, len(self.keys))
        return pltpu.make_async_remote_copy(
            src_ref=source,
            dst_ref=target,
            send_sem=self.send_sem.at[index],
            recv_sem=self.recv_sem.at[index],
            device_id=peer,
            device_id_type=MESH_ID,
        )


LANDED = [W_QKV, W_OUT, W_UP, W_DOWN, E2D_W, VECS]
LANDED_SHAPES = [(768, 1152), (384, 768), (768, 1536), (1536, 768), (768, 384), (16, 768)]
STORED = [
    ((OWN, D), FLOAT),
    ((ALL, D), HALF),
    ((ALL, 3 * D // 2), HALF),
    ((ALL, D // 2), HALF),
    ((OWN, D), FLOAT),
    ((ALL, D), HALF),
    ((ALL, FF // 2), FLOAT),
    ((ALL, FF // 2), HALF),
    ((OWN, D), FLOAT),
    ((OWN, D), HALF),
]


def forward_kernel(shared, *refs):
    sent, refs = dict(zip(SENT, refs[: len(SENT)])), refs[len(SENT) :]
    shown, ids, far_places, near_places, refs = refs[0], refs[1], refs[2], refs[3], refs[4:]
    got, refs = dict(zip(LANDED, refs[: len(LANDED)])), refs[len(LANDED) :]
    got[HEAD], reduced, refs = refs[0], refs[1], refs[2:]
    own, refs = dict(zip(DEC_PARTS, refs[: len(DEC_PARTS)])), refs[len(DEC_PARTS) :]
    other, refs = dict(zip(DEC_PARTS, refs[: len(DEC_PARTS)])), refs[len(DEC_PARTS) :]
    stream, normed, joined, blended, attended, second, upward, activated, encoded, final_enc = refs[:10]
    got[PATCH_LOW], patch_mid, got[PATCH_HIGH], part_sent, part_got, reduced_own, places = refs[10:17]
    send_sem, recv_sem, local_sem = refs[17:]
    g, z, x = lax.axis_index("group"), lax.axis_index("dp"), lax.axis_index("tensor")
    odd = lax.rem(g, 2)
    mate = (g + 1 - 2 * odd, z, x)
    across = (g, z, 1 - x)
    links = Links(send_sem, recv_sem)
    copy = links.copy
    barrier = pltpu.get_barrier_semaphore()

    def at(row, column=None):
        return (g, row, x if column is None else column)

    def greet(peer):
        pl.semaphore_signal(barrier, inc=1, device_id=peer, device_id_type=MESH_ID)

    greet(across)
    if shared:
        greet(mate)
    near = {0: [1], 1: [0, 2, 3], 2: [1, 3], 3: [2, 1]}
    for row, peers in near.items():

        @pl.when(z == row)
        def _():
            for peer in peers:
                greet(at(peer))
            if row != HOST:

                @pl.when(x != row // 2)
                def _():
                    greet(at(HOST, row // 2))

                pl.semaphore_wait(barrier, len(peers) + (2 if shared else 1))

    for column in range(2):

        @pl.when((z == HOST) & (x == column))
        def _():
            pl.semaphore_wait(barrier, 3 + (2 if shared else 1) + 1 + column)

    def part(ref, start, count, half, index=odd):
        if not half:
            return ref.at[pl.ds(start, count)]
        return ref.at[pl.ds(pl.multiple_of(start + index * (count // 2), 16), count // 2)]

    def twice(name):
        return not shared and name in (PATCH_LOW, PATCH_HIGH, E2D_W)

    keys = [(SEND_ENC, item[0], item[4]) for item in ENC_PARTS] + [(SEND_MATE, item[0], item[4]) for item in ENC_PARTS]
    for name in DEC_PARTS + [VECS, HEAD, HEAD_UP]:
        keys += [(label, name) for label in (CHAIN, CROSS, MATE_OWN, MATE_OTHER)]
    for key in keys + list(range(12)):
        links.keys[key] = len(links.keys)

    def enc_copy(item):
        name, count, owner, piece, first = item
        half, index = shared or twice(name), x if twice(name) else odd
        return copy(
            (SEND_ENC, name, first),
            part(sent[piece], 0, count, half, index),
            part(got[name], first, count, half, index),
            at(HOST),
        )

    def enc_mate(item):
        name, count, owner, piece, first = item
        half = part(got[name], first, count, True, x if twice(name) else odd)
        return copy((SEND_MATE, name, first), half, half, across if twice(name) else mate)

    def local(index, source, target):
        return pltpu.make_async_copy(source, target, local_sem.at[index])

    def chain(name, source, peer):
        target = got[name] if name in got else own[name]
        rows = source.shape[0]
        half = shared and name in own
        return copy((CHAIN, name), part(source, 0, rows, half), part(target, 0, rows, half), at(peer))

    def cross(name, source):
        rows = source.shape[0]
        return copy((CROSS, name), part(source, 0, rows, shared), part(other[name], 0, rows, shared), across)

    def mates(name, ref, label):
        half = part(ref, 0, ref.shape[0], True)
        return copy((label, name), half, half, mate)

    def owned(row):
        return [item for item in ENC_PARTS if item[2] == row and row != HOST]

    def head_up():
        return copy((CHAIN, HEAD_UP), sent[HEAD], got[HEAD], at(LAST))

    def finish_dec(name, source, here):
        cross(name, source).start()
        if shared and not here:
            mates(name, own[name], MATE_OWN).start()

    def end_all(source_of, here):
        for name in DEC_PARTS:
            cross(name, source_of[name]).wait()
            if shared:
                mates(name, other[name], MATE_OTHER).start()
        for name in DEC_PARTS:
            if shared:
                if not here:
                    mates(name, own[name], MATE_OWN).wait()
                mates(name, other[name], MATE_OTHER).wait()

    def give(column, clip):
        row = 2 * column + clip
        return [
            copy(8 + 2 * clip + side, reduced_own.at[clip], reduced, at(row, side))
            for side in range(2)
            if (row, side) != (HOST, column)
        ]

    @pl.when(z == LAST)
    def _():
        chain(VECS, sent[VECS], 2).start()
        locals_ = [local(i, sent[name], own[name]) for i, name in enumerate(DEC_PARTS)]
        locals_.append(local(len(DEC_PARTS), sent[VECS], got[VECS]))
        for one in locals_:
            one.start()
        for item in owned(LAST):
            enc_copy(item).start()
            enc_copy(item).wait_send()
        for i, name in enumerate(DEC_PARTS):
            chain(name, sent[name], 2).start()
            finish_dec(name, sent[name], True)
            if i:
                chain(DEC_PARTS[i - 1], sent[DEC_PARTS[i - 1]], 2).wait_send()
        chain(DEC_PARTS[-1], sent[DEC_PARTS[-1]], 2).wait_send()
        chain(VECS, sent[VECS], 2).wait_send()
        end_all(sent, True)
        for one in locals_:
            one.wait()
        head_up().wait_recv()

    @pl.when(z == 2)
    def _():
        first = local(0, sent[HEAD], got[HEAD])
        first.start()
        chain(VECS, sent[VECS], 2).wait_recv()
        chain(VECS, got[VECS], HOST).start()
        late = [item for item in owned(2) if item[0] == E2D_W]
        for item in owned(2):
            if item not in late:
                enc_copy(item).start()
                enc_copy(item).wait_send()
        head_up().start()
        chain(HEAD, sent[HEAD], HOST).start()
        for i, name in enumerate(DEC_PARTS):
            chain(name, sent[name], 2).wait_recv()
            chain(name, own[name], HOST).start()
            finish_dec(name, own[name], False)
            if i:
                chain(DEC_PARTS[i - 1], own[DEC_PARTS[i - 1]], HOST).wait_send()
        for item in late:
            enc_copy(item).start()
            enc_copy(item).wait_send()
        chain(DEC_PARTS[-1], own[DEC_PARTS[-1]], HOST).wait_send()
        end_all(own, False)
        chain(VECS, got[VECS], HOST).wait_send()
        chain(HEAD, sent[HEAD], HOST).wait_send()
        head_up().wait_send()
        first.wait()

    @pl.when(z == 0)
    def _():
        for item in owned(0):
            enc_copy(item).start()
            enc_copy(item).wait_send()
        for name in DEC_PARTS:
            chain(name, sent[name], 0).wait_recv()
            finish_dec(name, own[name], False)
        end_all(own, False)
        chain(VECS, sent[VECS], 0).wait_recv()
        chain(HEAD, sent[HEAD], 0).wait_recv()

    @pl.when(z == HOST)
    def _():
        mine = [
            local(i, sent[piece].at[pl.ds(0, count)], got[name].at[pl.ds(first, count)])
            for i, (name, count, owner, piece, first) in enumerate(ENC_PARTS)
            if owner == HOST
        ]
        mine.append(local(len(ENC_PARTS), sent[PATCH_ROWS], patch_mid))
        for one in mine:
            one.start()
        chain(VECS, sent[VECS], HOST).wait_recv()
        chain(VECS, got[VECS], 0).start()
        vec = got[VECS][...].astype(FLOAT)
        for one in mine:
            one.wait()

        def await_parts(names):
            items = [item for item in ENC_PARTS if item[2] != HOST and item[0] in names]
            for item in items:
                enc_copy(item).wait_recv()
                if shared or twice(item[0]):
                    enc_mate(item).start()
            for item in items:
                if shared or twice(item[0]):
                    enc_mate(item).wait()

        def pump(name):
            chain(name, sent[name], HOST).wait_recv()
            chain(name, own[name], 0).start()
            finish_dec(name, own[name], False)

        def normed_copy(i):
            return copy(i, normed.at[rows_at(i)], normed.at[rows_at(2 + i)], across)

        def out_copy(i):
            return copy(2 + i, part_sent.at[rows_at(i)], part_got.at[rows_at(i)], across)

        def second_copy(i):
            return copy(4 + i, second.at[rows_at(i)], second.at[rows_at(2 + i)], across)

        def down_copy(i):
            return copy(6 + i, part_sent.at[rows_at(2 + i)], part_got.at[rows_at(2 + i)], across)

        spots = lax.broadcasted_iota(jnp.int32, (OWN, 64), 1)
        high = ((ids[...] // 32) == spots).astype(FLOAT).astype(HALF)
        low_hot = (lax.rem(ids[...], 32) == spots).astype(FLOAT).astype(HALF)
        far = mm(high, far_places[0]) + mm(high, far_places[1]) + mm(high, far_places[2])
        near = mm(low_hot, near_places[0]) + mm(low_hot, near_places[1]) + mm(low_hot, near_places[2])
        places[...] = far[:, :D] * near[:, :D] + far[:, D:] * near[:, D:]
        await_parts((PATCH_LOW, PATCH_HIGH))
        for i in range(2):
            rows = rows_at(i)
            emb = places[rows] + vec[0:1]
            for start, depth, weight in zip(SPAN, DEPTH, (got[PATCH_LOW], patch_mid, got[PATCH_HIGH])):
                emb = emb + mm(shown[rows, start : start + depth], weight[...])
            stream[rows] = emb
            normed[rows] = norm_to(emb, vec[1:2], vec[2:3]).astype(HALF)
            normed_copy(i).start()
        await_parts((W_QKV,))

        def attend(c):
            rows = rows_at(c)
            joined[rows] = mm(normed[rows], got[W_QKV][...]).astype(HALF)
            width = D // 2
            thirds = [[joined[rows, t * width + h * HDIM : t * width + (h + 1) * HDIM] for h in range(width // HDIM)] for t in range(3)]
            scores = [mm_nt(one, two) * HDIM**-0.5 for one, two in zip(*thirds[:2])]
            weights = [jnp.exp(one - jnp.max(one, -1, keepdims=True)) for one in scores]
            probs = [(one * (1.0 / jnp.sum(one, -1, keepdims=True))).astype(HALF) for one in weights]
            blended[rows] = jnp.concatenate([mm(one, two) for one, two in zip(probs, thirds[2])], 1).astype(HALF)

        for i in range(2):
            attend(i)
            if i == 0:
                await_parts((W_OUT,))
            attended[rows_at(i)] = mm(blended[rows_at(i)], got[W_OUT][...]) + stream[rows_at(i)] + vec[3:4]
            normed_copy(i).wait_recv()
            attend(2 + i)
            part_sent[rows_at(i)] = mm(blended[rows_at(2 + i)], got[W_OUT][...]).astype(HALF)
            out_copy(i).start()

        def feed(c):
            rows = rows_at(c)
            up = mm(second[rows], got[W_UP][...])
            upward[rows] = up
            activated[rows] = gelu_to(up).astype(HALF)
            return mm(activated[rows], got[W_DOWN][...])

        for i in range(2):
            rows = rows_at(i)
            out_copy(i).wait_recv()
            after = attended[rows] + part_got[rows].astype(FLOAT)
            attended[rows] = after
            second[rows] = norm_to(after, vec[4:5], vec[5:6]).astype(HALF)
            second_copy(i).start()
        await_parts((W_UP, W_DOWN))
        chain(HEAD, sent[HEAD], HOST).wait_recv()
        chain(HEAD, got[HEAD], 0).start()
        pump(DEC_QKV)
        pump(DEC_OUT)
        for i in range(2):
            rows = rows_at(i)
            encoded[rows] = feed(i) + attended[rows] + vec[6:7]
            second_copy(i).wait_recv()
            part_sent[rows_at(2 + i)] = feed(2 + i).astype(HALF)
            down_copy(i).start()
            pump((DEC_UP, DEC_DOWN)[i])
        pump(HEAD_HALF)
        await_parts((E2D_W,))
        for i in range(2):
            rows = rows_at(i)
            down_copy(i).wait_recv()
            after = encoded[rows] + part_got[rows_at(2 + i)].astype(FLOAT)
            encoded[rows] = after
            low = norm_to(after, vec[7:8], vec[8:9]).astype(HALF)
            final_enc[rows] = low
            reduced_own[i] = mm(low, got[E2D_W][...])
            for column in range(2):

                @pl.when(x == column)
                def _():
                    for one in give(column, i):
                        one.start()

        for i in range(2):
            normed_copy(i).wait_send()
            out_copy(i).wait_send()
            second_copy(i).wait_send()
            down_copy(i).wait_send()
        for column in range(2):

            @pl.when(x == column)
            def _():
                for i in range(2):
                    for one in give(column, i):
                        one.wait_send()

        end_all(own, False)
        for name in DEC_PARTS:
            chain(name, own[name], 0).wait_send()
        chain(VECS, got[VECS], 0).wait_send()
        chain(HEAD, got[HEAD], 0).wait_send()

    @pl.when((z == HOST) & (x == 0))
    def _():
        mine = local(0, reduced_own.at[1], reduced)
        mine.start()
        mine.wait()

    for row in range(4):
        for side in range(2):
            if (row, side) != (HOST, 0):

                @pl.when((z == row) & (x == side))
                def _():
                    key = 8 + 2 * (row % 2) + side
                    copy(key, reduced_own.at[row % 2], reduced, at(HOST, row // 2)).wait_recv()


def encoder_forward(number, shared, pieces, shown_own, ids_and_places):
    side = lax.axis_index("tensor")
    vmem = pl.BlockSpec(memory_space=pltpu.VMEM)
    anywhere = pl.BlockSpec(memory_space=pl.ANY)
    dec_shapes = [(pieces[name].shape, HALF) for name in DEC_PARTS]
    shapes = [(one, HALF) for one in LANDED_SHAPES] + [((64, PATCH), HALF), ((VISIBLE, DD), FLOAT)]
    shapes = shapes + 2 * dec_shapes + STORED
    count = 2 * len(ENC_PARTS) + 4 * (len(DEC_PARTS) + 3) + 12
    scratch = [
        ((704, D), HALF),
        ((704, D), HALF),
        ((192, D), HALF),
        ((ALL, D), HALF),
        ((ALL, D), HALF),
        ((2, VISIBLE, DD), FLOAT),
        ((OWN, D), FLOAT),
    ]
    out = pl.pallas_call(
        functools.partial(forward_kernel, shared),
        name="encoder_forward",
        out_shape=[jax.ShapeDtypeStruct(*one) for one in shapes],
        in_specs=[anywhere] * len(SENT) + [vmem] * 4,
        out_specs=[vmem] * len(LANDED) + [anywhere, vmem] + [anywhere] * (2 * len(DEC_PARTS)) + [vmem] * len(STORED),
        scratch_shapes=[pltpu.VMEM(*one) for one in scratch]
        + [
            pltpu.SemaphoreType.DMA((count,)),
            pltpu.SemaphoreType.DMA((count,)),
            pltpu.SemaphoreType.DMA((len(ENC_PARTS) + 1,)),
        ],
        compiler_params=pltpu.CompilerParams(
            collective_id=number, has_side_effects=True, vmem_limit_bytes=56 << 20
        ),
    )(*[pieces[name] for name in SENT], shown_own, *ids_and_places)
    landed, out = out[: len(LANDED)], out[len(LANDED) :]
    head, reduced, out = out[0], out[1], out[2:]
    own, other, stored = out[: len(DEC_PARTS)], out[len(DEC_PARTS) : 2 * len(DEC_PARTS)], out[2 * len(DEC_PARTS) :]
    low, high = jnp.where(side == 0, own[4], other[4]), jnp.where(side == 0, other[4], own[4])
    head_w = jnp.concatenate([low, high], 1)
    head_w = jnp.concatenate([head_w[:64] + head, head_w[64:]], 0)
    enc_vec, dec_vec, head_b = split_flat(landed[5].astype(FLOAT).reshape(-1), [(9, D), (10, DD), (PATCH,)])
    enc_weights = (landed[:4], landed[4], jnp.pad(enc_vec, ((0, 7), (0, 0))))
    return reduced, stored, enc_weights, (own[:4], other[:4], head_w, dec_vec, head_b)


def encoder_backward_kernel(
    picked, shown, shown_other, w_qkv, w_out, w_up, w_down, e2d_w, vec,
    stream, normed, joined, blended, attended, second, upward, activated, encoded, final_enc,
    wide, tall, dec_qkv, small, normed_far, active_far,
    qkv_out, square_out, up_out, patch_out, e2d_out, vec_out,
    one_wide, one_tall, one_qkv, one_small, two_wide, two_tall, two_qkv, two_small,
    wide_sent, tall_sent, dec_qkv_sent, small_sent, wide_got, tall_got, dec_qkv_got, small_got,
    picks_got, low, grad_up_in, mid, grad_blend, grad_joined, part_sent, part_got, own_rows_grad, own_part,
    emb_low, emb_got, down_grad, up_grad, out_grad, qkv_grad, patch_low, patch_mid, patch_high, e2d_part, e2d_got, e2d_grad,
    vec_part, vec_got, send_sem, recv_sem, local_sem,
):
    g, z, x = lax.axis_index("group"), lax.axis_index("dp"), lax.axis_index("tensor")
    barrier = pltpu.get_barrier_semaphore()
    links = Links(send_sem, recv_sem)

    def at(row, column):
        return (g, row, column)

    def greet(peer):
        pl.semaphore_signal(barrier, inc=1, device_id=peer, device_id_type=MESH_ID)

    @pl.when(z != HOST)
    def _():
        greet(at(HOST, x))

    @pl.when(z == LAST)
    def _():
        greet(at(2, x))

    @pl.when((z == HOST) & (x == 0))
    def _():
        for peer in ((0, 0), (0, 1), (HOST, 1)):
            greet(at(*peer))

    @pl.when((z == HOST) & (x == 1))
    def _():
        for peer in ((2, 0), (2, 1), (3, 0), (3, 1), (0, 1), (HOST, 0)):
            greet(at(*peer))

    @pl.when(z == HOST)
    def _():
        pl.semaphore_wait(barrier, 4)

    @pl.when((z == 2) | ((z == 0) & (x == 1)))
    def _():
        pl.semaphore_wait(barrier, 2)

    @pl.when((z == LAST) | ((z == 0) & (x == 0)))
    def _():
        pl.semaphore_wait(barrier, 1)

    def pick_copy(row, side):
        return links.copy((row % 2) * 2 + side, picked, picks_got.at[row % 2, side], at(HOST, row // 2))

    for row in range(4):
        for side in range(2):
            if (row, side) != (HOST, 0):

                @pl.when((z == row) & (x == side))
                def _():
                    pick_copy(row, side).start()

    numbers = iter(range(4, 64))
    low_number = [next(numbers), next(numbers)]
    second_number = [next(numbers), next(numbers)]
    mid_number = [next(numbers), next(numbers)]
    normed_number = [next(numbers), next(numbers)]
    emb_number = [next(numbers), next(numbers)]
    e2d_number, vec_number = next(numbers), next(numbers)

    def row_copies(numbers_two, ref):
        return [
            links.copy(numbers_two[i], ref.at[rows_at(i)], ref.at[rows_at(2 + i)], at(HOST, 1 - x)) for i in range(2)
        ]

    def part_copies(numbers_two, first):
        return [
            links.copy(
                numbers_two[i], part_sent.at[rows_at(first + i)], part_got.at[rows_at(first + i)], at(HOST, 1 - x)
            )
            for i in range(2)
        ]

    out_rows, up_rows, down_rows = 288, 672, 1248
    next_row = jnp.minimum(z + 1, LAST)
    low_far = [links.copy(next(numbers), low.at[rows_at(c)], low.at[rows_at(c)], at(2, x)) for c in range(4)]
    down_far = links.copy(next(numbers), down_grad.at[pl.ds(96, 288)], square_out.at[pl.ds(0, 288)], at(LAST, x))
    joined_far = [
        links.copy(next(numbers), grad_joined.at[rows_at(c)], grad_joined.at[rows_at(c)], at(0, x)) for c in range(4)
    ]
    up_near = links.copy(next(numbers), up_grad.at[pl.ds(up_rows, 96)], up_out.at[pl.ds(0, 96)], at(2, x))
    out_near = links.copy(
        next(numbers), out_grad.at[pl.ds(0, out_rows)], square_out.at[pl.ds(0, out_rows)], at(0, x)
    )
    patch_one = links.copy(next(numbers), patch_low, patch_out, at(0, x))
    patch_two = links.copy(next(numbers), patch_high, patch_out.at[pl.ds(0, 192)], at(2, x))
    e2d_near = links.copy(next(numbers), e2d_grad, e2d_out, at(2, x))
    vec_far = links.copy(next(numbers), vec_part, vec_out, at(LAST, x))

    own_dec = (wide, tall, dec_qkv, small)
    sent_dec = (wide_sent, tall_sent, dec_qkv_sent, small_sent)
    got_dec = (wide_got, tall_got, dec_qkv_got, small_got)
    one_dec = (one_wide, one_tall, one_qkv, one_small)
    two_dec = (two_wide, two_tall, two_qkv, two_small)
    tree_one = [links.copy(next(numbers), sent_dec[i], got_dec[i], at(next_row, x)) for i in range(4)]
    tree_two = [links.copy(next(numbers), sent_dec[i], two_dec[i], at(LAST, x)) for i in range(4)]

    @pl.when((z == 0) | (z == 2))
    def _():
        for i in (3, 0, 1, 2):
            sent_dec[i][...] = own_dec[i][...].astype(sent_dec[i].dtype)
        for i in (3, 0, 1, 2):
            tree_one[i].start()
            if i != 3:
                tree_one[i].wait_send()

    def pass_on(*parts):
        for i in parts:
            tree_one[i].wait_recv()
            sent_dec[i][...] = (own_dec[i][...] + got_dec[i][...].astype(FLOAT)).astype(sent_dec[i].dtype)
            tree_two[i].start()

    def tall_product(left, right, target, step):
        def body(t, carry):
            columns = pl.ds(pl.multiple_of(t * step, step), step)
            target[columns] = mm_tn(left[:, columns], right[...]).astype(HALF)
            return carry

        lax.fori_loop(0, target.shape[0] // step, body, 0)

    @pl.when(z == HOST)
    def _():
        low_sent, mid_sent = row_copies(low_number, low), row_copies(mid_number, mid)
        second_sent, normed_sent = part_copies(second_number, 0), part_copies(normed_number, 2)
        emb_sent = [
            links.copy(
                emb_number[i],
                emb_low.at[1 - x, rows_at(i)],
                emb_got.at[rows_at(i)],
                at(HOST, 1 - x),
            )
            for i in range(2)
        ]
        e2d_sent = links.copy(e2d_number, e2d_part.at[1 - x], e2d_got, at(HOST, 1 - x))
        vec_sent = links.copy(vec_number, vec_part, vec_got, at(HOST, 1 - x))

        vec_part[...] = jnp.zeros_like(vec_part)

        def count(row, value):
            vec_part[row : row + 1] += value

        @pl.when(x == 0)
        def _():
            mine = pltpu.make_async_copy(picked, picks_got.at[1, 0], local_sem.at[0])
            mine.start()
            mine.wait()

        for clip in range(2):
            for side in range(2):
                waiting = links.copy(clip * 2 + side, picked, picks_got.at[clip, side], at(HOST, 0))
                if clip == HOST % 2 and side == 0:

                    @pl.when(x == 1)
                    def _():
                        waiting.wait_recv()

                else:
                    waiting.wait_recv()
        reduced_low = []
        for i in range(2):
            rows = rows_at(i)
            one = picks_got[i, 0] + picks_got[i, 1]
            reduced_low.append(one)
            grad, gain, bias = norm_from(encoded[rows], vec[7:8], mm_nt(one, e2d_w[...]))
            count(7, gain)
            count(8, bias)
            count(6, jnp.sum(grad, 0, keepdims=True))
            own_rows_grad[rows] = grad
            low[rows] = grad.astype(HALF)
            low_sent[i].start()
            low_far[i].start()
        whole_low = jnp.concatenate(reduced_low, 0)
        product = mm_tn(final_enc[...], whole_low)
        e2d_part[0] = product[: D // 2]
        e2d_part[1] = product[D // 2 :]
        e2d_sent.start()

        def feed_back(c):
            rows = rows_at(c)
            grad_up_in[rows] = (mm_nt(low[rows], w_down[...]) * gelu_slope(upward[rows])).astype(HALF)
            return mm_nt(grad_up_in[rows], w_up[...])

        for i in range(2):
            own_part[rows_at(i)] = feed_back(i)
            low_sent[i].wait_recv()
            low_far[2 + i].start()
            part_sent[rows_at(i)] = feed_back(2 + i).astype(HALF)
            second_sent[i].start()
        down_grad[pl.ds(0, 384)] = mm_tn(activated[:, 1152:], low[...]).astype(HALF)
        down_far.start()
        for i in range(2):
            rows = rows_at(i)
            second_sent[i].wait_recv()
            total = own_part[rows] + part_got[rows].astype(FLOAT)
            grad, gain, bias = norm_from(attended[rows], vec[4:5], total)
            count(4, gain)
            count(5, bias)
            grad = grad + own_rows_grad[rows]
            count(3, jnp.sum(grad, 0, keepdims=True))
            own_rows_grad[rows] = grad
            mid[rows] = grad.astype(HALF)
            mid_sent[i].start()
        e2d_sent.wait()
        e2d_grad[...] = (e2d_part[x] + e2d_got[...]).astype(HALF)
        e2d_near.start()

        def attend_back(c):
            rows = rows_at(c)
            width = D // 2
            grad_blend[...] = mm_nt(mid[rows], w_out[...]).astype(HALF)
            heads = range(width // HDIM)
            queries, keys, values = [[joined[rows, t * width + h * HDIM : t * width + (h + 1) * HDIM] for h in heads] for t in range(3)]
            grads = [grad_blend[:, h * HDIM : (h + 1) * HDIM] for h in heads]
            scores = [mm_nt(queries[h], keys[h]) * HDIM**-0.5 for h in heads]
            grad_probs = [mm_nt(grads[h], values[h]) for h in heads]
            weights = [jnp.exp(one - jnp.max(one, -1, keepdims=True)) for one in scores]
            probs = [one * (1.0 / jnp.sum(one, -1, keepdims=True)) for one in weights]
            sums = [jnp.sum(probs[h] * grad_probs[h], -1, keepdims=True) for h in heads]
            grad_scores = [(probs[h] * (grad_probs[h] - sums[h])).astype(HALF) for h in heads]
            parts = [mm(grad_scores[h], keys[h]) * HDIM**-0.5 for h in heads]
            parts += [mm_tn(grad_scores[h], queries[h]) * HDIM**-0.5 for h in heads]
            parts += [mm_tn(probs[h].astype(HALF), grads[h]) for h in heads]
            grad_joined[rows] = jnp.concatenate(parts, 1).astype(HALF)
            return mm_nt(grad_joined[rows], w_qkv[...])

        for i in range(2):
            own_part[rows_at(i)] = attend_back(i)
            joined_far[i].start()
            pass_on(*((3, 0), (1,))[i])
            mid_sent[i].wait_recv()
            part_sent[rows_at(2 + i)] = attend_back(2 + i).astype(HALF)
            normed_sent[i].start()
            joined_far[2 + i].start()
        pass_on(2)
        tall_product(blended, mid, out_grad, 384)
        out_near.start()
        for i in range(2):
            rows = rows_at(i)
            normed_sent[i].wait_recv()
            total = own_part[rows] + part_got[rows_at(2 + i)].astype(FLOAT)
            grad, gain, bias = norm_from(stream[rows], vec[1:2], total)
            count(1, gain)
            count(2, bias)
            grad = grad + own_rows_grad[rows]
            count(0, jnp.sum(grad, 0, keepdims=True))
            grad_low = grad.astype(HALF)
            emb_low[0, rows] = grad_low[:, : D // 2]
            emb_low[1, rows] = grad_low[:, D // 2 :]
            emb_sent[i].start()
        vec_sent.start()
        tall_product(second, grad_up_in, up_grad, 384)
        up_near.start()
        for one in emb_sent:
            one.wait()
        for start, depth, target in zip(SPAN, DEPTH, (patch_low, patch_mid, patch_high)):
            columns = slice(start, start + depth)
            target[...] = (mm_tn(shown[:, columns], emb_low[x]) + mm_tn(shown_other[:, columns], emb_got[...])).astype(HALF)
        patch_one.start()
        patch_two.start()
        vec_sent.wait()
        vec_part[...] += vec_got[...]
        vec_far.start()
        mine = [
            pltpu.make_async_copy(out_grad.at[pl.ds(out_rows, 96)], square_out.at[pl.ds(0, 96)], local_sem.at[1]),
            pltpu.make_async_copy(up_grad.at[pl.ds(0, up_rows)], up_out, local_sem.at[2]),
            pltpu.make_async_copy(patch_mid, patch_out, local_sem.at[3]),
        ]
        for one in mine:
            one.start()
        for one in low_sent + mid_sent + second_sent + normed_sent:
            one.wait_send()
        for one in (*low_far, down_far, *joined_far, up_near, out_near, patch_one, patch_two, e2d_near, vec_far):
            one.wait_send()
        for one in tree_two:
            one.wait_send()
        for one in mine:
            one.wait()

    for row in range(4):
        for side in range(2):
            if (row, side) != (HOST, 0):

                @pl.when((z == row) & (x == side))
                def _():
                    pick_copy(row, side).wait_send()

    for row, ones in ((0, (out_near, patch_one)), (2, (up_near, patch_two, e2d_near)), (LAST, (down_far, vec_far))):

        @pl.when(z == row)
        def _():
            for one in ones:
                one.wait_recv()

    @pl.when((z == 0) | (z == 2))
    def _():
        tree_one[3].wait_send()

    @pl.when(z == 2)
    def _():
        for one in low_far:
            one.wait_recv()
        tall_product(active_far, low, down_grad, 384)
        kept = pltpu.make_async_copy(down_grad.at[pl.ds(0, down_rows)], square_out, local_sem.at[0])
        kept.start()
        kept.wait()

    @pl.when(z == 0)
    def _():
        for one in joined_far:
            one.wait_recv()
        tall_product(normed_far, grad_joined, qkv_grad, 384)
        kept = pltpu.make_async_copy(qkv_grad, qkv_out, local_sem.at[0])
        kept.start()
        kept.wait()

    @pl.when(z == LAST)
    def _():
        kept = []
        for i in range(4):
            tree_one[i].wait_recv()
            kept.append(pltpu.make_async_copy(got_dec[i], one_dec[i], local_sem.at[i]))
            kept[i].start()
        for i in range(4):
            tree_two[i].wait_recv()
            kept[i].wait()


def encoder_backward(number, picked, shown, weights, stored, dec_grads, far):
    mats, e2d_w, vec = weights
    vmem = pl.BlockSpec(memory_space=pltpu.VMEM)
    anywhere = pl.BlockSpec(memory_space=pl.ANY)
    shapes = [
        ((D, 3 * D // 2), HALF),
        ((1248, D), HALF),
        ((672, FF // 2), HALF),
        ((704, D // 2), HALF),
        ((D // 2, DD), HALF),
        ((16, D), FLOAT),
    ]
    tree = [(one.shape, HALF) for one in dec_grads[:3]] + [(dec_grads[3].shape, FLOAT)]
    shapes = shapes + 2 * tree
    scratch = 2 * tree + [
        ((2, 2, VISIBLE, DD), HALF),
        ((ALL, D), HALF),
        ((ALL, FF // 2), HALF),
        ((ALL, D), HALF),
        ((VISIBLE, D // 2), HALF),
        ((ALL, 3 * D // 2), HALF),
        ((ALL, D), HALF),
        ((ALL, D), HALF),
        ((OWN, D), FLOAT),
        ((OWN, D), FLOAT),
        ((2, OWN, D // 2), HALF),
        ((OWN, D // 2), HALF),
        ((FF // 2, D), HALF),
        ((D, FF // 2), HALF),
        ((D // 2, D), HALF),
        ((D, 3 * D // 2), HALF),
        ((704, D // 2), HALF),
        ((704, D // 2), HALF),
        ((192, D // 2), HALF),
        ((2, D // 2, DD), FLOAT),
        ((D // 2, DD), FLOAT),
        ((D // 2, DD), HALF),
        ((16, D), FLOAT),
        ((16, D), FLOAT),
    ]
    return pl.pallas_call(
        encoder_backward_kernel,
        name="encoder_backward",
        out_shape=[jax.ShapeDtypeStruct(*one) for one in shapes],
        in_specs=[vmem] * 25,
        out_specs=[anywhere] * len(shapes),
        scratch_shapes=[pltpu.VMEM(*one) for one in scratch]
        + [pltpu.SemaphoreType.DMA((44,)), pltpu.SemaphoreType.DMA((44,)), pltpu.SemaphoreType.DMA((4,))],
        compiler_params=pltpu.CompilerParams(
            collective_id=number, has_side_effects=True, vmem_limit_bytes=60 << 20
        ),
    )(picked, *shown, *mats, e2d_w, vec, *stored, *dec_grads, *far)


LANES = 128
STEP_ROWS = 96
TEN_LANES = 8640
REP_LANES = 4056
LAID = [QKV, SQUARE, UP, PATCH_ROWS, E2D, HEAD, VECS, DEC_QKV, DEC_OUT, DEC_UP, DEC_DOWN, HEAD_HALF]
LAID_SHAPES = {**PIECES, HEAD_HALF: (384, 768)}
TEN_PLACES = [
    [(QKV, 768, 0), (SQUARE, 288, 6912)],
    [(SQUARE, 96, 0), (UP, 672, 576)],
    [(UP, 96, 0), (SQUARE, 1248, 1152)],
    [(SQUARE, 288, 0), (DEC_OUT, 192, 3456), (DEC_UP, 384, 4032), (DEC_DOWN, 768, 6336)],
]
DEC_QKV_PLACE = 1728
PATCH_COUNTS = (676, 676, 184)
E2D_PLACE = 1104
HEAD_PLACE = 3408
HEAD_TOP = 54
VEC_PLACE = 3960


def spread_rows(flat, place, blocks, count, read):
    def put(first, value):
        rows = value.shape[0]
        for j in range(blocks):
            flat[pl.ds(place + first * blocks + j, rows, stride=blocks), :] = value[:, j * LANES : (j + 1) * LANES]

    def body(t, carry):
        put(t * STEP_ROWS, read(pl.multiple_of(t * STEP_ROWS, 16), STEP_ROWS))
        return carry

    whole = count // STEP_ROWS
    if whole:
        lax.fori_loop(0, whole, body, 0)
    rest = count - whole * STEP_ROWS
    if rest:
        put(whole * STEP_ROWS, read(whole * STEP_ROWS, -(-rest // 16) * 16)[:rest])


def gather_rows(piece, flat, place, blocks, count):
    def put(first, rows, padded):
        for j in range(blocks):
            value = flat[pl.ds(place + first * blocks + j, rows, stride=blocks), :]
            if padded > rows:
                value = jnp.concatenate([value, jnp.zeros((padded - rows, LANES), FLOAT)], 0)
            piece[pl.ds(first, padded), j * LANES : (j + 1) * LANES] = value.astype(HALF)

    def body(t, carry):
        put(pl.multiple_of(t * STEP_ROWS, 16), STEP_ROWS, STEP_ROWS)
        return carry

    whole = count // STEP_ROWS
    if whole:
        lax.fori_loop(0, whole, body, 0)
    rest = count - whole * STEP_ROWS
    if rest:
        put(whole * STEP_ROWS, rest, -(-rest // 16) * 16)


def lay_out(z, x, ten, rep, pieces, wide_rows):
    for row in range(4):

        @pl.when(z == row)
        def _():
            for name, count, place in TEN_PLACES[row]:
                gather_rows(pieces[name], ten, place, PIECES[name][1] // LANES, count)
            if row < LAST:
                gather_rows(pieces[PATCH_ROWS], rep, 0, D // LANES, PATCH_COUNTS[row])
            if row < 2:
                pieces[PATCH_ROWS][pl.ds(688, 16)] = jnp.zeros((16, D), HALF)
            if row == 2:
                gather_rows(pieces[E2D], rep, E2D_PLACE, DD // LANES, D)
                gather_rows(pieces[HEAD], rep, HEAD_PLACE, PATCH // LANES, HEAD_TOP)
            if row == LAST:
                gather_rows(pieces[VECS], rep, VEC_PLACE, D // LANES, 16)
                for j in range(4):
                    wide_rows[j, pl.ds(0, 192, stride=2), :] = ten[pl.ds(DEC_QKV_PLACE + j, 192, stride=9), :]
                middle = ten[pl.ds(DEC_QKV_PLACE + 4, 192, stride=9), :]
                late = [middle[:, 64:]] + [ten[pl.ds(DEC_QKV_PLACE + 5 + j, 192, stride=9), :] for j in range(4)]
                late = jnp.concatenate(late + [jnp.zeros((192, 64), FLOAT)], 1)
                wide_rows[4, pl.ds(0, 192, stride=2), :] = middle
                for j in range(5):
                    columns = slice(j * LANES, (j + 1) * LANES)
                    wide_rows[j, pl.ds(1, 192, stride=2), :] = late[:, columns]
                for j in range(4):
                    columns = slice(j * LANES, (j + 1) * LANES)
                    pieces[DEC_QKV][:, columns] = wide_rows[j].astype(HALF)
                pieces[DEC_QKV][:, 512:576] = wide_rows[4][:, :64].astype(HALF)
                half = pieces[HEAD_HALF]
                blocks, offset = PATCH // LANES, x * 6
                half[pl.ds(0, 48)] = jnp.zeros((48, D), HALF)
                for j in range(6):
                    columns = slice(j * LANES, (j + 1) * LANES)
                    value = rep[pl.ds(offset + j, 42, stride=blocks), :]
                    half[pl.ds(48, 48), columns] = jnp.concatenate(
                        [jnp.zeros((6, LANES), FLOAT), value], 0
                    ).astype(HALF)
                    for t in range(1, 4):
                        value = rep[pl.ds((96 * t - HEAD_TOP) * blocks + offset + j, 96, stride=blocks), :]
                        half[pl.ds(96 * t, 96), columns] = value.astype(HALF)


def lay_out_kernel(ten, rep, *refs):
    pieces = dict(zip(LAID, refs))
    lay_out(lax.axis_index("dp"), lax.axis_index("tensor"), ten, rep, pieces, refs[len(LAID)])


def first_pieces(ten, rep):
    vmem = pl.BlockSpec(memory_space=pltpu.VMEM)
    out = pl.pallas_call(
        lay_out_kernel,
        name="lay_out",
        out_shape=[jax.ShapeDtypeStruct(LAID_SHAPES[name], HALF) for name in LAID],
        in_specs=[vmem] * 2,
        out_specs=[vmem] * len(LAID),
        scratch_shapes=[pltpu.VMEM((5, 384, LANES), FLOAT)],
        compiler_params=pltpu.CompilerParams(vmem_limit_bytes=61 << 20),
    )(ten, rep)
    return dict(zip(LAID, out))


def update_kernel(
    number, last,
    stats, qkv, square, up, patch, e2d, vec, wide, tall, dec_qkv, small,
    one_wide, one_tall, one_qkv, one_small, two_wide, two_tall, two_qkv, two_small,
    *refs,
):
    masters, refs = refs[:6], refs[6:]
    stats_out, outs, refs = refs[0], refs[1:7], refs[7:]
    pieces = {}
    if not last:
        pieces, refs = dict(zip(LAID, refs)), refs[len(LAID) :]
    held, refs = refs[:6], refs[6:]
    grad_ten, grad_rep, wide_rows, patch_other, e2d_other, head_own, head_other, slots, send_sem, recv_sem, local_sem = refs
    g, z, x = lax.axis_index("group"), lax.axis_index("dp"), lax.axis_index("tensor")
    me = 2 * z + x
    links = Links(send_sem, recv_sem)
    barrier = pltpu.get_barrier_semaphore()
    loads = [pltpu.make_async_copy(masters[i], held[i], local_sem.at[i]) for i in range(6)]
    for one in loads:
        one.start()

    def peer(shift):
        other = lax.rem(me + shift, 8)
        return (g, other // 2, lax.rem(other, 2))

    for shift in range(1, 8):
        pl.semaphore_signal(barrier, inc=1, device_id=peer(shift), device_id_type=MESH_ID)
    pl.semaphore_wait(barrier, 7)

    across = (g, z, 1 - x)
    patch_swap = links.copy(0, patch, patch_other, across)
    e2d_swap = links.copy(1, e2d, e2d_other, across)
    head_swap = links.copy(2, head_own, head_other, across)
    top_own = links.copy(3, head_own.at[pl.ds(0, 64)], head_own.at[pl.ds(0, 64)], (g, 2, x))
    top_other = links.copy(4, head_other.at[pl.ds(0, 64)], head_other.at[pl.ds(0, 64)], (g, 2, x))

    def plain(ref):
        return lambda first, rows: ref[pl.ds(first, rows)].astype(FLOAT)

    def joined(own, other):
        def read(first, rows):
            one, two = own[pl.ds(first, rows)].astype(FLOAT), other[pl.ds(first, rows)].astype(FLOAT)
            return jnp.concatenate([jnp.where(x == 0, one, two), jnp.where(x == 0, two, one)], 1)

        return read

    def total(own, one, two, top, columns):
        def read(first, rows):
            at = pl.ds(top + first, rows)
            return own[at, columns] + one[at, columns].astype(FLOAT) + two[at, columns].astype(FLOAT)

        return read

    @pl.when(z < LAST)
    def _():
        patch_swap.start()

    @pl.when(z == 2)
    def _():
        e2d_swap.start()

    fc = DFF // 2

    @pl.when(z == LAST)
    def _():
        head_own[...] = total(wide, one_wide, two_wide, 0, slice(fc, 2 * fc))(0, DD)
        head_swap.start()
        top_own.start()
        whole = slice(0, DD)
        spread_rows(grad_ten, 0, 6, 288, plain(square))
        spread_rows(grad_ten, 3456, 3, 192, total(tall, one_tall, two_tall, fc, whole))
        spread_rows(grad_ten, 4032, 6, 384, total(wide, one_wide, two_wide, 0, slice(0, fc)))
        spread_rows(grad_ten, 6336, 3, 768, total(tall, one_tall, two_tall, 0, whole))
        for j in range(4):
            columns = slice(j * LANES, (j + 1) * LANES)
            wide_rows[j] = total(dec_qkv, one_qkv, two_qkv, 0, columns)(0, DD)
        tail = total(dec_qkv, one_qkv, two_qkv, 0, slice(512, 576))(0, DD)
        wide_rows[4] = jnp.concatenate([tail, jnp.zeros((DD, 64), FLOAT)], 1)
        for j in range(4):
            grad_ten[pl.ds(DEC_QKV_PLACE + j, 192, stride=9), :] = wide_rows[j, pl.ds(0, 192, stride=2), :]
        late = jnp.concatenate([wide_rows[j, pl.ds(1, 192, stride=2), :] for j in range(5)], 1)
        early = wide_rows[4, pl.ds(0, 192, stride=2), :]
        grad_ten[pl.ds(DEC_QKV_PLACE + 4, 192, stride=9), :] = jnp.concatenate([early[:, :64], late[:, :64]], 1)
        for j in range(4):
            start = 64 + j * LANES
            grad_ten[pl.ds(DEC_QKV_PLACE + 5 + j, 192, stride=9), :] = late[:, start : start + LANES]
        for j in range(6):
            columns = slice(j * LANES, (j + 1) * LANES)
            grad_rep[pl.ds(VEC_PLACE + j, 9, stride=6), :] = vec[0:9, columns]
        rest = small[...] + one_small[...] + two_small[...]
        for j in range(3):
            grad_rep[pl.ds(VEC_PLACE + 54 + j, 14, stride=3), :] = rest[0:14, j * LANES : (j + 1) * LANES]
        head_swap.wait_recv()
        top_other.start()
        read = joined(head_own, head_other)

        def put(first, value):
            rows = value.shape[0]
            for j in range(12):
                grad_rep[pl.ds(first * 12 + j, rows, stride=12), :] = value[:, j * LANES : (j + 1) * LANES]

        put(0, read(48, 48)[6:])
        for t in range(1, 4):
            put(96 * t - HEAD_TOP, read(96 * t, 96))

    for row in range(3):

        @pl.when(z == row)
        def _():
            refs_of = {QKV: qkv, SQUARE: square, UP: up}
            for name, count, place in TEN_PLACES[row]:
                spread_rows(grad_ten, place, PIECES[name][1] // LANES, count, plain(refs_of[name]))
            patch_swap.wait_recv()
            spread_rows(grad_rep, 0, 6, PATCH_COUNTS[row], joined(patch, patch_other))
            if row == 2:
                e2d_swap.wait_recv()
                for half in range(2):

                    def read(first, rows):
                        one, two = e2d[pl.ds(first, rows)].astype(FLOAT), e2d_other[pl.ds(first, rows)].astype(FLOAT)
                        return jnp.where(x == half, one, two)

                    spread_rows(grad_rep, E2D_PLACE + half * 1152, 3, 384, read)
                top_own.wait_recv()
                top_other.wait_recv()
                spread_rows(grad_rep, HEAD_PLACE, 12, HEAD_TOP, joined(head_own, head_other))

    def square_sum(flat, step):
        def body(t, carry):
            value = flat[pl.ds(pl.multiple_of(t * step, 8), step), :]
            return carry + jnp.sum((value * value).reshape(step // 8, 8, LANES), 0)

        return jnp.sum(lax.fori_loop(0, flat.shape[0] // step, body, jnp.zeros((8, LANES), FLOAT)))

    squares = square_sum(grad_ten, 360) + square_sum(grad_rep, 312) * 0.5
    line = lax.broadcasted_iota(jnp.int32, (8, LANES), 0)
    slots[me] = jnp.where(line == 0, squares, stats[...])
    shares = [links.copy(4 + shift, slots.at[me], slots.at[me], peer(shift)) for shift in range(1, 8)]
    for one in shares:
        one.start()
    for one in shares:
        one.wait()
    whole = slots[0]
    for i in range(1, 8):
        whole = whole + slots[i]
    square_all, loss_all, count_all = whole[0:1], whole[1:2], whole[2:3]
    norm = jnp.sqrt(square_all + 1e-30) / count_all
    factor = jnp.minimum(1.0, CLIP / norm) / count_all
    stats_out[...] = jnp.where(line == 0, norm, whole)
    for one in loads:
        one.wait()

    def adam(master, first, second, grad, step):
        def body(t, carry):
            at = pl.ds(pl.multiple_of(t * step, 8), step)
            new = adamw(master[at, :], first[at, :], second[at, :], grad[at, :] * factor, number)
            master[at, :], first[at, :], second[at, :] = new
            return carry

        lax.fori_loop(0, master.shape[0] // step, body, 0)

    stores = [pltpu.make_async_copy(held[i], outs[i], local_sem.at[i]) for i in range(6)]
    adam(*held[:3], grad_ten, 240)
    for one in stores[:3]:
        one.start()
    adam(*held[3:], grad_rep, 312)
    for one in stores[3:]:
        one.start()
    if not last:
        lay_out(z, x, held[0], held[3], pieces, wide_rows)

    @pl.when(z < LAST)
    def _():
        patch_swap.wait_send()

    @pl.when(z == 2)
    def _():
        e2d_swap.wait_send()

    @pl.when(z == LAST)
    def _():
        head_swap.wait_send()
        top_own.wait_send()
        top_other.wait_send()

    for one in stores:
        one.wait()


def update(identity, number, last, stats, gradients, states):
    vmem = pl.BlockSpec(memory_space=pltpu.VMEM)
    anywhere = pl.BlockSpec(memory_space=pl.ANY)
    laid = [] if last else LAID
    flat = [(TEN_LANES, LANES)] * 3 + [(REP_LANES, LANES)] * 3
    scratch = [(one, FLOAT) for one in flat + [(TEN_LANES, LANES), (REP_LANES, LANES), (5, 384, LANES)]] + [
        ((704, D // 2), HALF),
        ((D // 2, DD), HALF),
        ((DD, PATCH // 2), FLOAT),
        ((DD, PATCH // 2), FLOAT),
        ((8, 8, LANES), FLOAT),
    ]
    out = pl.pallas_call(
        functools.partial(update_kernel, number, last),
        name="update",
        out_shape=[jax.ShapeDtypeStruct((8, LANES), FLOAT)]
        + [jax.ShapeDtypeStruct(one, FLOAT) for one in flat]
        + [jax.ShapeDtypeStruct(LAID_SHAPES[name], HALF) for name in laid],
        in_specs=[vmem] * (1 + len(gradients)) + [anywhere] * 6,
        out_specs=[vmem] + [anywhere] * 6 + [vmem] * len(laid),
        scratch_shapes=[pltpu.VMEM(*one) for one in scratch]
        + [pltpu.SemaphoreType.DMA((12,)), pltpu.SemaphoreType.DMA((12,)), pltpu.SemaphoreType.DMA((6,))],
        compiler_params=pltpu.CompilerParams(
            collective_id=identity, has_side_effects=True, vmem_limit_bytes=61 << 20
        ),
    )(stats, *gradients, *states)
    return out[0], out[1:7], dict(zip(laid, out[7:]))


def decoder_kernel(
    reduced, hot, shown, places, pixels, counted, qkv_own, qkv_oth,
    out_own, out_oth, up_own, up_oth, down_own, down_oth, head_w, vec, head_b,
    picked, wide, tall, qkv_grad, small, loss,
    normed, tokens, q_ref, k_ref, v_ref, parts, parts_got, grad_att, vec_grad, vec_got, head_b_grad,
    blended, blend_other, totals, upward, activated, second, final_low, pred_low, low, grad_up_in, mid, grad_blend,
    blend_sent, head_sent, head_got, wide_sent, wide_got, tall_sent, tall_got, dk_ref, dv_ref, send_sem, recv_sem,
):
    g, z, x = lax.axis_index("group"), lax.axis_index("dp"), lax.axis_index("tensor")
    across = (g, z, 1 - x)
    links = Links(send_sem, recv_sem)
    barrier = pltpu.get_barrier_semaphore()
    pl.semaphore_signal(barrier, inc=1, device_id=across, device_id_type=MESH_ID)
    half = pixels.shape[0]
    width = q_ref.shape[1]
    heads = width // HDIM
    tiles = q_ref.shape[0] // TILE
    fc = DFF // 2
    left = reduced[...] + vec[0:1]
    thirds = []
    for _ in range(3):
        thirds.append(left.astype(HALF))
        left = left - thirds[-1].astype(FLOAT)

    def embed(t, carry):
        rows = pl.ds(pl.multiple_of(t * TILE, TILE), TILE)
        placed = mm(hot[rows], thirds[0]) + mm(hot[rows], thirds[1]) + mm(hot[rows], thirds[2])
        values = jnp.where(shown[rows] > 0.5, placed, vec[1:2]) + places[rows]
        tokens[rows] = values
        low_rows = norm_to(values, vec[2:3], vec[3:4]).astype(HALF)
        normed[rows] = low_rows
        joined = mm(low_rows, qkv_own[...]).astype(HALF)
        q_ref[rows] = joined[:, :width]
        k_ref[rows] = joined[:, width : 2 * width]
        v_ref[rows] = joined[:, 2 * width :]
        return carry

    lax.fori_loop(0, tiles, embed, 0)
    parts[...] = jnp.zeros_like(parts)

    def attend(first, last):
        for h in range(heads):
            cols = slice(h * HDIM, (h + 1) * HDIM)
            keys = k_ref[:, cols] * HALF(HDIM**-0.5)
            turned = v_ref[:, cols].T

            def step(t, carry):
                rows = pl.ds(pl.multiple_of(t * TILE, TILE), TILE)
                scores = mm_nt(keys, q_ref[rows, cols])
                highest = jnp.max(scores, 0, keepdims=True)
                weights = jnp.exp(scores - highest)
                total = jnp.sum(weights, 0, keepdims=True)
                probs = (weights * (1.0 / total)).astype(HALF)
                blended[rows, cols] = mm(turned, probs).T.astype(HALF)
                totals[h, pl.ds(t, 1), :] = highest + jnp.log(total)
                return carry

            lax.fori_loop(first, last, step, 0)

    whole = half // TILE
    attend(whole, tiles)
    pl.semaphore_wait(barrier, 1)
    blend_swap = links.copy(0, blended.at[pl.ds(half, half)], blend_other, across)
    blend_swap.start()
    attend(0, whole)
    vec_grad[...] = jnp.zeros_like(vec_grad)
    head_b_grad[...] = jnp.zeros_like(head_b_grad)
    loss[...] = jnp.zeros_like(loss)
    blend_swap.wait_recv()

    def count(row, value):
        vec_grad[row : row + 1] += value

    grad_swaps = []
    start = 0
    for step, size in enumerate((400, 384)):
        rows = pl.ds(start, size)
        start += size
        attended = mm(blended[rows], out_own[...]) + mm(blend_other[rows], out_oth[...]) + tokens[rows] + vec[4:5]
        second[rows] = norm_to(attended, vec[5:6], vec[6:7]).astype(HALF)
        decoded = attended + vec[7:8]
        for side, (into, back) in enumerate(((up_own, down_own), (up_oth, down_oth))):
            cols = slice(side * fc, (side + 1) * fc)
            up = mm(second[rows], into[...])
            upward[rows, cols] = up
            activated[rows, cols] = gelu_to(up).astype(HALF)
            decoded = decoded + mm(activated[rows, cols], back[...])
        final_low[rows] = norm_to(decoded, vec[8:9], vec[9:10]).astype(HALF)
        differ = mm(final_low[rows], head_w[...]) + head_b[...]
        differ = differ - norm_parts(pixels[rows].astype(FLOAT))[0]
        share = counted[rows]
        loss[...] += jnp.sum(jnp.mean(differ * differ, -1, keepdims=True) * share)
        grad = (2.0 / PATCH) * differ * share
        head_b_grad[...] += jnp.sum(grad, 0, keepdims=True)
        pred_low[rows] = grad.astype(HALF)
        grad_out, gain, bias = norm_from(decoded, vec[8:9], mm_nt(pred_low[rows], head_w[...]))
        count(8, gain)
        count(9, bias)
        count(7, jnp.sum(grad_out, 0, keepdims=True))
        low[rows] = grad_out.astype(HALF)
        grad_second = jnp.zeros((size, DD), FLOAT)
        for side, (into, back) in enumerate(((up_own, down_own), (up_oth, down_oth))):
            cols = slice(side * fc, (side + 1) * fc)
            slope = gelu_slope(upward[rows, cols])
            grad_up_in[rows, cols] = (mm_nt(low[rows], back[...]) * slope).astype(HALF)
            grad_second = grad_second + mm_nt(grad_up_in[rows, cols], into[...])
        grad, gain, bias = norm_from(attended, vec[5:6], grad_second)
        count(5, gain)
        count(6, bias)
        grad = grad + grad_out
        count(4, jnp.sum(grad, 0, keepdims=True))
        grad_att[rows] = grad
        mid[rows] = grad.astype(HALF)
        grad_blend[rows] = mm_nt(mid[rows], out_own[...]).astype(HALF)
        blend_sent[rows] = mm_nt(mid[rows], out_oth[...]).astype(HALF)
        swap_rows = pl.ds(half + start - size, size)
        grad_swaps.append(links.copy(1 + step, blend_sent.at[rows], grad_blend.at[swap_rows], across))
        grad_swaps[-1].start()
    mine = pl.ds(pl.multiple_of(x * fc, LANES), fc)
    theirs = pl.ds(pl.multiple_of((1 - x) * fc, LANES), fc)
    head_sent[...] = mm_tn(final_low[...], pred_low[:, theirs])
    head_swap = links.copy(12, head_sent, head_got, across)
    head_swap.start()
    wide_sent[...] = mm_tn(second[...], grad_up_in[:, fc:]).astype(HALF)
    wide_swap = links.copy(3, wide_sent, wide_got, across)
    wide_swap.start()
    tall_sent[:fc] = mm_tn(activated[:, fc:], low[...]).astype(HALF)
    tall_sent[fc:] = mm_tn(blend_other[...], mid[...]).astype(HALF)
    tall_swap = links.copy(4, tall_sent, tall_got, across)
    tall_swap.start()
    wide[:, :fc] = mm_tn(second[...], grad_up_in[:, :fc])
    wide[:, fc:] = mm_tn(final_low[...], pred_low[:, mine])
    tall[:fc] = mm_tn(activated[:, :fc], low[...])
    tall[fc:] = mm_tn(blended[pl.ds(0, half)], mid[...])
    for one in grad_swaps:
        one.wait_recv()
    part_swaps = []

    def send_parts(block):
        for third in range(3):
            cols = pl.ds(256 * third + 128 * block, 128)
            one = links.copy(5 + 3 * block + third, parts.at[pl.ds(half, half), cols], parts_got.at[:, cols], across)
            one.start()
            part_swaps.append(one)

    for h in range(heads):
        cols = slice(h * HDIM, (h + 1) * HDIM)
        keys = k_ref[:, cols] * HALF(HDIM**-0.5)
        values = v_ref[:, cols]
        turned = keys.T
        dk_ref[...] = jnp.zeros_like(dk_ref)
        dv_ref[...] = jnp.zeros_like(dv_ref)

        def back_step(t, carry):
            rows = pl.ds(pl.multiple_of(t * TILE, TILE), TILE)
            queries, grads = q_ref[rows, cols], grad_blend[rows, cols]
            probs = jnp.exp(mm_nt(keys, queries) - totals[h, pl.ds(t, 1), :])
            dv_ref[...] += mm(probs.astype(HALF), grads)
            grad_probs = mm_nt(values, grads)
            grad_scores = (probs * (grad_probs - jnp.sum(probs * grad_probs, 0, keepdims=True))).astype(HALF)
            dk_ref[...] += mm(grad_scores, queries)
            parts[rows, cols] = mm(turned, grad_scores).T.astype(HALF)
            return carry

        lax.fori_loop(0, tiles, back_step, 0)
        parts[:, 256 + h * HDIM : 256 + (h + 1) * HDIM] = (dk_ref[...] * HDIM**-0.5).astype(HALF)
        parts[:, 512 + h * HDIM : 512 + (h + 1) * HDIM] = dv_ref[...].astype(HALF)
        if h == 1:
            send_parts(0)
    send_parts(1)

    def back(ref, rows, weights):
        total = jnp.zeros((half, DD), FLOAT)
        for third in range(3):
            columns = ref[rows, 256 * third : 256 * third + width]
            total = total + mm_nt(columns, weights[:, third * width : (third + 1) * width])
        return total

    own_rows_ = pl.ds(0, half)
    grad_normed = back(parts, own_rows_, qkv_own)
    product = mm_tn(normed[...], parts[...])
    for third in range(3):
        qkv_grad[:, third * width : (third + 1) * width] = product[:, 256 * third : 256 * third + width]
    head_swap.wait_recv()
    wide[:, fc:] += head_got[...]
    wide_swap.wait_recv()
    wide[:, :fc] += wide_got[...].astype(FLOAT)
    tall_swap.wait_recv()
    tall[...] += tall_got[...].astype(FLOAT)
    for one in part_swaps:
        one.wait_recv()
    grad_normed = grad_normed + back(parts_got, own_rows_, qkv_oth)
    grad, gain, bias = norm_from(tokens[own_rows_], vec[2:3], grad_normed)
    count(2, gain)
    count(3, bias)
    grad = grad + grad_att[...]
    seen = jnp.where(shown[own_rows_] > 0.5, grad, 0.0)
    count(0, jnp.sum(seen, 0, keepdims=True))
    count(1, jnp.sum(grad - seen, 0, keepdims=True))
    for i in range(PATCH // DD):
        count(10 + i, head_b_grad[:, i * DD : (i + 1) * DD])
    vec_swap = links.copy(11, vec_grad, vec_got, across)
    vec_swap.start()
    picked[...] = mm_tn(hot[own_rows_], grad.astype(HALF)).astype(HALF)
    vec_swap.wait_recv()
    small[...] = vec_grad[...] + vec_got[...]
    for one in [blend_swap, head_swap, wide_swap, tall_swap, vec_swap] + grad_swaps + part_swaps:
        one.wait_send()


def decoder_round(number, reduced, hot, shown, places, pixels_low, counted, weights):
    own, other, head_w, vec, head_b = weights
    count, rows, width = pixels_low.shape[0], hot.shape[0], DD // 2
    vmem = pl.BlockSpec(memory_space=pltpu.VMEM)
    shapes = [
        ((VISIBLE, DD), HALF),
        ((DD, DFF // 2 + PATCH // 2), FLOAT),
        ((DFF // 2 + width, DD), FLOAT),
        ((DD, 3 * width), FLOAT),
        ((16, DD), FLOAT),
        ((8, LANES), FLOAT),
    ]
    scratch = [
        ((rows, DD), HALF),
        ((rows, DD), FLOAT),
        ((rows, width), HALF),
        ((rows, width), HALF),
        ((rows, width), HALF),
        ((rows, 768), HALF),
        ((count, 768), HALF),
        ((count, DD), FLOAT),
        ((16, DD), FLOAT),
        ((16, DD), FLOAT),
        ((1, PATCH), FLOAT),
        ((rows, width), HALF),
        ((count, width), HALF),
        ((width // HDIM, rows // TILE, TILE), FLOAT),
        ((count, DFF), FLOAT),
        ((count, DFF), HALF),
        ((count, DD), HALF),
        ((count, DD), HALF),
        ((count, PATCH), HALF),
        ((count, DD), HALF),
        ((count, DFF), HALF),
        ((count, DD), HALF),
        ((rows, width), HALF),
        ((count, width), HALF),
        ((DD, PATCH // 2), FLOAT),
        ((DD, PATCH // 2), FLOAT),
        ((DD, DFF // 2), HALF),
        ((DD, DFF // 2), HALF),
        ((DFF // 2 + width, DD), HALF),
        ((DFF // 2 + width, DD), HALF),
        ((rows, HDIM), FLOAT),
        ((rows, HDIM), FLOAT),
    ]
    return pl.pallas_call(
        decoder_kernel,
        name="decoder",
        out_shape=[jax.ShapeDtypeStruct(*one) for one in shapes],
        in_specs=[vmem] * 17,
        out_specs=[vmem] * len(shapes),
        scratch_shapes=[pltpu.VMEM(*one) for one in scratch]
        + [pltpu.SemaphoreType.DMA((13,)), pltpu.SemaphoreType.DMA((13,))],
        compiler_params=pltpu.CompilerParams(
            collective_id=number, has_side_effects=True, vmem_limit_bytes=60 << 20
        ),
    )(
        reduced,
        hot,
        shown,
        places,
        pixels_low,
        counted[:, None],
        own[0],
        other[0],
        own[1],
        other[1],
        own[2],
        other[2],
        own[3],
        other[3],
        head_w,
        jnp.pad(vec, ((0, 6), (0, 0))),
        head_b[None],
    )


def hosted_round(
    patches,
    visible,
    frames_valid,
    clip_valid,
    rep_weights,
    ten_weights,
    rep_m,
    rep_v,
    ten_m,
    ten_v,
    rep_outer,
    ten_outer,
):
    side = lax.axis_index("tensor")
    z = lax.axis_index("dp")
    half_rows = TUBES // 2
    tube_ids = (jnp.arange(TUBES) + side * half_rows) % TUBES
    ids_one = hop(visible[:, 0, 0], ((0, 0), (HOST, 0)), ((2, 1), (HOST, 1)))
    ids_two = hop(visible[:, 0, 0], ((3, 1), (HOST, 1)))
    ids_two = jnp.where(side == 0, visible[:, 0, 0], ids_two)
    dec_table = sinus_all(DD)
    places = []
    for part in sinus_parts(D):
        part = jnp.pad(part, ((0, -part.shape[0] % 64), (0, 0)))
        places.append(jnp.stack(thirds_of(part)))
    dec_places = jnp.where(side == 0, dec_table, jnp.roll(dec_table, -half_rows, 0))
    states = [one.reshape(TEN_LANES, LANES) for one in (ten_weights, ten_m, ten_v)]
    states = states + [one.reshape(REP_LANES, LANES) for one in (rep_weights, rep_m, rep_v)]
    starts = states[0], states[3]
    pieces = first_pieces(*starts)
    rep_quarter = rep_weights.shape[0]
    source, target = jnp.arange(PATCH)[:, None], jnp.arange(WIDE)[None, :]
    cut = rep_quarter // D
    moved = lax.optimization_barrier(source + (SPAN[1] - cut) * (source // cut))
    layout = (target == moved).astype(HALF)
    shown_steps = []
    for s in range(STEPS):
        picks = (visible[s, 0, 0][:, None] == jnp.arange(TUBES)[None, :]).astype(HALF)
        rows = mm(picks, patches[s, 0, 0]).astype(HALF)
        rows = mm(rows, layout).astype(HALF)
        one = hop(rows, ((0, 0), (HOST, 0)), ((2, 1), (HOST, 1)))
        two = hop(rows, ((3, 1), (HOST, 1)))
        own = jnp.concatenate([one, jnp.where(side == 0, rows, two)], 0)
        shown_steps.append((own, swap(own, HOST)))
    loss_list, count_list, norm_list = [], [], []
    for s in range(STEPS):
        ids = visible[s, 0, 0]
        picks = tube_ids[:, None] == ids[None, :]
        shown_here = jnp.any(picks, 1)
        counted = (
            jnp.where(shown_here, 0.0, 1.0)
            * (tube_ids // (TUBES // FRAMES) < frames_valid[s, 0, 0])
            * (clip_valid[s, 0, 0] == 1)
        ).astype(FLOAT)[:half_rows]
        shown = shown_steps[s]
        vis = ids.shape[0]
        ids_own = jnp.concatenate([ids_one[s], ids_two[s]])
        reduced_clip, enc_stored, enc_weights, dec_weights = encoder_forward(
            3 + s, s == 0, pieces, shown[0], (ids_own[:, None], *places)
        )
        normed, activated = enc_stored[1], enc_stored[7]
        far = (
            hop_both(normed, (HOST, 0)),
            hop_both(activated, (HOST, 2)),
        )
        pixels_low = lax.dynamic_slice(patches, (s, 0, 0, side * half_rows, 0), (1, 1, 1, half_rows, PATCH))
        pixels_low = pixels_low.reshape(half_rows, PATCH)
        picked, wide, tall, qkv_grad, small, loss = decoder_round(
            9 + s,
            reduced_clip,
            picks.astype(HALF),
            shown_here[:, None].astype(FLOAT),
            dec_places,
            pixels_low,
            counted,
            dec_weights,
        )
        back = encoder_backward(5 + s, picked, shown, enc_weights, enc_stored, (wide, tall, qkv_grad, small), far)
        line = jnp.arange(8)[:, None]
        stats = jnp.where(line == 1, loss[0, 0], jnp.where(line == 2, jnp.sum(counted), 0.0))
        stats = jnp.broadcast_to(stats, (8, LANES))
        stats, states, pieces = update(
            7 + s, STEP_BEFORE + s + 1, s == STEPS - 1, stats, (*back[:6], wide, tall, qkv_grad, small, *back[6:]), states
        )
        norm_list.append(stats[0, 0])
        loss_list.append(stats[1, 0])
        count_list.append(stats[2, 0])
    one = jnp.where(count_list[-1] >= 0, 1.0, 0.0)
    ten_first, ten_second, rep_first, rep_second = [(one * part).reshape(-1) for part in (*states[1:3], *states[4:])]
    ten_diff, rep_diff = [group_mean(starts[i] - states[3 * i]).reshape(-1) for i in range(2)]
    rep_momentum = MOMENTUM * rep_outer + rep_diff
    ten_momentum = MOMENTUM * ten_outer[0] + ten_diff
    rep_new = rep_weights - LR_OUT * (rep_diff + MOMENTUM * rep_momentum)
    ten_new = ten_weights[0] - LR_OUT * (ten_diff + MOMENTUM * ten_momentum)
    return (
        jnp.stack(loss_list)[:, None],
        jnp.stack(count_list)[:, None],
        jnp.stack(norm_list)[:, None],
        rep_first[None],
        rep_second[None],
        ten_first[None, None],
        ten_second[None, None],
        rep_diff,
        ten_diff[None],
        rep_momentum,
        ten_momentum[None],
        rep_new,
        ten_new[None],
    )


def group_mean(diff):
    if lax.axis_size("group") != 4:
        return lax.psum(diff, "group") / lax.axis_size("group")
    odd = lax.axis_index("group") % 2 == 1
    half = diff.shape[0] // 2
    low, high = diff[:half], diff[half:]
    part = jnp.where(odd, high, low) + partner(jnp.where(odd, low, high))
    part_low = lax.optimization_barrier(part.astype(HALF))
    far = lax.ppermute(part_low, "group", [(g, g ^ 2) for g in range(4)])
    total = (part_low.astype(FLOAT) + far.astype(FLOAT)) * 0.25
    other = partner(total)
    return jnp.concatenate([jnp.where(odd, other, total), jnp.where(odd, total, other)])


def solution(mesh):
    placed = (
        P(None, "group", "dp", None, None),
        P(None, "group", "dp", None),
        P(None, "group", "dp"),
        P(None, "group", "dp"),
        P("dp"),
        P("tensor", "dp"),
        P("group", "dp"),
        P("group", "dp"),
        P("group", "tensor", "dp"),
        P("group", "tensor", "dp"),
        P("dp"),
        P("tensor", "dp"),
    )
    return jax.shard_map(
        hosted_round if mesh.shape["dp"] == 4 and mesh.shape["tensor"] == 2 and mesh.shape["group"] % 2 == 0 else on_device,
        mesh=mesh,
        in_specs=placed,
        out_specs=(
            P(None, "group"),
            P(None, "group"),
            P(None, "group"),
            P("group", "dp"),
            P("group", "dp"),
            P("group", "tensor", "dp"),
            P("group", "tensor", "dp"),
            P("dp"),
            P("tensor", "dp"),
            P("dp"),
            P("tensor", "dp"),
            P("dp"),
            P("tensor", "dp"),
        ),
        check_vma=False,
    )
```
